32 devices in a mesh: wide: 8 (over z, x), narrow: 4 (over y, core).
Axes of the slice: x: 2, y: 2, z: 4, core: 2. Of those that a mesh axis runs over, the one named last changes fastest.
Arguments:
- token_ids: int32 [128, 64], P(('wide', 'narrow')), may hold values from 0 to 51199
- targets: int32 [128, 64], P(('wide', 'narrow')), may hold values from -1 to 51199, as said below
- joint_weight: float32 [2304, 768], P('narrow'), may hold values from -0.21875 to 0.21875
- output_weight: float32 [768, 768], P('narrow'), may hold values from -0.625 to 0.625
- expand_weight: float32 [3072, 768], P('narrow'), may hold values from -0.21875 to 0.21875
- reduce_weight: float32 [3072, 768], P('narrow'), may hold values from -0.109375 to 0.109375
- joint_velocity: float32 [2304, 768], P('narrow'), may hold values from -4.5776367e-05 to 4.5776367e-05
- output_velocity: float32 [768, 768], P('narrow'), may hold values from -4.5776367e-05 to 4.5776367e-05
- expand_velocity: float32 [3072, 768], P('narrow'), may hold values from -4.5776367e-05 to 4.5776367e-05
- reduce_velocity: float32 [3072, 768], P('narrow'), may hold values from -4.5776367e-05 to 4.5776367e-05
- embedding: float32 [51200, 768], P(('wide', 'narrow')), may hold values from -0.4330127 to 0.4330127
- embed_moment: float32 [51200, 768], P(('wide', 'narrow')), may hold values from -4.7683716e-06 to 4.7683716e-06
- embed_square: float32 [51200, 768], P(('wide', 'narrow')), may hold values from 5.3810434e-14 to 2.1524174e-13
- positions: float32 [64, 768], replicated, may hold values from -1.75 to 1.75
- position_moment: float32 [64, 768], replicated, may hold values from -4.7683716e-06 to 4.7683716e-06
- position_square: float32 [64, 768], replicated, may hold values from 5.3810434e-14 to 2.1524174e-13
- norm_gains: float32 [3, 768], replicated, may hold values from 0.5 to 1.5
- gain_moment: float32 [3, 768], replicated, may hold values from -4.5776367e-05 to 4.5776367e-05
- gain_square: float32 [3, 768], replicated, may hold values from 5.3810433e-12 to 2.1524173e-11
- biases: float32 [8448], replicated, may hold values from -0.625 to 0.625
- bias_moment: float32 [8448], replicated, may hold values from -4.5776367e-05 to 4.5776367e-05
- bias_square: float32 [8448], replicated, may hold values from 5.3810433e-12 to 2.1524173e-11
Outputs:
- loss_sum: float32 [], replicated
- loss_count: float32 [], replicated
- grad_norm: float32 [], replicated
- joint_next: float32 [2304, 768], P('narrow')
- output_next: float32 [768, 768], P('narrow')
- expand_next: float32 [3072, 768], P('narrow')
- reduce_next: float32 [3072, 768], P('narrow')
- joint_carried: float32 [2304, 768], P('narrow')
- output_carried: float32 [768, 768], P('narrow')
- expand_carried: float32 [3072, 768], P('narrow')
- reduce_carried: float32 [3072, 768], P('narrow')
- embed_next: float32 [51200, 768], P(('wide', 'narrow'))
- embed_moments: float32 [51200, 768], P(('wide', 'narrow'))
- embed_squares: float32 [51200, 768], P(('wide', 'narrow'))
- position_next: float32 [64, 768], replicated
- position_moments: float32 [64, 768], replicated
- position_squares: float32 [64, 768], replicated
- gains_next: float32 [3, 768], replicated
- gain_moments: float32 [3, 768], replicated
- gain_squares: float32 [3, 768], replicated
- biases_next: float32 [8448], replicated
- bias_moments: float32 [8448], replicated
- bias_squares: float32 [8448], replicated
The draws below stay inside these ranges and needn't reach their ends.
Inputs may be any that keep to these rules, and one draw needn't show every extreme that they name: `targets`: -1 marks a position that does not count; at least one position counts.
All inputs are finite; a program needn't handle non-finite values.
Results may differ from the reference program's by a relative error of at most 0.014.
Values may be sent and summed in bfloat16 or wider, within the bound.
A program may use at most 320 MiB of HBM per device.

```python
import math
import jax
import jax.numpy as jnp
import numpy as np
from jax import lax

D = 768
HEADS = 12
HEAD = 64
FF = 3072
V = 51200
LENGTH = 64
NS_STEPS = 3
STEP = 10
RANKS_WIDE = 8
RANKS_NARROW = 4
SEQ_DEV = 4
SEQS = 128
NBIAS = 8448
PARAMS = 46459392


def draw_targets(key, part):
    key = jax.random.fold_in(key, 11)
    first_key, second_key = jax.random.split(key)
    span_wide = max(RANKS_WIDE - 1, 1)
    span_narrow = max(RANKS_NARROW - 1, 1)
    device_index = lax.broadcasted_iota(jnp.int32, (SEQS, LENGTH), 0) // SEQ_DEV
    wide_index = device_index // RANKS_NARROW
    narrow_index = device_index % RANKS_NARROW
    rolled = jax.random.randint(first_key, (SEQS, LENGTH), 0, 1000 * span_wide * span_narrow)
    counted = rolled < 100 * (span_wide + 2 * wide_index) * (span_narrow + 2 * narrow_index)
    drawn_ids = jax.random.randint(second_key, (SEQS, LENGTH), 0, V)
    result = jnp.where(counted, drawn_ids, -1)
    return result.at[0, 0].set(-1).at[SEQS - 1, LENGTH - 1].set(V - 1)


def draw_embedding(key, part):
    key = jax.random.fold_in(key, 23)
    shard_rows = V // (RANKS_WIDE * RANKS_NARROW)
    owner = lax.broadcasted_iota(jnp.int32, (V, 1), 0) // shard_rows % RANKS_NARROW
    level = owner.astype(jnp.float32) / max(RANKS_NARROW - 1, 1)
    factor = (1.0 + 2.0 * level) * D ** (-0.5)
    return jnp.clip(jax.random.normal(key, (V, D), jnp.float32), -4.0, 4.0) * factor


def plant(array, key, least, top_value):
    dims = array.shape
    place = [jax.random.randint(jax.random.fold_in(key, axis), (), 0, dims[axis]) for axis in range(len(dims))]
    array = array.at[tuple(place)].set(least)
    longest = dims.index(max(dims))
    place[longest] = (place[longest] + 1) % dims[longest]
    return array.at[tuple(place)].set(top_value)


def shard_levels(key, shape, shards, low, top_value):
    factor_of, own = 1.0, jax.random.fold_in(key, 6)
    for position, blocks in shards:
        steps = jnp.exp(jax.random.uniform(jax.random.fold_in(own, position), (blocks,), jnp.float32, low / len(shards), top_value / len(shards)))
        factor_of = factor_of * jnp.repeat(steps, shape[position] // blocks).reshape([-1 if axis == position else 1 for axis in range(len(shape))])
    return factor_of


def rank_table(count, skew):
    portions = [(1 << 20) // math.isqrt(standing ** skew) + 1 for standing in range(1, count + 1)]
    deviation = 1 + sum(portions) // (1 << 30)
    return np.cumsum(np.array([max(1, weight // deviation) for weight in portions]))


def ranked_ids(own_key, shape, amount, skew):
    table = rank_table(amount, skew)
    ticket = jax.random.randint(jax.random.fold_in(own_key, 1), shape, 0, int(table[amount - 1]))
    rank = jnp.searchsorted(jnp.asarray(table, jnp.int32), ticket, side="right")
    return jax.random.permutation(jax.random.fold_in(own_key, 2), amount)[rank].astype(jnp.int32)


def gaussian(own_key, shape, width, limit, cuts=(), kind=jnp.bfloat16):
    drawn = width * jax.random.normal(own_key, shape, jnp.float32)
    if cuts:
        drawn = drawn * shard_levels(own_key, shape, cuts, -0.22, 0.18)
    return jnp.clip(drawn, -limit, limit).astype(kind)


def setup_inputs(seed: int = 0) -> dict:
    key_of = jax.random.split(jax.random.key(seed), 23)
    return {
        "token_ids": plant(ranked_ids(key_of[0], (SEQS, LENGTH), V, 2), jax.random.fold_in(key_of[0], 3), 0, V - 1).astype(jnp.int32),
        "targets": draw_targets(jax.random.fold_in(key_of[22], 71), 0),
        "joint_weight": gaussian(key_of[2], (3 * D, D), D ** -0.5, 0.21875, ((0, 4),), jnp.float32),
        "output_weight": gaussian(key_of[3], (D, D), (D // 8) ** -0.5, 0.625, ((0, 4),), jnp.float32),
        "expand_weight": gaussian(key_of[4], (FF, D), D ** -0.5, 0.21875, ((0, 4),), jnp.float32),
        "reduce_weight": gaussian(key_of[5], (FF, D), FF ** -0.5, 0.109375, ((0, 4),), jnp.float32),
        "joint_velocity": gaussian(key_of[6], (3 * D, D), (0.05 / PARAMS ** 0.5), 4.57763671875e-05, ((0, 4),), jnp.float32),
        "output_velocity": gaussian(key_of[7], (D, D), (0.05 / PARAMS ** 0.5), 4.57763671875e-05, ((0, 4),), jnp.float32),
        "expand_velocity": gaussian(key_of[8], (FF, D), (0.05 / PARAMS ** 0.5), 4.57763671875e-05, ((0, 4),), jnp.float32),
        "reduce_velocity": gaussian(key_of[9], (FF, D), (0.05 / PARAMS ** 0.5), 4.57763671875e-05, ((0, 4),), jnp.float32),
        "embedding": draw_embedding(jax.random.fold_in(key_of[22], 71), 0),
        "embed_moment": gaussian(key_of[11], (V, D), (0.0055 / PARAMS ** 0.5), 4.76837158203125e-06, ((0, 32),), jnp.float32),
        "embed_square": jnp.clip(jnp.exp(math.log(2.1524173773618954e-13) - 1.3862944 * jax.random.uniform(key_of[12], (V, D), jnp.float32) ** shard_levels(key_of[12], (V, D), ((0, 32),), -0.2, 0.2)), 5.3810434434047386e-14, 2.1524173773618954e-13),
        "positions": gaussian(key_of[13], (LENGTH, D), 0.3, 1.75, (), jnp.float32),
        "position_moment": gaussian(key_of[14], (LENGTH, D), (0.0055 / PARAMS ** 0.5), 4.76837158203125e-06, (), jnp.float32),
        "position_square": jnp.clip(jnp.exp(jax.random.uniform(key_of[15], (LENGTH, D), jnp.float32, math.log(5.3810434434047386e-14), math.log(2.1524173773618954e-13))), 5.3810434434047386e-14, 2.1524173773618954e-13),
        "norm_gains": jnp.clip(1.0 + 0.1 * jax.random.normal(key_of[16], (3, D), jnp.float32), 0.5, 1.5),
        "gain_moment": gaussian(key_of[17], (3, D), (0.055 / PARAMS ** 0.5), 4.57763671875e-05, (), jnp.float32),
        "gain_square": jnp.clip(jnp.exp(jax.random.uniform(key_of[18], (3, D), jnp.float32, math.log(5.3810432672218855e-12), math.log(2.1524173068887542e-11))), 5.3810432672218855e-12, 2.1524173068887542e-11),
        "biases": gaussian(key_of[19], (NBIAS,), 0.1, 0.625, (), jnp.float32),
        "bias_moment": gaussian(key_of[20], (NBIAS,), (0.055 / PARAMS ** 0.5), 4.57763671875e-05, (), jnp.float32),
        "bias_square": jnp.clip(jnp.exp(jax.random.uniform(key_of[21], (NBIAS,), jnp.float32, math.log(5.3810432672218855e-12), math.log(2.1524173068887542e-11))), 5.3810432672218855e-12, 2.1524173068887542e-11),
    }


@jax.custom_vjp
def low(v):
    return lax.optimization_barrier(v.astype(jnp.bfloat16)).astype(jnp.float32)

@jax.custom_vjp
def low_back(v):
    return v

def low_keep(v):
    return (low(v), None)

def low_pass(kept, grad):
    return (grad,)

def back_keep(v):
    return (v, None)

def back_low(kept, grad):
    return (low(grad),)
low.defvjp(low_keep, low_pass)
low_back.defvjp(back_keep, back_low)
HIGH = lax.Precision.HIGHEST
EPS = 1e-05
CLIP = 0.05
MOMENTUM = 0.95
MUON_RATE = 0.5
DECAY = 0.1
BETA_ONE = 0.9
BETA_TWO = 0.999
EMBED_RATE = 0.02
PLACE_RATE = 0.1
SMALL_RATE = 0.2
NS_A = 3.4445
NS_B = -4.775
NS_C = 2.0315

def product(left, right):
    return jnp.dot(left, right, precision=HIGH, preferred_element_type=jnp.float32)

def norm_rows(stream, gain, shift):
    centred = stream - lax.optimization_barrier(jnp.mean(stream, -1, keepdims=True))
    inverse = lax.rsqrt(lax.optimization_barrier(jnp.mean(centred * centred, -1, keepdims=True)) + EPS)
    return centred * inverse * gain + shift

def sequence_loss(params, token_list, target_list):
    joint_w, output_w, expand_w, reduce_w, embedding, positions, norm_gains, biases = params
    seqs = token_list.shape[0]
    table_low = low(embedding)
    stream = (low_back(table_low[token_list]) + positions[None]).reshape(-1, D)
    shifts = biases[:3 * D].reshape(3, D)
    query_b = biases[3 * D:4 * D]
    value_b = biases[4 * D:5 * D]
    output_b = biases[5 * D:6 * D]
    reduce_b = biases[6 * D:7 * D]
    expand_b = biases[7 * D:]
    first_norm = low(norm_rows(stream, norm_gains[0], shifts[0]))
    joint_bias = jnp.concatenate([query_b, jnp.zeros_like(query_b), value_b])
    joint_proj = low(low_back(product(first_norm, low(joint_w).T) + joint_bias))
    heads_all = joint_proj.reshape(seqs, LENGTH, 3, HEADS, HEAD)
    queries, key_heads, values = (heads_all[:, :, 0], heads_all[:, :, 1], heads_all[:, :, 2])
    scores = low_back(jnp.einsum('sqhd,skhd->shqk', queries, key_heads, precision=HIGH) * HEAD ** (-0.5))
    causal = jnp.tril(jnp.ones((LENGTH, LENGTH), dtype=jnp.bool_))
    attn_probs = jax.nn.softmax(jnp.where(causal, scores, -1000000000.0), axis=-1)
    context = low(low_back(jnp.einsum('shqk,skhd->sqhd', low(attn_probs), values, precision=HIGH))).reshape(-1, D)
    stream = stream + low_back(product(context, low(output_w).T) + output_b)
    second_norm = low(norm_rows(stream, norm_gains[1], shifts[1]))
    upward = low_back(product(second_norm, low(expand_w).T) + expand_b)
    active = low(jax.nn.gelu(upward, approximate=True))
    stream = stream + low_back(product(active, low(reduce_w)) + reduce_b)
    final_norm = low(norm_rows(stream, norm_gains[2], shifts[2]))
    logits = low_back(product(final_norm, table_low.T))
    log_totals = jax.nn.logsumexp(logits, axis=-1)
    flat_targets = target_list.reshape(-1)
    picked = jnp.take_along_axis(logits, jnp.maximum(flat_targets, 0)[:, None], axis=1)[:, 0]
    return jnp.sum(jnp.where(flat_targets >= 0, log_totals - picked, 0.0))

def orthogonal(moment):
    gram_sum = product(moment.T, moment)
    magnitude = jnp.sqrt(jnp.trace(gram_sum)) + 1e-07
    current = moment / magnitude
    square_form = gram_sum / (magnitude * magnitude)
    for cycle_no in range(NS_STEPS):
        if cycle_no > 0:
            square_form = product(current.T, current)
        current = NS_A * current + product(current, NS_B * square_form + NS_C * product(square_form, square_form))
    return current

def adam_step(weight, moment, square, gradient, rate, decay):
    moment = BETA_ONE * moment + (1 - BETA_ONE) * gradient
    square = BETA_TWO * square + (1 - BETA_TWO) * gradient * gradient
    unbiased = moment / (1 - BETA_ONE ** STEP)
    spread = square / (1 - BETA_TWO ** STEP)
    return (weight - rate * (unbiased / (jnp.sqrt(spread) + 1e-08) + decay * weight), moment, square)

def reference(token_ids, targets, joint_weight, output_weight, expand_weight, reduce_weight, joint_velocity, output_velocity, expand_velocity, reduce_velocity, embedding, embed_moment, embed_square, positions, position_moment, position_square, norm_gains, gain_moment, gain_square, biases, bias_moment, bias_square):
    params = (joint_weight, output_weight, expand_weight, reduce_weight, embedding, positions, norm_gains, biases)
    blocks = token_ids.shape[0] // SEQ_DEV
    id_blocks = token_ids.reshape(blocks, SEQ_DEV, LENGTH)
    target_blocks = targets.reshape(blocks, SEQ_DEV, LENGTH)

    def total_loss(weights):
        piece_loss = jax.checkpoint(sequence_loss)

        def step_fn(running, id_pair):
            return (running + piece_loss(weights, id_pair[0], id_pair[1]), None)
        result, _ = lax.scan(step_fn, jnp.zeros((), jnp.float32), (id_blocks, target_blocks))
        return result
    loss_sum, pullback = jax.vjp(total_loss, params)
    gradients = pullback(jnp.ones((), jnp.float32))[0]
    loss_count = jnp.sum((targets >= 0).astype(jnp.float32))
    squares = sum((jnp.sum(gradient * gradient) for gradient in gradients))
    grad_norm = jnp.sqrt(squares) / loss_count
    factor = jnp.minimum(1.0, CLIP / (grad_norm + 1e-06)) / loss_count
    clipped = [gradient * factor for gradient in gradients]
    masters = (joint_weight, output_weight, expand_weight, reduce_weight)
    previous = (joint_velocity, output_velocity, expand_velocity, reduce_velocity)
    updated = []
    carried = []
    for master, before, gradient in zip(masters, previous, clipped[:4]):
        moment = MOMENTUM * before + gradient
        shape_factor = math.sqrt(max(1.0, master.shape[0] / master.shape[1]))
        updated.append(master * (1 - MUON_RATE * DECAY) - MUON_RATE * shape_factor * orthogonal(moment))
        carried.append(moment)
    table_out = adam_step(embedding, embed_moment, embed_square, clipped[4], EMBED_RATE, DECAY)
    place_out = adam_step(positions, position_moment, position_square, clipped[5], PLACE_RATE, DECAY)
    gain_out = adam_step(norm_gains, gain_moment, gain_square, clipped[6], SMALL_RATE, 0.0)
    bias_out = adam_step(biases, bias_moment, bias_square, clipped[7], SMALL_RATE, 0.0)
    return (loss_sum, loss_count, grad_norm, updated[0], updated[1], updated[2], updated[3], carried[0], carried[1], carried[2], carried[3], table_out[0], table_out[1], table_out[2], place_out[0], place_out[1], place_out[2], gain_out[0], gain_out[1], gain_out[2], bias_out[0], bias_out[1], bias_out[2])
```

```python
import math

import jax
import jax.numpy as jnp
from jax import lax
from jax.sharding import PartitionSpec as P

HEADS = 12
HEAD = 64
LENGTH = 64
NS_STEPS = 3
STEP = 10


HIGH = lax.Precision.HIGHEST
EPS = 1e-05
CLIP = 0.05
MOMENTUM = 0.95
MUON_RATE = 0.5
DECAY = 0.1
BETA_ONE = 0.9
BETA_TWO = 0.999
EMBED_RATE = 0.02
PLACE_RATE = 0.1
SMALL_RATE = 0.2
NS_A = 3.4445
NS_B = -4.775
NS_C = 2.0315


def times_t(left, right):
    return lax.dot_general(
        left, right, (((1,), (1,)), ((), ())), preferred_element_type=jnp.float32
    )


def outer_sum(left, right):
    return lax.dot_general(
        left, right, (((0,), (0,)), ((), ())), preferred_element_type=jnp.float32
    )


def plain(left, right):
    return jnp.dot(left, right, preferred_element_type=jnp.float32)


def norm_forward(stream, gain, shift):
    centred = stream - jnp.mean(stream, -1, keepdims=True)
    inverse = lax.rsqrt(jnp.mean(centred * centred, -1, keepdims=True) + EPS)
    normed = centred * inverse
    return (normed * gain + shift, normed, inverse)


def norm_backward(upstream, normed, inverse, gain):
    scaled = upstream * gain
    inner = inverse * (
        scaled
        - jnp.mean(scaled, -1, keepdims=True)
        - normed * jnp.mean(scaled * normed, -1, keepdims=True)
    )
    return (inner, jnp.sum(upstream * normed, 0), jnp.sum(upstream, 0))


def gelu_tanh(values):
    return jax.nn.gelu(values, approximate=True)


def causal_scores(queries, key_heads):
    raw = jnp.einsum(
        "sqhd,skhd->shqk", queries, key_heads, preferred_element_type=jnp.float32
    ) * HEAD ** (-0.5)
    causal = lax.broadcasted_iota(jnp.int32, (LENGTH, LENGTH), 0) >= lax.broadcasted_iota(
        jnp.int32, (LENGTH, LENGTH), 1
    )
    return jnp.where(causal, raw, -1000000000.0)


def layer_forward(stream_in, weights, norm_gains, biases):
    joint_w, output_w, expand_w, reduce_w = weights
    model_width = stream_in.shape[1]
    seqs = stream_in.shape[0] // LENGTH
    shifts = biases[: 3 * model_width].reshape(3, model_width)
    query_b = biases[3 * model_width : 4 * model_width]
    value_b = biases[4 * model_width : 5 * model_width]
    output_b = biases[5 * model_width : 6 * model_width]
    reduce_b = biases[6 * model_width : 7 * model_width]
    expand_b = biases[7 * model_width :]
    first_norm, normed_a, inverse_a = norm_forward(stream_in, norm_gains[0], shifts[0])
    first_low = first_norm.astype(jnp.bfloat16)
    joint_bias = jnp.concatenate([query_b, jnp.zeros_like(query_b), value_b])
    joint_low = (times_t(first_low, joint_w) + joint_bias).astype(jnp.bfloat16)
    heads_all = joint_low.reshape(seqs, LENGTH, 3, HEADS, HEAD)
    queries, key_heads, values = (heads_all[:, :, 0], heads_all[:, :, 1], heads_all[:, :, 2])
    scores = causal_scores(queries, key_heads)
    maxima = jnp.max(scores, -1, keepdims=True)
    log_totals = maxima + jnp.log(jnp.sum(jnp.exp(scores - maxima), -1, keepdims=True))
    attn_probs = jnp.exp(scores - log_totals).astype(jnp.bfloat16)
    context = (
        jnp.einsum("shqk,skhd->sqhd", attn_probs, values, preferred_element_type=jnp.float32)
        .astype(jnp.bfloat16)
        .reshape(-1, model_width)
    )
    stream_mid = stream_in + times_t(context, output_w) + output_b
    second_norm, normed_b, inverse_b = norm_forward(stream_mid, norm_gains[1], shifts[1])
    second_low = second_norm.astype(jnp.bfloat16)
    upward = times_t(second_low, expand_w) + expand_b
    active = gelu_tanh(upward).astype(jnp.bfloat16)
    stream_out = stream_mid + plain(active, reduce_w) + reduce_b
    saved = (
        normed_a,
        inverse_a,
        first_low,
        queries,
        key_heads,
        values,
        log_totals,
        context,
        normed_b,
        inverse_b,
        second_low,
        upward,
        active,
    )
    return (stream_out, saved)


def layer_backward(upstream, weights, norm_gains, saved):
    joint_w, output_w, expand_w, reduce_w = weights
    (
        normed_a,
        inverse_a,
        first_low,
        queries,
        key_heads,
        values,
        log_totals,
        context,
        normed_b,
        inverse_b,
        second_low,
        upward,
        active,
    ) = saved
    model_width = upstream.shape[1]
    down_grad = upstream.astype(jnp.bfloat16)
    reduce_bias_grad = jnp.sum(down_grad.astype(jnp.float32), 0)
    active_grad = times_t(down_grad, reduce_w)
    upward_grad = jax.vjp(gelu_tanh, upward)[1](active_grad)[0].astype(jnp.bfloat16)
    expand_bias_grad = jnp.sum(upward_grad.astype(jnp.float32), 0)
    second_grad = plain(upward_grad, expand_w)
    back_b, gain_b, shift_b = norm_backward(second_grad, normed_b, inverse_b, norm_gains[1])
    mid_grad = upstream + back_b
    attn_grad = mid_grad.astype(jnp.bfloat16)
    output_bias_grad = jnp.sum(attn_grad.astype(jnp.float32), 0)
    context_grad = plain(attn_grad, output_w).astype(jnp.bfloat16).reshape(queries.shape)
    scores = causal_scores(queries, key_heads)
    probs_full = jnp.exp(scores - log_totals)
    probs_low = probs_full.astype(jnp.bfloat16)
    probs_grad = jnp.einsum(
        "sqhd,skhd->shqk", context_grad, values, preferred_element_type=jnp.float32
    )
    values_grad = jnp.einsum(
        "shqk,sqhd->skhd", probs_low, context_grad, preferred_element_type=jnp.float32
    )
    score_grad = (
        probs_full * (probs_grad - jnp.sum(probs_full * probs_grad, -1, keepdims=True))
    ).astype(jnp.bfloat16)
    query_grad = jnp.einsum(
        "shqk,skhd->sqhd", score_grad, key_heads, preferred_element_type=jnp.float32
    ) * HEAD ** (-0.5)
    key_grad = jnp.einsum(
        "shqk,sqhd->skhd", score_grad, queries, preferred_element_type=jnp.float32
    ) * HEAD ** (-0.5)
    joint_grad = (
        jnp.stack([query_grad, key_grad, values_grad], 2)
        .reshape(-1, 3 * model_width)
        .astype(jnp.bfloat16)
    )
    joint_float = joint_grad.astype(jnp.float32)
    query_bias_grad = jnp.sum(joint_float[:, :model_width], 0)
    value_bias_grad = jnp.sum(joint_float[:, 2 * model_width :], 0)
    first_grad = plain(joint_grad, joint_w)
    back_a, gain_a, shift_a = norm_backward(first_grad, normed_a, inverse_a, norm_gains[0])
    stream_grad = mid_grad + back_a
    factors = (
        (joint_grad, first_low),
        (attn_grad, context),
        (upward_grad, second_low),
        (active, down_grad),
    )
    bias_tail = jnp.concatenate(
        [query_bias_grad, value_bias_grad, output_bias_grad, reduce_bias_grad, expand_bias_grad]
    )
    return (stream_grad, factors, (gain_a, gain_b), (shift_a, shift_b), bias_tail)


def adam_step(weight, moment, square, gradient, rate, decay):
    moment = BETA_ONE * moment + (1 - BETA_ONE) * gradient
    square = BETA_TWO * square + (1 - BETA_TWO) * gradient * gradient
    unbiased = moment / (1 - BETA_ONE**STEP)
    spread = square / (1 - BETA_TWO**STEP)
    return (
        weight - rate * (unbiased / (jnp.sqrt(spread) + 1e-08) + decay * weight),
        moment,
        square,
    )


def log_two(size):
    return size.bit_length() - 1


def lanes():
    wide, narrow = lax.axis_size("wide"), lax.axis_size("narrow")
    across = wide // 4
    x_bits = [("wide", 1 << i) for i in range(log_two(across))]
    z_bits = [("wide", across << i) for i in range(log_two(wide // across))]
    y_bits = [("narrow", 2 << i) for i in range(log_two(narrow // 2))]
    return ("narrow", 1), x_bits, y_bits, z_bits


def swap(array, bit):
    axis, mask = bit
    return lax.ppermute(array, axis, [(i, i ^ mask) for i in range(lax.axis_size(axis))])


def side(bit):
    axis, mask = bit
    return (lax.axis_index(axis) // mask) % 2


def join(mine, other, bit, dim=0):
    own = side(bit)
    return jnp.where(
        own == 0, jnp.concatenate([mine, other], dim), jnp.concatenate([other, mine], dim)
    )


def halves(array, bit):
    own = side(bit)
    half = array.shape[0] // 2
    keep = lax.dynamic_slice_in_dim(array, own * half, half)
    send = lax.dynamic_slice_in_dim(array, (1 - own) * half, half)
    return keep, send


def spread_one(array, bits):
    for bit in bits:
        array = jnp.concatenate([array, swap(array, bit)])
    return array


def collect_one(array, bits):
    for bit in reversed(bits):
        half = array.shape[0] // 2
        other = swap(array[half:].astype(jnp.bfloat16), bit)
        array = array[:half].astype(jnp.float32) + other.astype(jnp.float32)
    return array


def routes():
    _, _, y_bits, z_bits = lanes()
    far, near = z_bits[1:], z_bits[:1]
    return (far + near + y_bits, far + y_bits + near)


def cuts(rows):
    first = rows * 5 // 8
    return ((0, first), (first, rows))


def spread(array):
    rows = array.shape[0]
    return jnp.concatenate(
        [spread_one(array[a:b], bits) for (a, b), bits in zip(cuts(rows), routes())]
    )


def collect(array):
    times = 1 << len(routes()[0])
    rows = array.shape[0] // times
    return jnp.concatenate(
        [
            collect_one(array[a * times : b * times], bits)
            for (a, b), bits in zip(cuts(rows), routes())
        ]
    )


def gather_weight(weight):
    core, _, y_bits, z_bits = lanes()
    low = weight.astype(jnp.bfloat16)
    near = z_bits[0]
    rows, width = low.shape
    for index, bit in enumerate(y_bits):
        flat = low.reshape(-1, width)
        keep, _ = halves(flat, near)
        first = swap(keep, bit)
        second = swap(first, near)
        other = join(first, second, near).reshape(low.shape)
        low = join(low, other, bit)
    low = low.reshape(-1, 1, rows, width)
    return join(low, swap(low, core), core, 1).reshape(-1, width)


def all_sum(tree, bits):
    for bit in bits:
        tree = jax.tree.map(lambda a: a + swap(a, bit), tree)
    return tree


def scatter_bits(array, bits):
    for bit in bits:
        keep, send = halves(array, bit)
        array = keep.astype(jnp.float32) + swap(send.astype(jnp.bfloat16), bit).astype(jnp.float32)
    return array


def gather_bits(array, bits):
    for bit in reversed(bits):
        array = join(array, swap(array, bit), bit)
    return array


def reduce_narrow(grad, route):
    core, x_bits, y_bits, z_bits = lanes()
    groups = lax.axis_size("narrow")
    rows, width = grad.shape
    view = grad.reshape(groups // 2, 2, rows // groups, width)
    own = side(core)
    keep = lax.dynamic_index_in_dim(view, own, 1, False)
    send = lax.dynamic_index_in_dim(view, 1 - own, 1, False).astype(jnp.bfloat16)
    part = keep + swap(send, core).astype(jnp.float32)
    wide_bits = []
    for kind in route:
        if kind == "y":
            for bit in reversed(y_bits):
                own = side(bit)
                if wide_bits:
                    part = part
                count = part.shape[0] // 2
                keep = lax.dynamic_slice_in_dim(part, own * count, count)
                send = lax.dynamic_slice_in_dim(part, (1 - own) * count, count)
                part = keep + swap(send.astype(jnp.bfloat16), bit).astype(jnp.float32)
        else:
            bits = {"x": x_bits, "z": z_bits[:1], "f": z_bits[1:]}[kind]
            for bit in bits:
                own = side(bit)
                count = part.shape[1] // 2
                keep = lax.dynamic_slice_in_dim(part, own * count, count, 1)
                send = lax.dynamic_slice_in_dim(part, (1 - own) * count, count, 1)
                part = keep + swap(send.astype(jnp.bfloat16), bit).astype(jnp.float32)
                wide_bits.append(bit)
    return part.reshape(-1, width), wide_bits


def combine_stats(earlier, later):
    maxima = jnp.maximum(earlier[0], later[0])
    totals = earlier[1] * jnp.exp(earlier[0] - maxima) + later[1] * jnp.exp(later[0] - maxima)
    return (maxima, totals, earlier[2] + later[2])


def flipped(array, place, count):
    shape = array.shape
    view = array.reshape((1 << (count - 1 - place), 2, (1 << place), -1) + shape[1:])
    return lax.rev(view, (1,)).reshape(shape)


def merge_stats(stats):
    times = 1 << len(routes()[0])
    tokens = stats.shape[1] // times
    pieces = []
    for (a, b), bits in zip(cuts(tokens), routes()):
        pieces.append((stats[:, a * times : b * times], bits))
    core, _, y_bits, z_bits = lanes()
    for bit in z_bits[::-1] + y_bits:
        whole = jnp.concatenate(
            [
                lax.rev(
                    piece.reshape(
                        3, 1 << (len(bits) - 1 - bits.index(bit)), 2, -1
                    ),
                    (2,),
                ).reshape(3, -1)
                for piece, bits in pieces
            ],
            1,
        )
        other = swap(whole, bit)
        mine = jnp.concatenate([piece for piece, _ in pieces], 1)
        merged = jnp.stack(combine_stats(mine, other))
        edge = pieces[0][0].shape[1]
        pieces = [(merged[:, :edge], pieces[0][1]), (merged[:, edge:], pieces[1][1])]
    return jnp.concatenate([piece for piece, _ in pieces], 1)


def times_high(left, right):
    return jnp.dot(left, right, precision=lax.Precision.HIGH, preferred_element_type=jnp.float32)


def newton_schulz(square_form):
    size = square_form.shape[0]
    diagonal = (
        lax.broadcasted_iota(jnp.int32, (size, size), 0)
        == lax.broadcasted_iota(jnp.int32, (size, size), 1)
    ).astype(jnp.float32)
    total = None
    for cycle_no in range(NS_STEPS):
        rest = NS_B * square_form + NS_C * times_high(square_form, square_form)
        if total is None:
            total, scale = rest, NS_A
        else:
            total = NS_A * total + scale * rest + times_high(total, rest)
            scale = scale * NS_A
        if cycle_no < NS_STEPS - 1:
            half = NS_A * square_form + times_high(square_form, rest)
            square_form = NS_A * half + times_high(half, rest)
    return total


def on_device(
    token_ids,
    targets,
    joint_weight,
    output_weight,
    expand_weight,
    reduce_weight,
    joint_velocity,
    output_velocity,
    expand_velocity,
    reduce_velocity,
    embedding,
    embed_moment,
    embed_square,
    positions,
    position_moment,
    position_square,
    norm_gains,
    gain_moment,
    gain_square,
    biases,
    bias_moment,
    bias_square,
):
    core, x_bits, y_bits, z_bits = lanes()
    groups = lax.axis_size("narrow")
    wides = lax.axis_size("wide")
    across = 1 << len(x_bits)
    model_width = embedding.shape[1]
    shard_rows = embedding.shape[0]
    tokens = token_ids.shape[0] * LENGTH
    shifts = biases[: 3 * model_width].reshape(3, model_width)

    table = embedding.astype(jnp.bfloat16)
    for bit in x_bits:
        table = jnp.concatenate([table, swap(table, bit)])
    table = jnp.concatenate([table, swap(table, core)])
    vocab_here = table.shape[0]

    labels = spread(
        jnp.stack([token_ids.reshape(-1), targets.reshape(-1)], 1)
    )
    ids_group, targets_group = labels[:, 0], labels[:, 1]
    own_block = lax.axis_index("wide") * groups + lax.axis_index("narrow")
    table_mask = groups * (across - 1) + 1

    def locate(token_list):
        block = token_list // shard_rows
        differ = jnp.bitwise_xor(block, own_block)
        is_owned = (token_list >= 0) & (jnp.bitwise_and(differ, ~table_mask) == 0)
        place = (differ % 2) * across + (differ // groups) % across
        return is_owned, jnp.where(is_owned, place * shard_rows + token_list % shard_rows, -1)

    _, rows_ids = locate(ids_group)
    _, rows_targets = locate(targets_group)
    vocab_iota = lax.broadcasted_iota(jnp.int32, (1, vocab_here), 1)
    id_hot = (vocab_iota == rows_ids[:, None]).astype(jnp.bfloat16)
    embedded = collect(plain(id_hot, table).astype(jnp.bfloat16))
    stream_in = embedded + jnp.tile(positions, (token_ids.shape[0], 1))
    masters = (joint_weight, output_weight, expand_weight, reduce_weight)
    weights = tuple(gather_weight(master) for master in masters)
    stream_out, saved = layer_forward(stream_in, weights, norm_gains, biases)
    final_norm, normed_f, inverse_f = norm_forward(stream_out, norm_gains[2], shifts[2])
    group_rows = spread(final_norm.astype(jnp.bfloat16))
    logits = times_t(group_rows, table)
    maxima = jnp.max(logits, -1)
    totals = jnp.sum(jnp.exp(logits - maxima[:, None]), -1)
    target_hot = vocab_iota == rows_targets[:, None]
    picked = jnp.sum(jnp.where(target_hot, logits, 0.0), -1)
    stats = merge_stats(jnp.stack([maxima, totals, picked]))
    log_totals = stats[0] + jnp.log(stats[1])
    counted = targets_group >= 0
    losses = jnp.where(counted, log_totals - stats[2], 0.0)
    loss_part = jnp.sum(losses) / (1 << len(routes()[0]))
    logit_grad = jnp.where(
        counted[:, None],
        jnp.exp(logits - log_totals[:, None]) - target_hot.astype(jnp.float32),
        0.0,
    ).astype(jnp.bfloat16)
    final_grad = collect(plain(logit_grad, table))
    table_grad = outer_sum(logit_grad, group_rows)
    back_f, gain_f, shift_f = norm_backward(final_grad, normed_f, inverse_f, norm_gains[2])
    stream_grad, factors, gain_pair, shift_pair, bias_tail = layer_backward(
        back_f, weights, norm_gains, saved
    )
    rows_grad = spread(stream_grad.astype(jnp.bfloat16))
    table_grad = table_grad + outer_sum(id_hot, rows_grad)
    half = vocab_here // 2
    table_sum = table_grad[:half] + swap(table_grad[half:].astype(jnp.bfloat16), core).astype(
        jnp.float32
    )
    for bit in reversed(x_bits):
        half = table_sum.shape[0] // 2
        table_sum = table_sum[:half] + swap(table_sum[half:].astype(jnp.bfloat16), bit).astype(
            jnp.float32
        )
    position_grad = jnp.sum(stream_grad.reshape(-1, LENGTH, model_width), 0)
    gain_grad = jnp.stack([gain_pair[0], gain_pair[1], gain_f])
    bias_grad = jnp.concatenate([shift_pair[0], shift_pair[1], shift_f, bias_tail])
    scattered = [
        reduce_narrow(outer_sum(left, right), route)
        for (left, right), route in zip(factors, ("zyxf", "zyxf", "xzyf", "yxzf"))
    ]
    squares = sum((jnp.sum(part * part) for part, _ in scattered)) + jnp.sum(table_sum * table_sum)
    matrix_total = [
        gather_bits(part.astype(jnp.bfloat16), bits).astype(jnp.float32)
        for part, bits in scattered
    ]
    count_part = jnp.sum((targets >= 0).astype(jnp.float32))
    every = [core] + x_bits + y_bits + z_bits
    small = jnp.concatenate(
        [gain_grad.reshape(-1), bias_grad, position_grad.reshape(-1)]
    ).reshape(-1, model_width)
    small = all_sum(small, every)
    loss_sum, loss_count, squares = all_sum(jnp.stack([loss_part, count_part, squares]), every)
    squares = squares + jnp.sum(small * small)
    small = small.reshape(-1)
    gain_grad = small[: gain_grad.size].reshape(gain_grad.shape)
    bias_grad = small[gain_grad.size : gain_grad.size + bias_grad.size]
    position_grad = small[gain_grad.size + bias_grad.size :].reshape(position_grad.shape)
    grad_norm = jnp.sqrt(squares) / loss_count
    factor = jnp.minimum(1.0, CLIP / (grad_norm + 1e-06)) / loss_count
    previous = (joint_velocity, output_velocity, expand_velocity, reduce_velocity)
    carried = tuple(
        (MOMENTUM * before + gradient * factor for before, gradient in zip(previous, matrix_total))
    )
    grams = jnp.stack([outer_sum(c.astype(jnp.bfloat16), c.astype(jnp.bfloat16)) for c in carried])
    for bit in reversed(y_bits):
        if bit[1] >= 4:
            grams = grams + swap(grams.astype(jnp.bfloat16), bit).astype(jnp.float32)
    gram_bits = [y_bits[0], core]
    gram_sum = scatter_bits(grams, gram_bits)[0]
    magnitude = jnp.sqrt(jnp.trace(gram_sum)) + 1e-07
    rest = newton_schulz(gram_sum / (magnitude * magnitude))
    rest = (rest / magnitude).astype(jnp.bfloat16)[None]
    rests = gather_bits(rest, gram_bits)
    magnitudes = gather_bits(magnitude[None], gram_bits)
    updated = []
    for number, (master, moment) in enumerate(zip(masters, carried)):
        orth = moment * (NS_A**NS_STEPS / magnitudes[number]) + plain(
            moment.astype(jnp.bfloat16), rests[number]
        )
        shape_factor = math.sqrt(max(1.0, master.shape[0] * groups / master.shape[1]))
        updated.append(master * (1 - MUON_RATE * DECAY) - MUON_RATE * shape_factor * orth)
    table_out = adam_step(
        embedding, embed_moment, embed_square, table_sum * factor, EMBED_RATE, DECAY
    )
    place_out = adam_step(
        positions, position_moment, position_square, position_grad * factor, PLACE_RATE, DECAY
    )
    gain_out = adam_step(norm_gains, gain_moment, gain_square, gain_grad * factor, SMALL_RATE, 0.0)
    bias_out = adam_step(biases, bias_moment, bias_square, bias_grad * factor, SMALL_RATE, 0.0)
    return (
        loss_sum,
        loss_count,
        grad_norm,
        updated[0],
        updated[1],
        updated[2],
        updated[3],
        carried[0],
        carried[1],
        carried[2],
        carried[3],
        table_out[0],
        table_out[1],
        table_out[2],
        place_out[0],
        place_out[1],
        place_out[2],
        gain_out[0],
        gain_out[1],
        gain_out[2],
        bias_out[0],
        bias_out[1],
        bias_out[2],
    )


def solution(mesh):
    in_specs = (
        P(("wide", "narrow"), None),
        P(("wide", "narrow"), None),
        P("narrow", None),
        P("narrow", None),
        P("narrow", None),
        P("narrow", None),
        P("narrow", None),
        P("narrow", None),
        P("narrow", None),
        P("narrow", None),
        P(("wide", "narrow"), None),
        P(("wide", "narrow"), None),
        P(("wide", "narrow"), None),
        P(),
        P(),
        P(),
        P(),
        P(),
        P(),
        P(),
        P(),
        P(),
    )
    out_specs = (
        P(),
        P(),
        P(),
        P("narrow", None),
        P("narrow", None),
        P("narrow", None),
        P("narrow", None),
        P("narrow", None),
        P("narrow", None),
        P("narrow", None),
        P("narrow", None),
        P(("wide", "narrow"), None),
        P(("wide", "narrow"), None),
        P(("wide", "narrow"), None),
        P(),
        P(),
        P(),
        P(),
        P(),
        P(),
        P(),
        P(),
        P(),
    )
    return jax.shard_map(
        on_device, mesh=mesh, in_specs=in_specs, out_specs=out_specs, check_vma=False
    )
```

```python
import functools
import math

import jax
import jax.numpy as jnp
from jax import lax
from jax.experimental import pallas as pl
from jax.experimental.pallas import tpu as pltpu
from jax.sharding import PartitionSpec as P

HEADS = 12
HEAD = 64
LENGTH = 64
NS_STEPS = 3
STEP = 10


HIGH = lax.Precision.HIGHEST
EPS = 1e-05
CLIP = 0.05
MOMENTUM = 0.95
MUON_RATE = 0.5
DECAY = 0.1
BETA_ONE = 0.9
BETA_TWO = 0.999
EMBED_RATE = 0.02
PLACE_RATE = 0.1
SMALL_RATE = 0.2
NS_A = 3.4445
NS_B = -4.775
NS_C = 2.0315
MESH = pl.DeviceIdType.MESH
MIB = 1 << 20
TOKEN_TILE = 256
SLOTS = 16


def times_t(left, right):
    return lax.dot_general(
        left, right, (((1,), (1,)), ((), ())), preferred_element_type=jnp.float32
    )


def outer_sum(left, right):
    return lax.dot_general(
        left, right, (((0,), (0,)), ((), ())), preferred_element_type=jnp.float32
    )


def plain(left, right):
    return jnp.dot(left, right, preferred_element_type=jnp.float32)


def norm_forward(stream, gain, shift):
    centred = stream - jnp.mean(stream, -1, keepdims=True)
    inverse = lax.rsqrt(jnp.mean(centred * centred, -1, keepdims=True) + EPS)
    normed = centred * inverse
    return (normed * gain + shift, normed, inverse)


def norm_backward(upstream, normed, inverse, gain):
    scaled = upstream * gain
    inner = inverse * (
        scaled
        - jnp.mean(scaled, -1, keepdims=True)
        - normed * jnp.mean(scaled * normed, -1, keepdims=True)
    )
    return (inner, jnp.sum(upstream * normed, 0), jnp.sum(upstream, 0))


def gelu_tanh(values):
    return jax.nn.gelu(values, approximate=True)


def causal_scores(queries, key_heads):
    raw = jnp.einsum(
        "sqhd,skhd->shqk", queries, key_heads, preferred_element_type=jnp.float32
    ) * HEAD ** (-0.5)
    causal = lax.broadcasted_iota(jnp.int32, (LENGTH, LENGTH), 0) >= lax.broadcasted_iota(
        jnp.int32, (LENGTH, LENGTH), 1
    )
    return jnp.where(causal, raw, -1000000000.0)


def layer_forward(stream_in, weights, norm_gains, biases):
    joint_w, output_w, expand_w, reduce_w = weights
    model_width = stream_in.shape[1]
    seqs = stream_in.shape[0] // LENGTH
    shifts = biases[: 3 * model_width].reshape(3, model_width)
    query_b = biases[3 * model_width : 4 * model_width]
    value_b = biases[4 * model_width : 5 * model_width]
    output_b = biases[5 * model_width : 6 * model_width]
    reduce_b = biases[6 * model_width : 7 * model_width]
    expand_b = biases[7 * model_width :]
    first_norm, normed_a, inverse_a = norm_forward(stream_in, norm_gains[0], shifts[0])
    first_low = first_norm.astype(jnp.bfloat16)
    joint_bias = jnp.concatenate([query_b, jnp.zeros_like(query_b), value_b])
    joint_low = (times_t(first_low, joint_w) + joint_bias).astype(jnp.bfloat16)
    heads_all = joint_low.reshape(seqs, LENGTH, 3, HEADS, HEAD)
    queries, key_heads, values = (heads_all[:, :, 0], heads_all[:, :, 1], heads_all[:, :, 2])
    scores = causal_scores(queries, key_heads)
    maxima = jnp.max(scores, -1, keepdims=True)
    log_totals = maxima + jnp.log(jnp.sum(jnp.exp(scores - maxima), -1, keepdims=True))
    attn_probs = jnp.exp(scores - log_totals).astype(jnp.bfloat16)
    context = (
        jnp.einsum("shqk,skhd->sqhd", attn_probs, values, preferred_element_type=jnp.float32)
        .astype(jnp.bfloat16)
        .reshape(-1, model_width)
    )
    stream_mid = stream_in + times_t(context, output_w) + output_b
    second_norm, normed_b, inverse_b = norm_forward(stream_mid, norm_gains[1], shifts[1])
    second_low = second_norm.astype(jnp.bfloat16)
    upward = times_t(second_low, expand_w) + expand_b
    active = gelu_tanh(upward).astype(jnp.bfloat16)
    stream_out = stream_mid + plain(active, reduce_w) + reduce_b
    saved = (
        normed_a,
        inverse_a,
        first_low,
        queries,
        key_heads,
        values,
        log_totals,
        context,
        normed_b,
        inverse_b,
        second_low,
        upward,
        active,
    )
    return (stream_out, saved)


def layer_backward(upstream, weights, norm_gains, saved):
    joint_w, output_w, expand_w, reduce_w = weights
    (
        normed_a,
        inverse_a,
        first_low,
        queries,
        key_heads,
        values,
        log_totals,
        context,
        normed_b,
        inverse_b,
        second_low,
        upward,
        active,
    ) = saved
    model_width = upstream.shape[1]
    down_grad = upstream.astype(jnp.bfloat16)
    reduce_bias_grad = jnp.sum(down_grad.astype(jnp.float32), 0)
    active_grad = times_t(down_grad, reduce_w)
    upward_grad = jax.vjp(gelu_tanh, upward)[1](active_grad)[0].astype(jnp.bfloat16)
    expand_bias_grad = jnp.sum(upward_grad.astype(jnp.float32), 0)
    second_grad = plain(upward_grad, expand_w)
    back_b, gain_b, shift_b = norm_backward(second_grad, normed_b, inverse_b, norm_gains[1])
    mid_grad = upstream + back_b
    attn_grad = mid_grad.astype(jnp.bfloat16)
    output_bias_grad = jnp.sum(attn_grad.astype(jnp.float32), 0)
    context_grad = plain(attn_grad, output_w).astype(jnp.bfloat16).reshape(queries.shape)
    scores = causal_scores(queries, key_heads)
    probs_full = jnp.exp(scores - log_totals)
    probs_low = probs_full.astype(jnp.bfloat16)
    probs_grad = jnp.einsum(
        "sqhd,skhd->shqk", context_grad, values, preferred_element_type=jnp.float32
    )
    values_grad = jnp.einsum(
        "shqk,sqhd->skhd", probs_low, context_grad, preferred_element_type=jnp.float32
    )
    score_grad = (
        probs_full * (probs_grad - jnp.sum(probs_full * probs_grad, -1, keepdims=True))
    ).astype(jnp.bfloat16)
    query_grad = jnp.einsum(
        "shqk,skhd->sqhd", score_grad, key_heads, preferred_element_type=jnp.float32
    ) * HEAD ** (-0.5)
    key_grad = jnp.einsum(
        "shqk,sqhd->skhd", score_grad, queries, preferred_element_type=jnp.float32
    ) * HEAD ** (-0.5)
    joint_grad = (
        jnp.stack([query_grad, key_grad, values_grad], 2)
        .reshape(-1, 3 * model_width)
        .astype(jnp.bfloat16)
    )
    joint_float = joint_grad.astype(jnp.float32)
    query_bias_grad = jnp.sum(joint_float[:, :model_width], 0)
    value_bias_grad = jnp.sum(joint_float[:, 2 * model_width :], 0)
    first_grad = plain(joint_grad, joint_w)
    back_a, gain_a, shift_a = norm_backward(first_grad, normed_a, inverse_a, norm_gains[0])
    stream_grad = mid_grad + back_a
    factors = (
        (joint_grad, first_low),
        (attn_grad, context),
        (upward_grad, second_low),
        (active, down_grad),
    )
    bias_tail = jnp.concatenate(
        [query_bias_grad, value_bias_grad, output_bias_grad, reduce_bias_grad, expand_bias_grad]
    )
    return (stream_grad, factors, (gain_a, gain_b), (shift_a, shift_b), bias_tail)


def adam_step(weight, moment, square, gradient, rate, decay):
    moment = BETA_ONE * moment + (1 - BETA_ONE) * gradient
    square = BETA_TWO * square + (1 - BETA_TWO) * gradient * gradient
    unbiased = moment / (1 - BETA_ONE**STEP)
    spread = square / (1 - BETA_TWO**STEP)
    return (
        weight - rate * (unbiased / (jnp.sqrt(spread) + 1e-08) + decay * weight),
        moment,
        square,
    )


def log_two(size):
    return size.bit_length() - 1


def lanes():
    wide, narrow = lax.axis_size("wide"), lax.axis_size("narrow")
    across = wide // 4
    x_bits = [("wide", 1 << i) for i in range(log_two(across))]
    z_bits = [("wide", across << i) for i in range(log_two(wide // across))]
    y_bits = [("narrow", 2 << i) for i in range(log_two(narrow // 2))]
    return ("narrow", 1), x_bits, y_bits, z_bits


def swap(array, bit):
    axis, mask = bit
    return lax.ppermute(array, axis, [(i, i ^ mask) for i in range(lax.axis_size(axis))])


def side(bit):
    axis, mask = bit
    return (lax.axis_index(axis) // mask) % 2


def join(mine, other, bit, dim=0):
    own = side(bit)
    return jnp.where(
        own == 0, jnp.concatenate([mine, other], dim), jnp.concatenate([other, mine], dim)
    )


def halves(array, bit):
    own = side(bit)
    half = array.shape[0] // 2
    keep = lax.dynamic_slice_in_dim(array, own * half, half)
    send = lax.dynamic_slice_in_dim(array, (1 - own) * half, half)
    return keep, send


def spread_one(array, bits):
    for bit in bits:
        array = jnp.concatenate([array, swap(array, bit)])
    return array


def collect_one(array, bits):
    for bit in reversed(bits):
        half = array.shape[0] // 2
        other = swap(array[half:].astype(jnp.bfloat16), bit)
        array = array[:half].astype(jnp.float32) + other.astype(jnp.float32)
    return array


def routes():
    _, _, y_bits, z_bits = lanes()
    far, near = z_bits[1:], z_bits[:1]
    return (far + near + y_bits, far + y_bits + near)


def cuts(rows):
    first = rows * 5 // 8
    return ((0, first), (first, rows))


def spread(array):
    rows = array.shape[0]
    return jnp.concatenate(
        [spread_one(array[a:b], bits) for (a, b), bits in zip(cuts(rows), routes())]
    )


def collect(array):
    times = 1 << len(routes()[0])
    rows = array.shape[0] // times
    return jnp.concatenate(
        [
            collect_one(array[a * times : b * times], bits)
            for (a, b), bits in zip(cuts(rows), routes())
        ]
    )


def gather_weight(weight):
    core, _, y_bits, z_bits = lanes()
    low = weight.astype(jnp.bfloat16)
    near = z_bits[0]
    rows, width = low.shape
    for index, bit in enumerate(y_bits):
        flat = low.reshape(-1, width)
        keep, _ = halves(flat, near)
        first = swap(keep, bit)
        second = swap(first, near)
        other = join(first, second, near).reshape(low.shape)
        low = join(low, other, bit)
    low = low.reshape(-1, 1, rows, width)
    return join(low, swap(low, core), core, 1).reshape(-1, width)


def all_sum(tree, bits):
    for bit in bits:
        tree = jax.tree.map(lambda a: a + swap(a, bit), tree)
    return tree


def scatter_bits(array, bits):
    for bit in bits:
        keep, send = halves(array, bit)
        array = keep.astype(jnp.float32) + swap(send.astype(jnp.bfloat16), bit).astype(jnp.float32)
    return array


def gather_bits(array, bits):
    for bit in reversed(bits):
        array = join(array, swap(array, bit), bit)
    return array


def reduce_narrow(grad, route):
    core, x_bits, y_bits, z_bits = lanes()
    groups = lax.axis_size("narrow")
    rows, width = grad.shape
    view = grad.reshape(groups // 2, 2, rows // groups, width)
    own = side(core)
    keep = lax.dynamic_index_in_dim(view, own, 1, False)
    send = lax.dynamic_index_in_dim(view, 1 - own, 1, False).astype(jnp.bfloat16)
    part = keep + swap(send, core).astype(jnp.float32)
    wide_bits = []
    for kind in route:
        if kind == "y":
            for bit in reversed(y_bits):
                own = side(bit)
                count = part.shape[0] // 2
                keep = lax.dynamic_slice_in_dim(part, own * count, count)
                send = lax.dynamic_slice_in_dim(part, (1 - own) * count, count)
                part = keep + swap(send.astype(jnp.bfloat16), bit).astype(jnp.float32)
        else:
            bits = {"x": x_bits, "z": z_bits[:1], "f": z_bits[1:]}[kind]
            for bit in bits:
                own = side(bit)
                count = part.shape[1] // 2
                keep = lax.dynamic_slice_in_dim(part, own * count, count, 1)
                send = lax.dynamic_slice_in_dim(part, (1 - own) * count, count, 1)
                part = keep + swap(send.astype(jnp.bfloat16), bit).astype(jnp.float32)
                wide_bits.append(bit)
    return part.reshape(-1, width), wide_bits


def group_masks(bits):
    groups = lax.axis_size("narrow")
    masks = [0]
    for axis, mask in bits:
        flat = mask * groups if axis == "wide" else mask
        masks = masks + [other ^ flat for other in masks]
    return masks


def arranged(array):
    tokens = array.shape[1]
    return jnp.concatenate(
        [
            array[jnp.array(group_masks(bits)), a:b].reshape(-1)
            for (a, b), bits in zip(cuts(tokens), routes())
        ]
    )


def flip_index(place, mask, size):
    result = place * 0
    for bit in range(log_two(size)):
        one = (place // (1 << bit)) % 2
        two = (mask // (1 << bit)) % 2
        result = result + (one + two - 2 * one * two) * (1 << bit)
    return result


def exchange_kernel(masks, sizes, whole, x_ref, out_ref, send_sem, recv_sem, own_sem):
    wides, groups = sizes
    wide, narrow = lax.axis_index("wide"), lax.axis_index("narrow")
    count = wides * groups if masks is None else len(masks)

    def peer(mask):
        return (
            flip_index(wide, mask // groups, wides),
            flip_index(narrow, mask % groups, groups),
        )

    def each(step):
        if masks is None:
            lax.fori_loop(1, count, lambda k, carry: (step(k, k), carry)[1], 0)
        else:
            for k in range(1, count):
                step(k, masks[k])

    def copy(k, mask):
        return pltpu.make_async_remote_copy(
            src_ref=x_ref if whole else x_ref.at[k],
            dst_ref=out_ref.at[k],
            send_sem=send_sem.at[k],
            recv_sem=recv_sem.at[k],
            device_id=peer(mask),
            device_id_type=MESH,
        )

    barrier = pltpu.get_barrier_semaphore()
    each(
        lambda k, mask: pl.semaphore_signal(
            barrier, inc=1, device_id=peer(mask), device_id_type=MESH
        )
    )
    pl.semaphore_wait(barrier, count - 1)
    each(lambda k, mask: copy(k, mask).start())
    own = pltpu.make_async_copy(x_ref if whole else x_ref.at[0], out_ref.at[0], own_sem)
    own.start()
    own.wait()
    each(lambda k, mask: copy(k, mask).wait())


def exchange(array, number, name, masks=None, whole=True):
    sizes = (lax.axis_size("wide"), lax.axis_size("narrow"))
    count = sizes[0] * sizes[1] if masks is None else len(masks)
    shape = (count,) + array.shape if whole else array.shape
    return pl.pallas_call(
        functools.partial(exchange_kernel, masks, sizes, whole),
        out_shape=jax.ShapeDtypeStruct(shape, array.dtype),
        in_specs=[pl.BlockSpec(memory_space=pltpu.VMEM)],
        out_specs=pl.BlockSpec(memory_space=pltpu.VMEM),
        scratch_shapes=[
            pltpu.SemaphoreType.DMA((count,)),
            pltpu.SemaphoreType.DMA((count,)),
            pltpu.SemaphoreType.DMA,
        ],
        compiler_params=pltpu.CompilerParams(
            collective_id=number, has_side_effects=True, vmem_limit_bytes=32 * MIB
        ),
        name=name,
    )(array)


def merge_stats(stats):
    masks = group_masks(routes()[0])
    width = stats.shape[1]
    share = exchange(stats.reshape(-1, 128), 1, "stats_share", masks)
    share = share.reshape(len(masks), 3, width)
    times = len(masks)
    tokens = width // times
    pieces = []
    for k, mask in enumerate(masks):
        parts = []
        for (a, b), bits in zip(cuts(tokens), routes()):
            own = group_masks(bits)
            order = [own.index(m ^ mask) for m in own]
            piece = share[k, :, a * times : b * times].reshape(3, times, b - a)
            parts.append(
                jnp.concatenate([piece[:, i] for i in order], 1)
            )
        pieces.append(jnp.concatenate(parts, 1))
    every = jnp.stack(pieces)
    top = jnp.max(every[:, 0], 0)
    total = jnp.sum(every[:, 1] * jnp.exp(every[:, 0] - top), 0)
    return top + jnp.log(total), jnp.sum(every[:, 2], 0)


def score_kernel(rows_ref, table_ref, target_ref, exps_ref, max_ref, sum_ref, pick_ref):
    tile = pl.program_id(0)
    width = table_ref.shape[0]

    @pl.when(tile == 0)
    def _():
        max_ref[...] = jnp.full_like(max_ref, -jnp.inf)
        sum_ref[...] = jnp.zeros_like(sum_ref)
        pick_ref[...] = jnp.zeros_like(pick_ref)

    def step(block, carry):
        rows = pl.ds(pl.multiple_of(block * TOKEN_TILE, TOKEN_TILE), TOKEN_TILE)
        scores = lax.dot_general(
            rows_ref[rows, :],
            table_ref[...],
            (((1,), (1,)), ((), ())),
            preferred_element_type=jnp.float32,
        )
        top = jnp.max(scores, -1, keepdims=True)
        powers = jnp.exp(scores - top)
        exps_ref[rows, :] = powers.astype(jnp.bfloat16)
        total = jnp.sum(powers, -1, keepdims=True)
        columns = lax.broadcasted_iota(jnp.int32, (TOKEN_TILE, width), 1)
        wanted = target_ref[rows, :] - tile * width
        hit = jnp.sum(jnp.where(columns == wanted, scores, 0.0), -1, keepdims=True)
        here = lax.broadcasted_iota(jnp.int32, (TOKEN_TILE, 128), 1) == tile
        max_ref[rows, :] = jnp.where(here, top, max_ref[rows, :])
        sum_ref[rows, :] = jnp.where(here, total, sum_ref[rows, :])
        pick_ref[rows, :] = jnp.where(here, hit, pick_ref[rows, :])
        return carry

    lax.fori_loop(0, rows_ref.shape[0] // TOKEN_TILE, step, 0, unroll=8)


def vocab_tile(vocab):
    return 1280 if vocab % 1280 == 0 else 640


def head_scores(rows, table, targets):
    tokens, model = rows.shape
    vocab = table.shape[0]
    width = vocab_tile(vocab)
    stat = jax.ShapeDtypeStruct((tokens, 128), jnp.float32)
    whole = pl.BlockSpec((tokens, 128), lambda j: (0, 0))
    return pl.pallas_call(
        score_kernel,
        grid=(vocab // width,),
        out_shape=(jax.ShapeDtypeStruct((tokens, vocab), jnp.bfloat16), stat, stat, stat),
        in_specs=[
            pl.BlockSpec((tokens, model), lambda j: (0, 0)),
            pl.BlockSpec((width, model), lambda j: (j, 0)),
            pl.BlockSpec((tokens, 1), lambda j: (0, 0)),
        ],
        out_specs=(pl.BlockSpec((tokens, width), lambda j: (0, j)), whole, whole, whole),
        compiler_params=pltpu.CompilerParams(vmem_limit_bytes=56 * MIB),
        cost_estimate=pl.CostEstimate(
            flops=3 * tokens * vocab * model,
            bytes_accessed=2 * tokens * vocab,
            transcendentals=tokens * vocab,
        ),
        name="head_scores",
    )(rows, table, targets[:, None])


def slope_kernel(exps_ref, scale_ref, target_ref, table_ref, slope_ref, grad_ref, total_ref):
    tile = pl.program_id(0)
    width = table_ref.shape[0]

    @pl.when(tile == 0)
    def _():
        total_ref[...] = jnp.zeros_like(total_ref)

    def step(block, carry):
        rows = pl.ds(pl.multiple_of(block * TOKEN_TILE, TOKEN_TILE), TOKEN_TILE)
        here = lax.broadcasted_iota(jnp.int32, (TOKEN_TILE, 128), 1) == tile
        scale = jnp.sum(jnp.where(here, scale_ref[rows, :], 0.0), -1, keepdims=True)
        columns = lax.broadcasted_iota(jnp.int32, (TOKEN_TILE, width), 1)
        wanted = target_ref[rows, :] - tile * width
        probs = exps_ref[rows, :].astype(jnp.float32) * scale
        slope = jnp.where(columns == wanted, probs - 1.0, probs).astype(jnp.bfloat16)
        slope_ref[rows, :] = slope
        total_ref[rows, :] += jnp.dot(slope, table_ref[...], preferred_element_type=jnp.float32)
        return carry

    lax.fori_loop(0, exps_ref.shape[0] // TOKEN_TILE, step, 0, unroll=8)

    @pl.when(tile == pl.num_programs(0) - 1)
    def _():
        grad_ref[...] = total_ref[...].astype(jnp.bfloat16)


def head_slopes(exps, scale, targets, table):
    tokens, vocab = exps.shape
    model = table.shape[1]
    width = vocab_tile(vocab)
    return pl.pallas_call(
        slope_kernel,
        grid=(vocab // width,),
        out_shape=(
            jax.ShapeDtypeStruct((tokens, vocab), jnp.bfloat16),
            jax.ShapeDtypeStruct((tokens, model), jnp.bfloat16),
        ),
        in_specs=[
            pl.BlockSpec((tokens, width), lambda j: (0, j)),
            pl.BlockSpec((tokens, 128), lambda j: (0, 0)),
            pl.BlockSpec((tokens, 1), lambda j: (0, 0)),
            pl.BlockSpec((width, model), lambda j: (j, 0)),
        ],
        out_specs=(
            pl.BlockSpec((tokens, width), lambda j: (0, j)),
            pl.BlockSpec((tokens, model), lambda j: (0, 0)),
        ),
        scratch_shapes=[pltpu.VMEM((tokens, model), jnp.float32)],
        compiler_params=pltpu.CompilerParams(vmem_limit_bytes=60 * MIB),
        cost_estimate=pl.CostEstimate(
            flops=3 * tokens * vocab * model,
            bytes_accessed=4 * tokens * vocab,
            transcendentals=0,
        ),
        name="head_slopes",
    )(exps, scale, targets[:, None], table)


def one_hot(places, size):
    return (places.reshape(-1, 1) == jnp.arange(size)[None]).astype(jnp.bfloat16)


def token_plan(ids_all, shard_rows, own_block):
    devices, tokens = ids_all.shape
    owner = jnp.bitwise_xor(ids_all // shard_rows, own_block)
    local = ids_all % shard_rows
    row = lax.broadcasted_iota(jnp.int32, (tokens, tokens), 0)
    column = lax.broadcasted_iota(jnp.int32, (tokens, tokens), 1)
    before = column < row
    alike = ids_all[:, :, None] == ids_all[:, None, :]
    first = ~jnp.any(alike & before[None], 2)
    served = first & (owner == 0)
    earlier = before.astype(jnp.bfloat16)
    served_rank = times_t(served.astype(jnp.bfloat16), earlier).astype(jnp.int32)
    own_first = jnp.min(jnp.where(alike[0], column, tokens), 1)
    same_owner = owner[0][:, None] == owner[0][None]
    own_rank = jnp.sum((same_owner & first[0][None] & (column < own_first[:, None])).astype(jnp.int32), 1)
    most = jnp.max(
        jnp.sum(
            (first[:, :, None] & (owner[:, :, None] == jnp.arange(devices)[None, None])).astype(
                jnp.int32
            ),
            1,
        )
    )
    rounds = (most + SLOTS - 1) // SLOTS

    def plan(turn):
        slot = jnp.arange(SLOTS)[None, :, None] + turn * SLOTS
        chosen = served[:, None, :] & (served_rank[:, None, :] == slot)
        slot_rows = jnp.sum(jnp.where(chosen, local[:, None, :] + 1, 0), 2) - 1
        inside = own_rank - turn * SLOTS
        valid = (inside >= 0) & (inside < SLOTS)
        own_slots = jnp.where(valid, owner[0] * SLOTS + inside, -1)
        return one_hot(slot_rows, shard_rows), one_hot(own_slots, devices * SLOTS)

    return plan, rounds


def swap_rows(rows):
    devices = rows.shape[0] // SLOTS
    width = rows.shape[1]
    view = rows.astype(jnp.bfloat16).reshape(devices, SLOTS, width)
    return exchange(view, 2, "token_rows", whole=False).reshape(rows.shape)


def in_rounds(rounds, turn, initial):
    total = initial + turn(0)
    return lax.while_loop(
        lambda state: state[0] < rounds,
        lambda state: (state[0] + 1, state[1] + turn(state[0])),
        (jnp.ones((), jnp.int32), total),
    )[1]


def times_high(left, right):
    return jnp.dot(left, right, precision=lax.Precision.HIGH, preferred_element_type=jnp.float32)


def newton_schulz(square_form):
    size = square_form.shape[0]
    diagonal = (
        lax.broadcasted_iota(jnp.int32, (size, size), 0)
        == lax.broadcasted_iota(jnp.int32, (size, size), 1)
    ).astype(jnp.float32)
    total = None
    for cycle_no in range(NS_STEPS):
        rest = NS_B * square_form + NS_C * times_high(square_form, square_form)
        if total is None:
            total, scale = rest, NS_A
        else:
            total = NS_A * total + scale * rest + times_high(total, rest)
            scale = scale * NS_A
        if cycle_no < NS_STEPS - 1:
            half = NS_A * square_form + times_high(square_form, rest)
            square_form = NS_A * half + times_high(half, rest)
    return total


def on_device(
    token_ids,
    targets,
    joint_weight,
    output_weight,
    expand_weight,
    reduce_weight,
    joint_velocity,
    output_velocity,
    expand_velocity,
    reduce_velocity,
    embedding,
    embed_moment,
    embed_square,
    positions,
    position_moment,
    position_square,
    norm_gains,
    gain_moment,
    gain_square,
    biases,
    bias_moment,
    bias_square,
):
    core, x_bits, y_bits, z_bits = lanes()
    groups = lax.axis_size("narrow")
    wides = lax.axis_size("wide")
    across = 1 << len(x_bits)
    model_width = embedding.shape[1]
    shard_rows = embedding.shape[0]
    tokens = token_ids.shape[0] * LENGTH
    shifts = biases[: 3 * model_width].reshape(3, model_width)

    own_rows = embedding.astype(jnp.bfloat16)
    labels = jnp.concatenate([token_ids.reshape(-1, 128), targets.reshape(-1, 128)])
    spare = -labels.shape[0] % 8
    labels = exchange(jnp.pad(labels, ((0, spare), (0, 0))), 0, "label_share")
    ids_all = labels[:, : tokens // 128].reshape(-1, tokens)
    targets_all = labels[:, tokens // 128 : 2 * tokens // 128].reshape(-1, tokens)
    own_block = lax.axis_index("wide") * groups + lax.axis_index("narrow")
    plan, rounds = token_plan(ids_all, shard_rows, own_block)

    def fetch(turn):
        served, wanted = plan(turn)
        return plain(wanted, swap_rows(plain(served, own_rows)))

    embedded = in_rounds(rounds, fetch, jnp.zeros((tokens, model_width), jnp.float32))

    table = own_rows
    for bit in x_bits:
        table = jnp.concatenate([table, swap(table, bit)])
    table = jnp.concatenate([table, swap(table, core)])
    vocab_here = table.shape[0]

    targets_group = arranged(targets_all)
    table_mask = groups * (across - 1) + 1
    differ = jnp.bitwise_xor(targets_group // shard_rows, own_block)
    is_owned = (targets_group >= 0) & (jnp.bitwise_and(differ, ~table_mask) == 0)
    place = (differ % 2) * across + (differ // groups) % across
    rows_targets = jnp.where(is_owned, place * shard_rows + targets_group % shard_rows, -1)
    stream_in = embedded + jnp.tile(positions, (token_ids.shape[0], 1))
    masters = (joint_weight, output_weight, expand_weight, reduce_weight)
    weights = tuple(gather_weight(master) for master in masters)
    stream_out, saved = layer_forward(stream_in, weights, norm_gains, biases)
    final_norm, normed_f, inverse_f = norm_forward(stream_out, norm_gains[2], shifts[2])
    group_rows = spread(final_norm.astype(jnp.bfloat16))
    exps, maxima, totals, picked = head_scores(group_rows, table, rows_targets)
    top = jnp.max(maxima, -1)
    total = jnp.sum(totals * jnp.exp(maxima - top[:, None]), -1)
    log_totals, picked = merge_stats(jnp.stack([top, total, jnp.sum(picked, -1)]))
    counted = targets_group >= 0
    losses = jnp.where(counted, log_totals - picked, 0.0)
    loss_part = jnp.sum(losses) / len(group_masks(routes()[0]))
    scale = jnp.where(counted[:, None], jnp.exp(maxima - log_totals[:, None]), 0.0)
    slopes, final_part = head_slopes(exps, scale, rows_targets, table)
    half = vocab_here // 2
    other_grad = swap(outer_sum(slopes[:, half:], group_rows).astype(jnp.bfloat16), core)
    table_sum = outer_sum(slopes[:, :half], group_rows) + other_grad.astype(jnp.float32)
    for bit in reversed(x_bits):
        half = table_sum.shape[0] // 2
        table_sum = table_sum[:half] + swap(table_sum[half:].astype(jnp.bfloat16), bit).astype(
            jnp.float32
        )
    final_grad = collect(final_part)
    back_f, gain_f, shift_f = norm_backward(final_grad, normed_f, inverse_f, norm_gains[2])
    stream_grad, factors, gain_pair, shift_pair, bias_tail = layer_backward(
        back_f, weights, norm_gains, saved
    )
    low_grad = stream_grad.astype(jnp.bfloat16)

    def give(turn):
        served, wanted = plan(turn)
        return outer_sum(served, swap_rows(outer_sum(wanted, low_grad)))

    table_sum = in_rounds(rounds, give, table_sum)
    position_grad = jnp.sum(stream_grad.reshape(-1, LENGTH, model_width), 0)
    gain_grad = jnp.stack([gain_pair[0], gain_pair[1], gain_f])
    bias_grad = jnp.concatenate([shift_pair[0], shift_pair[1], shift_f, bias_tail])
    scattered = [
        reduce_narrow(outer_sum(left, right), route)
        for (left, right), route in zip(factors, ("zyxf", "zyxf", "xzyf", "yxzf"))
    ]
    squares = sum((jnp.sum(part * part) for part, _ in scattered)) + jnp.sum(table_sum * table_sum)
    matrix_total = [
        gather_bits(part.astype(jnp.bfloat16), bits).astype(jnp.float32)
        for part, bits in scattered
    ]
    count_part = jnp.sum((targets >= 0).astype(jnp.float32))
    every = [core] + x_bits + y_bits + z_bits
    small = jnp.concatenate(
        [gain_grad.reshape(-1), bias_grad, position_grad.reshape(-1)]
    ).reshape(-1, model_width)
    small = all_sum(small, every)
    scalars = jnp.pad(jnp.stack([loss_part, count_part, squares])[None], ((0, 7), (0, 125)))
    scalars = jnp.sum(exchange(scalars, 3, "scalar_share"), 0)
    loss_sum, loss_count, squares = scalars[0, 0], scalars[0, 1], scalars[0, 2]
    squares = squares + jnp.sum(small * small)
    small = small.reshape(-1)
    gain_grad = small[: gain_grad.size].reshape(gain_grad.shape)
    bias_grad = small[gain_grad.size : gain_grad.size + bias_grad.size]
    position_grad = small[gain_grad.size + bias_grad.size :].reshape(position_grad.shape)
    grad_norm = jnp.sqrt(squares) / loss_count
    factor = jnp.minimum(1.0, CLIP / (grad_norm + 1e-06)) / loss_count
    previous = (joint_velocity, output_velocity, expand_velocity, reduce_velocity)
    carried = tuple(
        (MOMENTUM * before + gradient * factor for before, gradient in zip(previous, matrix_total))
    )
    grams = jnp.stack([outer_sum(c.astype(jnp.bfloat16), c.astype(jnp.bfloat16)) for c in carried])
    for bit in reversed(y_bits):
        if bit[1] >= 4:
            grams = grams + swap(grams.astype(jnp.bfloat16), bit).astype(jnp.float32)
    gram_bits = [core, y_bits[0]]
    gram_sum = scatter_bits(grams, gram_bits)[0]
    magnitude = jnp.sqrt(jnp.trace(gram_sum)) + 1e-07
    rest = newton_schulz(gram_sum / (magnitude * magnitude))
    rest = (rest / magnitude).astype(jnp.bfloat16)[None]
    rests = gather_bits(rest, gram_bits)
    magnitudes = gather_bits(magnitude[None], gram_bits)
    updated = []
    for number, (master, moment) in enumerate(zip(masters, carried)):
        orth = moment * (NS_A**NS_STEPS / magnitudes[number]) + plain(
            moment.astype(jnp.bfloat16), rests[number]
        )
        shape_factor = math.sqrt(max(1.0, master.shape[0] * groups / master.shape[1]))
        updated.append(master * (1 - MUON_RATE * DECAY) - MUON_RATE * shape_factor * orth)
    table_out = adam_step(
        embedding, embed_moment, embed_square, table_sum * factor, EMBED_RATE, DECAY
    )
    place_out = adam_step(
        positions, position_moment, position_square, position_grad * factor, PLACE_RATE, DECAY
    )
    gain_out = adam_step(norm_gains, gain_moment, gain_square, gain_grad * factor, SMALL_RATE, 0.0)
    bias_out = adam_step(biases, bias_moment, bias_square, bias_grad * factor, SMALL_RATE, 0.0)
    return (
        loss_sum,
        loss_count,
        grad_norm,
        updated[0],
        updated[1],
        updated[2],
        updated[3],
        carried[0],
        carried[1],
        carried[2],
        carried[3],
        table_out[0],
        table_out[1],
        table_out[2],
        place_out[0],
        place_out[1],
        place_out[2],
        gain_out[0],
        gain_out[1],
        gain_out[2],
        bias_out[0],
        bias_out[1],
        bias_out[2],
    )


def solution(mesh):
    in_specs = (
        P(("wide", "narrow"), None),
        P(("wide", "narrow"), None),
        P("narrow", None),
        P("narrow", None),
        P("narrow", None),
        P("narrow", None),
        P("narrow", None),
        P("narrow", None),
        P("narrow", None),
        P("narrow", None),
        P(("wide", "narrow"), None),
        P(("wide", "narrow"), None),
        P(("wide", "narrow"), None),
        P(),
        P(),
        P(),
        P(),
        P(),
        P(),
        P(),
        P(),
        P(),
    )
    out_specs = (
        P(),
        P(),
        P(),
        P("narrow", None),
        P("narrow", None),
        P("narrow", None),
        P("narrow", None),
        P("narrow", None),
        P("narrow", None),
        P("narrow", None),
        P("narrow", None),
        P(("wide", "narrow"), None),
        P(("wide", "narrow"), None),
        P(("wide", "narrow"), None),
        P(),
        P(),
        P(),
        P(),
        P(),
        P(),
        P(),
        P(),
        P(),
    )
    return jax.shard_map(
        on_device, mesh=mesh, in_specs=in_specs, out_specs=out_specs, check_vma=False
    )
```

```python
import functools
import math

import jax
import jax.numpy as jnp
from jax import lax
from jax.experimental import pallas as pl
from jax.experimental.pallas import tpu as pltpu
from jax.sharding import PartitionSpec as P

HEADS = 12
HEAD = 64
LENGTH = 64
NS_STEPS = 3
STEP = 10


HIGH = lax.Precision.HIGHEST
EPS = 1e-05
CLIP = 0.05
MOMENTUM = 0.95
MUON_RATE = 0.5
DECAY = 0.1
BETA_ONE = 0.9
BETA_TWO = 0.999
EMBED_RATE = 0.02
PLACE_RATE = 0.1
SMALL_RATE = 0.2
NS_A = 3.4445
NS_B = -4.775
NS_C = 2.0315
MESH = pl.DeviceIdType.MESH
MIB = 1 << 20
TOKEN_TILE = 256
SLOTS = 32


def times_t(left, right):
    return lax.dot_general(
        left, right, (((1,), (1,)), ((), ())), preferred_element_type=jnp.float32
    )


def outer_sum(left, right):
    return lax.dot_general(
        left, right, (((0,), (0,)), ((), ())), preferred_element_type=jnp.float32
    )


def plain(left, right):
    return jnp.dot(left, right, preferred_element_type=jnp.float32)


def norm_forward(stream, gain, shift):
    centred = stream - jnp.mean(stream, -1, keepdims=True)
    inverse = lax.rsqrt(jnp.mean(centred * centred, -1, keepdims=True) + EPS)
    normed = centred * inverse
    return (normed * gain + shift, normed, inverse)


def norm_backward(upstream, normed, inverse, gain):
    scaled = upstream * gain
    inner = inverse * (
        scaled
        - jnp.mean(scaled, -1, keepdims=True)
        - normed * jnp.mean(scaled * normed, -1, keepdims=True)
    )
    return (inner, jnp.sum(upstream * normed, 0), jnp.sum(upstream, 0))


def gelu_tanh(values):
    return jax.nn.gelu(values, approximate=True)


def causal_scores(queries, key_heads):
    raw = jnp.einsum(
        "sqhd,skhd->shqk", queries, key_heads, preferred_element_type=jnp.float32
    ) * HEAD ** (-0.5)
    causal = lax.broadcasted_iota(jnp.int32, (LENGTH, LENGTH), 0) >= lax.broadcasted_iota(
        jnp.int32, (LENGTH, LENGTH), 1
    )
    return jnp.where(causal, raw, -1000000000.0)


def layer_forward(stream_in, weights, norm_gains, biases):
    joint_w, output_w, expand_w, reduce_w = weights
    model_width = stream_in.shape[1]
    seqs = stream_in.shape[0] // LENGTH
    shifts = biases[: 3 * model_width].reshape(3, model_width)
    query_b = biases[3 * model_width : 4 * model_width]
    value_b = biases[4 * model_width : 5 * model_width]
    output_b = biases[5 * model_width : 6 * model_width]
    reduce_b = biases[6 * model_width : 7 * model_width]
    expand_b = biases[7 * model_width :]
    first_norm, normed_a, inverse_a = norm_forward(stream_in, norm_gains[0], shifts[0])
    first_low = first_norm.astype(jnp.bfloat16)
    joint_bias = jnp.concatenate([query_b, jnp.zeros_like(query_b), value_b])
    joint_low = (times_t(first_low, joint_w) + joint_bias).astype(jnp.bfloat16)
    heads_all = joint_low.reshape(seqs, LENGTH, 3, HEADS, HEAD)
    queries, key_heads, values = (heads_all[:, :, 0], heads_all[:, :, 1], heads_all[:, :, 2])
    scores = causal_scores(queries, key_heads)
    maxima = jnp.max(scores, -1, keepdims=True)
    log_totals = maxima + jnp.log(jnp.sum(jnp.exp(scores - maxima), -1, keepdims=True))
    attn_probs = jnp.exp(scores - log_totals).astype(jnp.bfloat16)
    context = (
        jnp.einsum("shqk,skhd->sqhd", attn_probs, values, preferred_element_type=jnp.float32)
        .astype(jnp.bfloat16)
        .reshape(-1, model_width)
    )
    stream_mid = stream_in + times_t(context, output_w) + output_b
    second_norm, normed_b, inverse_b = norm_forward(stream_mid, norm_gains[1], shifts[1])
    second_low = second_norm.astype(jnp.bfloat16)
    upward = times_t(second_low, expand_w) + expand_b
    active = gelu_tanh(upward).astype(jnp.bfloat16)
    stream_out = stream_mid + plain(active, reduce_w) + reduce_b
    saved = (
        normed_a,
        inverse_a,
        first_low,
        queries,
        key_heads,
        values,
        log_totals,
        context,
        normed_b,
        inverse_b,
        second_low,
        upward,
        active,
    )
    return (stream_out, saved)


def layer_backward(upstream, weights, norm_gains, saved):
    joint_w, output_w, expand_w, reduce_w = weights
    (
        normed_a,
        inverse_a,
        first_low,
        queries,
        key_heads,
        values,
        log_totals,
        context,
        normed_b,
        inverse_b,
        second_low,
        upward,
        active,
    ) = saved
    model_width = upstream.shape[1]
    down_grad = upstream.astype(jnp.bfloat16)
    reduce_bias_grad = jnp.sum(down_grad.astype(jnp.float32), 0)
    active_grad = times_t(down_grad, reduce_w)
    upward_grad = jax.vjp(gelu_tanh, upward)[1](active_grad)[0].astype(jnp.bfloat16)
    expand_bias_grad = jnp.sum(upward_grad.astype(jnp.float32), 0)
    second_grad = plain(upward_grad, expand_w)
    back_b, gain_b, shift_b = norm_backward(second_grad, normed_b, inverse_b, norm_gains[1])
    mid_grad = upstream + back_b
    attn_grad = mid_grad.astype(jnp.bfloat16)
    output_bias_grad = jnp.sum(attn_grad.astype(jnp.float32), 0)
    context_grad = plain(attn_grad, output_w).astype(jnp.bfloat16).reshape(queries.shape)
    scores = causal_scores(queries, key_heads)
    probs_full = jnp.exp(scores - log_totals)
    probs_low = probs_full.astype(jnp.bfloat16)
    probs_grad = jnp.einsum(
        "sqhd,skhd->shqk", context_grad, values, preferred_element_type=jnp.float32
    )
    values_grad = jnp.einsum(
        "shqk,sqhd->skhd", probs_low, context_grad, preferred_element_type=jnp.float32
    )
    score_grad = (
        probs_full * (probs_grad - jnp.sum(probs_full * probs_grad, -1, keepdims=True))
    ).astype(jnp.bfloat16)
    query_grad = jnp.einsum(
        "shqk,skhd->sqhd", score_grad, key_heads, preferred_element_type=jnp.float32
    ) * HEAD ** (-0.5)
    key_grad = jnp.einsum(
        "shqk,sqhd->skhd", score_grad, queries, preferred_element_type=jnp.float32
    ) * HEAD ** (-0.5)
    joint_grad = (
        jnp.stack([query_grad, key_grad, values_grad], 2)
        .reshape(-1, 3 * model_width)
        .astype(jnp.bfloat16)
    )
    joint_float = joint_grad.astype(jnp.float32)
    query_bias_grad = jnp.sum(joint_float[:, :model_width], 0)
    value_bias_grad = jnp.sum(joint_float[:, 2 * model_width :], 0)
    first_grad = plain(joint_grad, joint_w)
    back_a, gain_a, shift_a = norm_backward(first_grad, normed_a, inverse_a, norm_gains[0])
    stream_grad = mid_grad + back_a
    factors = (
        (joint_grad, first_low),
        (attn_grad, context),
        (upward_grad, second_low),
        (active, down_grad),
    )
    bias_tail = jnp.concatenate(
        [query_bias_grad, value_bias_grad, output_bias_grad, reduce_bias_grad, expand_bias_grad]
    )
    return (stream_grad, factors, (gain_a, gain_b), (shift_a, shift_b), bias_tail)


def adam_step(weight, moment, square, gradient, rate, decay):
    moment = BETA_ONE * moment + (1 - BETA_ONE) * gradient
    square = BETA_TWO * square + (1 - BETA_TWO) * gradient * gradient
    unbiased = moment / (1 - BETA_ONE**STEP)
    spread = square / (1 - BETA_TWO**STEP)
    return (
        weight - rate * (unbiased / (jnp.sqrt(spread) + 1e-08) + decay * weight),
        moment,
        square,
    )


def log_two(size):
    return size.bit_length() - 1


def lanes():
    wide, narrow = lax.axis_size("wide"), lax.axis_size("narrow")
    across = wide // 4
    x_bits = [("wide", 1 << i) for i in range(log_two(across))]
    z_bits = [("wide", across << i) for i in range(log_two(wide // across))]
    y_bits = [("narrow", 2 << i) for i in range(log_two(narrow // 2))]
    return ("narrow", 1), x_bits, y_bits, z_bits


def swap(array, bit):
    axis, mask = bit
    return lax.ppermute(array, axis, [(i, i ^ mask) for i in range(lax.axis_size(axis))])


def side(bit):
    axis, mask = bit
    return (lax.axis_index(axis) // mask) % 2


def join(mine, other, bit, dim=0):
    own = side(bit)
    return jnp.where(
        own == 0, jnp.concatenate([mine, other], dim), jnp.concatenate([other, mine], dim)
    )


def halves(array, bit):
    own = side(bit)
    half = array.shape[0] // 2
    keep = lax.dynamic_slice_in_dim(array, own * half, half)
    send = lax.dynamic_slice_in_dim(array, (1 - own) * half, half)
    return keep, send


def scatter_bits(array, bits):
    for bit in bits:
        keep, send = halves(array, bit)
        array = keep.astype(jnp.float32) + swap(send.astype(jnp.bfloat16), bit).astype(jnp.float32)
    return array


def gather_bits(array, bits):
    for bit in reversed(bits):
        array = join(array, swap(array, bit), bit)
    return array


def group_bits():
    _, _, y_bits, z_bits = lanes()
    return z_bits + y_bits


def routes(rows, pieces):
    _, _, y_bits, z_bits = lanes()
    near, far = z_bits[:1], z_bits[1:]
    longer = rows * 5 // 8 // pieces
    shorter = rows // pieces - longer
    plan = []
    for piece in range(pieces):
        start = piece * (longer + shorter)
        plan.append((start, longer, far + near + y_bits))
        plan.append((start + longer, shorter, far + y_bits + near))
    return plan


def flat_mask(bit):
    axis, mask = bit
    return mask * lax.axis_size("narrow") if axis == "wide" else mask


def group_masks():
    masks = [0]
    for bit in group_bits():
        masks = masks + [other ^ flat_mask(bit) for other in masks]
    return masks


def neighbour(bit):
    axis, mask = bit
    wide, narrow = lax.axis_index("wide"), lax.axis_index("narrow")
    if axis == "wide":
        return wide + mask * (1 - 2 * ((wide // mask) % 2)), narrow
    return wide, narrow + mask * (1 - 2 * ((narrow // mask) % 2))


def greet(devices):
    barrier = pltpu.get_barrier_semaphore()
    for device in devices:
        pl.semaphore_signal(barrier, inc=1, device_id=device, device_id_type=MESH)
    pl.semaphore_wait(barrier, len(devices))


class Mail:
    def __init__(self, send_sem, recv_sem):
        self.send_sem, self.recv_sem = send_sem, recv_sem
        self.used, self.sent, self.open = 0, [], []

    def post(self, source, target, bit):
        copy = pltpu.make_async_remote_copy(
            src_ref=source,
            dst_ref=target,
            send_sem=self.send_sem.at[self.used],
            recv_sem=self.recv_sem.at[self.used],
            device_id=neighbour(bit),
            device_id_type=MESH,
        )
        copy.start()
        self.used += 1
        self.sent.append(copy)
        self.open.append(copy)
        return copy

    def keep(self, source, target):
        copy = pltpu.make_async_copy(source, target, self.recv_sem.at[self.used])
        copy.start()
        self.used += 1
        self.open.append(copy)
        return copy

    def take(self, copy):
        if any(other is copy for other in self.open):
            self.open = [other for other in self.open if other is not copy]
            if any(other is copy for other in self.sent):
                copy.wait_recv()
            else:
                copy.wait()

    def close(self):
        for copy in list(self.open):
            self.take(copy)
        for copy in self.sent:
            copy.wait_send()


def mail_sems(count):
    return [pltpu.SemaphoreType.DMA((count,)), pltpu.SemaphoreType.DMA((count,))]


def spread_kernel(bits, plan, x_ref, out_ref, send_sem, recv_sem):
    greet([neighbour(bit) for bit in bits])
    mail = Mail(send_sem, recv_sem)
    mail.keep(x_ref, out_ref.at[0])
    held = [{0: None} for _ in plan]
    for stage in range(len(bits)):
        for part, (first, rows, order) in enumerate(plan):
            bit = order[stage]
            step = 1 << bits.index(bit)
            span = pl.ds(first, rows)
            for block in list(held[part]):
                if block:
                    mail.take(held[part][block])
                source = out_ref.at[block, span] if block else x_ref.at[span]
                held[part][block ^ step] = mail.post(source, out_ref.at[block ^ step, span], bit)
    mail.close()


def spread(array):
    bits, plan = group_bits(), routes(array.shape[0], 1)
    count = 1 << len(bits)
    return pl.pallas_call(
        functools.partial(spread_kernel, bits, plan),
        out_shape=jax.ShapeDtypeStruct((count,) + array.shape, array.dtype),
        in_specs=[pl.BlockSpec(memory_space=pltpu.VMEM)],
        out_specs=pl.BlockSpec(memory_space=pl.ANY),
        scratch_shapes=mail_sems(len(plan) * count),
        compiler_params=pltpu.CompilerParams(
            collective_id=4, has_side_effects=True, vmem_limit_bytes=32 * MIB
        ),
        name="rows_spread",
    )(array)


def collect_kernel(bits, plan, x_ref, out_ref, sum_ref, got_ref, send_sem, recv_sem):
    greet([neighbour(bit) for bit in bits])
    mail = Mail(send_sem, recv_sem)
    state = []

    def launch(part, stage):
        first, rows, order = plan[part]
        bit = order[len(bits) - 1 - stage]
        step = 1 << bits.index(bit)
        span = pl.ds(first, rows)
        source = sum_ref if stage else x_ref
        kept = [block for block in state[part]["held"] if not block & step]
        base = (1 << len(bits)) - 2 * len(kept)
        state[part]["held"] = kept
        state[part]["copies"] = [
            (
                block,
                base + place,
                mail.post(source.at[block ^ step, span], got_ref.at[base + place, span], bit),
            )
            for place, block in enumerate(kept)
        ]

    for part in range(len(plan)):
        state.append({"held": list(range(1 << len(bits)))})
        launch(part, 0)
    for stage in range(len(bits)):
        for part, (first, rows, _) in enumerate(plan):
            span = pl.ds(first, rows)
            source = sum_ref if stage else x_ref
            for block, place, copy in state[part]["copies"]:
                mail.take(copy)
                total = source[block, span, :].astype(jnp.float32) + got_ref[
                    place, span, :
                ].astype(jnp.float32)
                if stage == len(bits) - 1:
                    out_ref[span, :] = total
                else:
                    sum_ref[block, span, :] = total.astype(jnp.bfloat16)
            if stage < len(bits) - 1:
                launch(part, stage + 1)
    mail.close()


def collect(array):
    bits, plan = group_bits(), routes(array.shape[1], 2)
    count, rows, width = array.shape
    return pl.pallas_call(
        functools.partial(collect_kernel, bits, plan),
        out_shape=jax.ShapeDtypeStruct((rows, width), jnp.float32),
        in_specs=[pl.BlockSpec(memory_space=pltpu.VMEM)],
        out_specs=pl.BlockSpec(memory_space=pltpu.VMEM),
        scratch_shapes=[
            pltpu.VMEM((count, rows, width), jnp.bfloat16),
            pltpu.VMEM((count - 1, rows, width), jnp.bfloat16),
        ]
        + mail_sems(len(plan) * count),
        compiler_params=pltpu.CompilerParams(
            collective_id=5, has_side_effects=True, vmem_limit_bytes=48 * MIB
        ),
        name="rows_collect",
    )(array)


def chip_sizes():
    wides, groups = lax.axis_size("wide"), lax.axis_size("narrow")
    return wides, groups // 2


def chip_peer(mask, sizes):
    wides, ups = sizes
    wide, narrow = lax.axis_index("wide"), lax.axis_index("narrow")
    up = flip_index(narrow // 2, mask % ups, ups)
    return flip_index(wide, mask // ups, wides), up * 2 + narrow % 2


class Rows:
    def __init__(self, sizes, x_ref, out_ref, send_sem, recv_sem):
        self.sizes, self.x_ref, self.out_ref = sizes, x_ref, out_ref
        self.send_sem, self.recv_sem = send_sem, recv_sem
        self.count = sizes[0] * sizes[1]

    def each(self, step):
        lax.fori_loop(1, self.count, lambda k, carry: (step(k), carry)[1], 0)

    def copy(self, k):
        return pltpu.make_async_remote_copy(
            src_ref=self.x_ref.at[k],
            dst_ref=self.out_ref.at[k],
            send_sem=self.send_sem.at[k],
            recv_sem=self.recv_sem.at[k],
            device_id=chip_peer(k, self.sizes),
            device_id_type=MESH,
        )

    def greet(self, others):
        barrier = pltpu.get_barrier_semaphore()
        self.each(
            lambda k: pl.semaphore_signal(
                barrier, inc=1, device_id=chip_peer(k, self.sizes), device_id_type=MESH
            )
        )
        for device in others:
            pl.semaphore_signal(barrier, inc=1, device_id=device, device_id_type=MESH)
        pl.semaphore_wait(barrier, self.count - 1 + len(others))

    def start(self):
        self.each(lambda k: self.copy(k).start())

    def own(self):
        return pltpu.make_async_copy(self.x_ref.at[0], self.out_ref.at[0], self.recv_sem.at[0])


def swap_rows_kernel(sizes, x_ref, out_ref, send_sem, recv_sem):
    rows = Rows(sizes, x_ref, out_ref, send_sem, recv_sem)
    rows.greet([])
    rows.start()
    own = rows.own()
    own.start()
    own.wait()
    rows.each(lambda k: rows.copy(k).wait())


def swap_rows(rows):
    sizes = chip_sizes()
    count = sizes[0] * sizes[1]
    return pl.pallas_call(
        functools.partial(swap_rows_kernel, sizes),
        out_shape=jax.ShapeDtypeStruct(rows.shape, rows.dtype),
        in_specs=[pl.BlockSpec(memory_space=pltpu.VMEM)],
        out_specs=pl.BlockSpec(memory_space=pl.ANY),
        scratch_shapes=mail_sems(count),
        compiler_params=pltpu.CompilerParams(collective_id=2, has_side_effects=True),
        name="token_rows",
    )(rows)


def load_kernel(sizes, lane_bits, *refs):
    core, x_bits, y_bits, z_bits = lane_bits
    near = z_bits[0]
    table_ref, weight_refs, rows_ref = refs[0], refs[1:5], refs[5]
    table_out, weight_outs, rows_out = refs[6], refs[7:11], refs[11]
    send_sem, recv_sem, rows_send, rows_recv, pass_send, pass_recv = refs[12:]
    wide, narrow = lax.axis_index("wide"), lax.axis_index("narrow")
    rows = Rows(sizes, rows_ref, rows_out.at[0], rows_send, rows_recv)
    rows.greet([neighbour(core)])
    mail = Mail(send_sem, recv_sem)
    side_near = (wide // near[1]) % 2

    def part(ref, number, half):
        count = ref.shape[1] // 2
        return ref.at[number, pl.ds(pl.multiple_of(half * count, 16), count)]

    def own_part(ref, half):
        count = ref.shape[0] // 2
        return ref.at[pl.ds(pl.multiple_of(half * count, 16), count)]

    tables = {0: mail.keep(table_ref, table_out.at[0, 0])}
    if x_bits:
        tables[1] = mail.post(table_ref, table_out.at[0, 1], x_bits[0])
    held = [0]
    first = []
    for ref, out in zip(weight_refs, weight_outs):
        if y_bits:
            first.append(
                mail.post(own_part(ref, side_near), part(out, narrow, side_near), y_bits[0])
            )
    rows.start()
    own_rows = rows.own()
    own_rows.start()
    mail.post(table_ref, table_out.at[1, 0], core)
    for ref, out in zip(weight_refs, weight_outs):
        mail.keep(ref, out.at[narrow])
        mail.post(ref, out.at[narrow], core)
    own_rows.wait()
    place = narrow
    blocks = [narrow]
    for level, bit in enumerate(y_bits):
        fresh = []
        arrivals = []
        for number, (ref, out) in enumerate(zip(weight_refs, weight_outs)):
            for spot, block in enumerate(blocks):
                other = block + bit[1] * (1 - 2 * ((block // bit[1]) % 2))
                if level == 0:
                    copy = first[number]
                else:
                    copy = mail.post(
                        part(out, block, side_near), part(out, block, side_near), bit
                    )
                arrivals.append((out, other, copy))
                if number == 0:
                    fresh.append(other)
        seconds = []
        for out, other, copy in arrivals:
            mail.take(copy)
            seconds.append(
                mail.post(part(out, other, side_near), part(out, other, side_near), near)
            )
            mail.post(part(out, other, side_near), part(out, other, side_near), core)
        for (out, other, _), copy in zip(arrivals, seconds):
            mail.take(copy)
            mail.post(part(out, other, 1 - side_near), part(out, other, 1 - side_near), core)
        blocks = blocks + fresh

    def hand(k):
        return pltpu.make_async_remote_copy(
            src_ref=rows_out.at[0, k],
            dst_ref=rows_out.at[1, k],
            send_sem=pass_send.at[k],
            recv_sem=pass_recv.at[k],
            device_id=neighbour(core),
            device_id_type=MESH,
        )

    hand(0).start()

    def forward(k):
        rows.copy(k).wait()
        hand(k).start()

    rows.each(forward)
    for level, bit in enumerate(x_bits):
        for block in range(1 << level):
            spot = block + (1 << level)
            if spot not in tables:
                tables[spot] = mail.post(table_out.at[0, block], table_out.at[0, spot], bit)
        for block in range(1 << level):
            spot = block + (1 << level)
            mail.take(tables[spot])
            mail.post(table_out.at[0, spot], table_out.at[1, spot], core)
    hand(0).wait()
    rows.each(lambda k: hand(k).wait())
    mail.close()


def load_all(table, weights, rows):
    lane_bits = lanes()
    sizes = chip_sizes()
    count = sizes[0] * sizes[1]
    groups = lax.axis_size("narrow")
    across = 1 << len(lane_bits[1])
    any_space = pl.BlockSpec(memory_space=pl.ANY)
    shapes = (
        [jax.ShapeDtypeStruct((2, across) + table.shape, table.dtype)]
        + [jax.ShapeDtypeStruct((groups,) + w.shape, w.dtype) for w in weights]
        + [jax.ShapeDtypeStruct((2,) + rows.shape, rows.dtype)]
    )
    table_all, *weights_all, rows_all = pl.pallas_call(
        functools.partial(load_kernel, sizes, lane_bits),
        out_shape=shapes,
        in_specs=[pl.BlockSpec(memory_space=pltpu.VMEM)] * 6,
        out_specs=[any_space] * 6,
        scratch_shapes=mail_sems(8 * 2 * groups + 2 * across + 4)
        + mail_sems(count)
        + mail_sems(count),
        compiler_params=pltpu.CompilerParams(
            collective_id=6, has_side_effects=True, vmem_limit_bytes=32 * MIB
        ),
        name="load_rows",
    )(table, *weights, rows)
    model = table.shape[1]
    return (
        table_all.reshape(-1, model),
        tuple(w.reshape(-1, model) for w in weights_all),
        rows_all,
    )


def tile_of(rows):
    return next(size for size in (128, 96, 64, 48, 32, 16) if rows % size == 0)


def run_flows(flows):
    while flows:
        flows = [flow for flow in flows if next(flow, None) is not None]


def reduce_kernel(sizes, lane_bits, kinds, grads_count, *refs):
    core, x_bits, y_bits, z_bits = lane_bits
    grad_refs, small_ref, rows_ref = refs[:grads_count], refs[grads_count], refs[grads_count + 1]
    outs = refs[grads_count + 2 :]
    out_refs, small_out, rows_out, square_out = (
        outs[:grads_count],
        outs[grads_count],
        outs[grads_count + 1],
        outs[grads_count + 2],
    )
    scratch = outs[grads_count + 3 :]
    got_refs = []
    sum_refs, scratch = scratch[: len(kinds)], scratch[len(kinds) :]
    for _, _, _, path in kinds:
        got_refs.append(scratch[: len(path) + 1])
        scratch = scratch[len(path) + 1 :]
    small_sum, small_got, send_sem, recv_sem, rows_send, rows_recv = scratch
    place = {"wide": lax.axis_index("wide"), "narrow": lax.axis_index("narrow")}
    rows = Rows(sizes, rows_ref, rows_out, rows_send, rows_recv)
    rows.greet([neighbour(core)])
    mail = Mail(send_sem, recv_sem)
    ups = sum_refs[0].shape[0]
    own = place["narrow"] % 2
    square_out[...] = jnp.zeros_like(square_out)

    def side_of(bit):
        return (place[bit[0]] // bit[1]) % 2

    def add(total_ref, got_ref, box):
        up, ups_here, first, height = box
        tile = tile_of(height)

        def step(i, carry):
            at = i // (height // tile)
            down = (i % (height // tile)) * tile
            span = pl.ds(pl.multiple_of(first + down, 16), tile)
            got = got_ref[at, pl.ds(pl.multiple_of(down, 16), tile), :]
            total = total_ref[up + at, span, :].astype(jnp.float32) + got.astype(jnp.float32)
            total_ref[up + at, span, :] = total.astype(jnp.bfloat16)
            return carry

        lax.fori_loop(0, ups_here * (height // tile), step, 0)

    def view(ref, box):
        up, ups_here, first, height = box
        return ref.at[pl.ds(up, ups_here), pl.ds(pl.multiple_of(first, 16), height)]

    def flow(number):
        which, offset, height, path = kinds[number]
        total_ref, got = sum_refs[number], got_refs[number]
        out_ref = out_refs[which]
        span = pl.ds(offset, height)
        firsts = [
            (
                mail.post(grad_refs[which].at[2 * up + 1 - own, span], got[0].at[up], core),
                mail.keep(grad_refs[which].at[2 * up + own, span], total_ref.at[up]),
            )
            for up in range(ups)
        ]
        yield True
        for remote, local in firsts:
            mail.take(local)
            mail.take(remote)
        box = (0, ups, 0, height)
        add(total_ref, got[0], box)
        for stage, (bit, halve) in enumerate(path):
            up, ups_here, first, height = box
            side = side_of(bit)
            if bit[0] == "narrow":
                half = ups_here // 2
                mine = (up + side * half, half, first, height)
                theirs = (up + (1 - side) * half, half, first, height)
            elif halve:
                half = height // 2
                mine = (up, ups_here, first + side * half, half)
                theirs = (up, ups_here, first + (1 - side) * half, half)
            else:
                mine = theirs = box
            copy = mail.post(view(total_ref, theirs), got[stage + 1], bit)
            yield True
            mail.take(copy)
            if not halve:
                copy.wait_send()
                mail.sent = [other for other in mail.sent if other is not copy]
            box = mine
            add(total_ref, got[stage + 1], box)
        up, _, first, height = box
        piece = total_ref[up, pl.ds(pl.multiple_of(first, 16), height), :]
        out_ref[pl.ds(pl.multiple_of(offset + first, 16), height), :] = piece
        full = piece.astype(jnp.float32)
        square_out[...] += jnp.sum((full * full).reshape(height // 8, 8, -1), 0)
        for bit, halve in reversed(path):
            if bit[0] == "wide" and halve:
                span = pl.ds(pl.multiple_of(offset + first, 16), height)
                copy = mail.post(out_ref.at[span], out_ref.at[span], bit)
                yield True
                mail.take(copy)
                first = first - side_of(bit) * height
                height = 2 * height

    def small_flow():
        bits = [core] + x_bits + y_bits + z_bits
        small_sum[0] = small_ref[...].astype(jnp.bfloat16)
        for stage, bit in enumerate(bits):
            copy = mail.post(small_sum.at[stage], small_got.at[stage], bit)
            yield True
            mail.take(copy)
            total = small_sum[stage].astype(jnp.float32) + small_got[stage].astype(jnp.float32)
            if stage == len(bits) - 1:
                small_out[...] = total
            else:
                small_sum[stage + 1] = total.astype(jnp.bfloat16)

    def rows_flow():
        yield True
        rows.start()
        own_rows = rows.own()
        own_rows.start()
        yield True
        own_rows.wait()

    run_flows([flow(number) for number in range(len(kinds))] + [small_flow(), rows_flow()])
    rows.each(lambda k: rows.copy(k).wait())
    mail.close()


def reduce_all(grads, small, rows):
    lane_bits = lanes()
    core, x_bits, y_bits, z_bits = lane_bits
    sizes = chip_sizes()
    near, far = z_bits[:1], z_bits[1:]
    groups, height, width = grads[0].shape
    ups = groups // 2
    downs = y_bits[::-1]
    half = height // 2
    orders = (
        (0, 0, x_bits + downs + near + far),
        (1, 0, downs + x_bits + near + far),
        (2, 0, near + x_bits + downs + far),
        (0, half, x_bits + near + downs + far),
        (1, half, downs + near + x_bits + far),
        (2, half, near + downs + x_bits + far),
    )
    kinds, got_shapes = [], []
    for which, offset, order in orders:
        path, ups_here, height_here = [], ups, half
        shapes = [(ups_here, height_here, width)]
        for bit in order:
            halve = True
            if bit[0] == "narrow":
                ups_here //= 2
            else:
                halve = (height_here // 2) % 16 == 0
                height_here = height_here // 2 if halve else height_here
            path.append((bit, halve))
            shapes.append((ups_here, height_here, width))
        kinds.append((which, offset, half, path))
        got_shapes += shapes
    count = sizes[0] * sizes[1]
    steps = 1 + len(orders[0][2])
    vmem = pl.BlockSpec(memory_space=pltpu.VMEM)
    any_space = pl.BlockSpec(memory_space=pl.ANY)
    outs = pl.pallas_call(
        functools.partial(reduce_kernel, sizes, lane_bits, kinds, len(grads)),
        out_shape=[jax.ShapeDtypeStruct((height, width), jnp.bfloat16) for _ in grads]
        + [
            jax.ShapeDtypeStruct(small.shape, small.dtype),
            jax.ShapeDtypeStruct(rows.shape, rows.dtype),
            jax.ShapeDtypeStruct((8, width), jnp.float32),
        ],
        in_specs=[any_space] * len(grads) + [vmem, vmem],
        out_specs=[vmem] * len(grads) + [vmem, any_space, vmem],
        scratch_shapes=[pltpu.VMEM((ups, half, width), jnp.bfloat16) for _ in kinds]
        + [pltpu.VMEM(shape, jnp.bfloat16) for shape in got_shapes]
        + [
            pltpu.VMEM((steps,) + small.shape, jnp.bfloat16),
            pltpu.VMEM((steps,) + small.shape, jnp.bfloat16),
        ]
        + mail_sems(len(kinds) * (2 * ups + 2 * steps) + steps)
        + mail_sems(count),
        compiler_params=pltpu.CompilerParams(
            collective_id=7, has_side_effects=True, vmem_limit_bytes=56 * MIB
        ),
        name="reduce_rows",
    )(*grads, small, rows)
    repeats = 1
    for bit, halve in kinds[0][3]:
        repeats *= 1 if halve else 2
    number = len(grads)
    return outs[:number], outs[number], outs[number + 1], jnp.sum(outs[number + 2]) / repeats


def flip_index(place, mask, size):
    result = place * 0
    for bit in range(log_two(size)):
        one = (place // (1 << bit)) % 2
        two = (mask // (1 << bit)) % 2
        result = result + (one + two - 2 * one * two) * (1 << bit)
    return result


def exchange_kernel(masks, sizes, whole, x_ref, out_ref, send_sem, recv_sem, own_sem):
    wides, groups = sizes
    wide, narrow = lax.axis_index("wide"), lax.axis_index("narrow")
    count = wides * groups if masks is None else len(masks)

    def peer(mask):
        return (
            flip_index(wide, mask // groups, wides),
            flip_index(narrow, mask % groups, groups),
        )

    def each(step):
        if masks is None:
            lax.fori_loop(1, count, lambda k, carry: (step(k, k), carry)[1], 0)
        else:
            for k in range(1, count):
                step(k, masks[k])

    def copy(k, mask):
        return pltpu.make_async_remote_copy(
            src_ref=x_ref if whole else x_ref.at[k],
            dst_ref=out_ref.at[k],
            send_sem=send_sem.at[k],
            recv_sem=recv_sem.at[k],
            device_id=peer(mask),
            device_id_type=MESH,
        )

    barrier = pltpu.get_barrier_semaphore()
    each(
        lambda k, mask: pl.semaphore_signal(
            barrier, inc=1, device_id=peer(mask), device_id_type=MESH
        )
    )
    pl.semaphore_wait(barrier, count - 1)
    each(lambda k, mask: copy(k, mask).start())
    own = pltpu.make_async_copy(x_ref if whole else x_ref.at[0], out_ref.at[0], own_sem)
    own.start()
    own.wait()
    each(lambda k, mask: copy(k, mask).wait())


def exchange(array, number, name, masks=None, whole=True):
    sizes = (lax.axis_size("wide"), lax.axis_size("narrow"))
    count = sizes[0] * sizes[1] if masks is None else len(masks)
    shape = (count,) + array.shape if whole else array.shape
    return pl.pallas_call(
        functools.partial(exchange_kernel, masks, sizes, whole),
        out_shape=jax.ShapeDtypeStruct(shape, array.dtype),
        in_specs=[pl.BlockSpec(memory_space=pltpu.VMEM)],
        out_specs=pl.BlockSpec(memory_space=pltpu.VMEM),
        scratch_shapes=[
            pltpu.SemaphoreType.DMA((count,)),
            pltpu.SemaphoreType.DMA((count,)),
            pltpu.SemaphoreType.DMA,
        ],
        compiler_params=pltpu.CompilerParams(
            collective_id=number, has_side_effects=True, vmem_limit_bytes=32 * MIB
        ),
        name=name,
    )(array)


def merge_stats(top, total, picked):
    masks = group_masks()
    blocks, tokens = top.shape
    parts = jnp.stack([top, total, picked], 1).reshape(blocks, -1, 128)
    parts = jnp.pad(parts, ((0, 0), (0, -parts.shape[1] % 8), (0, 0)))
    parts = exchange(parts, 1, "stats_swap", masks, False).reshape(blocks, -1)
    top, total, picked = (parts[:, i * tokens : (i + 1) * tokens] for i in range(3))
    highest = jnp.max(top, 0)
    own = highest + jnp.log(jnp.sum(total * jnp.exp(top - highest), 0))
    share = jnp.pad(own.reshape(-1, 128), ((0, -(tokens // 128) % 8), (0, 0)))
    share = exchange(share, 8, "stats_share", masks).reshape(blocks, -1)[:, :tokens]
    return share.reshape(-1), own, jnp.sum(picked, 0)


def score_kernel(rows_ref, table_ref, target_ref, exps_ref, max_ref, sum_ref, pick_ref):
    tile = pl.program_id(0)
    width = table_ref.shape[0]

    @pl.when(tile == 0)
    def _():
        max_ref[...] = jnp.full_like(max_ref, -jnp.inf)
        sum_ref[...] = jnp.zeros_like(sum_ref)
        pick_ref[...] = jnp.zeros_like(pick_ref)

    def step(block, carry):
        rows = pl.ds(pl.multiple_of(block * TOKEN_TILE, TOKEN_TILE), TOKEN_TILE)
        scores = lax.dot_general(
            rows_ref[rows, :],
            table_ref[...],
            (((1,), (1,)), ((), ())),
            preferred_element_type=jnp.float32,
        )
        top = jnp.max(scores, -1, keepdims=True)
        powers = jnp.exp(scores - top)
        exps_ref[rows, :] = powers.astype(jnp.bfloat16)
        total = jnp.sum(powers, -1, keepdims=True)
        columns = lax.broadcasted_iota(jnp.int32, (TOKEN_TILE, width), 1)
        wanted = target_ref[rows, :] - tile * width
        hit = jnp.sum(jnp.where(columns == wanted, scores, 0.0), -1, keepdims=True)
        here = lax.broadcasted_iota(jnp.int32, (TOKEN_TILE, 128), 1) == tile
        max_ref[rows, :] = jnp.where(here, top, max_ref[rows, :])
        sum_ref[rows, :] = jnp.where(here, total, sum_ref[rows, :])
        pick_ref[rows, :] = jnp.where(here, hit, pick_ref[rows, :])
        return carry

    lax.fori_loop(0, rows_ref.shape[0] // TOKEN_TILE, step, 0, unroll=8)


def vocab_tile(vocab):
    return 1280 if vocab % 1280 == 0 else 640


def head_scores(rows, table, targets):
    tokens, model = rows.shape
    vocab = table.shape[0]
    width = vocab_tile(vocab)
    stat = jax.ShapeDtypeStruct((tokens, 128), jnp.float32)
    whole = pl.BlockSpec((tokens, 128), lambda j: (0, 0))
    return pl.pallas_call(
        score_kernel,
        grid=(vocab // width,),
        out_shape=(jax.ShapeDtypeStruct((tokens, vocab), jnp.bfloat16), stat, stat, stat),
        in_specs=[
            pl.BlockSpec((tokens, model), lambda j: (0, 0)),
            pl.BlockSpec((width, model), lambda j: (j, 0)),
            pl.BlockSpec((tokens, 1), lambda j: (0, 0)),
        ],
        out_specs=(pl.BlockSpec((tokens, width), lambda j: (0, j)), whole, whole, whole),
        compiler_params=pltpu.CompilerParams(vmem_limit_bytes=56 * MIB),
        cost_estimate=pl.CostEstimate(
            flops=3 * tokens * vocab * model,
            bytes_accessed=2 * tokens * vocab,
            transcendentals=tokens * vocab,
        ),
        name="head_scores",
    )(rows, table, targets[:, None])


def slope_kernel(exps_ref, scale_ref, target_ref, table_ref, slope_ref, grad_ref, total_ref):
    tile = pl.program_id(0)
    width = table_ref.shape[0]

    @pl.when(tile == 0)
    def _():
        total_ref[...] = jnp.zeros_like(total_ref)

    def step(block, carry):
        rows = pl.ds(pl.multiple_of(block * TOKEN_TILE, TOKEN_TILE), TOKEN_TILE)
        here = lax.broadcasted_iota(jnp.int32, (TOKEN_TILE, 128), 1) == tile
        scale = jnp.sum(jnp.where(here, scale_ref[rows, :], 0.0), -1, keepdims=True)
        columns = lax.broadcasted_iota(jnp.int32, (TOKEN_TILE, width), 1)
        wanted = target_ref[rows, :] - tile * width
        probs = exps_ref[rows, :].astype(jnp.float32) * scale
        slope = jnp.where(columns == wanted, probs - 1.0, probs).astype(jnp.bfloat16)
        slope_ref[rows, :] = slope
        total_ref[rows, :] += jnp.dot(slope, table_ref[...], preferred_element_type=jnp.float32)
        return carry

    lax.fori_loop(0, exps_ref.shape[0] // TOKEN_TILE, step, 0, unroll=8)

    @pl.when(tile == pl.num_programs(0) - 1)
    def _():
        grad_ref[...] = total_ref[...].astype(jnp.bfloat16)


def head_slopes(exps, scale, targets, table):
    tokens, vocab = exps.shape
    model = table.shape[1]
    width = vocab_tile(vocab)
    return pl.pallas_call(
        slope_kernel,
        grid=(vocab // width,),
        out_shape=(
            jax.ShapeDtypeStruct((tokens, vocab), jnp.bfloat16),
            jax.ShapeDtypeStruct((tokens, model), jnp.bfloat16),
        ),
        in_specs=[
            pl.BlockSpec((tokens, width), lambda j: (0, j)),
            pl.BlockSpec((tokens, 128), lambda j: (0, 0)),
            pl.BlockSpec((tokens, 1), lambda j: (0, 0)),
            pl.BlockSpec((width, model), lambda j: (j, 0)),
        ],
        out_specs=(
            pl.BlockSpec((tokens, width), lambda j: (0, j)),
            pl.BlockSpec((tokens, model), lambda j: (0, 0)),
        ),
        scratch_shapes=[pltpu.VMEM((tokens, model), jnp.float32)],
        compiler_params=pltpu.CompilerParams(vmem_limit_bytes=60 * MIB),
        cost_estimate=pl.CostEstimate(
            flops=3 * tokens * vocab * model,
            bytes_accessed=4 * tokens * vocab,
            transcendentals=0,
        ),
        name="head_slopes",
    )(exps, scale, targets[:, None], table)


def one_hot(places, size):
    return (places.reshape(-1, 1) == jnp.arange(size)[None]).astype(jnp.bfloat16)


def token_plan(ids_all, shard_rows):
    chips, tokens = ids_all.shape
    wides, ups = chip_sizes()
    wide, narrow = lax.axis_index("wide"), lax.axis_index("narrow")
    own_core = narrow % 2
    own_chip = wide * ups + narrow // 2
    owner = ids_all // shard_rows
    owner_core = jnp.bitwise_xor(owner % 2, own_core)
    owner_chip = jnp.bitwise_xor(owner // 2, own_chip)
    local = ids_all % shard_rows
    row = lax.broadcasted_iota(jnp.int32, (tokens, tokens), 0)
    column = lax.broadcasted_iota(jnp.int32, (tokens, tokens), 1)
    before = column < row
    alike = ids_all[:, :, None] == ids_all[:, None, :]
    first = ~jnp.any(alike & before[None], 2)
    served = first & (owner_chip == 0) & (owner_core == 0)
    served_rank = times_t(served.astype(jnp.bfloat16), before.astype(jnp.bfloat16)).astype(
        jnp.int32
    )
    half = tokens // 2
    mine = lambda array: lax.dynamic_slice_in_dim(array, own_core * half, half)
    own_first = mine(jnp.min(jnp.where(alike[0], column, tokens), 1))
    same_owner = mine(owner[0])[:, None] == owner[0][None]
    own_rank = jnp.sum(
        (same_owner & first[0][None] & (column[:half] < own_first[:, None])).astype(jnp.int32), 1
    )
    own_block = mine(owner_core[0]) * chips + mine(owner_chip[0])
    most = jnp.max(
        jnp.sum(
            (
                first[:, None, :]
                & (owner[:, None, :] == jnp.arange(2 * chips)[None, :, None])
            ).astype(jnp.int32),
            2,
        )
    )
    rounds = (most + SLOTS - 1) // SLOTS

    def plan(turn):
        slot = jnp.arange(SLOTS)[None, :, None] + turn * SLOTS
        chosen = served[:, None, :] & (served_rank[:, None, :] == slot)
        slot_rows = jnp.sum(jnp.where(chosen, local[:, None, :] + 1, 0), 2) - 1
        inside = own_rank - turn * SLOTS
        valid = (inside >= 0) & (inside < SLOTS)
        own_slots = jnp.where(valid, own_block * SLOTS + inside, -1)
        return one_hot(slot_rows, shard_rows), one_hot(own_slots, 2 * chips * SLOTS)

    return plan, rounds


def later_rounds(rounds, turn, total):
    return lax.while_loop(
        lambda state: state[0] < rounds,
        lambda state: (state[0] + 1, state[1] + turn(state[0])),
        (jnp.ones((), jnp.int32), total),
    )[1]


def times_high(left, right):
    return jnp.dot(left, right, precision=lax.Precision.HIGH, preferred_element_type=jnp.float32)


def newton_schulz(square_form):
    size = square_form.shape[0]
    diagonal = (
        lax.broadcasted_iota(jnp.int32, (size, size), 0)
        == lax.broadcasted_iota(jnp.int32, (size, size), 1)
    ).astype(jnp.float32)
    total = None
    for cycle_no in range(NS_STEPS):
        rest = NS_B * square_form + NS_C * times_high(square_form, square_form)
        if total is None:
            total, scale = rest, NS_A
        else:
            total = NS_A * total + scale * rest + times_high(total, rest)
            scale = scale * NS_A
        if cycle_no < NS_STEPS - 1:
            half = NS_A * square_form + times_high(square_form, rest)
            square_form = NS_A * half + times_high(half, rest)
    return total


def on_device(
    token_ids,
    targets,
    joint_weight,
    output_weight,
    expand_weight,
    reduce_weight,
    joint_velocity,
    output_velocity,
    expand_velocity,
    reduce_velocity,
    embedding,
    embed_moment,
    embed_square,
    positions,
    position_moment,
    position_square,
    norm_gains,
    gain_moment,
    gain_square,
    biases,
    bias_moment,
    bias_square,
):
    core, x_bits, y_bits, z_bits = lanes()
    groups = lax.axis_size("narrow")
    wides = lax.axis_size("wide")
    across = 1 << len(x_bits)
    model_width = embedding.shape[1]
    shard_rows = embedding.shape[0]
    tokens = token_ids.shape[0] * LENGTH
    shifts = biases[: 3 * model_width].reshape(3, model_width)

    own_rows = embedding.astype(jnp.bfloat16)
    labels = jnp.concatenate([token_ids.reshape(-1, 128), targets.reshape(-1, 128)])
    spare = -labels.shape[0] % 8
    labels = exchange(jnp.pad(labels, ((0, spare), (0, 0))), 0, "label_share")
    ids_all = labels[:, : tokens // 128].reshape(-1, tokens)
    targets_all = labels[:, tokens // 128 : 2 * tokens // 128].reshape(-1, tokens)
    own_block = lax.axis_index("wide") * groups + lax.axis_index("narrow")
    wides, ups = chip_sizes()
    pairs = ids_all.reshape(wides, ups, 2, tokens)
    other_first = lax.axis_index("narrow") % 2 == 1
    ids_chips = jnp.where(other_first, lax.rev(pairs, (2,)), pairs).reshape(wides * ups, -1)
    plan, rounds = token_plan(ids_chips, shard_rows)

    def serve(served):
        return plain(served, own_rows).astype(jnp.bfloat16).reshape(-1, SLOTS, model_width)

    masters = (joint_weight, output_weight, expand_weight, reduce_weight)
    served, wanted = plan(0)
    table, weights, token_rows = load_all(
        own_rows, [master.astype(jnp.bfloat16) for master in masters], serve(served)
    )
    vocab_here = table.shape[0]

    def fetch(turn):
        more, places = plan(turn)
        got = swap_rows(serve(more))
        return plain(places, jnp.stack([got, swap(got, core)]).reshape(-1, model_width))

    embedded = later_rounds(rounds, fetch, plain(wanted, token_rows.reshape(-1, model_width)))

    block_masks = jnp.array(group_masks())
    targets_group = targets_all[block_masks].reshape(-1)
    table_mask = groups * (across - 1) + 1
    differ = jnp.bitwise_xor(targets_group // shard_rows, own_block)
    is_owned = (targets_group >= 0) & (jnp.bitwise_and(differ, ~table_mask) == 0)
    place = (differ % 2) * across + (differ // groups) % across
    rows_targets = jnp.where(is_owned, place * shard_rows + targets_group % shard_rows, -1)
    stream_in = embedded + jnp.tile(positions, (token_ids.shape[0], 1))
    stream_out, saved = layer_forward(stream_in, weights, norm_gains, biases)
    final_norm, normed_f, inverse_f = norm_forward(stream_out, norm_gains[2], shifts[2])
    group_rows = spread(final_norm.astype(jnp.bfloat16)).reshape(-1, model_width)
    exps, maxima, totals, picked = head_scores(group_rows, table, rows_targets)
    top = jnp.max(maxima, -1)
    total = jnp.sum(totals * jnp.exp(maxima - top[:, None]), -1)
    log_totals, own_logs, own_picked = merge_stats(
        *(part.reshape(-1, tokens) for part in (top, total, jnp.sum(picked, -1)))
    )
    loss_part = jnp.sum(jnp.where(targets.reshape(-1) >= 0, own_logs - own_picked, 0.0))
    scale = jnp.where(
        (targets_group >= 0)[:, None], jnp.exp(maxima - log_totals[:, None]), 0.0
    )
    slopes, final_part = head_slopes(exps, scale, rows_targets, table)
    half = vocab_here // 2
    other_grad = swap(outer_sum(slopes[:, half:], group_rows).astype(jnp.bfloat16), core)
    table_sum = outer_sum(slopes[:, :half], group_rows) + other_grad.astype(jnp.float32)
    for bit in reversed(x_bits):
        half = table_sum.shape[0] // 2
        table_sum = table_sum[:half] + swap(table_sum[half:].astype(jnp.bfloat16), bit).astype(
            jnp.float32
        )
    final_grad = collect(final_part.reshape(-1, tokens, model_width))
    back_f, gain_f, shift_f = norm_backward(final_grad, normed_f, inverse_f, norm_gains[2])
    stream_grad, factors, gain_pair, shift_pair, bias_tail = layer_backward(
        back_f, weights, norm_gains, saved
    )
    low_grad = stream_grad.astype(jnp.bfloat16)

    def bundle(places):
        both = outer_sum(places, low_grad).astype(jnp.bfloat16)
        both = both.reshape(2, -1, SLOTS, model_width)
        other = swap(both[1], core)
        return (both[0].astype(jnp.float32) + other.astype(jnp.float32)).astype(jnp.bfloat16)

    position_grad = jnp.sum(stream_grad.reshape(-1, LENGTH, model_width), 0)
    gain_grad = jnp.stack([gain_pair[0], gain_pair[1], gain_f])
    bias_grad = jnp.concatenate([shift_pair[0], shift_pair[1], shift_f, bias_tail])
    count_part = jnp.sum((targets >= 0).astype(jnp.float32))
    small = jnp.concatenate(
        [gain_grad.reshape(-1), bias_grad, position_grad.reshape(-1)]
    ).reshape(-1, model_width)
    small_rows = small.shape[0]
    small = jnp.pad(small, ((0, -small_rows % 16), (0, 0)))

    def by_owner(pair):
        return outer_sum(*pair).astype(jnp.bfloat16).reshape(groups, -1, model_width)

    joint_part, output_part, expand_part, reduce_part = (by_owner(pair) for pair in factors)
    joint_rows = joint_part.shape[1]
    (front, expand_sum, reduce_sum), small, row_sums, squares = reduce_all(
        [jnp.concatenate([joint_part, output_part], 1), expand_part, reduce_part],
        small,
        bundle(wanted),
    )
    table_sum = table_sum + outer_sum(served, row_sums.reshape(-1, model_width))

    def give(turn):
        more, places = plan(turn)
        return outer_sum(more, swap_rows(bundle(places)).reshape(-1, model_width))

    table_sum = later_rounds(rounds, give, table_sum)
    matrix_total = [
        part.astype(jnp.float32)
        for part in (front[:joint_rows], front[joint_rows:], expand_sum, reduce_sum)
    ]
    small = small[:small_rows]
    squares = squares + jnp.sum(table_sum * table_sum)
    scalars = jnp.pad(jnp.stack([loss_part, count_part, squares])[None], ((0, 7), (0, 125)))
    scalars = jnp.sum(exchange(scalars, 3, "scalar_share"), 0)
    loss_sum, loss_count, squares = scalars[0, 0], scalars[0, 1], scalars[0, 2]
    squares = squares + jnp.sum(small * small)
    small = small.reshape(-1)
    gain_grad = small[: gain_grad.size].reshape(gain_grad.shape)
    bias_grad = small[gain_grad.size : gain_grad.size + bias_grad.size]
    position_grad = small[gain_grad.size + bias_grad.size :].reshape(position_grad.shape)
    grad_norm = jnp.sqrt(squares) / loss_count
    factor = jnp.minimum(1.0, CLIP / (grad_norm + 1e-06)) / loss_count
    previous = (joint_velocity, output_velocity, expand_velocity, reduce_velocity)
    carried = tuple(
        (MOMENTUM * before + gradient * factor for before, gradient in zip(previous, matrix_total))
    )
    grams = jnp.stack([outer_sum(c.astype(jnp.bfloat16), c.astype(jnp.bfloat16)) for c in carried])
    for bit in reversed(y_bits):
        if bit[1] >= 4:
            grams = grams + swap(grams.astype(jnp.bfloat16), bit).astype(jnp.float32)
    gram_bits = [core, y_bits[0]]
    gram_sum = scatter_bits(grams, gram_bits)[0]
    magnitude = jnp.sqrt(jnp.trace(gram_sum)) + 1e-07
    rest = newton_schulz(gram_sum / (magnitude * magnitude))
    rest = (rest / magnitude).astype(jnp.bfloat16)[None]
    rests = gather_bits(rest, gram_bits)
    magnitudes = gather_bits(magnitude[None], gram_bits)
    updated = []
    for number, (master, moment) in enumerate(zip(masters, carried)):
        orth = moment * (NS_A**NS_STEPS / magnitudes[number]) + plain(
            moment.astype(jnp.bfloat16), rests[number]
        )
        shape_factor = math.sqrt(max(1.0, master.shape[0] * groups / master.shape[1]))
        updated.append(master * (1 - MUON_RATE * DECAY) - MUON_RATE * shape_factor * orth)
    table_out = adam_step(
        embedding, embed_moment, embed_square, table_sum * factor, EMBED_RATE, DECAY
    )
    place_out = adam_step(
        positions, position_moment, position_square, position_grad * factor, PLACE_RATE, DECAY
    )
    gain_out = adam_step(norm_gains, gain_moment, gain_square, gain_grad * factor, SMALL_RATE, 0.0)
    bias_out = adam_step(biases, bias_moment, bias_square, bias_grad * factor, SMALL_RATE, 0.0)
    return (
        loss_sum,
        loss_count,
        grad_norm,
        updated[0],
        updated[1],
        updated[2],
        updated[3],
        carried[0],
        carried[1],
        carried[2],
        carried[3],
        table_out[0],
        table_out[1],
        table_out[2],
        place_out[0],
        place_out[1],
        place_out[2],
        gain_out[0],
        gain_out[1],
        gain_out[2],
        bias_out[0],
        bias_out[1],
        bias_out[2],
    )


def solution(mesh):
    in_specs = (
        P(("wide", "narrow"), None),
        P(("wide", "narrow"), None),
        P("narrow", None),
        P("narrow", None),
        P("narrow", None),
        P("narrow", None),
        P("narrow", None),
        P("narrow", None),
        P("narrow", None),
        P("narrow", None),
        P(("wide", "narrow"), None),
        P(("wide", "narrow"), None),
        P(("wide", "narrow"), None),
        P(),
        P(),
        P(),
        P(),
        P(),
        P(),
        P(),
        P(),
        P(),
    )
    out_specs = (
        P(),
        P(),
        P(),
        P("narrow", None),
        P("narrow", None),
        P("narrow", None),
        P("narrow", None),
        P("narrow", None),
        P("narrow", None),
        P("narrow", None),
        P("narrow", None),
        P(("wide", "narrow"), None),
        P(("wide", "narrow"), None),
        P(("wide", "narrow"), None),
        P(),
        P(),
        P(),
        P(),
        P(),
        P(),
        P(),
        P(),
        P(),
    )
    return jax.shard_map(
        on_device, mesh=mesh, in_specs=in_specs, out_specs=out_specs, check_vma=False
    )
```

```python
import functools
import math

import jax
import jax.numpy as jnp
from jax import lax
from jax.experimental import pallas as pl
from jax.experimental.pallas import tpu as pltpu
from jax.sharding import PartitionSpec as P

HEADS = 12
HEAD = 64
LENGTH = 64
NS_STEPS = 3
STEP = 10


HIGH = lax.Precision.HIGHEST
EPS = 1e-05
CLIP = 0.05
MOMENTUM = 0.95
MUON_RATE = 0.5
DECAY = 0.1
BETA_ONE = 0.9
BETA_TWO = 0.999
EMBED_RATE = 0.02
PLACE_RATE = 0.1
SMALL_RATE = 0.2
NS_A = 3.4445
NS_B = -4.775
NS_C = 2.0315
MESH = pl.DeviceIdType.MESH
MIB = 1 << 20
TOKEN_TILE = 256
SLOTS = 32


def times_t(left, right):
    return lax.dot_general(
        left, right, (((1,), (1,)), ((), ())), preferred_element_type=jnp.float32
    )


def outer_sum(left, right):
    return lax.dot_general(
        left, right, (((0,), (0,)), ((), ())), preferred_element_type=jnp.float32
    )


def plain(left, right):
    return jnp.dot(left, right, preferred_element_type=jnp.float32)


def norm_forward(stream, gain, shift):
    centred = stream - jnp.mean(stream, -1, keepdims=True)
    inverse = lax.rsqrt(jnp.mean(centred * centred, -1, keepdims=True) + EPS)
    normed = centred * inverse
    return (normed * gain + shift, normed, inverse)


def norm_backward(upstream, normed, inverse, gain):
    scaled = upstream * gain
    inner = inverse * (
        scaled
        - jnp.mean(scaled, -1, keepdims=True)
        - normed * jnp.mean(scaled * normed, -1, keepdims=True)
    )
    return (inner, jnp.sum(upstream * normed, 0), jnp.sum(upstream, 0))


def gelu_tanh(values):
    return jax.nn.gelu(values, approximate=True)


def causal_scores(queries, key_heads):
    raw = jnp.einsum(
        "sqhd,skhd->shqk", queries, key_heads, preferred_element_type=jnp.float32
    ) * HEAD ** (-0.5)
    causal = lax.broadcasted_iota(jnp.int32, (LENGTH, LENGTH), 0) >= lax.broadcasted_iota(
        jnp.int32, (LENGTH, LENGTH), 1
    )
    return jnp.where(causal, raw, -1000000000.0)


def layer_forward(stream_in, weights, norm_gains, biases):
    joint_w, output_w, expand_w, reduce_w = weights
    model_width = stream_in.shape[1]
    seqs = stream_in.shape[0] // LENGTH
    shifts = biases[: 3 * model_width].reshape(3, model_width)
    query_b = biases[3 * model_width : 4 * model_width]
    value_b = biases[4 * model_width : 5 * model_width]
    output_b = biases[5 * model_width : 6 * model_width]
    reduce_b = biases[6 * model_width : 7 * model_width]
    expand_b = biases[7 * model_width :]
    first_norm, normed_a, inverse_a = norm_forward(stream_in, norm_gains[0], shifts[0])
    first_low = first_norm.astype(jnp.bfloat16)
    joint_bias = jnp.concatenate([query_b, jnp.zeros_like(query_b), value_b])
    joint_low = (times_t(first_low, joint_w) + joint_bias).astype(jnp.bfloat16)
    heads_all = joint_low.reshape(seqs, LENGTH, 3, HEADS, HEAD)
    queries, key_heads, values = (heads_all[:, :, 0], heads_all[:, :, 1], heads_all[:, :, 2])
    scores = causal_scores(queries, key_heads)
    maxima = jnp.max(scores, -1, keepdims=True)
    log_totals = maxima + jnp.log(jnp.sum(jnp.exp(scores - maxima), -1, keepdims=True))
    attn_probs = jnp.exp(scores - log_totals).astype(jnp.bfloat16)
    context = (
        jnp.einsum("shqk,skhd->sqhd", attn_probs, values, preferred_element_type=jnp.float32)
        .astype(jnp.bfloat16)
        .reshape(-1, model_width)
    )
    stream_mid = stream_in + times_t(context, output_w) + output_b
    second_norm, normed_b, inverse_b = norm_forward(stream_mid, norm_gains[1], shifts[1])
    second_low = second_norm.astype(jnp.bfloat16)
    upward = times_t(second_low, expand_w) + expand_b
    active = gelu_tanh(upward).astype(jnp.bfloat16)
    stream_out = stream_mid + plain(active, reduce_w) + reduce_b
    saved = (
        normed_a,
        inverse_a,
        first_low,
        queries,
        key_heads,
        values,
        log_totals,
        context,
        normed_b,
        inverse_b,
        second_low,
        upward,
        active,
    )
    return (stream_out, saved)


def layer_backward(upstream, weights, norm_gains, saved):
    joint_w, output_w, expand_w, reduce_w = weights
    (
        normed_a,
        inverse_a,
        first_low,
        queries,
        key_heads,
        values,
        log_totals,
        context,
        normed_b,
        inverse_b,
        second_low,
        upward,
        active,
    ) = saved
    model_width = upstream.shape[1]
    down_grad = upstream.astype(jnp.bfloat16)
    reduce_bias_grad = jnp.sum(down_grad.astype(jnp.float32), 0)
    active_grad = times_t(down_grad, reduce_w)
    upward_grad = jax.vjp(gelu_tanh, upward)[1](active_grad)[0].astype(jnp.bfloat16)
    expand_bias_grad = jnp.sum(upward_grad.astype(jnp.float32), 0)
    second_grad = plain(upward_grad, expand_w)
    back_b, gain_b, shift_b = norm_backward(second_grad, normed_b, inverse_b, norm_gains[1])
    mid_grad = upstream + back_b
    attn_grad = mid_grad.astype(jnp.bfloat16)
    output_bias_grad = jnp.sum(attn_grad.astype(jnp.float32), 0)
    context_grad = plain(attn_grad, output_w).astype(jnp.bfloat16).reshape(queries.shape)
    scores = causal_scores(queries, key_heads)
    probs_full = jnp.exp(scores - log_totals)
    probs_low = probs_full.astype(jnp.bfloat16)
    probs_grad = jnp.einsum(
        "sqhd,skhd->shqk", context_grad, values, preferred_element_type=jnp.float32
    )
    values_grad = jnp.einsum(
        "shqk,sqhd->skhd", probs_low, context_grad, preferred_element_type=jnp.float32
    )
    score_grad = (
        probs_full * (probs_grad - jnp.sum(probs_full * probs_grad, -1, keepdims=True))
    ).astype(jnp.bfloat16)
    query_grad = jnp.einsum(
        "shqk,skhd->sqhd", score_grad, key_heads, preferred_element_type=jnp.float32
    ) * HEAD ** (-0.5)
    key_grad = jnp.einsum(
        "shqk,sqhd->skhd", score_grad, queries, preferred_element_type=jnp.float32
    ) * HEAD ** (-0.5)
    joint_grad = (
        jnp.stack([query_grad, key_grad, values_grad], 2)
        .reshape(-1, 3 * model_width)
        .astype(jnp.bfloat16)
    )
    joint_float = joint_grad.astype(jnp.float32)
    query_bias_grad = jnp.sum(joint_float[:, :model_width], 0)
    value_bias_grad = jnp.sum(joint_float[:, 2 * model_width :], 0)
    first_grad = plain(joint_grad, joint_w)
    back_a, gain_a, shift_a = norm_backward(first_grad, normed_a, inverse_a, norm_gains[0])
    stream_grad = mid_grad + back_a
    factors = (
        (joint_grad, first_low),
        (attn_grad, context),
        (upward_grad, second_low),
        (active, down_grad),
    )
    bias_tail = jnp.concatenate(
        [query_bias_grad, value_bias_grad, output_bias_grad, reduce_bias_grad, expand_bias_grad]
    )
    return (stream_grad, factors, (gain_a, gain_b), (shift_a, shift_b), bias_tail)


def adam_step(weight, moment, square, gradient, rate, decay):
    moment = BETA_ONE * moment + (1 - BETA_ONE) * gradient
    square = BETA_TWO * square + (1 - BETA_TWO) * gradient * gradient
    unbiased = moment / (1 - BETA_ONE**STEP)
    spread = square / (1 - BETA_TWO**STEP)
    return (
        weight - rate * (unbiased / (jnp.sqrt(spread) + 1e-08) + decay * weight),
        moment,
        square,
    )


def log_two(size):
    return size.bit_length() - 1


def lanes():
    wide, narrow = lax.axis_size("wide"), lax.axis_size("narrow")
    across = wide // 4
    x_bits = [("wide", 1 << i) for i in range(log_two(across))]
    z_bits = [("wide", across << i) for i in range(log_two(wide // across))]
    y_bits = [("narrow", 2 << i) for i in range(log_two(narrow // 2))]
    return ("narrow", 1), x_bits, y_bits, z_bits


def swap(array, bit):
    axis, mask = bit
    return lax.ppermute(array, axis, [(i, i ^ mask) for i in range(lax.axis_size(axis))])


def side(bit):
    axis, mask = bit
    return (lax.axis_index(axis) // mask) % 2


def join(mine, other, bit, dim=0):
    own = side(bit)
    return jnp.where(
        own == 0, jnp.concatenate([mine, other], dim), jnp.concatenate([other, mine], dim)
    )


def halves(array, bit):
    own = side(bit)
    half = array.shape[0] // 2
    keep = lax.dynamic_slice_in_dim(array, own * half, half)
    send = lax.dynamic_slice_in_dim(array, (1 - own) * half, half)
    return keep, send


def group_bits():
    _, _, y_bits, z_bits = lanes()
    return z_bits + y_bits


def routes(rows, pieces):
    _, _, y_bits, z_bits = lanes()
    near, far = z_bits[:1], z_bits[1:]
    longer = rows * 5 // 8 // pieces
    shorter = rows // pieces - longer
    plan = []
    for piece in range(pieces):
        start = piece * (longer + shorter)
        plan.append((start, longer, far + near + y_bits))
        plan.append((start + longer, shorter, far + y_bits + near))
    return plan


def flat_mask(bit):
    axis, mask = bit
    return mask * lax.axis_size("narrow") if axis == "wide" else mask


def group_masks():
    masks = [0]
    for bit in group_bits():
        masks = masks + [other ^ flat_mask(bit) for other in masks]
    return masks


def neighbour(bit):
    axis, mask = bit
    wide, narrow = lax.axis_index("wide"), lax.axis_index("narrow")
    if axis == "wide":
        return wide + mask * (1 - 2 * ((wide // mask) % 2)), narrow
    return wide, narrow + mask * (1 - 2 * ((narrow // mask) % 2))


def greet(devices):
    barrier = pltpu.get_barrier_semaphore()
    for device in devices:
        pl.semaphore_signal(barrier, inc=1, device_id=device, device_id_type=MESH)
    pl.semaphore_wait(barrier, len(devices))


class Mail:
    def __init__(self, send_sem, recv_sem):
        self.send_sem, self.recv_sem = send_sem, recv_sem
        self.used, self.sent, self.open = 0, [], []

    def post(self, source, target, bit):
        copy = pltpu.make_async_remote_copy(
            src_ref=source,
            dst_ref=target,
            send_sem=self.send_sem.at[self.used],
            recv_sem=self.recv_sem.at[self.used],
            device_id=neighbour(bit),
            device_id_type=MESH,
        )
        copy.start()
        self.used += 1
        self.sent.append(copy)
        self.open.append(copy)
        return copy

    def keep(self, source, target):
        copy = pltpu.make_async_copy(source, target, self.recv_sem.at[self.used])
        copy.start()
        self.used += 1
        self.open.append(copy)
        return copy

    def take(self, copy):
        if any(other is copy for other in self.open):
            self.open = [other for other in self.open if other is not copy]
            if any(other is copy for other in self.sent):
                copy.wait_recv()
            else:
                copy.wait()

    def close(self):
        for copy in list(self.open):
            self.take(copy)
        for copy in self.sent:
            copy.wait_send()


def mail_sems(count):
    return [pltpu.SemaphoreType.DMA((count,)), pltpu.SemaphoreType.DMA((count,))]


def spread_kernel(bits, plan, x_ref, out_ref, send_sem, recv_sem):
    greet([neighbour(bit) for bit in bits])
    mail = Mail(send_sem, recv_sem)
    mail.keep(x_ref, out_ref.at[0])
    held = [{0: None} for _ in plan]
    for stage in range(len(bits)):
        for part, (first, rows, order) in enumerate(plan):
            bit = order[stage]
            step = 1 << bits.index(bit)
            span = pl.ds(first, rows)
            for block in list(held[part]):
                if block:
                    mail.take(held[part][block])
                source = out_ref.at[block, span] if block else x_ref.at[span]
                held[part][block ^ step] = mail.post(source, out_ref.at[block ^ step, span], bit)
    mail.close()


def spread(array):
    bits, plan = group_bits(), routes(array.shape[0], 1)
    count = 1 << len(bits)
    return pl.pallas_call(
        functools.partial(spread_kernel, bits, plan),
        out_shape=jax.ShapeDtypeStruct((count,) + array.shape, array.dtype),
        in_specs=[pl.BlockSpec(memory_space=pltpu.VMEM)],
        out_specs=pl.BlockSpec(memory_space=pl.ANY),
        scratch_shapes=mail_sems(len(plan) * count),
        compiler_params=pltpu.CompilerParams(
            collective_id=4, has_side_effects=True, vmem_limit_bytes=32 * MIB
        ),
        name="rows_spread",
    )(array)


def run_flows(flows):
    while flows:
        flows = [flow for flow in flows if next(flow, None) is not None]


def collect_flow(mail, bits, part, refs):
    first, rows, order = part
    x_ref, out_ref, sum_ref, got_ref = refs
    span = pl.ds(first, rows)
    held = list(range(1 << len(bits)))
    for stage, bit in enumerate(reversed(order)):
        step = 1 << bits.index(bit)
        source = sum_ref if stage else x_ref
        held = [block for block in held if not block & step]
        base = (1 << len(bits)) - 2 * len(held)
        copies = [
            mail.post(source.at[block ^ step, span], got_ref.at[base + place, span], bit)
            for place, block in enumerate(held)
        ]
        yield True
        for place, (block, copy) in enumerate(zip(held, copies)):
            mail.take(copy)
            total = source[block, span, :].astype(jnp.float32) + got_ref[
                base + place, span, :
            ].astype(jnp.float32)
            if stage == len(bits) - 1:
                out_ref[span, :] = total
            else:
                sum_ref[block, span, :] = total.astype(jnp.bfloat16)


def head_back_kernel(lane_bits, plan, tile, x_ref, *refs):
    core, _, y_bits, z_bits = lane_bits
    bits = z_bits + y_bits
    if tile:
        slope_ref, rows_ref, out_ref, keep_ref, pass_ref = refs[:5]
        sum_ref, got_ref, send_sem, recv_sem = refs[5:9]
        loads, sent_ref, other_ref, load_sem = refs[9:]
        half = sent_ref.shape[0]
        count = half // tile
        order = [count + i for i in range(count)] + [count - 1 - i for i in range(count)]

        def load(number):
            return pltpu.make_async_copy(
                slope_ref.at[:, pl.ds(order[number] * tile, tile)],
                loads.at[number % 2],
                load_sem.at[number % 2],
            )

        load(0).start()
        greet([neighbour(bit) for bit in bits + [core]])
    else:
        out_ref, sum_ref, got_ref, send_sem, recv_sem = refs
        greet([neighbour(bit) for bit in bits])
    mail = Mail(send_sem, recv_sem)
    flows = [
        collect_flow(mail, bits, part, (x_ref, out_ref, sum_ref, got_ref)) for part in plan
    ]
    if tile:

        def table_flow():
            arrivals = {}
            border = keep_ref.shape[0]
            for number, block in enumerate(order):
                if number + 1 < len(order):
                    load(number + 1).start()
                load(number).wait()
                grad = lax.dot_general(
                    loads[number % 2],
                    rows_ref[...],
                    (((0,), (0,)), ((), ())),
                    preferred_element_type=jnp.float32,
                )
                start = block * tile % half
                span = pl.ds(start, tile)
                if block >= count:
                    sent_ref[span, :] = grad.astype(jnp.bfloat16)
                    arrivals[start] = mail.post(sent_ref.at[span], other_ref.at[span], core)
                else:
                    mail.take(arrivals[start])
                    grad = grad + other_ref[span, :].astype(jnp.float32)
                    lower = min(max(border - start, 0), tile)
                    if lower:
                        keep_ref[pl.ds(start, lower), :] = grad[:lower]
                    if lower < tile:
                        pass_ref[pl.ds(start + lower - border, tile - lower), :] = grad[
                            lower:
                        ].astype(jnp.bfloat16)
                yield True

        run_flows([slowed(flow, 4) for flow in flows] + [table_flow()])
    else:
        run_flows(flows)
    mail.close()


def slowed(flow, turns):
    while next(flow, None) is not None:
        for _ in range(turns):
            yield True


def head_back(array, slopes, group_rows):
    lane_bits = lanes()
    bits, plan = group_bits(), routes(array.shape[1], 2)
    count, rows, width = array.shape
    vocab = slopes.shape[1]
    half = vocab // 2
    tile = 640 if half % 640 == 0 else 0
    vmem = pl.BlockSpec(memory_space=pltpu.VMEM)
    shapes = [jax.ShapeDtypeStruct((rows, width), jnp.float32)]
    scratch = [
        pltpu.VMEM((count, rows, width), jnp.bfloat16),
        pltpu.VMEM((count - 1, rows, width), jnp.bfloat16),
    ] + mail_sems(len(plan) * count + (half // tile if tile else 0))
    operands, specs = [array], [vmem]
    if tile:
        shapes += [
            jax.ShapeDtypeStruct((half // 2, width), jnp.float32),
            jax.ShapeDtypeStruct((half // 2, width), jnp.bfloat16),
        ]
        scratch += [
            pltpu.VMEM((2, slopes.shape[0], tile), jnp.bfloat16),
            pltpu.VMEM((half, width), jnp.bfloat16),
            pltpu.VMEM((half, width), jnp.bfloat16),
            pltpu.SemaphoreType.DMA((2,)),
        ]
        operands += [slopes, group_rows]
        specs += [pl.BlockSpec(memory_space=pl.ANY), vmem]
    outs = pl.pallas_call(
        functools.partial(head_back_kernel, lane_bits, plan, tile),
        out_shape=shapes,
        in_specs=specs,
        out_specs=[vmem] * len(shapes),
        scratch_shapes=scratch,
        compiler_params=pltpu.CompilerParams(
            collective_id=5, has_side_effects=True, vmem_limit_bytes=56 * MIB
        ),
        name="head_back",
    )(*operands)
    if tile:
        return outs
    core = lane_bits[0]
    other = swap(outer_sum(slopes[:, half:], group_rows).astype(jnp.bfloat16), core)
    table_sum = outer_sum(slopes[:, :half], group_rows) + other.astype(jnp.float32)
    return outs[0], table_sum[: half // 2], table_sum[half // 2 :].astype(jnp.bfloat16)


def chip_sizes():
    wides, groups = lax.axis_size("wide"), lax.axis_size("narrow")
    return wides, groups // 2


class Rows:
    def __init__(self, sizes, x_ref, out_ref, send_sem, recv_sem):
        self.sizes, self.x_ref, self.out_ref = sizes, x_ref, out_ref
        self.send_sem, self.recv_sem = send_sem, recv_sem
        self.count = sizes[0] * sizes[1]
        self.place = Place(sizes[0], 2 * sizes[1])

    def peer(self, k):
        ups = self.sizes[1]
        return self.place.peer(k // ups, 2 * (k % ups))

    def each(self, step):
        for k in range(1, self.count):
            step(k)

    def copy(self, k):
        return pltpu.make_async_remote_copy(
            src_ref=self.x_ref.at[k],
            dst_ref=self.out_ref.at[k],
            send_sem=self.send_sem.at[k],
            recv_sem=self.recv_sem.at[k],
            device_id=self.peer(k),
            device_id_type=MESH,
        )

    def greet(self, others):
        barrier = pltpu.get_barrier_semaphore()
        self.each(
            lambda k: pl.semaphore_signal(
                barrier, inc=1, device_id=self.peer(k), device_id_type=MESH
            )
        )
        for device in others:
            pl.semaphore_signal(barrier, inc=1, device_id=device, device_id_type=MESH)
        pl.semaphore_wait(barrier, self.count - 1 + len(others))

    def start(self):
        self.each(lambda k: self.copy(k).start())

    def own(self):
        return pltpu.make_async_copy(self.x_ref.at[0], self.out_ref.at[0], self.recv_sem.at[0])


def swap_rows_kernel(sizes, x_ref, out_ref, send_sem, recv_sem):
    rows = Rows(sizes, x_ref, out_ref, send_sem, recv_sem)
    rows.greet([])
    rows.start()
    own = rows.own()
    own.start()
    own.wait()
    rows.each(lambda k: rows.copy(k).wait())


def swap_rows(rows):
    sizes = chip_sizes()
    count = sizes[0] * sizes[1]
    return pl.pallas_call(
        functools.partial(swap_rows_kernel, sizes),
        out_shape=jax.ShapeDtypeStruct(rows.shape, rows.dtype),
        in_specs=[pl.BlockSpec(memory_space=pltpu.VMEM)],
        out_specs=pl.BlockSpec(memory_space=pl.ANY),
        scratch_shapes=mail_sems(count),
        compiler_params=pltpu.CompilerParams(collective_id=2, has_side_effects=True),
        name="token_rows",
    )(rows)


def load_kernel(sizes, lane_bits, *refs):
    core, x_bits, y_bits, z_bits = lane_bits
    near = z_bits[0]
    table_ref, weight_refs, rows_ref = refs[0], refs[1:5], refs[5]
    table_out, weight_outs, rows_out = refs[6], refs[7:11], refs[11]
    send_sem, recv_sem, rows_send, rows_recv, pass_send, pass_recv = refs[12:]
    wide, narrow = lax.axis_index("wide"), lax.axis_index("narrow")
    rows = Rows(sizes, rows_ref, rows_out.at[0], rows_send, rows_recv)
    rows.greet([neighbour(core)])
    mail = Mail(send_sem, recv_sem)
    side_near = (wide // near[1]) % 2

    def part(ref, number, half):
        count = ref.shape[1] // 2
        return ref.at[number, pl.ds(pl.multiple_of(half * count, 16), count)]

    def own_part(ref, half):
        count = ref.shape[0] // 2
        return ref.at[pl.ds(pl.multiple_of(half * count, 16), count)]

    tables = {0: mail.keep(table_ref, table_out.at[0, 0])}
    if x_bits:
        tables[1] = mail.post(table_ref, table_out.at[0, 1], x_bits[0])
    held = [0]
    first = []
    for ref, out in zip(weight_refs, weight_outs):
        if y_bits:
            first.append(
                mail.post(own_part(ref, side_near), part(out, narrow, side_near), y_bits[0])
            )
    rows.start()
    own_rows = rows.own()
    own_rows.start()
    mail.post(table_ref, table_out.at[1, 0], core)
    for ref, out in zip(weight_refs, weight_outs):
        mail.keep(ref, out.at[narrow])
        mail.post(ref, out.at[narrow], core)
    own_rows.wait()
    place = narrow
    blocks = [narrow]
    for level, bit in enumerate(y_bits):
        fresh = []
        arrivals = []
        for number, (ref, out) in enumerate(zip(weight_refs, weight_outs)):
            for spot, block in enumerate(blocks):
                other = block + bit[1] * (1 - 2 * ((block // bit[1]) % 2))
                if level == 0:
                    copy = first[number]
                else:
                    copy = mail.post(
                        part(out, block, side_near), part(out, block, side_near), bit
                    )
                arrivals.append((out, other, copy))
                if number == 0:
                    fresh.append(other)
        seconds = []
        for out, other, copy in arrivals:
            mail.take(copy)
            seconds.append(
                mail.post(part(out, other, side_near), part(out, other, side_near), near)
            )
            mail.post(part(out, other, side_near), part(out, other, side_near), core)
        for (out, other, _), copy in zip(arrivals, seconds):
            mail.take(copy)
            mail.post(part(out, other, 1 - side_near), part(out, other, 1 - side_near), core)
        blocks = blocks + fresh

    def hand(k):
        return pltpu.make_async_remote_copy(
            src_ref=rows_out.at[0, k],
            dst_ref=rows_out.at[1, k],
            send_sem=pass_send.at[k],
            recv_sem=pass_recv.at[k],
            device_id=neighbour(core),
            device_id_type=MESH,
        )

    hand(0).start()

    def forward(k):
        rows.copy(k).wait()
        hand(k).start()

    rows.each(forward)
    for level, bit in enumerate(x_bits):
        for block in range(1 << level):
            spot = block + (1 << level)
            if spot not in tables:
                tables[spot] = mail.post(table_out.at[0, block], table_out.at[0, spot], bit)
        for block in range(1 << level):
            spot = block + (1 << level)
            mail.take(tables[spot])
            mail.post(table_out.at[0, spot], table_out.at[1, spot], core)
    hand(0).wait()
    rows.each(lambda k: hand(k).wait())
    mail.close()


def load_all(table, weights, rows):
    lane_bits = lanes()
    sizes = chip_sizes()
    count = sizes[0] * sizes[1]
    groups = lax.axis_size("narrow")
    across = 1 << len(lane_bits[1])
    any_space = pl.BlockSpec(memory_space=pl.ANY)
    shapes = (
        [jax.ShapeDtypeStruct((2, across) + table.shape, table.dtype)]
        + [jax.ShapeDtypeStruct((groups,) + w.shape, w.dtype) for w in weights]
        + [jax.ShapeDtypeStruct((2,) + rows.shape, rows.dtype)]
    )
    table_all, *weights_all, rows_all = pl.pallas_call(
        functools.partial(load_kernel, sizes, lane_bits),
        out_shape=shapes,
        in_specs=[pl.BlockSpec(memory_space=pltpu.VMEM)] * 6,
        out_specs=[any_space] * 6,
        scratch_shapes=mail_sems(8 * 2 * groups + 2 * across + 4)
        + mail_sems(count)
        + mail_sems(count),
        compiler_params=pltpu.CompilerParams(
            collective_id=6, has_side_effects=True, vmem_limit_bytes=32 * MIB
        ),
        name="load_rows",
    )(table, *weights, rows)
    model = table.shape[1]
    return (
        table_all.reshape(-1, model),
        tuple(w.reshape(-1, model) for w in weights_all),
        rows_all,
    )


def tile_of(rows):
    return next(size for size in (128, 96, 64, 48, 32, 16) if rows % size == 0)


def reduce_kernel(sizes, lane_bits, kinds, grads_count, *refs):
    core, x_bits, y_bits, z_bits = lane_bits
    grad_refs, small_ref, rows_ref = refs[:grads_count], refs[grads_count], refs[grads_count + 1]
    outs = refs[grads_count + 2 :]
    out_refs, small_out, rows_out, square_out = (
        outs[:grads_count],
        outs[grads_count],
        outs[grads_count + 1],
        outs[grads_count + 2],
    )
    scratch = outs[grads_count + 3 :]
    got_refs = []
    sum_refs, scratch = scratch[: len(kinds)], scratch[len(kinds) :]
    for _, _, _, path in kinds:
        got_refs.append(scratch[: len(path) + 1])
        scratch = scratch[len(path) + 1 :]
    small_sum, small_got, send_sem, recv_sem, rows_send, rows_recv = scratch
    place = {"wide": lax.axis_index("wide"), "narrow": lax.axis_index("narrow")}
    rows = Rows(sizes, rows_ref, rows_out, rows_send, rows_recv)
    rows.greet([neighbour(core)])
    mail = Mail(send_sem, recv_sem)
    ups = sum_refs[0].shape[0]
    own = place["narrow"] % 2
    square_out[...] = jnp.zeros_like(square_out)

    def side_of(bit):
        return (place[bit[0]] // bit[1]) % 2

    def add(total_ref, got_ref, box):
        up, ups_here, first, height = box
        tile = tile_of(height)

        def step(i, carry):
            at = i // (height // tile)
            down = (i % (height // tile)) * tile
            span = pl.ds(pl.multiple_of(first + down, 16), tile)
            got = got_ref[at, pl.ds(pl.multiple_of(down, 16), tile), :]
            total = total_ref[up + at, span, :].astype(jnp.float32) + got.astype(jnp.float32)
            total_ref[up + at, span, :] = total.astype(jnp.bfloat16)
            return carry

        lax.fori_loop(0, ups_here * (height // tile), step, 0)

    def view(ref, box):
        up, ups_here, first, height = box
        return ref.at[pl.ds(up, ups_here), pl.ds(pl.multiple_of(first, 16), height)]

    def flow(number):
        which, offset, height, path = kinds[number]
        total_ref, got = sum_refs[number], got_refs[number]
        out_ref = out_refs[which]
        span = pl.ds(offset, height)
        firsts = [
            (
                mail.post(grad_refs[which].at[2 * up + 1 - own, span], got[0].at[up], core),
                mail.keep(grad_refs[which].at[2 * up + own, span], total_ref.at[up]),
            )
            for up in range(ups)
        ]
        yield True
        for remote, local in firsts:
            mail.take(local)
            mail.take(remote)
        box = (0, ups, 0, height)
        add(total_ref, got[0], box)
        for stage, (bit, halve) in enumerate(path):
            up, ups_here, first, height = box
            side = side_of(bit)
            if bit[0] == "narrow":
                half = ups_here // 2
                mine = (up + side * half, half, first, height)
                theirs = (up + (1 - side) * half, half, first, height)
            elif halve:
                half = height // 2
                mine = (up, ups_here, first + side * half, half)
                theirs = (up, ups_here, first + (1 - side) * half, half)
            else:
                mine = theirs = box
            copy = mail.post(view(total_ref, theirs), got[stage + 1], bit)
            yield True
            mail.take(copy)
            if not halve:
                copy.wait_send()
                mail.sent = [other for other in mail.sent if other is not copy]
            box = mine
            add(total_ref, got[stage + 1], box)
        up, _, first, height = box
        piece = total_ref[up, pl.ds(pl.multiple_of(first, 16), height), :]
        out_ref[pl.ds(pl.multiple_of(offset + first, 16), height), :] = piece
        full = piece.astype(jnp.float32)
        square_out[...] += jnp.sum((full * full).reshape(height // 8, 8, -1), 0)
        for bit, halve in reversed(path):
            if bit[0] == "wide" and halve:
                span = pl.ds(pl.multiple_of(offset + first, 16), height)
                copy = mail.post(out_ref.at[span], out_ref.at[span], bit)
                yield True
                mail.take(copy)
                first = first - side_of(bit) * height
                height = 2 * height

    def small_flow():
        bits = [core] + x_bits + y_bits + z_bits
        small_sum[0] = small_ref[...].astype(jnp.bfloat16)
        for stage, bit in enumerate(bits):
            copy = mail.post(small_sum.at[stage], small_got.at[stage], bit)
            yield True
            mail.take(copy)
            total = small_sum[stage].astype(jnp.float32) + small_got[stage].astype(jnp.float32)
            if stage == len(bits) - 1:
                small_out[...] = total
            else:
                small_sum[stage + 1] = total.astype(jnp.bfloat16)

    def rows_flow():
        yield True
        rows.start()
        own_rows = rows.own()
        own_rows.start()
        yield True
        own_rows.wait()

    run_flows([flow(number) for number in range(len(kinds))] + [small_flow(), rows_flow()])
    rows.each(lambda k: rows.copy(k).wait())
    mail.close()


def reduce_all(grads, small, rows):
    lane_bits = lanes()
    core, x_bits, y_bits, z_bits = lane_bits
    sizes = chip_sizes()
    near, far = z_bits[:1], z_bits[1:]
    groups, height, width = grads[0].shape
    ups = groups // 2
    downs = y_bits[::-1]
    half = height // 2
    orders = (
        (0, 0, x_bits + downs + near + far),
        (1, 0, downs + x_bits + near + far),
        (2, 0, near + x_bits + downs + far),
        (0, half, x_bits + near + downs + far),
        (1, half, downs + near + x_bits + far),
        (2, half, near + downs + x_bits + far),
    )
    kinds, got_shapes = [], []
    for which, offset, order in orders:
        path, ups_here, height_here = [], ups, half
        shapes = [(ups_here, height_here, width)]
        for bit in order:
            halve = True
            if bit[0] == "narrow":
                ups_here //= 2
            else:
                halve = (height_here // 2) % 16 == 0
                height_here = height_here // 2 if halve else height_here
            path.append((bit, halve))
            shapes.append((ups_here, height_here, width))
        kinds.append((which, offset, half, path))
        got_shapes += shapes
    count = sizes[0] * sizes[1]
    steps = 1 + len(orders[0][2])
    vmem = pl.BlockSpec(memory_space=pltpu.VMEM)
    any_space = pl.BlockSpec(memory_space=pl.ANY)
    outs = pl.pallas_call(
        functools.partial(reduce_kernel, sizes, lane_bits, kinds, len(grads)),
        out_shape=[jax.ShapeDtypeStruct((height, width), jnp.bfloat16) for _ in grads]
        + [
            jax.ShapeDtypeStruct(small.shape, small.dtype),
            jax.ShapeDtypeStruct(rows.shape, rows.dtype),
            jax.ShapeDtypeStruct((8, width), jnp.float32),
        ],
        in_specs=[any_space] * len(grads) + [vmem, vmem],
        out_specs=[vmem] * len(grads) + [vmem, any_space, vmem],
        scratch_shapes=[pltpu.VMEM((ups, half, width), jnp.bfloat16) for _ in kinds]
        + [pltpu.VMEM(shape, jnp.bfloat16) for shape in got_shapes]
        + [
            pltpu.VMEM((steps,) + small.shape, jnp.bfloat16),
            pltpu.VMEM((steps,) + small.shape, jnp.bfloat16),
        ]
        + mail_sems(len(kinds) * (2 * ups + 2 * steps) + steps)
        + mail_sems(count),
        compiler_params=pltpu.CompilerParams(
            collective_id=7, has_side_effects=True, vmem_limit_bytes=56 * MIB
        ),
        name="reduce_rows",
    )(*grads, small, rows)
    repeats = 1
    for bit, halve in kinds[0][3]:
        repeats *= 1 if halve else 2
    number = len(grads)
    return outs[:number], outs[number], outs[number + 1], jnp.sum(outs[number + 2]) / repeats


class Place:
    def __init__(self, wides, groups):
        self.wide, self.narrow = lax.axis_index("wide"), lax.axis_index("narrow")
        self.wide_steps = self.steps(self.wide, wides)
        self.narrow_steps = self.steps(self.narrow, groups)

    def steps(self, place, size):
        masks = [1 << bit for bit in range(log_two(size))]
        return {mask: mask * (1 - 2 * ((place // mask) % 2)) for mask in masks}

    def peer(self, wide_mask, narrow_mask):
        wide, narrow = self.wide, self.narrow
        for mask, step in self.wide_steps.items():
            wide = wide + step if mask & wide_mask else wide
        for mask, step in self.narrow_steps.items():
            narrow = narrow + step if mask & narrow_mask else narrow
        return wide, narrow


def exchange_kernel(masks, sizes, whole, x_ref, out_ref, send_sem, recv_sem, own_sem):
    wides, groups = sizes
    place = Place(wides, groups)
    masks = list(range(wides * groups)) if masks is None else masks
    count = len(masks)

    def peer(mask):
        return place.peer(mask // groups, mask % groups)

    def each(step):
        for k in range(1, count):
            step(k, masks[k])

    def copy(k, mask):
        return pltpu.make_async_remote_copy(
            src_ref=x_ref if whole else x_ref.at[k],
            dst_ref=out_ref.at[k],
            send_sem=send_sem.at[k],
            recv_sem=recv_sem.at[k],
            device_id=peer(mask),
            device_id_type=MESH,
        )

    barrier = pltpu.get_barrier_semaphore()
    each(
        lambda k, mask: pl.semaphore_signal(
            barrier, inc=1, device_id=peer(mask), device_id_type=MESH
        )
    )
    pl.semaphore_wait(barrier, count - 1)
    each(lambda k, mask: copy(k, mask).start())
    own = pltpu.make_async_copy(x_ref if whole else x_ref.at[0], out_ref.at[0], own_sem)
    own.start()
    own.wait()
    each(lambda k, mask: copy(k, mask).wait())


def exchange(array, number, name, masks=None, whole=True):
    sizes = (lax.axis_size("wide"), lax.axis_size("narrow"))
    count = sizes[0] * sizes[1] if masks is None else len(masks)
    shape = (count,) + array.shape if whole else array.shape
    return pl.pallas_call(
        functools.partial(exchange_kernel, masks, sizes, whole),
        out_shape=jax.ShapeDtypeStruct(shape, array.dtype),
        in_specs=[pl.BlockSpec(memory_space=pltpu.VMEM)],
        out_specs=pl.BlockSpec(memory_space=pltpu.VMEM),
        scratch_shapes=[
            pltpu.SemaphoreType.DMA((count,)),
            pltpu.SemaphoreType.DMA((count,)),
            pltpu.SemaphoreType.DMA,
        ],
        compiler_params=pltpu.CompilerParams(
            collective_id=number, has_side_effects=True, vmem_limit_bytes=32 * MIB
        ),
        name=name,
    )(array)


def merge_stats(stats):
    masks = group_masks()
    rows = stats.shape[1] // 4
    parts = exchange(stats, 1, "stats_swap", masks, False)
    top, total, picked = (parts[:, i * rows : (i + 1) * rows] for i in range(3))
    highest = jnp.max(top, 0)
    own = highest + jnp.log(jnp.sum(total * jnp.exp(top - highest), 0))
    share = exchange(jnp.pad(own, ((0, -rows % 8), (0, 0))), 8, "stats_share", masks)
    return share[:, :rows], own, jnp.sum(picked, 0)


def put_columns(rows_ref, column_ref):
    turned = rows_ref[...].T
    for place in range(rows_ref.shape[0]):
        column_ref[pl.ds(place * 128, 128), :] = turned[:, place : place + 1]


def as_rows(column):
    count = column.shape[0] // 128
    return jnp.concatenate(
        [column[place * 128 : (place + 1) * 128] for place in range(count)], 1
    ).T


def score_kernel(
    rows_ref, table_ref, target_ref, exps_ref, max_ref, stat_ref, sum_ref, pick_ref, column_ref
):
    tile = pl.program_id(0)
    width = table_ref.shape[0]

    @pl.when(tile == 0)
    def _():
        max_ref[...] = jnp.full_like(max_ref, -jnp.inf)
        sum_ref[...] = jnp.zeros_like(sum_ref)
        pick_ref[...] = jnp.zeros_like(pick_ref)
        put_columns(target_ref, column_ref)

    def step(block, carry):
        rows = pl.ds(pl.multiple_of(block * TOKEN_TILE, TOKEN_TILE), TOKEN_TILE)
        scores = lax.dot_general(
            rows_ref[rows, :],
            table_ref[...],
            (((1,), (1,)), ((), ())),
            preferred_element_type=jnp.float32,
        )
        top = jnp.max(scores, -1, keepdims=True)
        powers = jnp.exp(scores - top)
        exps_ref[rows, :] = powers.astype(jnp.bfloat16)
        total = jnp.sum(powers, -1, keepdims=True)
        columns = lax.broadcasted_iota(jnp.int32, (TOKEN_TILE, width), 1)
        wanted = column_ref[rows, :] - tile * width
        hit = jnp.sum(jnp.where(columns == wanted, scores, 0.0), -1, keepdims=True)
        here = lax.broadcasted_iota(jnp.int32, (TOKEN_TILE, 128), 1) == tile
        max_ref[rows, :] = jnp.where(here, top, max_ref[rows, :])
        sum_ref[rows, :] = jnp.where(here, total, sum_ref[rows, :])
        pick_ref[rows, :] = jnp.where(here, hit, pick_ref[rows, :])
        return carry

    lax.fori_loop(0, rows_ref.shape[0] // TOKEN_TILE, step, 0, unroll=8)

    @pl.when(tile == pl.num_programs(0) - 1)
    def _():
        maxima = max_ref[...]
        top = jnp.max(maxima, -1, keepdims=True)
        total = jnp.sum(sum_ref[...] * jnp.exp(maxima - top), -1, keepdims=True)
        picked = jnp.sum(pick_ref[...], -1, keepdims=True)
        blocks, height, _ = stat_ref.shape
        rows = height // 4
        stat_ref[...] = jnp.zeros_like(stat_ref)
        for number, column in enumerate((top, total, picked)):
            lines = as_rows(column)
            for block in range(blocks):
                stat_ref[block, pl.ds(number * rows, rows), :] = lines[
                    block * rows : (block + 1) * rows
                ]


def vocab_tile(vocab):
    return 1280 if vocab % 1280 == 0 else 640


def head_scores(rows, table, targets, blocks):
    tokens, model = rows.shape
    vocab = table.shape[0]
    width = vocab_tile(vocab)
    stat = pltpu.VMEM((tokens, 128), jnp.float32)
    whole = pl.BlockSpec((tokens, 128), lambda j: (0, 0))
    height = 4 * (tokens // blocks // 128)
    return pl.pallas_call(
        score_kernel,
        grid=(vocab // width,),
        out_shape=(
            jax.ShapeDtypeStruct((tokens, vocab), jnp.bfloat16),
            jax.ShapeDtypeStruct((tokens, 128), jnp.float32),
            jax.ShapeDtypeStruct((blocks, height, 128), jnp.float32),
        ),
        in_specs=[
            pl.BlockSpec((tokens, model), lambda j: (0, 0)),
            pl.BlockSpec((width, model), lambda j: (j, 0)),
            pl.BlockSpec(targets.shape, lambda j: (0, 0)),
        ],
        out_specs=(
            pl.BlockSpec((tokens, width), lambda j: (0, j)),
            whole,
            pl.BlockSpec((blocks, height, 128), lambda j: (0, 0, 0)),
        ),
        scratch_shapes=[stat, stat, pltpu.VMEM((tokens, 1), jnp.int32)],
        compiler_params=pltpu.CompilerParams(vmem_limit_bytes=60 * MIB),
        cost_estimate=pl.CostEstimate(
            flops=3 * tokens * vocab * model,
            bytes_accessed=2 * tokens * vocab,
            transcendentals=tokens * vocab,
        ),
        name="head_scores",
    )(rows, table, targets)


def slope_kernel(
    exps_ref,
    max_ref,
    log_ref,
    target_ref,
    table_ref,
    slope_ref,
    grad_ref,
    total_ref,
    column_ref,
    log_column_ref,
):
    tile = pl.program_id(0)
    width = table_ref.shape[0]

    @pl.when(tile == 0)
    def _():
        total_ref[...] = jnp.zeros_like(total_ref)
        put_columns(target_ref, column_ref)
        put_columns(log_ref, log_column_ref)

    def step(block, carry):
        rows = pl.ds(pl.multiple_of(block * TOKEN_TILE, TOKEN_TILE), TOKEN_TILE)
        here = lax.broadcasted_iota(jnp.int32, (TOKEN_TILE, 128), 1) == tile
        top = jnp.sum(jnp.where(here, max_ref[rows, :], 0.0), -1, keepdims=True)
        scale = jnp.exp(top - log_column_ref[rows, :])
        columns = lax.broadcasted_iota(jnp.int32, (TOKEN_TILE, width), 1)
        wanted = column_ref[rows, :] - tile * width
        probs = exps_ref[rows, :].astype(jnp.float32) * scale
        slope = jnp.where(columns == wanted, probs - 1.0, probs).astype(jnp.bfloat16)
        slope_ref[rows, :] = slope
        total_ref[rows, :] += jnp.dot(slope, table_ref[...], preferred_element_type=jnp.float32)
        return carry

    lax.fori_loop(0, exps_ref.shape[0] // TOKEN_TILE, step, 0, unroll=8)

    @pl.when(tile == pl.num_programs(0) - 1)
    def _():
        grad_ref[...] = total_ref[...].astype(jnp.bfloat16)


def head_slopes(exps, maxima, logs, targets, table):
    tokens, vocab = exps.shape
    model = table.shape[1]
    width = vocab_tile(vocab)
    return pl.pallas_call(
        slope_kernel,
        grid=(vocab // width,),
        out_shape=(
            jax.ShapeDtypeStruct((tokens, vocab), jnp.bfloat16),
            jax.ShapeDtypeStruct((tokens, model), jnp.bfloat16),
        ),
        in_specs=[
            pl.BlockSpec((tokens, width), lambda j: (0, j)),
            pl.BlockSpec((tokens, 128), lambda j: (0, 0)),
            pl.BlockSpec(logs.shape, lambda j: (0, 0)),
            pl.BlockSpec(targets.shape, lambda j: (0, 0)),
            pl.BlockSpec((width, model), lambda j: (j, 0)),
        ],
        out_specs=(
            pl.BlockSpec((tokens, width), lambda j: (0, j)),
            pl.BlockSpec((tokens, model), lambda j: (0, 0)),
        ),
        scratch_shapes=[
            pltpu.VMEM((tokens, model), jnp.float32),
            pltpu.VMEM((tokens, 1), jnp.int32),
            pltpu.VMEM((tokens, 1), jnp.float32),
        ],
        compiler_params=pltpu.CompilerParams(vmem_limit_bytes=60 * MIB),
        cost_estimate=pl.CostEstimate(
            flops=3 * tokens * vocab * model,
            bytes_accessed=4 * tokens * vocab,
            transcendentals=0,
        ),
        name="head_slopes",
    )(exps, maxima, logs, targets, table)


def one_hot(places, size):
    return (places.reshape(-1, 1) == jnp.arange(size)[None]).astype(jnp.bfloat16)


def token_plan(ids_all, shard_rows):
    chips, tokens = ids_all.shape
    wides, ups = chip_sizes()
    wide, narrow = lax.axis_index("wide"), lax.axis_index("narrow")
    own_core = narrow % 2
    own_chip = wide * ups + narrow // 2
    owner = ids_all // shard_rows
    owner_core = jnp.bitwise_xor(owner % 2, own_core)
    owner_chip = jnp.bitwise_xor(owner // 2, own_chip)
    local = ids_all % shard_rows
    row = lax.broadcasted_iota(jnp.int32, (tokens, tokens), 0)
    column = lax.broadcasted_iota(jnp.int32, (tokens, tokens), 1)
    before = column < row
    alike = ids_all[:, :, None] == ids_all[:, None, :]
    first = ~jnp.any(alike & before[None], 2)
    served = first & (owner_chip == 0) & (owner_core == 0)
    served_rank = times_t(served.astype(jnp.bfloat16), before.astype(jnp.bfloat16)).astype(
        jnp.int32
    )
    half = tokens // 2
    mine = lambda array: lax.dynamic_slice_in_dim(array, own_core * half, half)
    own_first = mine(jnp.min(jnp.where(alike[0], column, tokens), 1))
    same_owner = mine(owner[0])[:, None] == owner[0][None]
    own_rank = jnp.sum(
        (same_owner & first[0][None] & (column[:half] < own_first[:, None])).astype(jnp.int32), 1
    )
    own_block = mine(owner_core[0]) * chips + mine(owner_chip[0])
    most = jnp.max(
        jnp.sum(
            (
                first[:, None, :]
                & (owner[:, None, :] == jnp.arange(2 * chips)[None, :, None])
            ).astype(jnp.int32),
            2,
        )
    )
    rounds = (most + SLOTS - 1) // SLOTS

    def plan(turn):
        slot = jnp.arange(SLOTS)[None, :, None] + turn * SLOTS
        chosen = served[:, None, :] & (served_rank[:, None, :] == slot)
        slot_rows = jnp.sum(jnp.where(chosen, local[:, None, :] + 1, 0), 2) - 1
        inside = own_rank - turn * SLOTS
        valid = (inside >= 0) & (inside < SLOTS)
        own_slots = jnp.where(valid, own_block * SLOTS + inside, -1)
        return one_hot(slot_rows, shard_rows), one_hot(own_slots, 2 * chips * SLOTS)

    return plan, rounds


def later_rounds(rounds, turn, total):
    return lax.while_loop(
        lambda state: state[0] < rounds,
        lambda state: (state[0] + 1, state[1] + turn(state[0])),
        (jnp.ones((), jnp.int32), total),
    )[1]


def upper_blocks(count):
    return [(i, j) for i in range(count) for j in range(i, count)]


def muon_kernel(lane_bits, *refs):
    core, _, y_bits, _ = lane_bits
    low_refs = refs[:4]
    rest_out, size_out = refs[4:6]
    gram, sent, got, back, full, total, half, low_a, low_b, low_c, send_sem, recv_sem = refs[6:]
    width = full.shape[0]
    block = gram.shape[-1]
    places = upper_blocks(width // block)
    wide, narrow = lax.axis_index("wide"), lax.axis_index("narrow")
    greet([neighbour(bit) for bit in [core] + y_bits])
    mail = Mail(send_sem, recv_sem)
    own_core, own_up = narrow % 2, (narrow // 2) % 2
    own = 2 * own_core + own_up

    for number, low_ref in enumerate(low_refs):
        for place, (i, j) in enumerate(places):
            product = lax.dot_general(
                low_ref[:, i * block : (i + 1) * block],
                low_ref[:, j * block : (j + 1) * block],
                (((0,), (0,)), ((), ())),
                preferred_element_type=jnp.float32,
            )
            gram[number, place] = product
    for slot in range(2):
        sent[slot] = gram[2 * (1 - own_core) + slot].astype(jnp.bfloat16)
    mail.take(mail.post(sent.at[pl.ds(0, 2)], got.at[pl.ds(0, 2)], core))

    def add(number, slot):
        for place in range(len(places)):
            gram[number, place] += got[slot, place].astype(jnp.float32)

    def pass_on(number, slot, bit):
        sent[slot] = gram[number].astype(jnp.bfloat16)
        return mail.post(sent.at[slot], got.at[slot], bit)

    other_up = 2 * own_core + 1 - own_up
    if y_bits:
        add(other_up, 1 - own_up)
        over_y = pass_on(other_up, 2, y_bits[0])
        add(own, own_up)
        mail.take(over_y)
        add(own, 2)
    for level, bit in enumerate(y_bits[1:]):
        mail.take(pass_on(own, 3 + level, bit))
        add(own, 3 + level)

    def unpack(source, target):
        for place, (i, j) in enumerate(places):
            piece = source(place)
            target(i, j, piece)
            if i != j:
                target(j, i, piece.T)

    def spans(i, j):
        return pl.ds(i * block, block), pl.ds(j * block, block)

    def put_full(i, j, piece):
        full[spans(i, j)] = piece

    unpack(lambda place: gram[own, place], put_full)
    diagonal = lax.broadcasted_iota(jnp.int32, (block, block), 0) == lax.broadcasted_iota(
        jnp.int32, (block, block), 1
    )
    trace = jnp.zeros((1, 1), jnp.float32)
    for i in range(width // block):
        trace = trace + jnp.sum(jnp.where(diagonal, full[spans(i, i)], 0.0), keepdims=True)
    magnitude = jnp.sqrt(trace) + 1e-07
    inverse = 1.0 / magnitude

    def rows(step):
        def body(i, carry):
            step(pl.ds(pl.multiple_of(i * block, block), block))
            return carry

        lax.fori_loop(0, width // block, body, 0)

    def times(left, right, span):
        return jnp.dot(left[span, :], right[...], preferred_element_type=jnp.float32)

    def start(span):
        scaled = full[span, :] * (inverse * inverse)
        full[span, :] = scaled
        low_a[span, :] = scaled.astype(jnp.bfloat16)

    rows(start)
    scale = NS_A
    for cycle_no in range(NS_STEPS):

        def rest_step(span):
            rest = NS_B * full[span, :] + NS_C * times(low_a, low_a, span)
            low_b[span, :] = rest.astype(jnp.bfloat16)
            if cycle_no == 0:
                total[span, :] = rest
            else:
                total[span, :] = NS_A * total[span, :] + scale * rest

        rows(rest_step)
        if cycle_no:

            def total_step(span):
                total[span, :] += times(low_c, low_b, span)

            rows(total_step)
            scale = scale * NS_A
        if cycle_no < NS_STEPS - 1:

            def keep_total(span):
                low_c[span, :] = total[span, :].astype(jnp.bfloat16)

            def half_step(span):
                half[span, :] = NS_A * full[span, :] + times(low_a, low_b, span)

            def full_step(span):
                value = half[span, :]
                low_a[span, :] = value.astype(jnp.bfloat16)
                full[span, :] = NS_A * value + times(low_a, low_b, span)

            def low_step(span):
                low_a[span, :] = full[span, :].astype(jnp.bfloat16)

            rows(keep_total)
            rows(half_step)
            rows(full_step)
            rows(low_step)

    for place, (i, j) in enumerate(places):
        back[own, place] = (total[spans(i, j)] * inverse).astype(jnp.bfloat16)
    lane = lax.broadcasted_iota(jnp.int32, (8, 128), 1)
    size_out[own] = jnp.where(lane >= 0, inverse, 0.0)
    mail.close()
    mail = Mail(send_sem.at[pl.ds(16, 16)], recv_sem.at[pl.ds(16, 16)])
    mine = mail.post(back.at[own], back.at[own], core)
    mine_size = mail.post(size_out.at[own], size_out.at[own], core)
    if y_bits:
        over_y = mail.post(back.at[own], back.at[own], y_bits[0])
        over_size = mail.post(size_out.at[own], size_out.at[own], y_bits[0])
        mail.take(over_y)
        mail.take(over_size)
        mail.post(back.at[other_up], back.at[other_up], core)
        mail.post(size_out.at[other_up], size_out.at[other_up], core)
    mail.close()
    for number in range(4):

        def put_out(i, j, piece, number=number):
            rest_out[(number,) + spans(i, j)] = piece.astype(jnp.bfloat16)

        unpack(lambda place: back[number, place].astype(jnp.float32), put_out)


def muon_factors(lows):
    width = lows[0].shape[1]
    block = 256
    count = len(upper_blocks(width // block))
    lane_bits = lanes()
    extra = max(len(lane_bits[2]) - 1, 0)
    vmem = pl.BlockSpec(memory_space=pltpu.VMEM)
    square = (width, width)
    rests, sizes = pl.pallas_call(
        functools.partial(muon_kernel, lane_bits),
        out_shape=(
            jax.ShapeDtypeStruct((4,) + square, jnp.bfloat16),
            jax.ShapeDtypeStruct((4, 8, 128), jnp.float32),
        ),
        in_specs=[vmem] * 4,
        out_specs=(vmem, vmem),
        scratch_shapes=[
            pltpu.VMEM((4, count, block, block), jnp.float32),
            pltpu.VMEM((3 + extra, count, block, block), jnp.bfloat16),
            pltpu.VMEM((3 + extra, count, block, block), jnp.bfloat16),
            pltpu.VMEM((4, count, block, block), jnp.bfloat16),
        ]
        + [pltpu.VMEM(square, jnp.float32) for _ in range(3)]
        + [pltpu.VMEM(square, jnp.bfloat16) for _ in range(3)]
        + mail_sems(32),
        compiler_params=pltpu.CompilerParams(
            collective_id=9, has_side_effects=True, vmem_limit_bytes=56 * MIB
        ),
        name="muon_factors",
    )(*lows)
    return rests, sizes[:, 0, 0]


def on_device(
    token_ids,
    targets,
    joint_weight,
    output_weight,
    expand_weight,
    reduce_weight,
    joint_velocity,
    output_velocity,
    expand_velocity,
    reduce_velocity,
    embedding,
    embed_moment,
    embed_square,
    positions,
    position_moment,
    position_square,
    norm_gains,
    gain_moment,
    gain_square,
    biases,
    bias_moment,
    bias_square,
):
    core, x_bits, y_bits, z_bits = lanes()
    groups = lax.axis_size("narrow")
    wides = lax.axis_size("wide")
    across = 1 << len(x_bits)
    model_width = embedding.shape[1]
    shard_rows = embedding.shape[0]
    tokens = token_ids.shape[0] * LENGTH
    shifts = biases[: 3 * model_width].reshape(3, model_width)

    own_rows = embedding.astype(jnp.bfloat16)
    labels = jnp.concatenate([token_ids.reshape(-1, 128), targets.reshape(-1, 128)])
    spare = -labels.shape[0] % 8
    labels = exchange(jnp.pad(labels, ((0, spare), (0, 0))), 0, "label_share")
    ids_all = labels[:, : tokens // 128].reshape(-1, tokens)
    lines = tokens // 128
    own_block = lax.axis_index("wide") * groups + lax.axis_index("narrow")
    wides, ups = chip_sizes()
    pairs = ids_all.reshape(wides, ups, 2, tokens)
    other_first = lax.axis_index("narrow") % 2 == 1
    ids_chips = jnp.where(other_first, lax.rev(pairs, (2,)), pairs).reshape(wides * ups, -1)
    plan, rounds = token_plan(ids_chips, shard_rows)

    def serve(served):
        return plain(served, own_rows).astype(jnp.bfloat16).reshape(-1, SLOTS, model_width)

    masters = (joint_weight, output_weight, expand_weight, reduce_weight)
    served, wanted = plan(0)
    table, weights, token_rows = load_all(
        own_rows, [master.astype(jnp.bfloat16) for master in masters], serve(served)
    )
    vocab_here = table.shape[0]

    def fetch(turn):
        more, places = plan(turn)
        got = swap_rows(serve(more))
        return plain(places, jnp.stack([got, swap(got, core)]).reshape(-1, model_width))

    embedded = later_rounds(rounds, fetch, plain(wanted, token_rows.reshape(-1, model_width)))

    block_masks = jnp.array(group_masks())
    targets_group = labels[block_masks, lines : 2 * lines].reshape(-1, 128)
    table_mask = groups * (across - 1) + 1
    differ = jnp.bitwise_xor(targets_group // shard_rows, own_block)
    is_owned = (targets_group >= 0) & (jnp.bitwise_and(differ, ~table_mask) == 0)
    place = (differ % 2) * across + (differ // groups) % across
    rows_targets = jnp.where(is_owned, place * shard_rows + targets_group % shard_rows, -1)
    stream_in = embedded + jnp.tile(positions, (token_ids.shape[0], 1))
    stream_out, saved = layer_forward(stream_in, weights, norm_gains, biases)
    final_norm, normed_f, inverse_f = norm_forward(stream_out, norm_gains[2], shifts[2])
    group_rows = spread(final_norm.astype(jnp.bfloat16)).reshape(-1, model_width)
    blocks = len(group_masks())
    exps, maxima, stats = head_scores(group_rows, table, rows_targets, blocks)
    logs, own_logs, own_picked = merge_stats(stats)
    loss_part = jnp.sum(
        jnp.where(targets.reshape(-1, 128) >= 0, own_logs - own_picked, 0.0)
    )
    logs = jnp.where(targets_group >= 0, logs.reshape(-1, 128), jnp.inf)
    slopes, final_part = head_slopes(exps, maxima, logs, rows_targets, table)
    final_grad, table_sum, passed = head_back(
        final_part.reshape(-1, tokens, model_width), slopes, group_rows
    )
    for bit in reversed(x_bits):
        table_sum = table_sum + swap(passed, bit).astype(jnp.float32)
        half = table_sum.shape[0] // 2
        if bit != x_bits[0]:
            table_sum, passed = table_sum[:half], table_sum[half:].astype(jnp.bfloat16)
    back_f, gain_f, shift_f = norm_backward(final_grad, normed_f, inverse_f, norm_gains[2])
    stream_grad, factors, gain_pair, shift_pair, bias_tail = layer_backward(
        back_f, weights, norm_gains, saved
    )
    low_grad = stream_grad.astype(jnp.bfloat16)

    def bundle(places):
        both = outer_sum(places, low_grad).astype(jnp.bfloat16)
        both = both.reshape(2, -1, SLOTS, model_width)
        other = swap(both[1], core)
        return (both[0].astype(jnp.float32) + other.astype(jnp.float32)).astype(jnp.bfloat16)

    position_grad = jnp.sum(stream_grad.reshape(-1, LENGTH, model_width), 0)
    gain_grad = jnp.stack([gain_pair[0], gain_pair[1], gain_f])
    bias_grad = jnp.concatenate([shift_pair[0], shift_pair[1], shift_f, bias_tail])
    count_part = jnp.sum((targets >= 0).astype(jnp.float32))
    small = jnp.concatenate(
        [gain_grad.reshape(-1), bias_grad, position_grad.reshape(-1)]
    ).reshape(-1, model_width)
    small_rows = small.shape[0]
    small = jnp.pad(small, ((0, -small_rows % 16), (0, 0)))

    def by_owner(pair):
        return outer_sum(*pair).astype(jnp.bfloat16).reshape(groups, -1, model_width)

    joint_part, output_part, expand_part, reduce_part = (by_owner(pair) for pair in factors)
    joint_rows = joint_part.shape[1]
    (front, expand_sum, reduce_sum), small, row_sums, squares = reduce_all(
        [jnp.concatenate([joint_part, output_part], 1), expand_part, reduce_part],
        small,
        bundle(wanted),
    )
    table_sum = table_sum + outer_sum(served, row_sums.reshape(-1, model_width))

    def give(turn):
        more, places = plan(turn)
        return outer_sum(more, swap_rows(bundle(places)).reshape(-1, model_width))

    table_sum = later_rounds(rounds, give, table_sum)
    matrix_total = [
        part.astype(jnp.float32)
        for part in (front[:joint_rows], front[joint_rows:], expand_sum, reduce_sum)
    ]
    small = small[:small_rows]
    squares = squares + jnp.sum(table_sum * table_sum)
    scalars = jnp.pad(jnp.stack([loss_part, count_part, squares])[None], ((0, 7), (0, 125)))
    scalars = jnp.sum(exchange(scalars, 3, "scalar_share"), 0)
    loss_sum, loss_count, squares = scalars[0, 0], scalars[0, 1], scalars[0, 2]
    squares = squares + jnp.sum(small * small)
    small = small.reshape(-1)
    gain_grad = small[: gain_grad.size].reshape(gain_grad.shape)
    bias_grad = small[gain_grad.size : gain_grad.size + bias_grad.size]
    position_grad = small[gain_grad.size + bias_grad.size :].reshape(position_grad.shape)
    grad_norm = jnp.sqrt(squares) / loss_count
    factor = jnp.minimum(1.0, CLIP / (grad_norm + 1e-06)) / loss_count
    previous = (joint_velocity, output_velocity, expand_velocity, reduce_velocity)
    carried = tuple(
        (MOMENTUM * before + gradient * factor for before, gradient in zip(previous, matrix_total))
    )
    lows = [moment.astype(jnp.bfloat16) for moment in carried]
    rests, inverses = muon_factors(lows)
    updated = []
    for number, (master, moment) in enumerate(zip(masters, carried)):
        orth = moment * (NS_A**NS_STEPS * inverses[number]) + plain(
            lows[number], rests[number]
        )
        shape_factor = math.sqrt(max(1.0, master.shape[0] * groups / master.shape[1]))
        updated.append(master * (1 - MUON_RATE * DECAY) - MUON_RATE * shape_factor * orth)
    table_out = adam_step(
        embedding, embed_moment, embed_square, table_sum * factor, EMBED_RATE, DECAY
    )
    place_out = adam_step(
        positions, position_moment, position_square, position_grad * factor, PLACE_RATE, DECAY
    )
    gain_out = adam_step(norm_gains, gain_moment, gain_square, gain_grad * factor, SMALL_RATE, 0.0)
    bias_out = adam_step(biases, bias_moment, bias_square, bias_grad * factor, SMALL_RATE, 0.0)
    return (
        loss_sum,
        loss_count,
        grad_norm,
        updated[0],
        updated[1],
        updated[2],
        updated[3],
        carried[0],
        carried[1],
        carried[2],
        carried[3],
        table_out[0],
        table_out[1],
        table_out[2],
        place_out[0],
        place_out[1],
        place_out[2],
        gain_out[0],
        gain_out[1],
        gain_out[2],
        bias_out[0],
        bias_out[1],
        bias_out[2],
    )


def solution(mesh):
    in_specs = (
        P(("wide", "narrow"), None),
        P(("wide", "narrow"), None),
        P("narrow", None),
        P("narrow", None),
        P("narrow", None),
        P("narrow", None),
        P("narrow", None),
        P("narrow", None),
        P("narrow", None),
        P("narrow", None),
        P(("wide", "narrow"), None),
        P(("wide", "narrow"), None),
        P(("wide", "narrow"), None),
        P(),
        P(),
        P(),
        P(),
        P(),
        P(),
        P(),
        P(),
        P(),
    )
    out_specs = (
        P(),
        P(),
        P(),
        P("narrow", None),
        P("narrow", None),
        P("narrow", None),
        P("narrow", None),
        P("narrow", None),
        P("narrow", None),
        P("narrow", None),
        P("narrow", None),
        P(("wide", "narrow"), None),
        P(("wide", "narrow"), None),
        P(("wide", "narrow"), None),
        P(),
        P(),
        P(),
        P(),
        P(),
        P(),
        P(),
        P(),
        P(),
    )
    return jax.shard_map(
        on_device, mesh=mesh, in_specs=in_specs, out_specs=out_specs, check_vma=False
    )
```

```python
import functools
import math

import jax
import jax.numpy as jnp
from jax import lax
from jax.experimental import pallas as pl
from jax.experimental.pallas import tpu as pltpu
from jax.sharding import PartitionSpec as P

HEADS = 12
HEAD = 64
LENGTH = 64
NS_STEPS = 3
STEP = 10


HIGH = lax.Precision.HIGHEST
EPS = 1e-05
CLIP = 0.05
MOMENTUM = 0.95
MUON_RATE = 0.5
DECAY = 0.1
BETA_ONE = 0.9
BETA_TWO = 0.999
EMBED_RATE = 0.02
PLACE_RATE = 0.1
SMALL_RATE = 0.2
NS_A = 3.4445
NS_B = -4.775
NS_C = 2.0315
MESH = pl.DeviceIdType.MESH
MIB = 1 << 20
TOKEN_TILE = 256
SLOTS = 32


def times_t(left, right):
    return lax.dot_general(
        left, right, (((1,), (1,)), ((), ())), preferred_element_type=jnp.float32
    )


def outer_sum(left, right):
    return lax.dot_general(
        left, right, (((0,), (0,)), ((), ())), preferred_element_type=jnp.float32
    )


def plain(left, right):
    return jnp.dot(left, right, preferred_element_type=jnp.float32)


def norm_forward(stream, gain, shift):
    centred = stream - jnp.mean(stream, -1, keepdims=True)
    inverse = lax.rsqrt(jnp.mean(centred * centred, -1, keepdims=True) + EPS)
    normed = centred * inverse
    return (normed * gain + shift, normed, inverse)


def norm_backward(upstream, normed, inverse, gain):
    scaled = upstream * gain
    inner = inverse * (
        scaled
        - jnp.mean(scaled, -1, keepdims=True)
        - normed * jnp.mean(scaled * normed, -1, keepdims=True)
    )
    return (
        inner,
        jnp.sum(upstream * normed, 0, keepdims=True),
        jnp.sum(upstream, 0, keepdims=True),
    )


def gelu_tanh(values):
    return jax.nn.gelu(values, approximate=True)


def column_sum(values):
    return jnp.sum(values.astype(jnp.float32), 0, keepdims=True)


def pair_masks(tokens):
    first = lax.broadcasted_iota(jnp.int32, (tokens, 2 * HEAD), 1) < HEAD
    row = lax.broadcasted_iota(jnp.int32, (tokens, tokens), 0)
    column = lax.broadcasted_iota(jnp.int32, (tokens, tokens), 1)
    return first, (row // LENGTH == column // LENGTH) & (column <= row)


def head_probs(queries, key_heads, seen):
    scores = times_t(queries, key_heads) * HEAD ** (-0.5)
    scores = jnp.where(seen, scores, -1000000000.0)
    powers = jnp.exp(scores - jnp.max(scores, -1, keepdims=True))
    return powers * (1.0 / jnp.sum(powers, -1, keepdims=True))


def forward_kernel(
    x_ref,
    place_ref,
    gain_ref,
    bias_ref,
    joint_hbm,
    output_hbm,
    expand_hbm,
    reduce_hbm,
    low_ref,
    normed_ref,
    inverse_ref,
    joint_out,
    context_ref,
    upward_ref,
    joint_ref,
    output_ref,
    expand_ref,
    reduce_ref,
    load_sem,
):
    pairs = ((joint_hbm, joint_ref), (output_hbm, output_ref), (expand_hbm, expand_ref), (reduce_hbm, reduce_ref))
    loads = [
        pltpu.make_async_copy(source, target, load_sem.at[number])
        for number, (source, target) in enumerate(pairs)
    ]
    for load in loads:
        load.start()
    tokens, width = x_ref.shape

    def norm(number, stream):
        result, normed, inverse = norm_forward(
            stream, gain_ref[number : number + 1, :], bias_ref[number : number + 1, :]
        )
        normed_ref[number] = normed
        inverse_ref[number] = jnp.broadcast_to(inverse, (tokens, 128))
        return result.astype(jnp.bfloat16)

    stream = x_ref[...] + jnp.concatenate([place_ref[...]] * (tokens // LENGTH), 0)
    first_low = norm(0, stream)
    loads[0].wait()
    for part in range(3):
        span = pl.ds(part * width, width)
        result = times_t(first_low, joint_ref[span, :])
        if part != 1:
            row = 3 if part == 0 else 4
            result = result + bias_ref[row : row + 1, :]
        joint_out[:, span] = result.astype(jnp.bfloat16)
    first, seen = pair_masks(tokens)
    zero = jnp.zeros((), jnp.bfloat16)
    for pair in range(HEADS // 2):
        queries = joint_out[:, pl.ds(pair * 128, 128)]
        key_heads = joint_out[:, pl.ds(width + pair * 128, 128)]
        values = joint_out[:, pl.ds(2 * width + pair * 128, 128)]
        parts = []
        for mine in (first, ~first):
            probs = head_probs(jnp.where(mine, queries, zero), key_heads, seen)
            parts.append(plain(probs.astype(jnp.bfloat16), values))
        context_ref[:, pl.ds(pair * 128, 128)] = jnp.where(first, *parts).astype(jnp.bfloat16)
    loads[1].wait()
    stream = stream + times_t(context_ref[...], output_ref[...]) + bias_ref[5:6, :]
    second_low = norm(1, stream)
    stream = stream + bias_ref[6:7, :]
    loads[2].wait()
    loads[3].wait()
    for part in range(expand_ref.shape[0] // width):
        span = pl.ds(part * width, width)
        upward = times_t(second_low, expand_ref[span, :]) + bias_ref[7 + part : 8 + part, :]
        upward_ref[:, span] = upward
        stream = stream + plain(gelu_tanh(upward).astype(jnp.bfloat16), reduce_ref[span, :])
    low_ref[...] = norm(2, stream)


def layer_forward(embedded, positions, norm_gains, bias_rows, weights):
    tokens, width = embedded.shape
    vmem, any_space = pl.BlockSpec(memory_space=pltpu.VMEM), pl.BlockSpec(memory_space=pl.ANY)
    shape = jax.ShapeDtypeStruct
    hidden = weights[2].shape[0]
    return pl.pallas_call(
        forward_kernel,
        out_shape=(
            shape((tokens, width), jnp.bfloat16),
            shape((3, tokens, width), jnp.float32),
            shape((3, tokens, 128), jnp.float32),
            shape((tokens, 3 * width), jnp.bfloat16),
            shape((tokens, width), jnp.bfloat16),
            shape((tokens, hidden), jnp.float32),
        ),
        in_specs=[vmem] * 4 + [any_space] * 4,
        out_specs=[vmem] * 6,
        scratch_shapes=[pltpu.VMEM(w.shape, w.dtype) for w in weights]
        + [pltpu.SemaphoreType.DMA((4,))],
        compiler_params=pltpu.CompilerParams(vmem_limit_bytes=56 * MIB),
        name="layer_forward",
    )(embedded, positions, norm_gains, bias_rows, *weights)


def gelu_slope(values):
    inner = math.sqrt(2.0 / math.pi)
    squared = values * values
    bent = jnp.tanh(inner * (values + 0.044715 * squared * values))
    return 0.5 * values * (1.0 + bent), 0.5 * (1.0 + bent) + 0.5 * values * (
        1.0 - bent * bent
    ) * (inner * (1.0 + 3 * 0.044715 * squared))


def backward_flow(ins, outs, scratch):
    (final_ref, gain_ref, bias_ref, normed_ref, inverse_ref, joint_in, context_ref, upward_ref) = ins
    (stream_ref, small_ref, front_ref, expand_out, reduce_out) = outs
    (joint_ref, output_ref, expand_ref, reduce_ref, waits, joint_grad, context_grad) = scratch
    tokens, width = final_ref.shape
    groups, height, _ = front_ref.shape

    def gain(number):
        return gain_ref[number : number + 1, :]

    def normed_low(number):
        return (normed_ref[number] * gain(number) + bias_ref[number : number + 1, :]).astype(
            jnp.bfloat16
        )

    def back(number, upstream):
        inner, gain_row, shift_row = norm_backward(
            upstream, normed_ref[number], inverse_ref[number][:, :1], gain(number)
        )
        small_ref[number : number + 1, :] = gain_row
        small_ref[3 + number : 4 + number, :] = shift_row
        return inner

    small_ref[...] = jnp.zeros_like(small_ref)
    back_f = back(2, final_ref[...])
    down = back_f.astype(jnp.bfloat16)
    small_ref[9:10, :] = column_sum(down)
    second_low = normed_low(1)
    second_grad = jnp.zeros((tokens, width), jnp.float32)
    waits[2].wait()
    waits[3].wait()
    for part in range(expand_ref.shape[0] // width):
        span = pl.ds(part * width, width)
        active, slope = gelu_slope(upward_ref[:, span])
        upward_grad = (times_t(down, reduce_ref[span, :]) * slope).astype(jnp.bfloat16)
        small_ref[10 + part : 11 + part, :] = column_sum(upward_grad)
        second_grad = second_grad + plain(upward_grad, expand_ref[span, :])
        expand_out[span, :] = outer_sum(upward_grad, second_low).astype(jnp.bfloat16)
        reduce_out[span, :] = outer_sum(active.astype(jnp.bfloat16), down).astype(jnp.bfloat16)
    yield True
    mid_grad = back_f + back(1, second_grad)
    stream_ref[...] = mid_grad
    attn_grad = mid_grad.astype(jnp.bfloat16)
    small_ref[8:9, :] = column_sum(attn_grad)
    waits[1].wait()
    context_grad[...] = plain(attn_grad, output_ref[...]).astype(jnp.bfloat16)
    output_grad = outer_sum(attn_grad, context_ref[...]).astype(jnp.bfloat16)
    rows = width // groups
    joint_rows = height - rows
    for group in range(groups):
        front_ref[group, pl.ds(joint_rows, rows), :] = output_grad[
            group * rows : (group + 1) * rows
        ]
    yield True
    first, seen = pair_masks(tokens)
    zero = jnp.zeros((), jnp.bfloat16)
    for pair in range(HEADS // 2):
        spans = [pl.ds(part * width + pair * 128, 128) for part in range(3)]
        queries, key_heads, values = (joint_in[:, span] for span in spans)
        upstream = context_grad[:, spans[0]]
        parts = []
        for mine in (first, ~first):
            probs = head_probs(jnp.where(mine, queries, zero), key_heads, seen)
            probs_grad = times_t(jnp.where(mine, upstream, zero), values)
            score_grad = (
                probs * (probs_grad - jnp.sum(probs * probs_grad, -1, keepdims=True))
            ).astype(jnp.bfloat16)
            parts.append(
                (
                    plain(score_grad, key_heads) * HEAD ** (-0.5),
                    outer_sum(score_grad, queries) * HEAD ** (-0.5),
                    outer_sum(probs.astype(jnp.bfloat16), upstream),
                )
            )
        for span, one, two in zip(spans, *parts):
            joint_grad[:, span] = jnp.where(first, one, two).astype(jnp.bfloat16)
        if pair % 2:
            yield True
    first_low = normed_low(0)
    waits[0].wait()
    first_grad = jnp.zeros((tokens, width), jnp.float32)
    for part in range(3):
        span = pl.ds(part * width, width)
        piece = joint_grad[:, span]
        if part != 1:
            row = 6 if part == 0 else 7
            small_ref[row : row + 1, :] = column_sum(piece)
        first_grad = first_grad + plain(piece, joint_ref[span, :])
        grad = outer_sum(piece, first_low).astype(jnp.bfloat16)
        for group in range(groups):
            start = max(group * joint_rows, part * width)
            end = min((group + 1) * joint_rows, (part + 1) * width)
            if start < end:
                front_ref[group, pl.ds(start - group * joint_rows, end - start), :] = grad[
                    start - part * width : end - part * width
                ]
        yield True
    stream = stream_ref[...] + back(0, first_grad)
    stream_ref[...] = stream
    placed = stream[:LENGTH]
    for sequence in range(1, tokens // LENGTH):
        placed = placed + stream[sequence * LENGTH : (sequence + 1) * LENGTH]
    small_ref[14 : 14 + LENGTH, :] = placed


def backward_kernel(*refs):
    ins, hbm, outs = refs[:8], refs[8:12], refs[12:17]
    weights, load_sem, joint_grad, context_grad = refs[17:21], refs[21], refs[22], refs[23]
    waits = [
        pltpu.make_async_copy(source, target, load_sem.at[number])
        for number, (source, target) in enumerate(zip(hbm, weights))
    ]
    for load in waits:
        load.start()
    for _ in backward_flow(ins, outs, (*weights, waits, joint_grad, context_grad)):
        pass


def layer_backward(final_grad, norm_gains, bias_rows, saved, weights):
    tokens, width = final_grad.shape
    groups = lax.axis_size("narrow")
    hidden = weights[2].shape[0]
    vmem, any_space = pl.BlockSpec(memory_space=pltpu.VMEM), pl.BlockSpec(memory_space=pl.ANY)
    shape = jax.ShapeDtypeStruct
    small_rows = 14 + LENGTH
    return pl.pallas_call(
        backward_kernel,
        out_shape=(
            shape((tokens, width), jnp.float32),
            shape((small_rows + -small_rows % 16, width), jnp.float32),
            shape((groups, 4 * width // groups, width), jnp.bfloat16),
            shape((hidden, width), jnp.bfloat16),
            shape((hidden, width), jnp.bfloat16),
        ),
        in_specs=[vmem] * 8 + [any_space] * 4,
        out_specs=[vmem] * 5,
        scratch_shapes=[pltpu.VMEM(w.shape, w.dtype) for w in weights]
        + [
            pltpu.SemaphoreType.DMA((4,)),
            pltpu.VMEM((tokens, 3 * width), jnp.bfloat16),
            pltpu.VMEM((tokens, width), jnp.bfloat16),
        ],
        compiler_params=pltpu.CompilerParams(vmem_limit_bytes=62 * MIB),
        name="layer_backward",
    )(final_grad, norm_gains, bias_rows, *saved, *weights)


def adam_step(weight, moment, square, gradient, rate, decay):
    moment = BETA_ONE * moment + (1 - BETA_ONE) * gradient
    square = BETA_TWO * square + (1 - BETA_TWO) * gradient * gradient
    unbiased = moment / (1 - BETA_ONE**STEP)
    spread = square / (1 - BETA_TWO**STEP)
    return (
        weight - rate * (unbiased / (jnp.sqrt(spread) + 1e-08) + decay * weight),
        moment,
        square,
    )


def log_two(size):
    return size.bit_length() - 1


def lanes():
    wide, narrow = lax.axis_size("wide"), lax.axis_size("narrow")
    across = wide // 4
    x_bits = [("wide", 1 << i) for i in range(log_two(across))]
    z_bits = [("wide", across << i) for i in range(log_two(wide // across))]
    y_bits = [("narrow", 2 << i) for i in range(log_two(narrow // 2))]
    return ("narrow", 1), x_bits, y_bits, z_bits


def swap(array, bit):
    axis, mask = bit
    return lax.ppermute(array, axis, [(i, i ^ mask) for i in range(lax.axis_size(axis))])


def side(bit):
    axis, mask = bit
    return (lax.axis_index(axis) // mask) % 2


def join(mine, other, bit, dim=0):
    own = side(bit)
    return jnp.where(
        own == 0, jnp.concatenate([mine, other], dim), jnp.concatenate([other, mine], dim)
    )


def halves(array, bit):
    own = side(bit)
    half = array.shape[0] // 2
    keep = lax.dynamic_slice_in_dim(array, own * half, half)
    send = lax.dynamic_slice_in_dim(array, (1 - own) * half, half)
    return keep, send


def group_bits():
    _, _, y_bits, z_bits = lanes()
    return z_bits + y_bits


def routes(rows, pieces):
    _, _, y_bits, z_bits = lanes()
    near, far = z_bits[:1], z_bits[1:]
    longer = rows * 5 // 8 // pieces
    shorter = rows // pieces - longer
    plan = []
    for piece in range(pieces):
        start = piece * (longer + shorter)
        plan.append((start, longer, far + near + y_bits))
        plan.append((start + longer, shorter, far + y_bits + near))
    return plan


def flat_mask(bit):
    axis, mask = bit
    return mask * lax.axis_size("narrow") if axis == "wide" else mask


def group_masks():
    masks = [0]
    for bit in group_bits():
        masks = masks + [other ^ flat_mask(bit) for other in masks]
    return masks


def neighbour(bit):
    axis, mask = bit
    wide, narrow = lax.axis_index("wide"), lax.axis_index("narrow")
    if axis == "wide":
        return wide + mask * (1 - 2 * ((wide // mask) % 2)), narrow
    return wide, narrow + mask * (1 - 2 * ((narrow // mask) % 2))


def greet(devices):
    barrier = pltpu.get_barrier_semaphore()
    for device in devices:
        pl.semaphore_signal(barrier, inc=1, device_id=device, device_id_type=MESH)
    pl.semaphore_wait(barrier, len(devices))


class Mail:
    def __init__(self, send_sem, recv_sem):
        self.send_sem, self.recv_sem = send_sem, recv_sem
        self.used, self.sent, self.open = 0, [], []

    def post(self, source, target, bit):
        copy = pltpu.make_async_remote_copy(
            src_ref=source,
            dst_ref=target,
            send_sem=self.send_sem.at[self.used],
            recv_sem=self.recv_sem.at[self.used],
            device_id=neighbour(bit),
            device_id_type=MESH,
        )
        copy.start()
        self.used += 1
        self.sent.append(copy)
        self.open.append(copy)
        return copy

    def keep(self, source, target):
        copy = pltpu.make_async_copy(source, target, self.recv_sem.at[self.used])
        copy.start()
        self.used += 1
        self.open.append(copy)
        return copy

    def take(self, copy):
        if any(other is copy for other in self.open):
            self.open = [other for other in self.open if other is not copy]
            if any(other is copy for other in self.sent):
                copy.wait_recv()
            else:
                copy.wait()

    def close(self):
        for copy in list(self.open):
            self.take(copy)
        for copy in self.sent:
            copy.wait_send()


def mail_sems(count):
    return [pltpu.SemaphoreType.DMA((count,)), pltpu.SemaphoreType.DMA((count,))]


def spread_kernel(bits, plan, x_ref, out_ref, send_sem, recv_sem):
    greet([neighbour(bit) for bit in bits])
    mail = Mail(send_sem, recv_sem)
    mail.keep(x_ref, out_ref.at[0])
    held = [{0: None} for _ in plan]
    for stage in range(len(bits)):
        for part, (first, rows, order) in enumerate(plan):
            bit = order[stage]
            step = 1 << bits.index(bit)
            span = pl.ds(first, rows)
            for block in list(held[part]):
                if block:
                    mail.take(held[part][block])
                source = out_ref.at[block, span] if block else x_ref.at[span]
                held[part][block ^ step] = mail.post(source, out_ref.at[block ^ step, span], bit)
    mail.close()


def spread(array):
    bits, plan = group_bits(), routes(array.shape[0], 1)
    count = 1 << len(bits)
    return pl.pallas_call(
        functools.partial(spread_kernel, bits, plan),
        out_shape=jax.ShapeDtypeStruct((count,) + array.shape, array.dtype),
        in_specs=[pl.BlockSpec(memory_space=pltpu.VMEM)],
        out_specs=pl.BlockSpec(memory_space=pl.ANY),
        scratch_shapes=mail_sems(len(plan) * count),
        compiler_params=pltpu.CompilerParams(
            collective_id=4, has_side_effects=True, vmem_limit_bytes=32 * MIB
        ),
        name="rows_spread",
    )(array)


def run_flows(flows):
    while flows:
        flows = [flow for flow in flows if next(flow, None) is not None]


def collect_flow(mail, bits, part, refs):
    first, rows, order = part
    x_ref, out_ref, sum_ref, got_ref = refs
    span = pl.ds(first, rows)
    held = list(range(1 << len(bits)))
    for stage, bit in enumerate(reversed(order)):
        step = 1 << bits.index(bit)
        source = sum_ref if stage else x_ref
        held = [block for block in held if not block & step]
        base = (1 << len(bits)) - 2 * len(held)
        copies = [
            mail.post(source.at[block ^ step, span], got_ref.at[base + place, span], bit)
            for place, block in enumerate(held)
        ]
        yield True
        for place, (block, copy) in enumerate(zip(held, copies)):
            mail.take(copy)
            total = source[block, span, :].astype(jnp.float32) + got_ref[
                base + place, span, :
            ].astype(jnp.float32)
            if stage == len(bits) - 1:
                out_ref[span, :] = total
            else:
                sum_ref[block, span, :] = total.astype(jnp.bfloat16)


def head_back_kernel(lane_bits, plan, tile, x_ref, *refs):
    core, _, y_bits, z_bits = lane_bits
    bits = z_bits + y_bits
    if tile:
        slope_ref, rows_ref, out_ref, keep_ref, pass_ref = refs[:5]
        sum_ref, got_ref, send_sem, recv_sem = refs[5:9]
        loads, sent_ref, other_ref, load_sem = refs[9:]
        half = sent_ref.shape[0]
        count = half // tile
        order = [count + i for i in range(count)] + [count - 1 - i for i in range(count)]

        def load(number):
            return pltpu.make_async_copy(
                slope_ref.at[:, pl.ds(order[number] * tile, tile)],
                loads.at[number % 2],
                load_sem.at[number % 2],
            )

        load(0).start()
        greet([neighbour(bit) for bit in bits + [core]])
    else:
        out_ref, sum_ref, got_ref, send_sem, recv_sem = refs
        greet([neighbour(bit) for bit in bits])
    mail = Mail(send_sem, recv_sem)
    flows = [
        collect_flow(mail, bits, part, (x_ref, out_ref, sum_ref, got_ref)) for part in plan
    ]
    if tile:

        def table_flow():
            arrivals = {}
            border = keep_ref.shape[0]
            for number, block in enumerate(order):
                if number + 1 < len(order):
                    load(number + 1).start()
                load(number).wait()
                grad = lax.dot_general(
                    loads[number % 2],
                    rows_ref[...],
                    (((0,), (0,)), ((), ())),
                    preferred_element_type=jnp.float32,
                )
                start = block * tile % half
                span = pl.ds(start, tile)
                if block >= count:
                    sent_ref[span, :] = grad.astype(jnp.bfloat16)
                    arrivals[start] = mail.post(sent_ref.at[span], other_ref.at[span], core)
                else:
                    mail.take(arrivals[start])
                    grad = grad + other_ref[span, :].astype(jnp.float32)
                    lower = min(max(border - start, 0), tile)
                    if lower:
                        keep_ref[pl.ds(start, lower), :] = grad[:lower]
                    if lower < tile:
                        pass_ref[pl.ds(start + lower - border, tile - lower), :] = grad[
                            lower:
                        ].astype(jnp.bfloat16)
                yield True

        run_flows([slowed(flow, 4) for flow in flows] + [table_flow()])
    else:
        run_flows(flows)
    mail.close()


def slowed(flow, turns):
    while next(flow, None) is not None:
        for _ in range(turns):
            yield True


def head_back(array, slopes, group_rows):
    lane_bits = lanes()
    bits, plan = group_bits(), routes(array.shape[1], 2)
    count, rows, width = array.shape
    vocab = slopes.shape[1]
    half = vocab // 2
    tile = 640 if half % 640 == 0 else 0
    vmem = pl.BlockSpec(memory_space=pltpu.VMEM)
    shapes = [jax.ShapeDtypeStruct((rows, width), jnp.float32)]
    scratch = [
        pltpu.VMEM((count, rows, width), jnp.bfloat16),
        pltpu.VMEM((count - 1, rows, width), jnp.bfloat16),
    ] + mail_sems(len(plan) * count + (half // tile if tile else 0))
    operands, specs = [array], [vmem]
    if tile:
        shapes += [
            jax.ShapeDtypeStruct((half // 2, width), jnp.float32),
            jax.ShapeDtypeStruct((half // 2, width), jnp.bfloat16),
        ]
        scratch += [
            pltpu.VMEM((2, slopes.shape[0], tile), jnp.bfloat16),
            pltpu.VMEM((half, width), jnp.bfloat16),
            pltpu.VMEM((half, width), jnp.bfloat16),
            pltpu.SemaphoreType.DMA((2,)),
        ]
        operands += [slopes, group_rows]
        specs += [pl.BlockSpec(memory_space=pl.ANY), vmem]
    outs = pl.pallas_call(
        functools.partial(head_back_kernel, lane_bits, plan, tile),
        out_shape=shapes,
        in_specs=specs,
        out_specs=[vmem] * len(shapes),
        scratch_shapes=scratch,
        compiler_params=pltpu.CompilerParams(
            collective_id=5, has_side_effects=True, vmem_limit_bytes=56 * MIB
        ),
        name="head_back",
    )(*operands)
    if tile:
        return outs
    core = lane_bits[0]
    other = swap(outer_sum(slopes[:, half:], group_rows).astype(jnp.bfloat16), core)
    table_sum = outer_sum(slopes[:, :half], group_rows) + other.astype(jnp.float32)
    return outs[0], table_sum[: half // 2], table_sum[half // 2 :].astype(jnp.bfloat16)


def chip_sizes():
    wides, groups = lax.axis_size("wide"), lax.axis_size("narrow")
    return wides, groups // 2


class Rows:
    def __init__(self, sizes, x_ref, out_ref, send_sem, recv_sem):
        self.sizes, self.x_ref, self.out_ref = sizes, x_ref, out_ref
        self.send_sem, self.recv_sem = send_sem, recv_sem
        self.count = sizes[0] * sizes[1]
        self.place = Place(sizes[0], 2 * sizes[1])

    def peer(self, k):
        ups = self.sizes[1]
        return self.place.peer(k // ups, 2 * (k % ups))

    def each(self, step):
        for k in range(1, self.count):
            step(k)

    def copy(self, k):
        return pltpu.make_async_remote_copy(
            src_ref=self.x_ref.at[k],
            dst_ref=self.out_ref.at[k],
            send_sem=self.send_sem.at[k],
            recv_sem=self.recv_sem.at[k],
            device_id=self.peer(k),
            device_id_type=MESH,
        )

    def greet(self, others):
        barrier = pltpu.get_barrier_semaphore()
        self.each(
            lambda k: pl.semaphore_signal(
                barrier, inc=1, device_id=self.peer(k), device_id_type=MESH
            )
        )
        for device in others:
            pl.semaphore_signal(barrier, inc=1, device_id=device, device_id_type=MESH)
        pl.semaphore_wait(barrier, self.count - 1 + len(others))

    def start(self):
        self.each(lambda k: self.copy(k).start())

    def own(self):
        return pltpu.make_async_copy(self.x_ref.at[0], self.out_ref.at[0], self.recv_sem.at[0])


def swap_rows_kernel(sizes, x_ref, out_ref, send_sem, recv_sem):
    rows = Rows(sizes, x_ref, out_ref, send_sem, recv_sem)
    rows.greet([])
    rows.start()
    own = rows.own()
    own.start()
    own.wait()
    rows.each(lambda k: rows.copy(k).wait())


def swap_rows(rows):
    sizes = chip_sizes()
    count = sizes[0] * sizes[1]
    return pl.pallas_call(
        functools.partial(swap_rows_kernel, sizes),
        out_shape=jax.ShapeDtypeStruct(rows.shape, rows.dtype),
        in_specs=[pl.BlockSpec(memory_space=pltpu.VMEM)],
        out_specs=pl.BlockSpec(memory_space=pl.ANY),
        scratch_shapes=mail_sems(count),
        compiler_params=pltpu.CompilerParams(collective_id=2, has_side_effects=True),
        name="token_rows",
    )(rows)


def load_kernel(sizes, lane_bits, *refs):
    core, x_bits, y_bits, z_bits = lane_bits
    near = z_bits[0]
    table_ref, weight_refs, rows_ref = refs[0], refs[1:5], refs[5]
    table_out, weight_outs, rows_out = refs[6], refs[7:11], refs[11]
    send_sem, recv_sem, rows_send, rows_recv, pass_send, pass_recv = refs[12:]
    wide, narrow = lax.axis_index("wide"), lax.axis_index("narrow")
    rows = Rows(sizes, rows_ref, rows_out.at[0], rows_send, rows_recv)
    rows.greet([neighbour(core)])
    mail = Mail(send_sem, recv_sem)
    side_near = (wide // near[1]) % 2

    def part(ref, number, half):
        count = ref.shape[1] // 2
        return ref.at[number, pl.ds(pl.multiple_of(half * count, 16), count)]

    def own_part(ref, half):
        count = ref.shape[0] // 2
        return ref.at[pl.ds(pl.multiple_of(half * count, 16), count)]

    tables = {0: mail.keep(table_ref, table_out.at[0, 0])}
    if x_bits:
        tables[1] = mail.post(table_ref, table_out.at[0, 1], x_bits[0])
    held = [0]
    first = []
    for ref, out in zip(weight_refs, weight_outs):
        if y_bits:
            first.append(
                mail.post(own_part(ref, side_near), part(out, narrow, side_near), y_bits[0])
            )
    rows.start()
    own_rows = rows.own()
    own_rows.start()
    mail.post(table_ref, table_out.at[1, 0], core)
    for ref, out in zip(weight_refs, weight_outs):
        mail.keep(ref, out.at[narrow])
        mail.post(ref, out.at[narrow], core)
    own_rows.wait()
    place = narrow
    blocks = [narrow]
    for level, bit in enumerate(y_bits):
        fresh = []
        arrivals = []
        for number, (ref, out) in enumerate(zip(weight_refs, weight_outs)):
            for spot, block in enumerate(blocks):
                other = block + bit[1] * (1 - 2 * ((block // bit[1]) % 2))
                if level == 0:
                    copy = first[number]
                else:
                    copy = mail.post(
                        part(out, block, side_near), part(out, block, side_near), bit
                    )
                arrivals.append((out, other, copy))
                if number == 0:
                    fresh.append(other)
        seconds = []
        for out, other, copy in arrivals:
            mail.take(copy)
            seconds.append(
                mail.post(part(out, other, side_near), part(out, other, side_near), near)
            )
            mail.post(part(out, other, side_near), part(out, other, side_near), core)
        for (out, other, _), copy in zip(arrivals, seconds):
            mail.take(copy)
            mail.post(part(out, other, 1 - side_near), part(out, other, 1 - side_near), core)
        blocks = blocks + fresh

    def hand(k):
        return pltpu.make_async_remote_copy(
            src_ref=rows_out.at[0, k],
            dst_ref=rows_out.at[1, k],
            send_sem=pass_send.at[k],
            recv_sem=pass_recv.at[k],
            device_id=neighbour(core),
            device_id_type=MESH,
        )

    hand(0).start()

    def forward(k):
        rows.copy(k).wait()
        hand(k).start()

    rows.each(forward)
    for level, bit in enumerate(x_bits):
        for block in range(1 << level):
            spot = block + (1 << level)
            if spot not in tables:
                tables[spot] = mail.post(table_out.at[0, block], table_out.at[0, spot], bit)
        for block in range(1 << level):
            spot = block + (1 << level)
            mail.take(tables[spot])
            mail.post(table_out.at[0, spot], table_out.at[1, spot], core)
    hand(0).wait()
    rows.each(lambda k: hand(k).wait())
    mail.close()


def load_all(table, weights, rows):
    lane_bits = lanes()
    sizes = chip_sizes()
    count = sizes[0] * sizes[1]
    groups = lax.axis_size("narrow")
    across = 1 << len(lane_bits[1])
    any_space = pl.BlockSpec(memory_space=pl.ANY)
    shapes = (
        [jax.ShapeDtypeStruct((2, across) + table.shape, table.dtype)]
        + [jax.ShapeDtypeStruct((groups,) + w.shape, w.dtype) for w in weights]
        + [jax.ShapeDtypeStruct((2,) + rows.shape, rows.dtype)]
    )
    table_all, *weights_all, rows_all = pl.pallas_call(
        functools.partial(load_kernel, sizes, lane_bits),
        out_shape=shapes,
        in_specs=[pl.BlockSpec(memory_space=pltpu.VMEM)] * 6,
        out_specs=[any_space] * 6,
        scratch_shapes=mail_sems(8 * 2 * groups + 2 * across + 4)
        + mail_sems(count)
        + mail_sems(count),
        compiler_params=pltpu.CompilerParams(
            collective_id=6, has_side_effects=True, vmem_limit_bytes=32 * MIB
        ),
        name="load_rows",
    )(table, *weights, rows)
    model = table.shape[1]
    return (
        table_all.reshape(-1, model),
        tuple(w.reshape(-1, model) for w in weights_all),
        rows_all,
    )


def tile_of(rows):
    return next(size for size in (128, 96, 64, 48, 32, 16) if rows % size == 0)


def reduce_kernel(sizes, lane_bits, kinds, grads_count, *refs):
    core, x_bits, y_bits, z_bits = lane_bits
    grad_refs, small_ref, rows_ref = refs[:grads_count], refs[grads_count], refs[grads_count + 1]
    outs = refs[grads_count + 2 :]
    out_refs, small_out, rows_out, square_out = (
        outs[:grads_count],
        outs[grads_count],
        outs[grads_count + 1],
        outs[grads_count + 2],
    )
    scratch = outs[grads_count + 3 :]
    got_refs = []
    sum_refs, scratch = scratch[: len(kinds)], scratch[len(kinds) :]
    for _, _, _, path in kinds:
        got_refs.append(scratch[: len(path) + 1])
        scratch = scratch[len(path) + 1 :]
    small_sum, small_got, send_sem, recv_sem, rows_send, rows_recv = scratch
    place = {"wide": lax.axis_index("wide"), "narrow": lax.axis_index("narrow")}
    rows = Rows(sizes, rows_ref, rows_out, rows_send, rows_recv)
    rows.greet([neighbour(core)])
    mail = Mail(send_sem, recv_sem)
    ups = sum_refs[0].shape[0]
    own = place["narrow"] % 2
    square_out[...] = jnp.zeros_like(square_out)

    def side_of(bit):
        return (place[bit[0]] // bit[1]) % 2

    def add(total_ref, got_ref, box):
        up, ups_here, first, height = box
        tile = tile_of(height)

        def step(i, carry):
            at = i // (height // tile)
            down = (i % (height // tile)) * tile
            span = pl.ds(pl.multiple_of(first + down, 16), tile)
            got = got_ref[at, pl.ds(pl.multiple_of(down, 16), tile), :]
            total = total_ref[up + at, span, :].astype(jnp.float32) + got.astype(jnp.float32)
            total_ref[up + at, span, :] = total.astype(jnp.bfloat16)
            return carry

        lax.fori_loop(0, ups_here * (height // tile), step, 0)

    def view(ref, box):
        up, ups_here, first, height = box
        return ref.at[pl.ds(up, ups_here), pl.ds(pl.multiple_of(first, 16), height)]

    def flow(number):
        which, offset, height, path = kinds[number]
        total_ref, got = sum_refs[number], got_refs[number]
        out_ref = out_refs[which]
        span = pl.ds(offset, height)
        firsts = [
            (
                mail.post(grad_refs[which].at[2 * up + 1 - own, span], got[0].at[up], core),
                mail.keep(grad_refs[which].at[2 * up + own, span], total_ref.at[up]),
            )
            for up in range(ups)
        ]
        yield True
        for remote, local in firsts:
            mail.take(local)
            mail.take(remote)
        box = (0, ups, 0, height)
        add(total_ref, got[0], box)
        for stage, (bit, halve) in enumerate(path):
            up, ups_here, first, height = box
            side = side_of(bit)
            if bit[0] == "narrow":
                half = ups_here // 2
                mine = (up + side * half, half, first, height)
                theirs = (up + (1 - side) * half, half, first, height)
            elif halve:
                half = height // 2
                mine = (up, ups_here, first + side * half, half)
                theirs = (up, ups_here, first + (1 - side) * half, half)
            else:
                mine = theirs = box
            copy = mail.post(view(total_ref, theirs), got[stage + 1], bit)
            yield True
            mail.take(copy)
            if not halve:
                copy.wait_send()
                mail.sent = [other for other in mail.sent if other is not copy]
            box = mine
            add(total_ref, got[stage + 1], box)
        up, _, first, height = box
        piece = total_ref[up, pl.ds(pl.multiple_of(first, 16), height), :]
        out_ref[pl.ds(pl.multiple_of(offset + first, 16), height), :] = piece
        full = piece.astype(jnp.float32)
        square_out[...] += jnp.sum((full * full).reshape(height // 8, 8, -1), 0)
        for bit, halve in reversed(path):
            if bit[0] == "wide" and halve:
                span = pl.ds(pl.multiple_of(offset + first, 16), height)
                copy = mail.post(out_ref.at[span], out_ref.at[span], bit)
                yield True
                mail.take(copy)
                first = first - side_of(bit) * height
                height = 2 * height

    def small_flow():
        bits = [core] + x_bits + y_bits + z_bits
        small_sum[0] = small_ref[...].astype(jnp.bfloat16)
        for stage, bit in enumerate(bits):
            copy = mail.post(small_sum.at[stage], small_got.at[stage], bit)
            yield True
            mail.take(copy)
            total = small_sum[stage].astype(jnp.float32) + small_got[stage].astype(jnp.float32)
            if stage == len(bits) - 1:
                small_out[...] = total
            else:
                small_sum[stage + 1] = total.astype(jnp.bfloat16)

    def rows_flow():
        yield True
        rows.start()
        own_rows = rows.own()
        own_rows.start()
        yield True
        own_rows.wait()

    run_flows([flow(number) for number in range(len(kinds))] + [small_flow(), rows_flow()])
    rows.each(lambda k: rows.copy(k).wait())
    mail.close()


def reduce_all(grads, small, rows):
    lane_bits = lanes()
    core, x_bits, y_bits, z_bits = lane_bits
    sizes = chip_sizes()
    near, far = z_bits[:1], z_bits[1:]
    groups, height, width = grads[0].shape
    ups = groups // 2
    downs = y_bits[::-1]
    half = height // 2
    orders = (
        (0, 0, x_bits + downs + near + far),
        (1, 0, downs + x_bits + near + far),
        (2, 0, near + x_bits + downs + far),
        (0, half, x_bits + near + downs + far),
        (1, half, downs + near + x_bits + far),
        (2, half, near + downs + x_bits + far),
    )
    kinds, got_shapes = [], []
    for which, offset, order in orders:
        path, ups_here, height_here = [], ups, half
        shapes = [(ups_here, height_here, width)]
        for bit in order:
            halve = True
            if bit[0] == "narrow":
                ups_here //= 2
            else:
                halve = (height_here // 2) % 16 == 0
                height_here = height_here // 2 if halve else height_here
            path.append((bit, halve))
            shapes.append((ups_here, height_here, width))
        kinds.append((which, offset, half, path))
        got_shapes += shapes
    count = sizes[0] * sizes[1]
    steps = 1 + len(orders[0][2])
    vmem = pl.BlockSpec(memory_space=pltpu.VMEM)
    any_space = pl.BlockSpec(memory_space=pl.ANY)
    outs = pl.pallas_call(
        functools.partial(reduce_kernel, sizes, lane_bits, kinds, len(grads)),
        out_shape=[jax.ShapeDtypeStruct((height, width), jnp.bfloat16) for _ in grads]
        + [
            jax.ShapeDtypeStruct(small.shape, small.dtype),
            jax.ShapeDtypeStruct(rows.shape, rows.dtype),
            jax.ShapeDtypeStruct((8, width), jnp.float32),
        ],
        in_specs=[any_space] * len(grads) + [vmem, vmem],
        out_specs=[vmem] * len(grads) + [vmem, any_space, vmem],
        scratch_shapes=[pltpu.VMEM((ups, half, width), jnp.bfloat16) for _ in kinds]
        + [pltpu.VMEM(shape, jnp.bfloat16) for shape in got_shapes]
        + [
            pltpu.VMEM((steps,) + small.shape, jnp.bfloat16),
            pltpu.VMEM((steps,) + small.shape, jnp.bfloat16),
        ]
        + mail_sems(len(kinds) * (2 * ups + 2 * steps) + steps)
        + mail_sems(count),
        compiler_params=pltpu.CompilerParams(
            collective_id=7, has_side_effects=True, vmem_limit_bytes=56 * MIB
        ),
        name="reduce_rows",
    )(*grads, small, rows)
    repeats = 1
    for bit, halve in kinds[0][3]:
        repeats *= 1 if halve else 2
    number = len(grads)
    return outs[:number], outs[number], outs[number + 1], jnp.sum(outs[number + 2]) / repeats


class Place:
    def __init__(self, wides, groups):
        self.wide, self.narrow = lax.axis_index("wide"), lax.axis_index("narrow")
        self.wide_steps = self.steps(self.wide, wides)
        self.narrow_steps = self.steps(self.narrow, groups)

    def steps(self, place, size):
        masks = [1 << bit for bit in range(log_two(size))]
        return {mask: mask * (1 - 2 * ((place // mask) % 2)) for mask in masks}

    def peer(self, wide_mask, narrow_mask):
        wide, narrow = self.wide, self.narrow
        for mask, step in self.wide_steps.items():
            wide = wide + step if mask & wide_mask else wide
        for mask, step in self.narrow_steps.items():
            narrow = narrow + step if mask & narrow_mask else narrow
        return wide, narrow


def exchange_kernel(masks, sizes, whole, x_ref, out_ref, send_sem, recv_sem, own_sem):
    wides, groups = sizes
    place = Place(wides, groups)
    masks = list(range(wides * groups)) if masks is None else masks
    count = len(masks)

    def peer(mask):
        return place.peer(mask // groups, mask % groups)

    def each(step):
        for k in range(1, count):
            step(k, masks[k])

    def copy(k, mask):
        return pltpu.make_async_remote_copy(
            src_ref=x_ref if whole else x_ref.at[k],
            dst_ref=out_ref.at[k],
            send_sem=send_sem.at[k],
            recv_sem=recv_sem.at[k],
            device_id=peer(mask),
            device_id_type=MESH,
        )

    barrier = pltpu.get_barrier_semaphore()
    each(
        lambda k, mask: pl.semaphore_signal(
            barrier, inc=1, device_id=peer(mask), device_id_type=MESH
        )
    )
    pl.semaphore_wait(barrier, count - 1)
    each(lambda k, mask: copy(k, mask).start())
    own = pltpu.make_async_copy(x_ref if whole else x_ref.at[0], out_ref.at[0], own_sem)
    own.start()
    own.wait()
    each(lambda k, mask: copy(k, mask).wait())


def exchange(array, number, name, masks=None, whole=True):
    sizes = (lax.axis_size("wide"), lax.axis_size("narrow"))
    count = sizes[0] * sizes[1] if masks is None else len(masks)
    shape = (count,) + array.shape if whole else array.shape
    return pl.pallas_call(
        functools.partial(exchange_kernel, masks, sizes, whole),
        out_shape=jax.ShapeDtypeStruct(shape, array.dtype),
        in_specs=[pl.BlockSpec(memory_space=pltpu.VMEM)],
        out_specs=pl.BlockSpec(memory_space=pltpu.VMEM),
        scratch_shapes=[
            pltpu.SemaphoreType.DMA((count,)),
            pltpu.SemaphoreType.DMA((count,)),
            pltpu.SemaphoreType.DMA,
        ],
        compiler_params=pltpu.CompilerParams(
            collective_id=number, has_side_effects=True, vmem_limit_bytes=32 * MIB
        ),
        name=name,
    )(array)


def merge_stats(stats):
    masks = group_masks()
    rows = stats.shape[1] // 4
    parts = exchange(stats, 1, "stats_swap", masks, False)
    top, total, picked = (parts[:, i * rows : (i + 1) * rows] for i in range(3))
    highest = jnp.max(top, 0)
    own = highest + jnp.log(jnp.sum(total * jnp.exp(top - highest), 0))
    share = exchange(jnp.pad(own, ((0, -rows % 8), (0, 0))), 8, "stats_share", masks)
    return share[:, :rows], own, jnp.sum(picked, 0)


def put_columns(rows_ref, column_ref):
    turned = rows_ref[...].T
    for place in range(rows_ref.shape[0]):
        column_ref[pl.ds(place * 128, 128), :] = turned[:, place : place + 1]


def as_rows(column):
    count = column.shape[0] // 128
    return jnp.concatenate(
        [column[place * 128 : (place + 1) * 128] for place in range(count)], 1
    ).T


def score_kernel(
    rows_ref, table_ref, target_ref, exps_ref, max_ref, stat_ref, sum_ref, pick_ref, column_ref
):
    tile = pl.program_id(0)
    width = table_ref.shape[0]

    @pl.when(tile == 0)
    def _():
        max_ref[...] = jnp.full_like(max_ref, -jnp.inf)
        sum_ref[...] = jnp.zeros_like(sum_ref)
        pick_ref[...] = jnp.zeros_like(pick_ref)
        put_columns(target_ref, column_ref)

    def step(block, carry):
        rows = pl.ds(pl.multiple_of(block * TOKEN_TILE, TOKEN_TILE), TOKEN_TILE)
        scores = lax.dot_general(
            rows_ref[rows, :],
            table_ref[...],
            (((1,), (1,)), ((), ())),
            preferred_element_type=jnp.float32,
        )
        top = jnp.max(scores, -1, keepdims=True)
        powers = jnp.exp(scores - top)
        exps_ref[rows, :] = powers.astype(jnp.bfloat16)
        total = jnp.sum(powers, -1, keepdims=True)
        columns = lax.broadcasted_iota(jnp.int32, (TOKEN_TILE, width), 1)
        wanted = column_ref[rows, :] - tile * width
        hit = jnp.sum(jnp.where(columns == wanted, scores, 0.0), -1, keepdims=True)
        here = lax.broadcasted_iota(jnp.int32, (TOKEN_TILE, 128), 1) == tile
        max_ref[rows, :] = jnp.where(here, top, max_ref[rows, :])
        sum_ref[rows, :] = jnp.where(here, total, sum_ref[rows, :])
        pick_ref[rows, :] = jnp.where(here, hit, pick_ref[rows, :])
        return carry

    lax.fori_loop(0, rows_ref.shape[0] // TOKEN_TILE, step, 0, unroll=8)

    @pl.when(tile == pl.num_programs(0) - 1)
    def _():
        maxima = max_ref[...]
        top = jnp.max(maxima, -1, keepdims=True)
        total = jnp.sum(sum_ref[...] * jnp.exp(maxima - top), -1, keepdims=True)
        picked = jnp.sum(pick_ref[...], -1, keepdims=True)
        blocks, height, _ = stat_ref.shape
        rows = height // 4
        stat_ref[...] = jnp.zeros_like(stat_ref)
        for number, column in enumerate((top, total, picked)):
            lines = as_rows(column)
            for block in range(blocks):
                stat_ref[block, pl.ds(number * rows, rows), :] = lines[
                    block * rows : (block + 1) * rows
                ]


def vocab_tile(vocab):
    return 1280 if vocab % 1280 == 0 else 640


def head_scores(rows, table, targets, blocks):
    tokens, model = rows.shape
    vocab = table.shape[0]
    width = vocab_tile(vocab)
    stat = pltpu.VMEM((tokens, 128), jnp.float32)
    whole = pl.BlockSpec((tokens, 128), lambda j: (0, 0))
    height = 4 * (tokens // blocks // 128)
    return pl.pallas_call(
        score_kernel,
        grid=(vocab // width,),
        out_shape=(
            jax.ShapeDtypeStruct((tokens, vocab), jnp.bfloat16),
            jax.ShapeDtypeStruct((tokens, 128), jnp.float32),
            jax.ShapeDtypeStruct((blocks, height, 128), jnp.float32),
        ),
        in_specs=[
            pl.BlockSpec((tokens, model), lambda j: (0, 0)),
            pl.BlockSpec((width, model), lambda j: (j, 0)),
            pl.BlockSpec(targets.shape, lambda j: (0, 0)),
        ],
        out_specs=(
            pl.BlockSpec((tokens, width), lambda j: (0, j)),
            whole,
            pl.BlockSpec((blocks, height, 128), lambda j: (0, 0, 0)),
        ),
        scratch_shapes=[stat, stat, pltpu.VMEM((tokens, 1), jnp.int32)],
        compiler_params=pltpu.CompilerParams(vmem_limit_bytes=60 * MIB),
        cost_estimate=pl.CostEstimate(
            flops=3 * tokens * vocab * model,
            bytes_accessed=2 * tokens * vocab,
            transcendentals=tokens * vocab,
        ),
        name="head_scores",
    )(rows, table, targets)


def slope_kernel(
    exps_ref,
    max_ref,
    log_ref,
    target_ref,
    table_ref,
    slope_ref,
    grad_ref,
    total_ref,
    column_ref,
    log_column_ref,
):
    tile = pl.program_id(0)
    width = table_ref.shape[0]

    @pl.when(tile == 0)
    def _():
        total_ref[...] = jnp.zeros_like(total_ref)
        put_columns(target_ref, column_ref)
        put_columns(log_ref, log_column_ref)

    def step(block, carry):
        rows = pl.ds(pl.multiple_of(block * TOKEN_TILE, TOKEN_TILE), TOKEN_TILE)
        here = lax.broadcasted_iota(jnp.int32, (TOKEN_TILE, 128), 1) == tile
        top = jnp.sum(jnp.where(here, max_ref[rows, :], 0.0), -1, keepdims=True)
        scale = jnp.exp(top - log_column_ref[rows, :])
        columns = lax.broadcasted_iota(jnp.int32, (TOKEN_TILE, width), 1)
        wanted = column_ref[rows, :] - tile * width
        probs = exps_ref[rows, :].astype(jnp.float32) * scale
        slope = jnp.where(columns == wanted, probs - 1.0, probs).astype(jnp.bfloat16)
        slope_ref[rows, :] = slope
        total_ref[rows, :] += jnp.dot(slope, table_ref[...], preferred_element_type=jnp.float32)
        return carry

    lax.fori_loop(0, exps_ref.shape[0] // TOKEN_TILE, step, 0, unroll=8)

    @pl.when(tile == pl.num_programs(0) - 1)
    def _():
        grad_ref[...] = total_ref[...].astype(jnp.bfloat16)


def head_slopes(exps, maxima, logs, targets, table):
    tokens, vocab = exps.shape
    model = table.shape[1]
    width = vocab_tile(vocab)
    return pl.pallas_call(
        slope_kernel,
        grid=(vocab // width,),
        out_shape=(
            jax.ShapeDtypeStruct((tokens, vocab), jnp.bfloat16),
            jax.ShapeDtypeStruct((tokens, model), jnp.bfloat16),
        ),
        in_specs=[
            pl.BlockSpec((tokens, width), lambda j: (0, j)),
            pl.BlockSpec((tokens, 128), lambda j: (0, 0)),
            pl.BlockSpec(logs.shape, lambda j: (0, 0)),
            pl.BlockSpec(targets.shape, lambda j: (0, 0)),
            pl.BlockSpec((width, model), lambda j: (j, 0)),
        ],
        out_specs=(
            pl.BlockSpec((tokens, width), lambda j: (0, j)),
            pl.BlockSpec((tokens, model), lambda j: (0, 0)),
        ),
        scratch_shapes=[
            pltpu.VMEM((tokens, model), jnp.float32),
            pltpu.VMEM((tokens, 1), jnp.int32),
            pltpu.VMEM((tokens, 1), jnp.float32),
        ],
        compiler_params=pltpu.CompilerParams(vmem_limit_bytes=60 * MIB),
        cost_estimate=pl.CostEstimate(
            flops=3 * tokens * vocab * model,
            bytes_accessed=4 * tokens * vocab,
            transcendentals=0,
        ),
        name="head_slopes",
    )(exps, maxima, logs, targets, table)


def one_hot(places, size):
    return (places.reshape(-1, 1) == jnp.arange(size)[None]).astype(jnp.bfloat16)


def token_plan(ids_all, shard_rows):
    chips, tokens = ids_all.shape
    wides, ups = chip_sizes()
    wide, narrow = lax.axis_index("wide"), lax.axis_index("narrow")
    own_core = narrow % 2
    own_chip = wide * ups + narrow // 2
    owner = ids_all // shard_rows
    owner_core = jnp.bitwise_xor(owner % 2, own_core)
    owner_chip = jnp.bitwise_xor(owner // 2, own_chip)
    local = ids_all % shard_rows
    row = lax.broadcasted_iota(jnp.int32, (tokens, tokens), 0)
    column = lax.broadcasted_iota(jnp.int32, (tokens, tokens), 1)
    before = column < row
    alike = ids_all[:, :, None] == ids_all[:, None, :]
    first = ~jnp.any(alike & before[None], 2)
    served = first & (owner_chip == 0) & (owner_core == 0)
    served_rank = times_t(served.astype(jnp.bfloat16), before.astype(jnp.bfloat16)).astype(
        jnp.int32
    )
    half = tokens // 2
    mine = lambda array: lax.dynamic_slice_in_dim(array, own_core * half, half)
    own_first = mine(jnp.min(jnp.where(alike[0], column, tokens), 1))
    same_owner = mine(owner[0])[:, None] == owner[0][None]
    own_rank = jnp.sum(
        (same_owner & first[0][None] & (column[:half] < own_first[:, None])).astype(jnp.int32), 1
    )
    own_block = mine(owner_core[0]) * chips + mine(owner_chip[0])
    most = jnp.max(
        jnp.sum(
            (
                first[:, None, :]
                & (owner[:, None, :] == jnp.arange(2 * chips)[None, :, None])
            ).astype(jnp.int32),
            2,
        )
    )
    rounds = (most + SLOTS - 1) // SLOTS

    def plan(turn):
        slot = jnp.arange(SLOTS)[None, :, None] + turn * SLOTS
        chosen = served[:, None, :] & (served_rank[:, None, :] == slot)
        slot_rows = jnp.sum(jnp.where(chosen, local[:, None, :] + 1, 0), 2) - 1
        inside = own_rank - turn * SLOTS
        valid = (inside >= 0) & (inside < SLOTS)
        own_slots = jnp.where(valid, own_block * SLOTS + inside, -1)
        return one_hot(slot_rows, shard_rows), one_hot(own_slots, 2 * chips * SLOTS)

    return plan, rounds


def later_rounds(rounds, turn, total):
    return lax.while_loop(
        lambda state: state[0] < rounds,
        lambda state: (state[0] + 1, state[1] + turn(state[0])),
        (jnp.ones((), jnp.int32), total),
    )[1]


def upper_blocks(count):
    return [(i, j) for i in range(count) for j in range(i, count)]


def muon_kernel(lane_bits, *refs):
    core, _, y_bits, _ = lane_bits
    low_refs = refs[:4]
    rest_out, size_out = refs[4:6]
    gram, sent, got, back, full, total, half, low_a, low_b, low_c, send_sem, recv_sem = refs[6:]
    width = full.shape[0]
    block = gram.shape[-1]
    places = upper_blocks(width // block)
    wide, narrow = lax.axis_index("wide"), lax.axis_index("narrow")
    greet([neighbour(bit) for bit in [core] + y_bits])
    mail = Mail(send_sem, recv_sem)
    own_core, own_up = narrow % 2, (narrow // 2) % 2
    own = 2 * own_core + own_up

    for number, low_ref in enumerate(low_refs):
        for place, (i, j) in enumerate(places):
            product = lax.dot_general(
                low_ref[:, i * block : (i + 1) * block],
                low_ref[:, j * block : (j + 1) * block],
                (((0,), (0,)), ((), ())),
                preferred_element_type=jnp.float32,
            )
            gram[number, place] = product
    for slot in range(2):
        sent[slot] = gram[2 * (1 - own_core) + slot].astype(jnp.bfloat16)
    mail.take(mail.post(sent.at[pl.ds(0, 2)], got.at[pl.ds(0, 2)], core))

    def add(number, slot):
        for place in range(len(places)):
            gram[number, place] += got[slot, place].astype(jnp.float32)

    def pass_on(number, slot, bit):
        sent[slot] = gram[number].astype(jnp.bfloat16)
        return mail.post(sent.at[slot], got.at[slot], bit)

    other_up = 2 * own_core + 1 - own_up
    if y_bits:
        add(other_up, 1 - own_up)
        over_y = pass_on(other_up, 2, y_bits[0])
        add(own, own_up)
        mail.take(over_y)
        add(own, 2)
    for level, bit in enumerate(y_bits[1:]):
        mail.take(pass_on(own, 3 + level, bit))
        add(own, 3 + level)

    def unpack(source, target):
        for place, (i, j) in enumerate(places):
            piece = source(place)
            target(i, j, piece)
            if i != j:
                target(j, i, piece.T)

    def spans(i, j):
        return pl.ds(i * block, block), pl.ds(j * block, block)

    def put_full(i, j, piece):
        full[spans(i, j)] = piece

    unpack(lambda place: gram[own, place], put_full)
    diagonal = lax.broadcasted_iota(jnp.int32, (block, block), 0) == lax.broadcasted_iota(
        jnp.int32, (block, block), 1
    )
    trace = jnp.zeros((1, 1), jnp.float32)
    for i in range(width // block):
        trace = trace + jnp.sum(jnp.where(diagonal, full[spans(i, i)], 0.0), keepdims=True)
    magnitude = jnp.sqrt(trace) + 1e-07
    inverse = 1.0 / magnitude

    def rows(step):
        def body(i, carry):
            step(pl.ds(pl.multiple_of(i * block, block), block))
            return carry

        lax.fori_loop(0, width // block, body, 0)

    def times(left, right, span):
        return jnp.dot(left[span, :], right[...], preferred_element_type=jnp.float32)

    def start(span):
        scaled = full[span, :] * (inverse * inverse)
        full[span, :] = scaled
        low_a[span, :] = scaled.astype(jnp.bfloat16)

    rows(start)
    scale = NS_A
    for cycle_no in range(NS_STEPS):

        def rest_step(span):
            rest = NS_B * full[span, :] + NS_C * times(low_a, low_a, span)
            low_b[span, :] = rest.astype(jnp.bfloat16)
            if cycle_no == 0:
                total[span, :] = rest
            else:
                total[span, :] = NS_A * total[span, :] + scale * rest

        rows(rest_step)
        if cycle_no:

            def total_step(span):
                total[span, :] += times(low_c, low_b, span)

            rows(total_step)
            scale = scale * NS_A
        if cycle_no < NS_STEPS - 1:

            def keep_total(span):
                low_c[span, :] = total[span, :].astype(jnp.bfloat16)

            def half_step(span):
                half[span, :] = NS_A * full[span, :] + times(low_a, low_b, span)

            def full_step(span):
                value = half[span, :]
                low_a[span, :] = value.astype(jnp.bfloat16)
                full[span, :] = NS_A * value + times(low_a, low_b, span)

            def low_step(span):
                low_a[span, :] = full[span, :].astype(jnp.bfloat16)

            rows(keep_total)
            rows(half_step)
            rows(full_step)
            rows(low_step)

    for place, (i, j) in enumerate(places):
        back[own, place] = (total[spans(i, j)] * inverse).astype(jnp.bfloat16)
    lane = lax.broadcasted_iota(jnp.int32, (8, 128), 1)
    size_out[own] = jnp.where(lane >= 0, inverse, 0.0)
    mail.close()
    mail = Mail(send_sem.at[pl.ds(16, 16)], recv_sem.at[pl.ds(16, 16)])
    mine = mail.post(back.at[own], back.at[own], core)
    mine_size = mail.post(size_out.at[own], size_out.at[own], core)
    if y_bits:
        over_y = mail.post(back.at[own], back.at[own], y_bits[0])
        over_size = mail.post(size_out.at[own], size_out.at[own], y_bits[0])
        mail.take(over_y)
        mail.take(over_size)
        mail.post(back.at[other_up], back.at[other_up], core)
        mail.post(size_out.at[other_up], size_out.at[other_up], core)
    mail.close()
    for number in range(4):

        def put_out(i, j, piece, number=number):
            rest_out[(number,) + spans(i, j)] = piece.astype(jnp.bfloat16)

        unpack(lambda place: back[number, place].astype(jnp.float32), put_out)


def muon_factors(lows):
    width = lows[0].shape[1]
    block = 256
    count = len(upper_blocks(width // block))
    lane_bits = lanes()
    extra = max(len(lane_bits[2]) - 1, 0)
    vmem = pl.BlockSpec(memory_space=pltpu.VMEM)
    square = (width, width)
    rests, sizes = pl.pallas_call(
        functools.partial(muon_kernel, lane_bits),
        out_shape=(
            jax.ShapeDtypeStruct((4,) + square, jnp.bfloat16),
            jax.ShapeDtypeStruct((4, 8, 128), jnp.float32),
        ),
        in_specs=[vmem] * 4,
        out_specs=(vmem, vmem),
        scratch_shapes=[
            pltpu.VMEM((4, count, block, block), jnp.float32),
            pltpu.VMEM((3 + extra, count, block, block), jnp.bfloat16),
            pltpu.VMEM((3 + extra, count, block, block), jnp.bfloat16),
            pltpu.VMEM((4, count, block, block), jnp.bfloat16),
        ]
        + [pltpu.VMEM(square, jnp.float32) for _ in range(3)]
        + [pltpu.VMEM(square, jnp.bfloat16) for _ in range(3)]
        + mail_sems(32),
        compiler_params=pltpu.CompilerParams(
            collective_id=9, has_side_effects=True, vmem_limit_bytes=56 * MIB
        ),
        name="muon_factors",
    )(*lows)
    return rests, sizes[:, 0, 0]


def on_device(
    token_ids,
    targets,
    joint_weight,
    output_weight,
    expand_weight,
    reduce_weight,
    joint_velocity,
    output_velocity,
    expand_velocity,
    reduce_velocity,
    embedding,
    embed_moment,
    embed_square,
    positions,
    position_moment,
    position_square,
    norm_gains,
    gain_moment,
    gain_square,
    biases,
    bias_moment,
    bias_square,
):
    core, x_bits, y_bits, z_bits = lanes()
    groups = lax.axis_size("narrow")
    wides = lax.axis_size("wide")
    across = 1 << len(x_bits)
    model_width = embedding.shape[1]
    shard_rows = embedding.shape[0]
    tokens = token_ids.shape[0] * LENGTH
    bias_rows = biases.reshape(-1, model_width)

    own_rows = embedding.astype(jnp.bfloat16)
    labels = jnp.concatenate([token_ids.reshape(-1, 128), targets.reshape(-1, 128)])
    spare = -labels.shape[0] % 8
    labels = exchange(jnp.pad(labels, ((0, spare), (0, 0))), 0, "label_share")
    ids_all = labels[:, : tokens // 128].reshape(-1, tokens)
    lines = tokens // 128
    own_block = lax.axis_index("wide") * groups + lax.axis_index("narrow")
    wides, ups = chip_sizes()
    pairs = ids_all.reshape(wides, ups, 2, tokens)
    other_first = lax.axis_index("narrow") % 2 == 1
    ids_chips = jnp.where(other_first, lax.rev(pairs, (2,)), pairs).reshape(wides * ups, -1)
    plan, rounds = token_plan(ids_chips, shard_rows)

    def serve(served):
        return plain(served, own_rows).astype(jnp.bfloat16).reshape(-1, SLOTS, model_width)

    masters = (joint_weight, output_weight, expand_weight, reduce_weight)
    served, wanted = plan(0)
    table, weights, token_rows = load_all(
        own_rows, [master.astype(jnp.bfloat16) for master in masters], serve(served)
    )
    vocab_here = table.shape[0]

    def fetch(turn):
        more, places = plan(turn)
        got = swap_rows(serve(more))
        return plain(places, jnp.stack([got, swap(got, core)]).reshape(-1, model_width))

    embedded = later_rounds(rounds, fetch, plain(wanted, token_rows.reshape(-1, model_width)))

    block_masks = jnp.array(group_masks())
    targets_group = labels[block_masks, lines : 2 * lines].reshape(-1, 128)
    table_mask = groups * (across - 1) + 1
    differ = jnp.bitwise_xor(targets_group // shard_rows, own_block)
    is_owned = (targets_group >= 0) & (jnp.bitwise_and(differ, ~table_mask) == 0)
    place = (differ % 2) * across + (differ // groups) % across
    rows_targets = jnp.where(is_owned, place * shard_rows + targets_group % shard_rows, -1)
    final_low, *saved = layer_forward(embedded, positions, norm_gains, bias_rows, weights)
    group_rows = spread(final_low).reshape(-1, model_width)
    blocks = len(group_masks())
    exps, maxima, stats = head_scores(group_rows, table, rows_targets, blocks)
    logs, own_logs, own_picked = merge_stats(stats)
    loss_part = jnp.sum(
        jnp.where(targets.reshape(-1, 128) >= 0, own_logs - own_picked, 0.0)
    )
    logs = jnp.where(targets_group >= 0, logs.reshape(-1, 128), jnp.inf)
    slopes, final_part = head_slopes(exps, maxima, logs, rows_targets, table)
    final_grad, table_sum, passed = head_back(
        final_part.reshape(-1, tokens, model_width), slopes, group_rows
    )
    for bit in reversed(x_bits):
        table_sum = table_sum + swap(passed, bit).astype(jnp.float32)
        half = table_sum.shape[0] // 2
        if bit != x_bits[0]:
            table_sum, passed = table_sum[:half], table_sum[half:].astype(jnp.bfloat16)
    stream_grad, small, front, expand_part, reduce_part = layer_backward(
        final_grad, norm_gains, bias_rows, saved, weights
    )
    low_grad = stream_grad.astype(jnp.bfloat16)

    def bundle(places):
        both = outer_sum(places, low_grad).astype(jnp.bfloat16)
        both = both.reshape(2, -1, SLOTS, model_width)
        other = swap(both[1], core)
        return (both[0].astype(jnp.float32) + other.astype(jnp.float32)).astype(jnp.bfloat16)

    count_part = jnp.sum((targets >= 0).astype(jnp.float32))
    by_owner = (groups, -1, model_width)
    (front, expand_sum, reduce_sum), small, row_sums, squares = reduce_all(
        [front, expand_part.reshape(by_owner), reduce_part.reshape(by_owner)],
        small,
        bundle(wanted),
    )
    joint_rows = joint_weight.shape[0]
    table_sum = table_sum + outer_sum(served, row_sums.reshape(-1, model_width))

    def give(turn):
        more, places = plan(turn)
        return outer_sum(more, swap_rows(bundle(places)).reshape(-1, model_width))

    table_sum = later_rounds(rounds, give, table_sum)
    matrix_total = [
        part.astype(jnp.float32)
        for part in (front[:joint_rows], front[joint_rows:], expand_sum, reduce_sum)
    ]
    small = small[: 14 + LENGTH]
    squares = squares + jnp.sum(table_sum * table_sum)
    scalars = jnp.pad(jnp.stack([loss_part, count_part, squares])[None], ((0, 7), (0, 125)))
    scalars = jnp.sum(exchange(scalars, 3, "scalar_share"), 0)
    loss_sum, loss_count, squares = scalars[0, 0], scalars[0, 1], scalars[0, 2]
    squares = squares + jnp.sum(small * small)
    gain_grad, position_grad = small[:3], small[14:]
    bias_grad = small[3:14].reshape(-1)
    grad_norm = jnp.sqrt(squares) / loss_count
    factor = jnp.minimum(1.0, CLIP / (grad_norm + 1e-06)) / loss_count
    previous = (joint_velocity, output_velocity, expand_velocity, reduce_velocity)
    carried = tuple(
        (MOMENTUM * before + gradient * factor for before, gradient in zip(previous, matrix_total))
    )
    lows = [moment.astype(jnp.bfloat16) for moment in carried]
    rests, inverses = muon_factors(lows)
    updated = []
    for number, (master, moment) in enumerate(zip(masters, carried)):
        orth = moment * (NS_A**NS_STEPS * inverses[number]) + plain(
            lows[number], rests[number]
        )
        shape_factor = math.sqrt(max(1.0, master.shape[0] * groups / master.shape[1]))
        updated.append(master * (1 - MUON_RATE * DECAY) - MUON_RATE * shape_factor * orth)
    table_out = adam_step(
        embedding, embed_moment, embed_square, table_sum * factor, EMBED_RATE, DECAY
    )
    place_out = adam_step(
        positions, position_moment, position_square, position_grad * factor, PLACE_RATE, DECAY
    )
    gain_out = adam_step(norm_gains, gain_moment, gain_square, gain_grad * factor, SMALL_RATE, 0.0)
    bias_out = adam_step(biases, bias_moment, bias_square, bias_grad * factor, SMALL_RATE, 0.0)
    return (
        loss_sum,
        loss_count,
        grad_norm,
        updated[0],
        updated[1],
        updated[2],
        updated[3],
        carried[0],
        carried[1],
        carried[2],
        carried[3],
        table_out[0],
        table_out[1],
        table_out[2],
        place_out[0],
        place_out[1],
        place_out[2],
        gain_out[0],
        gain_out[1],
        gain_out[2],
        bias_out[0],
        bias_out[1],
        bias_out[2],
    )


def solution(mesh):
    in_specs = (
        P(("wide", "narrow"), None),
        P(("wide", "narrow"), None),
        P("narrow", None),
        P("narrow", None),
        P("narrow", None),
        P("narrow", None),
        P("narrow", None),
        P("narrow", None),
        P("narrow", None),
        P("narrow", None),
        P(("wide", "narrow"), None),
        P(("wide", "narrow"), None),
        P(("wide", "narrow"), None),
        P(),
        P(),
        P(),
        P(),
        P(),
        P(),
        P(),
        P(),
        P(),
    )
    out_specs = (
        P(),
        P(),
        P(),
        P("narrow", None),
        P("narrow", None),
        P("narrow", None),
        P("narrow", None),
        P("narrow", None),
        P("narrow", None),
        P("narrow", None),
        P("narrow", None),
        P(("wide", "narrow"), None),
        P(("wide", "narrow"), None),
        P(("wide", "narrow"), None),
        P(),
        P(),
        P(),
        P(),
        P(),
        P(),
        P(),
        P(),
        P(),
    )
    return jax.shard_map(
        on_device, mesh=mesh, in_specs=in_specs, out_specs=out_specs, check_vma=False
    )
```

```python
import functools
import math

import jax
import jax.numpy as jnp
from jax import lax
from jax.experimental import pallas as pl
from jax.experimental.pallas import tpu as pltpu
from jax.sharding import PartitionSpec as P

HEADS = 12
HEAD = 64
LENGTH = 64
NS_STEPS = 3
STEP = 10


HIGH = lax.Precision.HIGHEST
EPS = 1e-05
CLIP = 0.05
MOMENTUM = 0.95
MUON_RATE = 0.5
DECAY = 0.1
BETA_ONE = 0.9
BETA_TWO = 0.999
EMBED_RATE = 0.02
PLACE_RATE = 0.1
SMALL_RATE = 0.2
NS_A = 3.4445
NS_B = -4.775
NS_C = 2.0315
MESH = pl.DeviceIdType.MESH
MIB = 1 << 20
TOKEN_TILE = 256


def times_t(left, right):
    return lax.dot_general(
        left, right, (((1,), (1,)), ((), ())), preferred_element_type=jnp.float32
    )


def outer_sum(left, right):
    return lax.dot_general(
        left, right, (((0,), (0,)), ((), ())), preferred_element_type=jnp.float32
    )


def plain(left, right):
    return jnp.dot(left, right, preferred_element_type=jnp.float32)


def norm_forward(stream, gain, shift):
    centred = stream - jnp.mean(stream, -1, keepdims=True)
    inverse = lax.rsqrt(jnp.mean(centred * centred, -1, keepdims=True) + EPS)
    normed = centred * inverse
    return (normed * gain + shift, normed, inverse)


def norm_backward(upstream, normed, inverse, gain):
    scaled = upstream * gain
    inner = inverse * (
        scaled
        - jnp.mean(scaled, -1, keepdims=True)
        - normed * jnp.mean(scaled * normed, -1, keepdims=True)
    )
    return (
        inner,
        jnp.sum(upstream * normed, 0, keepdims=True),
        jnp.sum(upstream, 0, keepdims=True),
    )


def gelu_tanh(values):
    return jax.nn.gelu(values, approximate=True)


def column_sum(values):
    return jnp.sum(values.astype(jnp.float32), 0, keepdims=True)


def pair_masks(tokens):
    first = lax.broadcasted_iota(jnp.int32, (tokens, 2 * HEAD), 1) < HEAD
    row = lax.broadcasted_iota(jnp.int32, (tokens, tokens), 0)
    column = lax.broadcasted_iota(jnp.int32, (tokens, tokens), 1)
    return first, (row // LENGTH == column // LENGTH) & (column <= row)


def head_probs(queries, key_heads, seen):
    scores = times_t(queries, key_heads) * HEAD ** (-0.5)
    scores = jnp.where(seen, scores, -1000000000.0)
    powers = jnp.exp(scores - jnp.max(scores, -1, keepdims=True))
    return powers * (1.0 / jnp.sum(powers, -1, keepdims=True))


def forward_kernel(
    x_ref,
    place_ref,
    gain_ref,
    bias_ref,
    joint_hbm,
    output_hbm,
    expand_hbm,
    reduce_hbm,
    low_ref,
    normed_ref,
    inverse_ref,
    joint_out,
    context_ref,
    upward_ref,
    joint_ref,
    output_ref,
    expand_ref,
    reduce_ref,
    load_sem,
):
    pairs = ((joint_hbm, joint_ref), (output_hbm, output_ref), (expand_hbm, expand_ref), (reduce_hbm, reduce_ref))
    loads = [
        pltpu.make_async_copy(source, target, load_sem.at[number])
        for number, (source, target) in enumerate(pairs)
    ]
    for load in loads:
        load.start()
    tokens, width = x_ref.shape

    def norm(number, stream):
        result, normed, inverse = norm_forward(
            stream, gain_ref[number : number + 1, :], bias_ref[number : number + 1, :]
        )
        normed_ref[number] = normed
        inverse_ref[number] = jnp.broadcast_to(inverse, (tokens, 128))
        return result.astype(jnp.bfloat16)

    stream = x_ref[...] + jnp.concatenate([place_ref[...]] * (tokens // LENGTH), 0)
    first_low = norm(0, stream)
    loads[0].wait()
    for part in range(3):
        span = pl.ds(part * width, width)
        result = times_t(first_low, joint_ref[span, :])
        if part != 1:
            row = 3 if part == 0 else 4
            result = result + bias_ref[row : row + 1, :]
        joint_out[:, span] = result.astype(jnp.bfloat16)
    first, seen = pair_masks(tokens)
    zero = jnp.zeros((), jnp.bfloat16)
    for pair in range(HEADS // 2):
        queries = joint_out[:, pl.ds(pair * 128, 128)]
        key_heads = joint_out[:, pl.ds(width + pair * 128, 128)]
        values = joint_out[:, pl.ds(2 * width + pair * 128, 128)]
        parts = []
        for mine in (first, ~first):
            probs = head_probs(jnp.where(mine, queries, zero), key_heads, seen)
            parts.append(plain(probs.astype(jnp.bfloat16), values))
        context_ref[:, pl.ds(pair * 128, 128)] = jnp.where(first, *parts).astype(jnp.bfloat16)
    loads[1].wait()
    stream = stream + times_t(context_ref[...], output_ref[...]) + bias_ref[5:6, :]
    second_low = norm(1, stream)
    stream = stream + bias_ref[6:7, :]
    loads[2].wait()
    loads[3].wait()
    for part in range(expand_ref.shape[0] // width):
        span = pl.ds(part * width, width)
        upward = times_t(second_low, expand_ref[span, :]) + bias_ref[7 + part : 8 + part, :]
        upward_ref[:, span] = upward
        stream = stream + plain(gelu_tanh(upward).astype(jnp.bfloat16), reduce_ref[span, :])
    low_ref[...] = norm(2, stream)


def layer_forward(embedded, positions, norm_gains, bias_rows, weights):
    tokens, width = embedded.shape
    vmem, any_space = pl.BlockSpec(memory_space=pltpu.VMEM), pl.BlockSpec(memory_space=pl.ANY)
    shape = jax.ShapeDtypeStruct
    hidden = weights[2].shape[0]
    return pl.pallas_call(
        forward_kernel,
        out_shape=(
            shape((tokens, width), jnp.bfloat16),
            shape((3, tokens, width), jnp.float32),
            shape((3, tokens, 128), jnp.float32),
            shape((tokens, 3 * width), jnp.bfloat16),
            shape((tokens, width), jnp.bfloat16),
            shape((tokens, hidden), jnp.float32),
        ),
        in_specs=[vmem] * 4 + [any_space] * 4,
        out_specs=[vmem] * 6,
        scratch_shapes=[pltpu.VMEM(w.shape, w.dtype) for w in weights]
        + [pltpu.SemaphoreType.DMA((4,))],
        compiler_params=pltpu.CompilerParams(vmem_limit_bytes=56 * MIB),
        name="layer_forward",
    )(embedded, positions, norm_gains, bias_rows, *weights)


def gelu_slope(values):
    inner = math.sqrt(2.0 / math.pi)
    squared = values * values
    bent = jnp.tanh(inner * (values + 0.044715 * squared * values))
    return 0.5 * values * (1.0 + bent), 0.5 * (1.0 + bent) + 0.5 * values * (
        1.0 - bent * bent
    ) * (inner * (1.0 + 3 * 0.044715 * squared))


def backward_flow(ins, outs, scratch):
    (final_ref, gain_ref, bias_ref, normed_ref, inverse_ref, joint_in, context_ref, upward_ref) = ins
    (stream_ref, small_ref, front_ref, expand_out, reduce_out) = outs
    (joint_ref, output_ref, expand_ref, reduce_ref, waits) = scratch
    hold = reduce_ref
    tokens, width = final_ref.shape
    _, ups, height, _ = front_ref.shape
    groups = 2 * ups

    def put(ref, start, grad):
        for group in range(groups):
            low = max(group * height, start)
            high = min((group + 1) * height, start + grad.shape[0])
            if low < high:
                ref[group % 2, group // 2, pl.ds(low - group * height, high - low), :] = grad[
                    low - start : high - start
                ]

    def gain(number):
        return gain_ref[number : number + 1, :]

    def normed_low(number):
        return (normed_ref[number] * gain(number) + bias_ref[number : number + 1, :]).astype(
            jnp.bfloat16
        )

    def back(number, upstream):
        inner, gain_row, shift_row = norm_backward(
            upstream, normed_ref[number], inverse_ref[number][:, :1], gain(number)
        )
        small_ref[number : number + 1, :] = gain_row
        small_ref[3 + number : 4 + number, :] = shift_row
        return inner

    small_ref[...] = jnp.zeros_like(small_ref)
    back_f = back(2, final_ref[...])
    down = back_f.astype(jnp.bfloat16)
    small_ref[9:10, :] = column_sum(down)
    second_low = normed_low(1)
    second_grad = jnp.zeros((tokens, width), jnp.float32)
    waits[2].wait()
    waits[3].wait()
    for part in range(expand_ref.shape[0] // width):
        span = pl.ds(part * width, width)
        active, slope = gelu_slope(upward_ref[:, span])
        upward_grad = (times_t(down, reduce_ref[span, :]) * slope).astype(jnp.bfloat16)
        small_ref[10 + part : 11 + part, :] = column_sum(upward_grad)
        second_grad = second_grad + plain(upward_grad, expand_ref[span, :])
        put(expand_out, part * width, outer_sum(upward_grad, second_low).astype(jnp.bfloat16))
        put(reduce_out, part * width, outer_sum(active.astype(jnp.bfloat16), down).astype(jnp.bfloat16))
    yield 0.0
    mid_grad = back_f + back(1, second_grad)
    stream_ref[...] = mid_grad
    attn_grad = mid_grad.astype(jnp.bfloat16)
    small_ref[8:9, :] = column_sum(attn_grad)
    waits[1].wait()
    last = pl.ds(3 * tokens, tokens)
    hold[last, :] = plain(attn_grad, output_ref[...]).astype(jnp.bfloat16)
    output_grad = outer_sum(attn_grad, context_ref[...]).astype(jnp.bfloat16)
    rows = width // groups
    joint_rows = height - rows
    for group in range(groups):
        front_ref[group % 2, group // 2, pl.ds(joint_rows, rows), :] = output_grad[
            group * rows : (group + 1) * rows
        ]
    yield 2.0
    first, seen = pair_masks(tokens)
    zero = jnp.zeros((), jnp.bfloat16)
    for pair in range(HEADS // 2):
        spans = [pl.ds(part * width + pair * 128, 128) for part in range(3)]
        queries, key_heads, values = (joint_in[:, span] for span in spans)
        upstream = hold[last, spans[0]]
        parts = []
        for mine in (first, ~first):
            probs = head_probs(jnp.where(mine, queries, zero), key_heads, seen)
            probs_grad = times_t(jnp.where(mine, upstream, zero), values)
            score_grad = (
                probs * (probs_grad - jnp.sum(probs * probs_grad, -1, keepdims=True))
            ).astype(jnp.bfloat16)
            parts.append(
                (
                    plain(score_grad, key_heads) * HEAD ** (-0.5),
                    outer_sum(score_grad, queries) * HEAD ** (-0.5),
                    outer_sum(probs.astype(jnp.bfloat16), upstream),
                )
            )
        for part, (one, two) in enumerate(zip(*parts)):
            hold[pl.ds(part * tokens, tokens), spans[0]] = jnp.where(first, one, two).astype(
                jnp.bfloat16
            )
        yield 1.5
    first_low = normed_low(0)
    waits[0].wait()
    first_grad = jnp.zeros((tokens, width), jnp.float32)
    for part in range(3):
        span = pl.ds(part * width, width)
        piece = hold[pl.ds(part * tokens, tokens), :]
        if part != 1:
            row = 6 if part == 0 else 7
            small_ref[row : row + 1, :] = column_sum(piece)
        first_grad = first_grad + plain(piece, joint_ref[span, :])
        grad = outer_sum(piece, first_low).astype(jnp.bfloat16)
        for group in range(groups):
            start = max(group * joint_rows, part * width)
            end = min((group + 1) * joint_rows, (part + 1) * width)
            if start < end:
                front_ref[
                    group % 2, group // 2, pl.ds(start - group * joint_rows, end - start), :
                ] = grad[start - part * width : end - part * width]
        yield 1.5
    stream = stream_ref[...] + back(0, first_grad)
    stream_ref[...] = stream
    placed = stream[:LENGTH]
    for sequence in range(1, tokens // LENGTH):
        placed = placed + stream[sequence * LENGTH : (sequence + 1) * LENGTH]
    small_ref[14 : 14 + LENGTH, :] = placed


def adam_step(weight, moment, square, gradient, rate, decay):
    moment = BETA_ONE * moment + (1 - BETA_ONE) * gradient
    square = BETA_TWO * square + (1 - BETA_TWO) * gradient * gradient
    unbiased = moment / (1 - BETA_ONE**STEP)
    spread = square / (1 - BETA_TWO**STEP)
    return (
        weight - rate * (unbiased / (jnp.sqrt(spread) + 1e-08) + decay * weight),
        moment,
        square,
    )


def log_two(size):
    return size.bit_length() - 1


def lanes():
    wide, narrow = lax.axis_size("wide"), lax.axis_size("narrow")
    across = wide // 4
    x_bits = [("wide", 1 << i) for i in range(log_two(across))]
    z_bits = [("wide", across << i) for i in range(log_two(wide // across))]
    y_bits = [("narrow", 2 << i) for i in range(log_two(narrow // 2))]
    return ("narrow", 1), x_bits, y_bits, z_bits


def swap(array, bit):
    axis, mask = bit
    return lax.ppermute(array, axis, [(i, i ^ mask) for i in range(lax.axis_size(axis))])


def side(bit):
    axis, mask = bit
    return (lax.axis_index(axis) // mask) % 2


def join(mine, other, bit, dim=0):
    own = side(bit)
    return jnp.where(
        own == 0, jnp.concatenate([mine, other], dim), jnp.concatenate([other, mine], dim)
    )


def halves(array, bit):
    own = side(bit)
    half = array.shape[0] // 2
    keep = lax.dynamic_slice_in_dim(array, own * half, half)
    send = lax.dynamic_slice_in_dim(array, (1 - own) * half, half)
    return keep, send


def group_bits():
    _, _, y_bits, z_bits = lanes()
    return z_bits + y_bits


SPREAD_ORDERS = ("nyf", "fny", "nfy", "fyn")
COLLECT_ORDERS = ("yfn", "ynf", "nyf", "fyn")


def routes(rows, orders):
    _, _, y_bits, z_bits = lanes()
    kinds = {"y": y_bits, "n": z_bits[:1], "f": z_bits[1:]}
    size = rows // len(orders)
    return [
        (number * size, size, [bit for kind in order for bit in kinds[kind]])
        for number, order in enumerate(orders)
    ]


def flat_mask(bit):
    axis, mask = bit
    return mask * lax.axis_size("narrow") if axis == "wide" else mask


def group_masks():
    masks = [0]
    for bit in group_bits():
        masks = masks + [other ^ flat_mask(bit) for other in masks]
    return masks


def neighbour(bit):
    axis, mask = bit
    wide, narrow = lax.axis_index("wide"), lax.axis_index("narrow")
    if axis == "wide":
        return wide + mask * (1 - 2 * ((wide // mask) % 2)), narrow
    return wide, narrow + mask * (1 - 2 * ((narrow // mask) % 2))


def greet(devices):
    barrier = pltpu.get_barrier_semaphore()
    for device in devices:
        pl.semaphore_signal(barrier, inc=1, device_id=device, device_id_type=MESH)
    pl.semaphore_wait(barrier, len(devices))


class Mail:
    def __init__(self, send_sem, recv_sem, lane_bits):
        core, x_bits, y_bits, z_bits = lane_bits
        self.send_sem, self.recv_sem = send_sem, recv_sem
        self.used, self.sent, self.open = 0, [], []
        self.links = {core: (("core", 1 / 600e3),)}
        self.links.update({bit: (("x", 2 / 91e3),) for bit in x_bits})
        self.links.update({bit: (("y", 2 / 91e3),) for bit in y_bits})
        self.links.update({bit: (("z", 2 / 91e3),) for bit in z_bits[:1]})
        self.links.update({bit: (("z", 2 / 91e3), ("far", 4 / 91e3)) for bit in z_bits[1:]})
        self.free, self.now, self.ready = {}, 0.0, []

    def expect(self, source, bit):
        size = math.prod(source.shape) * source.dtype.itemsize
        due = self.now
        for link, rate in self.links[bit]:
            self.free[link] = max(self.free.get(link, 0.0), self.now) + size * rate
            due = max(due, self.free[link])
        return due + 3.5

    def post(self, source, target, bit):
        copy = pltpu.make_async_remote_copy(
            src_ref=source,
            dst_ref=target,
            send_sem=self.send_sem.at[self.used],
            recv_sem=self.recv_sem.at[self.used],
            device_id=neighbour(bit),
            device_id_type=MESH,
        )
        copy.start()
        self.due = self.expect(source, bit)
        self.used += 1
        self.sent.append(copy)
        self.open.append(copy)
        return copy

    def keep(self, source, target):
        copy = pltpu.make_async_copy(source, target, self.recv_sem.at[self.used])
        copy.start()
        self.used += 1
        self.open.append(copy)
        return copy

    def take(self, copy):
        if any(other is copy for other in self.open):
            self.open = [other for other in self.open if other is not copy]
            if any(other is copy for other in self.sent):
                copy.wait_recv()
            else:
                copy.wait()

    def spend(self, time):
        self.now += time
        return self.now

    def run(self, flows):
        waiting = [(next(flow, None), flow) for flow in flows]
        while True:
            waiting += [(next(flow, None), flow) for flow in self.ready]
            self.ready = []
            waiting = [entry for entry in waiting if entry[0] is not None]
            if not waiting:
                return
            place = min(range(len(waiting)), key=lambda i: waiting[i][0])
            due, flow = waiting.pop(place)
            self.now = max(self.now, due) + 0.4
            waiting.append((next(flow, None), flow))

    def close(self):
        for copy in list(self.open):
            self.take(copy)
        for copy in self.sent:
            copy.wait_send()


def mail_sems(count):
    return [pltpu.SemaphoreType.DMA((count,)), pltpu.SemaphoreType.DMA((count,))]


def spread_flow(mail, bits, part, x_ref, out_ref):
    first, rows, order = part
    span = pl.ds(first, rows)
    held = {0: None}
    for bit in order:
        step = 1 << bits.index(bit)
        for block in list(held):
            if block:
                mail.take(held[block])
            source = out_ref.at[block, span] if block else x_ref.at[span]
            held[block ^ step] = mail.post(source, out_ref.at[block ^ step, span], bit)
        yield mail.due


def spread_kernel(lane_bits, plan, x_ref, out_ref, send_sem, recv_sem):
    bits = lane_bits[3] + lane_bits[2]
    greet([neighbour(bit) for bit in bits])
    mail = Mail(send_sem, recv_sem, lane_bits)
    mail.run([spread_flow(mail, bits, part, x_ref, out_ref) for part in plan])
    mail.keep(x_ref, out_ref.at[0])
    mail.close()


def spread(array):
    bits, plan = group_bits(), routes(array.shape[0], SPREAD_ORDERS)
    count = 1 << len(bits)
    return pl.pallas_call(
        functools.partial(spread_kernel, lanes(), plan),
        out_shape=jax.ShapeDtypeStruct((count,) + array.shape, array.dtype),
        in_specs=[pl.BlockSpec(memory_space=pltpu.VMEM)],
        out_specs=pl.BlockSpec(memory_space=pl.ANY),
        scratch_shapes=mail_sems(len(plan) * count),
        compiler_params=pltpu.CompilerParams(
            collective_id=4, has_side_effects=True, vmem_limit_bytes=32 * MIB
        ),
        name="rows_spread",
    )(array)


def collect_flow(mail, bits, part, refs):
    first, rows, order = part
    x_ref, out_ref, sum_ref, got_ref = refs
    span = pl.ds(first, rows)
    held = list(range(1 << len(bits)))
    for stage, bit in enumerate(order):
        step = 1 << bits.index(bit)
        source = sum_ref if stage else x_ref
        held = [block for block in held if not block & step]
        base = (1 << len(bits)) - 2 * len(held)
        copies = [
            mail.post(source.at[block ^ step, span], got_ref.at[base + place, span], bit)
            for place, block in enumerate(held)
        ]
        yield mail.due
        for place, (block, copy) in enumerate(zip(held, copies)):
            mail.take(copy)
            total = source[block, span, :].astype(jnp.float32) + got_ref[
                base + place, span, :
            ].astype(jnp.float32)
            if stage == len(bits) - 1:
                out_ref[span, :] = total
            else:
                sum_ref[block, span, :] = total.astype(jnp.bfloat16)


def head_back_kernel(lane_bits, plan, tile, x_ref, *refs):
    core, _, y_bits, z_bits = lane_bits
    bits = z_bits + y_bits
    if tile:
        slope_ref, rows_ref, out_ref, keep_ref, pass_ref = refs[:5]
        sum_ref, got_ref, send_sem, recv_sem = refs[5:9]
        loads, sent_ref, other_ref, load_sem = refs[9:]
        half = sent_ref.shape[0]
        count = half // tile
        order = [count + i for i in range(count)] + [count - 1 - i for i in range(count)]

        def load(number):
            return pltpu.make_async_copy(
                slope_ref.at[:, pl.ds(order[number] * tile, tile)],
                loads.at[number % 2],
                load_sem.at[number % 2],
            )

        load(0).start()
        greet([neighbour(bit) for bit in bits + [core]])
    else:
        out_ref, sum_ref, got_ref, send_sem, recv_sem = refs
        greet([neighbour(bit) for bit in bits])
    mail = Mail(send_sem, recv_sem, lane_bits)
    flows = [
        collect_flow(mail, bits, part, (x_ref, out_ref, sum_ref, got_ref)) for part in plan
    ]
    if tile:

        def table_flow():
            arrivals = {}
            border = keep_ref.shape[0]
            for number, block in enumerate(order):
                if number + 1 < len(order):
                    load(number + 1).start()
                load(number).wait()
                grad = lax.dot_general(
                    loads[number % 2],
                    rows_ref[...],
                    (((0,), (0,)), ((), ())),
                    preferred_element_type=jnp.float32,
                )
                start = block * tile % half
                span = pl.ds(start, tile)
                if block >= count:
                    sent_ref[span, :] = grad.astype(jnp.bfloat16)
                    arrivals[start] = mail.post(sent_ref.at[span], other_ref.at[span], core)
                else:
                    mail.take(arrivals[start])
                    grad = grad + other_ref[span, :].astype(jnp.float32)
                    lower = min(max(border - start, 0), tile)
                    if lower:
                        keep_ref[pl.ds(start, lower), :] = grad[:lower]
                    if lower < tile:
                        pass_ref[pl.ds(start + lower - border, tile - lower), :] = grad[
                            lower:
                        ].astype(jnp.bfloat16)
                yield mail.spend(2.7)

        flows.append(table_flow())
    mail.run(flows)
    mail.close()


def head_back(array, slopes, group_rows):
    lane_bits = lanes()
    bits, plan = group_bits(), routes(array.shape[1], COLLECT_ORDERS)
    count, rows, width = array.shape
    vocab = slopes.shape[1]
    half = vocab // 2
    tile = 640 if half % 640 == 0 else 0
    vmem = pl.BlockSpec(memory_space=pltpu.VMEM)
    shapes = [jax.ShapeDtypeStruct((rows, width), jnp.float32)]
    scratch = [
        pltpu.VMEM((count, rows, width), jnp.bfloat16),
        pltpu.VMEM((count - 1, rows, width), jnp.bfloat16),
    ] + mail_sems(len(plan) * count + (half // tile if tile else 0))
    operands, specs = [array], [vmem]
    if tile:
        shapes += [
            jax.ShapeDtypeStruct((half // 2, width), jnp.float32),
            jax.ShapeDtypeStruct((half // 2, width), jnp.bfloat16),
        ]
        scratch += [
            pltpu.VMEM((2, slopes.shape[0], tile), jnp.bfloat16),
            pltpu.VMEM((half, width), jnp.bfloat16),
            pltpu.VMEM((half, width), jnp.bfloat16),
            pltpu.SemaphoreType.DMA((2,)),
        ]
        operands += [slopes, group_rows]
        specs += [pl.BlockSpec(memory_space=pl.ANY), vmem]
    outs = pl.pallas_call(
        functools.partial(head_back_kernel, lane_bits, plan, tile),
        out_shape=shapes,
        in_specs=specs,
        out_specs=[vmem] * len(shapes),
        scratch_shapes=scratch,
        compiler_params=pltpu.CompilerParams(
            collective_id=5, has_side_effects=True, vmem_limit_bytes=56 * MIB
        ),
        name="head_back",
    )(*operands)
    if tile:
        return outs
    core = lane_bits[0]
    other = swap(outer_sum(slopes[:, half:], group_rows).astype(jnp.bfloat16), core)
    table_sum = outer_sum(slopes[:, :half], group_rows) + other.astype(jnp.float32)
    return outs[0], table_sum[: half // 2], table_sum[half // 2 :].astype(jnp.bfloat16)


def chip_sizes():
    wides, groups = lax.axis_size("wide"), lax.axis_size("narrow")
    return wides, groups // 2


class Rows:
    def __init__(self, sizes, x_ref, out_ref, send_sem, recv_sem):
        self.sizes, self.x_ref, self.out_ref = sizes, x_ref, out_ref
        self.send_sem, self.recv_sem = send_sem, recv_sem
        self.count = sizes[0] * sizes[1]
        self.place = Place(sizes[0], 2 * sizes[1])

    def peer(self, k):
        ups = self.sizes[1]
        return self.place.peer(k // ups, 2 * (k % ups))

    def each(self, step):
        for k in range(1, self.count):
            step(k)

    def copy(self, k):
        return pltpu.make_async_remote_copy(
            src_ref=self.x_ref.at[k],
            dst_ref=self.out_ref.at[k],
            send_sem=self.send_sem.at[k],
            recv_sem=self.recv_sem.at[k],
            device_id=self.peer(k),
            device_id_type=MESH,
        )

    def greet(self, others):
        self.call(others)
        self.meet(others)

    def call(self, others):
        barrier = pltpu.get_barrier_semaphore()
        self.each(
            lambda k: pl.semaphore_signal(
                barrier, inc=1, device_id=self.peer(k), device_id_type=MESH
            )
        )
        for device in others:
            pl.semaphore_signal(barrier, inc=1, device_id=device, device_id_type=MESH)

    def meet(self, others):
        pl.semaphore_wait(pltpu.get_barrier_semaphore(), self.count - 1 + len(others))

    def start(self):
        self.each(lambda k: self.copy(k).start())

    def own(self):
        return pltpu.make_async_copy(self.x_ref.at[0], self.out_ref.at[0], self.recv_sem.at[0])


def swap_rows_kernel(sizes, x_ref, out_ref, send_sem, recv_sem):
    rows = Rows(sizes, x_ref, out_ref, send_sem, recv_sem)
    rows.greet([])
    rows.start()
    own = rows.own()
    own.start()
    own.wait()
    rows.each(lambda k: rows.copy(k).wait())


def swap_rows(rows):
    sizes = chip_sizes()
    count = sizes[0] * sizes[1]
    return pl.pallas_call(
        functools.partial(swap_rows_kernel, sizes),
        out_shape=jax.ShapeDtypeStruct(rows.shape, rows.dtype),
        in_specs=[pl.BlockSpec(memory_space=pltpu.VMEM)],
        out_specs=pl.BlockSpec(memory_space=pl.ANY),
        scratch_shapes=mail_sems(count),
        compiler_params=pltpu.CompilerParams(collective_id=2, has_side_effects=True),
        name="token_rows",
    )(rows)


def load_kernel(sizes, lane_bits, *refs):
    core, x_bits, y_bits, z_bits = lane_bits
    near = z_bits[0]
    table_ref, weight_refs, rows_ref = refs[0], refs[1:5], refs[5]
    table_out, weight_outs, rows_out = refs[6], refs[7:11], refs[11]
    send_sem, recv_sem, rows_send, rows_recv, pass_send, pass_recv = refs[12:]
    wide, narrow = lax.axis_index("wide"), lax.axis_index("narrow")
    rows = Rows(sizes, rows_ref, rows_out.at[0], rows_send, rows_recv)
    rows.greet([neighbour(core)])
    mail = Mail(send_sem, recv_sem, lane_bits)
    side_near = (wide // near[1]) % 2

    def part(ref, number, half):
        count = ref.shape[1] // 2
        return ref.at[number, pl.ds(pl.multiple_of(half * count, 16), count)]

    def own_part(ref, half):
        count = ref.shape[0] // 2
        return ref.at[pl.ds(pl.multiple_of(half * count, 16), count)]

    tables = {0: mail.keep(table_ref, table_out.at[0, 0])}
    if x_bits:
        tables[1] = mail.post(table_ref, table_out.at[0, 1], x_bits[0])
    held = [0]
    first = []
    for ref, out in zip(weight_refs, weight_outs):
        if y_bits:
            first.append(
                mail.post(own_part(ref, side_near), part(out, narrow, side_near), y_bits[0])
            )
    rows.start()
    own_rows = rows.own()
    own_rows.start()
    mail.post(table_ref, table_out.at[1, 0], core)
    for ref, out in zip(weight_refs, weight_outs):
        mail.keep(ref, out.at[narrow])
        mail.post(ref, out.at[narrow], core)
    own_rows.wait()
    place = narrow
    blocks = [narrow]
    for level, bit in enumerate(y_bits):
        fresh = []
        arrivals = []
        for number, (ref, out) in enumerate(zip(weight_refs, weight_outs)):
            for spot, block in enumerate(blocks):
                other = block + bit[1] * (1 - 2 * ((block // bit[1]) % 2))
                if level == 0:
                    copy = first[number]
                else:
                    copy = mail.post(
                        part(out, block, side_near), part(out, block, side_near), bit
                    )
                arrivals.append((out, other, copy))
                if number == 0:
                    fresh.append(other)
        seconds = []
        for out, other, copy in arrivals:
            mail.take(copy)
            seconds.append(
                mail.post(part(out, other, side_near), part(out, other, side_near), near)
            )
            mail.post(part(out, other, side_near), part(out, other, side_near), core)
        for (out, other, _), copy in zip(arrivals, seconds):
            mail.take(copy)
            mail.post(part(out, other, 1 - side_near), part(out, other, 1 - side_near), core)
        blocks = blocks + fresh

    def hand(k):
        return pltpu.make_async_remote_copy(
            src_ref=rows_out.at[0, k],
            dst_ref=rows_out.at[1, k],
            send_sem=pass_send.at[k],
            recv_sem=pass_recv.at[k],
            device_id=neighbour(core),
            device_id_type=MESH,
        )

    hand(0).start()

    def forward(k):
        rows.copy(k).wait()
        hand(k).start()

    rows.each(forward)
    for level, bit in enumerate(x_bits):
        for block in range(1 << level):
            spot = block + (1 << level)
            if spot not in tables:
                tables[spot] = mail.post(table_out.at[0, block], table_out.at[0, spot], bit)
        for block in range(1 << level):
            spot = block + (1 << level)
            mail.take(tables[spot])
            mail.post(table_out.at[0, spot], table_out.at[1, spot], core)
    hand(0).wait()
    rows.each(lambda k: hand(k).wait())
    mail.close()


def load_all(table, weights, rows):
    lane_bits = lanes()
    sizes = chip_sizes()
    count = sizes[0] * sizes[1]
    groups = lax.axis_size("narrow")
    across = 1 << len(lane_bits[1])
    any_space = pl.BlockSpec(memory_space=pl.ANY)
    shapes = (
        [jax.ShapeDtypeStruct((2, across) + table.shape, table.dtype)]
        + [jax.ShapeDtypeStruct((groups,) + w.shape, w.dtype) for w in weights]
        + [jax.ShapeDtypeStruct((2,) + rows.shape, rows.dtype)]
    )
    table_all, *weights_all, rows_all = pl.pallas_call(
        functools.partial(load_kernel, sizes, lane_bits),
        out_shape=shapes,
        in_specs=[pl.BlockSpec(memory_space=pltpu.VMEM)] * 6,
        out_specs=[any_space] * 6,
        scratch_shapes=mail_sems(8 * 2 * groups + 2 * across + 4)
        + mail_sems(count)
        + mail_sems(count),
        compiler_params=pltpu.CompilerParams(
            collective_id=6, has_side_effects=True, vmem_limit_bytes=32 * MIB
        ),
        name="load_rows",
    )(table, *weights, rows)
    model = table.shape[1]
    return (
        table_all.reshape(-1, model),
        tuple(w.reshape(-1, model) for w in weights_all),
        rows_all,
    )


def tile_of(rows):
    return next(size for size in (128, 96, 64, 48, 32, 16) if rows % size == 0)


def back_reduce_kernel(sizes, lane_bits, kinds, *refs):
    core, x_bits, y_bits, z_bits = lane_bits
    ins, wanted_ref, hbm = refs[:8], refs[8], refs[9:13]
    out_refs, small_out, rows_out, square_out, low_out = refs[13:16], *refs[16:20]
    scratch = refs[20:]
    weights, load_sem, stream_ref, small_ref = scratch[:4], scratch[4], scratch[5], small_out
    grad_refs = scratch[6:9]
    both_ref, core_got = scratch[9:11]
    small_sum, small_got, send_sem, recv_sem, rows_send, rows_recv = scratch[11:17]
    rest = scratch[17:]
    got_refs = []
    for _, _, _, path in kinds:
        got_refs.append(rest[: len(path) + 1])
        rest = rest[len(path) + 1 :]
    waits = [
        pltpu.make_async_copy(source, target, load_sem.at[number])
        for number, (source, target) in enumerate(zip(hbm, weights))
    ]
    for load in waits:
        load.start()
    place = {"wide": lax.axis_index("wide"), "narrow": lax.axis_index("narrow")}
    rows = Rows(sizes, both_ref.at[0], rows_out, rows_send, rows_recv)
    rows.call([neighbour(core)])
    mail = Mail(send_sem, recv_sem, lane_bits)
    ups = grad_refs[0].shape[1]
    own = place["narrow"] % 2
    square_out[...] = jnp.zeros_like(square_out)

    def side_of(bit):
        return (place[bit[0]] // bit[1]) % 2

    def add(total_ref, got_ref, box):
        up, ups_here, first, height = box
        tile = tile_of(height)

        def step(i, carry):
            at = i // (height // tile)
            down = (i % (height // tile)) * tile
            span = pl.ds(pl.multiple_of(first + down, 16), tile)
            got = got_ref[at, pl.ds(pl.multiple_of(down, 16), tile), :]
            total = total_ref[own, up + at, span, :].astype(jnp.float32) + got.astype(jnp.float32)
            total_ref[own, up + at, span, :] = total.astype(jnp.bfloat16)
            return carry

        lax.fori_loop(0, ups_here * (height // tile), step, 0)

    def view(ref, box):
        up, ups_here, first, height = box
        return ref.at[own, pl.ds(up, ups_here), pl.ds(pl.multiple_of(first, 16), height)]

    def flow(number):
        which, offset, height, path = kinds[number]
        total_ref, got, out_ref = grad_refs[which], got_refs[number], out_refs[which]
        span = pl.ds(offset, height)
        copy = mail.post(total_ref.at[1 - own, :, span], got[0], core)
        yield mail.due
        mail.take(copy)
        box = (0, ups, offset, height)
        add(total_ref, got[0], box)
        for stage, (bit, halve) in enumerate(path):
            up, ups_here, first, height = box
            side = side_of(bit)
            if bit[0] == "narrow":
                half = ups_here // 2
                mine = (up + side * half, half, first, height)
                theirs = (up + (1 - side) * half, half, first, height)
            elif halve:
                half = height // 2
                mine = (up, ups_here, first + side * half, half)
                theirs = (up, ups_here, first + (1 - side) * half, half)
            else:
                mine = theirs = box
            copy = mail.post(view(total_ref, theirs), got[stage + 1], bit)
            yield mail.due
            mail.take(copy)
            if not halve:
                copy.wait_send()
                mail.sent = [other for other in mail.sent if other is not copy]
            box = mine
            add(total_ref, got[stage + 1], box)
        up, _, first, height = box
        piece = total_ref[own, up, pl.ds(pl.multiple_of(first, 16), height), :]
        out_ref[pl.ds(pl.multiple_of(first, 16), height), :] = piece
        full = piece.astype(jnp.float32)
        square_out[...] += jnp.sum((full * full).reshape(height // 8, 8, -1), 0)
        for bit, halve in reversed(path):
            if bit[0] == "wide" and halve:
                span = pl.ds(pl.multiple_of(first, 16), height)
                copy = mail.post(out_ref.at[span], out_ref.at[span], bit)
                yield mail.due
                mail.take(copy)
                first = first - side_of(bit) * height
                height = 2 * height

    def small_flow():
        bits = [core] + x_bits + y_bits + z_bits
        small_sum[0] = small_ref[...].astype(jnp.bfloat16)
        for stage, bit in enumerate(bits):
            copy = mail.post(small_sum.at[stage], small_got.at[stage], bit)
            yield mail.due
            mail.take(copy)
            total = small_sum[stage].astype(jnp.float32) + small_got[stage].astype(jnp.float32)
            if stage == len(bits) - 1:
                small_out[...] = total
            else:
                small_sum[stage + 1] = total.astype(jnp.bfloat16)

    def rows_flow():
        low = stream_ref[...].astype(jnp.bfloat16)
        low_out[...] = low
        both = outer_sum(wanted_ref[...], low).astype(jnp.bfloat16)
        both_ref[...] = both.reshape(both_ref.shape)
        copy = mail.post(both_ref.at[1], core_got, core)
        yield mail.due
        mail.take(copy)
        summed = both_ref[0].astype(jnp.float32) + core_got[...].astype(jnp.float32)
        both_ref[0] = summed.astype(jnp.bfloat16)
        rows.start()
        own_rows = rows.own()
        own_rows.start()
        yield mail.due
        own_rows.wait()

    back = backward_flow(
        ins,
        (stream_ref, small_ref) + tuple(grad_refs),
        (*weights, waits),
    )
    next(back)
    rows.meet([neighbour(core)])

    def back_flow():
        for cost in back:
            yield mail.spend(cost)
        mail.ready += [flow(number) for number in range(4, len(kinds))]
        mail.ready += [rows_flow(), small_flow()]

    mail.run([flow(number) for number in range(4)] + [back_flow()])
    rows.each(lambda k: rows.copy(k).wait())
    mail.close()


def back_reduce(final_grad, norm_gains, bias_rows, saved, weights, wanted):
    lane_bits = lanes()
    core, x_bits, y_bits, z_bits = lane_bits
    sizes = chip_sizes()
    tokens, width = final_grad.shape
    ups = sizes[1]
    height = 4 * width // (2 * ups)
    half = height // 2
    bits = {"x": x_bits, "y": y_bits[::-1], "z": z_bits[:1], "f": z_bits[1:]}
    kinds, got_shapes = [], []
    for which, offset, order in (
        (1, 0, "yzfx"),
        (2, 0, "yxzf"),
        (1, half, "yzxf"),
        (2, half, "zyxf"),
        (0, 0, "yxfz"),
        (0, half, "yxzf"),
    ):
        path, ups_here, height_here = [], ups, half
        shapes = [(ups_here, height_here, width)]
        for bit in [bit for kind in order for bit in bits[kind]]:
            halve = True
            if bit[0] == "narrow":
                ups_here //= 2
            else:
                halve = (height_here // 2) % 16 == 0
                height_here = height_here // 2 if halve else height_here
            path.append((bit, halve))
            shapes.append((ups_here, height_here, width))
        kinds.append((which, offset, half, path))
        got_shapes += shapes
    count = sizes[0] * sizes[1]
    steps = 1 + len(kinds[0][3])
    small_rows = 14 + LENGTH
    small = (small_rows + -small_rows % 16, width)
    row_shape = (count, slots(), width)
    vmem, any_space = pl.BlockSpec(memory_space=pltpu.VMEM), pl.BlockSpec(memory_space=pl.ANY)
    shape, low = jax.ShapeDtypeStruct, jnp.bfloat16
    outs = pl.pallas_call(
        functools.partial(back_reduce_kernel, sizes, lane_bits, kinds),
        out_shape=[shape((height, width), low)] * 3
        + [
            shape(small, jnp.float32),
            shape(row_shape, low),
            shape((8, width), jnp.float32),
            shape((tokens, width), low),
        ],
        in_specs=[vmem] * 9 + [any_space] * 4,
        out_specs=[vmem] * 4 + [any_space, vmem, vmem],
        scratch_shapes=[pltpu.VMEM(w.shape, w.dtype) for w in weights]
        + [
            pltpu.SemaphoreType.DMA((4,)),
            pltpu.VMEM((tokens, width), jnp.float32),
        ]
        + [pltpu.VMEM((2, ups, height, width), low) for _ in range(3)]
        + [pltpu.VMEM((2,) + row_shape, low), pltpu.VMEM(row_shape, low)]
        + [pltpu.VMEM((steps,) + small, low), pltpu.VMEM((steps,) + small, low)]
        + mail_sems(len(kinds) * 2 * steps + steps + 1)
        + mail_sems(count)
        + [pltpu.VMEM(one, low) for one in got_shapes],
        compiler_params=pltpu.CompilerParams(
            collective_id=7, has_side_effects=True, vmem_limit_bytes=63 * MIB
        ),
        name="back_reduce",
    )(final_grad, norm_gains, bias_rows, *saved, wanted, *weights)
    repeats = 1
    for bit, halve in kinds[0][3]:
        repeats *= 1 if halve else 2
    return outs[:3], outs[3], outs[4], jnp.sum(outs[5]) / repeats, outs[6]


class Place:
    def __init__(self, wides, groups):
        self.wide, self.narrow = lax.axis_index("wide"), lax.axis_index("narrow")
        self.wide_steps = self.steps(self.wide, wides)
        self.narrow_steps = self.steps(self.narrow, groups)

    def steps(self, place, size):
        masks = [1 << bit for bit in range(log_two(size))]
        return {mask: mask * (1 - 2 * ((place // mask) % 2)) for mask in masks}

    def peer(self, wide_mask, narrow_mask):
        wide, narrow = self.wide, self.narrow
        for mask, step in self.wide_steps.items():
            wide = wide + step if mask & wide_mask else wide
        for mask, step in self.narrow_steps.items():
            narrow = narrow + step if mask & narrow_mask else narrow
        return wide, narrow


def exchange_kernel(masks, sizes, whole, x_ref, out_ref, send_sem, recv_sem, own_sem):
    wides, groups = sizes
    place = Place(wides, groups)
    masks = list(range(wides * groups)) if masks is None else masks
    count = len(masks)

    def peer(mask):
        return place.peer(mask // groups, mask % groups)

    def each(step):
        for k in range(1, count):
            step(k, masks[k])

    def copy(k, mask):
        return pltpu.make_async_remote_copy(
            src_ref=x_ref if whole else x_ref.at[k],
            dst_ref=out_ref.at[k],
            send_sem=send_sem.at[k],
            recv_sem=recv_sem.at[k],
            device_id=peer(mask),
            device_id_type=MESH,
        )

    barrier = pltpu.get_barrier_semaphore()
    each(
        lambda k, mask: pl.semaphore_signal(
            barrier, inc=1, device_id=peer(mask), device_id_type=MESH
        )
    )
    pl.semaphore_wait(barrier, count - 1)
    each(lambda k, mask: copy(k, mask).start())
    own = pltpu.make_async_copy(x_ref if whole else x_ref.at[0], out_ref.at[0], own_sem)
    own.start()
    own.wait()
    each(lambda k, mask: copy(k, mask).wait())


def exchange(array, number, name, masks=None, whole=True):
    sizes = (lax.axis_size("wide"), lax.axis_size("narrow"))
    count = sizes[0] * sizes[1] if masks is None else len(masks)
    shape = (count,) + array.shape if whole else array.shape
    return pl.pallas_call(
        functools.partial(exchange_kernel, masks, sizes, whole),
        out_shape=jax.ShapeDtypeStruct(shape, array.dtype),
        in_specs=[pl.BlockSpec(memory_space=pltpu.VMEM)],
        out_specs=pl.BlockSpec(memory_space=pltpu.VMEM),
        scratch_shapes=[
            pltpu.SemaphoreType.DMA((count,)),
            pltpu.SemaphoreType.DMA((count,)),
            pltpu.SemaphoreType.DMA,
        ],
        compiler_params=pltpu.CompilerParams(
            collective_id=number, has_side_effects=True, vmem_limit_bytes=32 * MIB
        ),
        name=name,
    )(array)


def merge_stats(stats):
    masks = group_masks()
    rows = stats.shape[1] // 4
    parts = exchange(stats, 1, "stats_swap", masks, False)
    top, total, picked = (parts[:, i * rows : (i + 1) * rows] for i in range(3))
    highest = jnp.max(top, 0)
    own = highest + jnp.log(jnp.sum(total * jnp.exp(top - highest), 0))
    share = exchange(jnp.pad(own, ((0, -rows % 8), (0, 0))), 8, "stats_share", masks)
    return share[:, :rows], own, jnp.sum(picked, 0)


def put_columns(rows_ref, column_ref):
    turned = rows_ref[...].T
    for place in range(rows_ref.shape[0]):
        column_ref[pl.ds(place * 128, 128), :] = turned[:, place : place + 1]


def as_rows(column):
    count = column.shape[0] // 128
    return jnp.concatenate(
        [column[place * 128 : (place + 1) * 128] for place in range(count)], 1
    ).T


def score_kernel(
    rows_ref, table_ref, target_ref, exps_ref, max_ref, stat_ref, sum_ref, pick_ref, column_ref
):
    tile = pl.program_id(0)
    width = table_ref.shape[0]

    @pl.when(tile == 0)
    def _():
        max_ref[...] = jnp.full_like(max_ref, -jnp.inf)
        sum_ref[...] = jnp.zeros_like(sum_ref)
        pick_ref[...] = jnp.zeros_like(pick_ref)
        put_columns(target_ref, column_ref)

    def step(block, carry):
        rows = pl.ds(pl.multiple_of(block * TOKEN_TILE, TOKEN_TILE), TOKEN_TILE)
        scores = lax.dot_general(
            rows_ref[rows, :],
            table_ref[...],
            (((1,), (1,)), ((), ())),
            preferred_element_type=jnp.float32,
        )
        top = jnp.max(scores, -1, keepdims=True)
        powers = jnp.exp(scores - top)
        exps_ref[rows, :] = powers.astype(jnp.bfloat16)
        total = jnp.sum(powers, -1, keepdims=True)
        columns = lax.broadcasted_iota(jnp.int32, (TOKEN_TILE, width), 1)
        wanted = column_ref[rows, :] - tile * width
        hit = jnp.sum(jnp.where(columns == wanted, scores, 0.0), -1, keepdims=True)
        here = lax.broadcasted_iota(jnp.int32, (TOKEN_TILE, 128), 1) == tile
        max_ref[rows, :] = jnp.where(here, top, max_ref[rows, :])
        sum_ref[rows, :] = jnp.where(here, total, sum_ref[rows, :])
        pick_ref[rows, :] = jnp.where(here, hit, pick_ref[rows, :])
        return carry

    lax.fori_loop(0, rows_ref.shape[0] // TOKEN_TILE, step, 0, unroll=8)

    @pl.when(tile == pl.num_programs(0) - 1)
    def _():
        maxima = max_ref[...]
        top = jnp.max(maxima, -1, keepdims=True)
        total = jnp.sum(sum_ref[...] * jnp.exp(maxima - top), -1, keepdims=True)
        picked = jnp.sum(pick_ref[...], -1, keepdims=True)
        blocks, height, _ = stat_ref.shape
        rows = height // 4
        stat_ref[...] = jnp.zeros_like(stat_ref)
        for number, column in enumerate((top, total, picked)):
            lines = as_rows(column)
            for block in range(blocks):
                stat_ref[block, pl.ds(number * rows, rows), :] = lines[
                    block * rows : (block + 1) * rows
                ]


def vocab_tile(vocab):
    return 1280 if vocab % 1280 == 0 else 640


def head_scores(rows, table, targets, blocks):
    tokens, model = rows.shape
    vocab = table.shape[0]
    width = vocab_tile(vocab)
    stat = pltpu.VMEM((tokens, 128), jnp.float32)
    whole = pl.BlockSpec((tokens, 128), lambda j: (0, 0))
    height = 4 * (tokens // blocks // 128)
    return pl.pallas_call(
        score_kernel,
        grid=(vocab // width,),
        out_shape=(
            jax.ShapeDtypeStruct((tokens, vocab), jnp.bfloat16),
            jax.ShapeDtypeStruct((tokens, 128), jnp.float32),
            jax.ShapeDtypeStruct((blocks, height, 128), jnp.float32),
        ),
        in_specs=[
            pl.BlockSpec((tokens, model), lambda j: (0, 0)),
            pl.BlockSpec((width, model), lambda j: (j, 0)),
            pl.BlockSpec(targets.shape, lambda j: (0, 0)),
        ],
        out_specs=(
            pl.BlockSpec((tokens, width), lambda j: (0, j)),
            whole,
            pl.BlockSpec((blocks, height, 128), lambda j: (0, 0, 0)),
        ),
        scratch_shapes=[stat, stat, pltpu.VMEM((tokens, 1), jnp.int32)],
        compiler_params=pltpu.CompilerParams(vmem_limit_bytes=60 * MIB),
        cost_estimate=pl.CostEstimate(
            flops=3 * tokens * vocab * model,
            bytes_accessed=2 * tokens * vocab,
            transcendentals=tokens * vocab,
        ),
        name="head_scores",
    )(rows, table, targets)


def slope_kernel(
    exps_ref,
    max_ref,
    log_ref,
    target_ref,
    table_ref,
    slope_ref,
    grad_ref,
    total_ref,
    column_ref,
    log_column_ref,
):
    tile = pl.program_id(0)
    width = table_ref.shape[0]

    @pl.when(tile == 0)
    def _():
        total_ref[...] = jnp.zeros_like(total_ref)
        put_columns(target_ref, column_ref)
        put_columns(log_ref, log_column_ref)

    def step(block, carry):
        rows = pl.ds(pl.multiple_of(block * TOKEN_TILE, TOKEN_TILE), TOKEN_TILE)
        here = lax.broadcasted_iota(jnp.int32, (TOKEN_TILE, 128), 1) == tile
        top = jnp.sum(jnp.where(here, max_ref[rows, :], 0.0), -1, keepdims=True)
        scale = jnp.exp(top - log_column_ref[rows, :])
        columns = lax.broadcasted_iota(jnp.int32, (TOKEN_TILE, width), 1)
        wanted = column_ref[rows, :] - tile * width
        probs = exps_ref[rows, :].astype(jnp.float32) * scale
        slope = jnp.where(columns == wanted, probs - 1.0, probs).astype(jnp.bfloat16)
        slope_ref[rows, :] = slope
        total_ref[rows, :] += jnp.dot(slope, table_ref[...], preferred_element_type=jnp.float32)
        return carry

    lax.fori_loop(0, exps_ref.shape[0] // TOKEN_TILE, step, 0, unroll=8)

    @pl.when(tile == pl.num_programs(0) - 1)
    def _():
        grad_ref[...] = total_ref[...].astype(jnp.bfloat16)


def head_slopes(exps, maxima, logs, targets, table):
    tokens, vocab = exps.shape
    model = table.shape[1]
    width = vocab_tile(vocab)
    return pl.pallas_call(
        slope_kernel,
        grid=(vocab // width,),
        out_shape=(
            jax.ShapeDtypeStruct((tokens, vocab), jnp.bfloat16),
            jax.ShapeDtypeStruct((tokens, model), jnp.bfloat16),
        ),
        in_specs=[
            pl.BlockSpec((tokens, width), lambda j: (0, j)),
            pl.BlockSpec((tokens, 128), lambda j: (0, 0)),
            pl.BlockSpec(logs.shape, lambda j: (0, 0)),
            pl.BlockSpec(targets.shape, lambda j: (0, 0)),
            pl.BlockSpec((width, model), lambda j: (j, 0)),
        ],
        out_specs=(
            pl.BlockSpec((tokens, width), lambda j: (0, j)),
            pl.BlockSpec((tokens, model), lambda j: (0, 0)),
        ),
        scratch_shapes=[
            pltpu.VMEM((tokens, model), jnp.float32),
            pltpu.VMEM((tokens, 1), jnp.int32),
            pltpu.VMEM((tokens, 1), jnp.float32),
        ],
        compiler_params=pltpu.CompilerParams(vmem_limit_bytes=60 * MIB),
        cost_estimate=pl.CostEstimate(
            flops=3 * tokens * vocab * model,
            bytes_accessed=4 * tokens * vocab,
            transcendentals=0,
        ),
        name="head_slopes",
    )(exps, maxima, logs, targets, table)


def slots():
    wides, ups = chip_sizes()
    return 32 if wides * ups <= 16 else 16


def one_hot(places, size):
    return (places.reshape(-1, 1) == jnp.arange(size)[None]).astype(jnp.bfloat16)


def token_plan(ids_all, shard_rows):
    chips, tokens = ids_all.shape
    wides, ups = chip_sizes()
    wide, narrow = lax.axis_index("wide"), lax.axis_index("narrow")
    own_core = narrow % 2
    own_chip = wide * ups + narrow // 2
    owner = ids_all // shard_rows
    owner_core = jnp.bitwise_xor(owner % 2, own_core)
    owner_chip = jnp.bitwise_xor(owner // 2, own_chip)
    local = ids_all % shard_rows
    row = lax.broadcasted_iota(jnp.int32, (tokens, tokens), 0)
    column = lax.broadcasted_iota(jnp.int32, (tokens, tokens), 1)
    before = column < row
    alike = ids_all[:, :, None] == ids_all[:, None, :]
    first = ~jnp.any(alike & before[None], 2)
    served = first & (owner_chip == 0) & (owner_core == 0)
    served_rank = times_t(served.astype(jnp.bfloat16), before.astype(jnp.bfloat16)).astype(
        jnp.int32
    )
    half = tokens // 2
    mine = lambda array: lax.dynamic_slice_in_dim(array, own_core * half, half)
    own_first = mine(jnp.min(jnp.where(alike[0], column, tokens), 1))
    same_owner = mine(owner[0])[:, None] == owner[0][None]
    own_rank = jnp.sum(
        (same_owner & first[0][None] & (column[:half] < own_first[:, None])).astype(jnp.int32), 1
    )
    own_block = mine(owner_core[0]) * chips + mine(owner_chip[0])
    most = jnp.max(
        jnp.sum(
            (
                first[:, None, :]
                & (owner[:, None, :] == jnp.arange(2 * chips)[None, :, None])
            ).astype(jnp.int32),
            2,
        )
    )
    rounds = (most + slots() - 1) // slots()

    def plan(turn):
        slot = jnp.arange(slots())[None, :, None] + turn * slots()
        chosen = served[:, None, :] & (served_rank[:, None, :] == slot)
        slot_rows = jnp.sum(jnp.where(chosen, local[:, None, :] + 1, 0), 2) - 1
        inside = own_rank - turn * slots()
        valid = (inside >= 0) & (inside < slots())
        own_slots = jnp.where(valid, own_block * slots() + inside, -1)
        return one_hot(slot_rows, shard_rows), one_hot(own_slots, 2 * chips * slots())

    return plan, rounds


def later_rounds(rounds, turn, total):
    return lax.while_loop(
        lambda state: state[0] < rounds,
        lambda state: (state[0] + 1, state[1] + turn(state[0])),
        (jnp.ones((), jnp.int32), total),
    )[1]


def upper_blocks(count):
    return [(i, j) for i in range(count) for j in range(i, count)]


def muon_kernel(lane_bits, *refs):
    core, _, y_bits, _ = lane_bits
    low_refs = refs[:4]
    rest_out, size_out = refs[4:6]
    gram, sent, got, back, full, total, half, low_a, low_b, low_c, send_sem, recv_sem = refs[6:]
    width = full.shape[0]
    block = gram.shape[-1]
    places = upper_blocks(width // block)
    wide, narrow = lax.axis_index("wide"), lax.axis_index("narrow")
    greet([neighbour(bit) for bit in [core] + y_bits])
    mail = Mail(send_sem, recv_sem, lane_bits)
    own_core, own_up = narrow % 2, (narrow // 2) % 2
    own = 2 * own_core + own_up

    for number, low_ref in enumerate(low_refs):
        for place, (i, j) in enumerate(places):
            product = lax.dot_general(
                low_ref[:, i * block : (i + 1) * block],
                low_ref[:, j * block : (j + 1) * block],
                (((0,), (0,)), ((), ())),
                preferred_element_type=jnp.float32,
            )
            gram[number, place] = product
    for slot in range(2):
        sent[slot] = gram[2 * (1 - own_core) + slot].astype(jnp.bfloat16)
    mail.take(mail.post(sent.at[pl.ds(0, 2)], got.at[pl.ds(0, 2)], core))

    def add(number, slot):
        for place in range(len(places)):
            gram[number, place] += got[slot, place].astype(jnp.float32)

    def pass_on(number, slot, bit):
        sent[slot] = gram[number].astype(jnp.bfloat16)
        return mail.post(sent.at[slot], got.at[slot], bit)

    other_up = 2 * own_core + 1 - own_up
    if y_bits:
        add(other_up, 1 - own_up)
        over_y = pass_on(other_up, 2, y_bits[0])
        add(own, own_up)
        mail.take(over_y)
        add(own, 2)
    for level, bit in enumerate(y_bits[1:]):
        mail.take(pass_on(own, 3 + level, bit))
        add(own, 3 + level)

    def unpack(source, target):
        for place, (i, j) in enumerate(places):
            piece = source(place)
            target(i, j, piece)
            if i != j:
                target(j, i, piece.T)

    def spans(i, j):
        return pl.ds(i * block, block), pl.ds(j * block, block)

    def put_full(i, j, piece):
        full[spans(i, j)] = piece

    unpack(lambda place: gram[own, place], put_full)
    diagonal = lax.broadcasted_iota(jnp.int32, (block, block), 0) == lax.broadcasted_iota(
        jnp.int32, (block, block), 1
    )
    trace = jnp.zeros((1, 1), jnp.float32)
    for i in range(width // block):
        trace = trace + jnp.sum(jnp.where(diagonal, full[spans(i, i)], 0.0), keepdims=True)
    magnitude = jnp.sqrt(trace) + 1e-07
    inverse = 1.0 / magnitude

    def rows(step):
        def body(i, carry):
            step(pl.ds(pl.multiple_of(i * block, block), block))
            return carry

        lax.fori_loop(0, width // block, body, 0)

    def times(left, right, span):
        return jnp.dot(left[span, :], right[...], preferred_element_type=jnp.float32)

    def start(span):
        scaled = full[span, :] * (inverse * inverse)
        full[span, :] = scaled
        low_a[span, :] = scaled.astype(jnp.bfloat16)

    rows(start)
    scale = NS_A
    for cycle_no in range(NS_STEPS):

        def rest_step(span):
            rest = NS_B * full[span, :] + NS_C * times(low_a, low_a, span)
            low_b[span, :] = rest.astype(jnp.bfloat16)
            if cycle_no == 0:
                total[span, :] = rest
            else:
                total[span, :] = NS_A * total[span, :] + scale * rest

        rows(rest_step)
        if cycle_no:

            def total_step(span):
                total[span, :] += times(low_c, low_b, span)

            rows(total_step)
            scale = scale * NS_A
        if cycle_no < NS_STEPS - 1:

            def keep_total(span):
                low_c[span, :] = total[span, :].astype(jnp.bfloat16)

            def half_step(span):
                half[span, :] = NS_A * full[span, :] + times(low_a, low_b, span)

            def full_step(span):
                value = half[span, :]
                low_a[span, :] = value.astype(jnp.bfloat16)
                full[span, :] = NS_A * value + times(low_a, low_b, span)

            def low_step(span):
                low_a[span, :] = full[span, :].astype(jnp.bfloat16)

            rows(keep_total)
            rows(half_step)
            rows(full_step)
            rows(low_step)

    for place, (i, j) in enumerate(places):
        back[own, place] = (total[spans(i, j)] * inverse).astype(jnp.bfloat16)
    lane = lax.broadcasted_iota(jnp.int32, (8, 128), 1)
    size_out[own] = jnp.where(lane >= 0, inverse, 0.0)
    mail.close()
    mail = Mail(send_sem.at[pl.ds(16, 16)], recv_sem.at[pl.ds(16, 16)], lane_bits)
    mine = mail.post(back.at[own], back.at[own], core)
    mine_size = mail.post(size_out.at[own], size_out.at[own], core)
    if y_bits:
        over_y = mail.post(back.at[own], back.at[own], y_bits[0])
        over_size = mail.post(size_out.at[own], size_out.at[own], y_bits[0])
        mail.take(over_y)
        mail.take(over_size)
        mail.post(back.at[other_up], back.at[other_up], core)
        mail.post(size_out.at[other_up], size_out.at[other_up], core)
    mail.close()
    for number in range(4):

        def put_out(i, j, piece, number=number):
            rest_out[(number,) + spans(i, j)] = piece.astype(jnp.bfloat16)

        unpack(lambda place: back[number, place].astype(jnp.float32), put_out)


def muon_factors(lows):
    width = lows[0].shape[1]
    block = 256
    count = len(upper_blocks(width // block))
    lane_bits = lanes()
    extra = max(len(lane_bits[2]) - 1, 0)
    vmem = pl.BlockSpec(memory_space=pltpu.VMEM)
    square = (width, width)
    rests, sizes = pl.pallas_call(
        functools.partial(muon_kernel, lane_bits),
        out_shape=(
            jax.ShapeDtypeStruct((4,) + square, jnp.bfloat16),
            jax.ShapeDtypeStruct((4, 8, 128), jnp.float32),
        ),
        in_specs=[vmem] * 4,
        out_specs=(vmem, vmem),
        scratch_shapes=[
            pltpu.VMEM((4, count, block, block), jnp.float32),
            pltpu.VMEM((3 + extra, count, block, block), jnp.bfloat16),
            pltpu.VMEM((3 + extra, count, block, block), jnp.bfloat16),
            pltpu.VMEM((4, count, block, block), jnp.bfloat16),
        ]
        + [pltpu.VMEM(square, jnp.float32) for _ in range(3)]
        + [pltpu.VMEM(square, jnp.bfloat16) for _ in range(3)]
        + mail_sems(32),
        compiler_params=pltpu.CompilerParams(
            collective_id=9, has_side_effects=True, vmem_limit_bytes=56 * MIB
        ),
        name="muon_factors",
    )(*lows)
    return rests, sizes[:, 0, 0]


def on_device(
    token_ids,
    targets,
    joint_weight,
    output_weight,
    expand_weight,
    reduce_weight,
    joint_velocity,
    output_velocity,
    expand_velocity,
    reduce_velocity,
    embedding,
    embed_moment,
    embed_square,
    positions,
    position_moment,
    position_square,
    norm_gains,
    gain_moment,
    gain_square,
    biases,
    bias_moment,
    bias_square,
):
    core, x_bits, y_bits, z_bits = lanes()
    groups = lax.axis_size("narrow")
    wides = lax.axis_size("wide")
    across = 1 << len(x_bits)
    model_width = embedding.shape[1]
    shard_rows = embedding.shape[0]
    tokens = token_ids.shape[0] * LENGTH
    bias_rows = biases.reshape(-1, model_width)

    own_rows = embedding.astype(jnp.bfloat16)
    labels = jnp.concatenate([token_ids.reshape(-1, 128), targets.reshape(-1, 128)])
    spare = -labels.shape[0] % 8
    labels = exchange(jnp.pad(labels, ((0, spare), (0, 0))), 0, "label_share")
    ids_all = labels[:, : tokens // 128].reshape(-1, tokens)
    lines = tokens // 128
    own_block = lax.axis_index("wide") * groups + lax.axis_index("narrow")
    wides, ups = chip_sizes()
    pairs = ids_all.reshape(wides, ups, 2, tokens)
    other_first = lax.axis_index("narrow") % 2 == 1
    ids_chips = jnp.where(other_first, lax.rev(pairs, (2,)), pairs).reshape(wides * ups, -1)
    plan, rounds = token_plan(ids_chips, shard_rows)

    def serve(served):
        return plain(served, own_rows).astype(jnp.bfloat16).reshape(-1, slots(), model_width)

    masters = (joint_weight, output_weight, expand_weight, reduce_weight)
    served, wanted = plan(0)
    table, weights, token_rows = load_all(
        own_rows, [master.astype(jnp.bfloat16) for master in masters], serve(served)
    )
    vocab_here = table.shape[0]

    def fetch(turn):
        more, places = plan(turn)
        got = swap_rows(serve(more))
        return plain(places, jnp.stack([got, swap(got, core)]).reshape(-1, model_width))

    embedded = later_rounds(rounds, fetch, plain(wanted, token_rows.reshape(-1, model_width)))

    block_masks = jnp.array(group_masks())
    targets_group = labels[block_masks, lines : 2 * lines].reshape(-1, 128)
    table_mask = groups * (across - 1) + 1
    differ = jnp.bitwise_xor(targets_group // shard_rows, own_block)
    is_owned = (targets_group >= 0) & (jnp.bitwise_and(differ, ~table_mask) == 0)
    place = (differ % 2) * across + (differ // groups) % across
    rows_targets = jnp.where(is_owned, place * shard_rows + targets_group % shard_rows, -1)
    final_low, *saved = layer_forward(embedded, positions, norm_gains, bias_rows, weights)
    group_rows = spread(final_low).reshape(-1, model_width)
    blocks = len(group_masks())
    exps, maxima, stats = head_scores(group_rows, table, rows_targets, blocks)
    logs, own_logs, own_picked = merge_stats(stats)
    loss_part = jnp.sum(
        jnp.where(targets.reshape(-1, 128) >= 0, own_logs - own_picked, 0.0)
    )
    logs = jnp.where(targets_group >= 0, logs.reshape(-1, 128), jnp.inf)
    slopes, final_part = head_slopes(exps, maxima, logs, rows_targets, table)
    final_grad, table_sum, passed = head_back(
        final_part.reshape(-1, tokens, model_width), slopes, group_rows
    )
    for bit in reversed(x_bits):
        table_sum = table_sum + swap(passed, bit).astype(jnp.float32)
        half = table_sum.shape[0] // 2
        if bit != x_bits[0]:
            table_sum, passed = table_sum[:half], table_sum[half:].astype(jnp.bfloat16)
    (front, expand_sum, reduce_sum), small, row_sums, squares, low_grad = back_reduce(
        final_grad, norm_gains, bias_rows, saved, weights, wanted
    )
    count_part = jnp.sum((targets >= 0).astype(jnp.float32))

    def bundle(places):
        both = outer_sum(places, low_grad).astype(jnp.bfloat16)
        both = both.reshape(2, -1, slots(), model_width)
        other = swap(both[1], core)
        return (both[0].astype(jnp.float32) + other.astype(jnp.float32)).astype(jnp.bfloat16)

    joint_rows = joint_weight.shape[0]
    table_sum = table_sum + outer_sum(served, row_sums.reshape(-1, model_width))

    def give(turn):
        more, places = plan(turn)
        return outer_sum(more, swap_rows(bundle(places)).reshape(-1, model_width))

    table_sum = later_rounds(rounds, give, table_sum)
    matrix_total = [
        part.astype(jnp.float32)
        for part in (front[:joint_rows], front[joint_rows:], expand_sum, reduce_sum)
    ]
    small = small[: 14 + LENGTH]
    squares = squares + jnp.sum(table_sum * table_sum)
    scalars = jnp.pad(jnp.stack([loss_part, count_part, squares])[None], ((0, 7), (0, 125)))
    scalars = jnp.sum(exchange(scalars, 3, "scalar_share"), 0)
    loss_sum, loss_count, squares = scalars[0, 0], scalars[0, 1], scalars[0, 2]
    squares = squares + jnp.sum(small * small)
    gain_grad, position_grad = small[:3], small[14:]
    bias_grad = small[3:14].reshape(-1)
    grad_norm = jnp.sqrt(squares) / loss_count
    factor = jnp.minimum(1.0, CLIP / (grad_norm + 1e-06)) / loss_count
    previous = (joint_velocity, output_velocity, expand_velocity, reduce_velocity)
    carried = tuple(
        (MOMENTUM * before + gradient * factor for before, gradient in zip(previous, matrix_total))
    )
    lows = [moment.astype(jnp.bfloat16) for moment in carried]
    rests, inverses = muon_factors(lows)
    updated = []
    for number, (master, moment) in enumerate(zip(masters, carried)):
        orth = moment * (NS_A**NS_STEPS * inverses[number]) + plain(
            lows[number], rests[number]
        )
        shape_factor = math.sqrt(max(1.0, master.shape[0] * groups / master.shape[1]))
        updated.append(master * (1 - MUON_RATE * DECAY) - MUON_RATE * shape_factor * orth)
    table_out = adam_step(
        embedding, embed_moment, embed_square, table_sum * factor, EMBED_RATE, DECAY
    )
    place_out = adam_step(
        positions, position_moment, position_square, position_grad * factor, PLACE_RATE, DECAY
    )
    gain_out = adam_step(norm_gains, gain_moment, gain_square, gain_grad * factor, SMALL_RATE, 0.0)
    bias_out = adam_step(biases, bias_moment, bias_square, bias_grad * factor, SMALL_RATE, 0.0)
    return (
        loss_sum,
        loss_count,
        grad_norm,
        updated[0],
        updated[1],
        updated[2],
        updated[3],
        carried[0],
        carried[1],
        carried[2],
        carried[3],
        table_out[0],
        table_out[1],
        table_out[2],
        place_out[0],
        place_out[1],
        place_out[2],
        gain_out[0],
        gain_out[1],
        gain_out[2],
        bias_out[0],
        bias_out[1],
        bias_out[2],
    )


def solution(mesh):
    in_specs = (
        P(("wide", "narrow"), None),
        P(("wide", "narrow"), None),
        P("narrow", None),
        P("narrow", None),
        P("narrow", None),
        P("narrow", None),
        P("narrow", None),
        P("narrow", None),
        P("narrow", None),
        P("narrow", None),
        P(("wide", "narrow"), None),
        P(("wide", "narrow"), None),
        P(("wide", "narrow"), None),
        P(),
        P(),
        P(),
        P(),
        P(),
        P(),
        P(),
        P(),
        P(),
    )
    out_specs = (
        P(),
        P(),
        P(),
        P("narrow", None),
        P("narrow", None),
        P("narrow", None),
        P("narrow", None),
        P("narrow", None),
        P("narrow", None),
        P("narrow", None),
        P("narrow", None),
        P(("wide", "narrow"), None),
        P(("wide", "narrow"), None),
        P(("wide", "narrow"), None),
        P(),
        P(),
        P(),
        P(),
        P(),
        P(),
        P(),
        P(),
        P(),
    )
    return jax.shard_map(
        on_device, mesh=mesh, in_specs=in_specs, out_specs=out_specs, check_vma=False
    )
```

```python
import functools
import math

import jax
import jax.numpy as jnp
from jax import lax
from jax.experimental import pallas as pl
from jax.experimental.pallas import tpu as pltpu
from jax.sharding import PartitionSpec as P

HEADS = 12
HEAD = 64
LENGTH = 64
NS_STEPS = 3
STEP = 10


HIGH = lax.Precision.HIGHEST
EPS = 1e-05
CLIP = 0.05
MOMENTUM = 0.95
MUON_RATE = 0.5
DECAY = 0.1
BETA_ONE = 0.9
BETA_TWO = 0.999
EMBED_RATE = 0.02
PLACE_RATE = 0.1
SMALL_RATE = 0.2
NS_A = 3.4445
NS_B = -4.775
NS_C = 2.0315
MESH = pl.DeviceIdType.MESH
MIB = 1 << 20
TOKEN_TILE = 256


def times_t(left, right):
    return lax.dot_general(
        left, right, (((1,), (1,)), ((), ())), preferred_element_type=jnp.float32
    )


def outer_sum(left, right):
    return lax.dot_general(
        left, right, (((0,), (0,)), ((), ())), preferred_element_type=jnp.float32
    )


def plain(left, right):
    return jnp.dot(left, right, preferred_element_type=jnp.float32)


def norm_forward(stream, gain, shift):
    centred = stream - jnp.mean(stream, -1, keepdims=True)
    inverse = lax.rsqrt(jnp.mean(centred * centred, -1, keepdims=True) + EPS)
    normed = centred * inverse
    return (normed * gain + shift, normed, inverse)


def norm_backward(upstream, normed, inverse, gain):
    scaled = upstream * gain
    inner = inverse * (
        scaled
        - jnp.mean(scaled, -1, keepdims=True)
        - normed * jnp.mean(scaled * normed, -1, keepdims=True)
    )
    return (
        inner,
        jnp.sum(upstream * normed, 0, keepdims=True),
        jnp.sum(upstream, 0, keepdims=True),
    )


def gelu_tanh(values):
    return jax.nn.gelu(values, approximate=True)


def column_sum(values):
    return jnp.sum(values.astype(jnp.float32), 0, keepdims=True)


def pair_masks(tokens):
    first = lax.broadcasted_iota(jnp.int32, (tokens, 2 * HEAD), 1) < HEAD
    row = lax.broadcasted_iota(jnp.int32, (tokens, tokens), 0)
    column = lax.broadcasted_iota(jnp.int32, (tokens, tokens), 1)
    return first, (row // LENGTH == column // LENGTH) & (column <= row)


def head_probs(queries, key_heads, seen):
    scores = times_t(queries, key_heads) * HEAD ** (-0.5)
    scores = jnp.where(seen, scores, -1000000000.0)
    powers = jnp.exp(scores - jnp.max(scores, -1, keepdims=True))
    return powers * (1.0 / jnp.sum(powers, -1, keepdims=True))


def forward_kernel(
    x_ref,
    place_ref,
    gain_ref,
    bias_ref,
    joint_hbm,
    output_hbm,
    expand_hbm,
    reduce_hbm,
    low_ref,
    normed_ref,
    inverse_ref,
    joint_out,
    context_ref,
    upward_ref,
    joint_ref,
    output_ref,
    expand_ref,
    reduce_ref,
    load_sem,
):
    pairs = ((joint_hbm, joint_ref), (output_hbm, output_ref), (expand_hbm, expand_ref), (reduce_hbm, reduce_ref))
    loads = [
        pltpu.make_async_copy(source, target, load_sem.at[number])
        for number, (source, target) in enumerate(pairs)
    ]
    for load in loads:
        load.start()
    tokens, width = x_ref.shape

    def norm(number, stream):
        result, normed, inverse = norm_forward(
            stream, gain_ref[number : number + 1, :], bias_ref[number : number + 1, :]
        )
        normed_ref[number] = normed
        inverse_ref[number] = jnp.broadcast_to(inverse, (tokens, 128))
        return result.astype(jnp.bfloat16)

    stream = x_ref[...] + jnp.concatenate([place_ref[...]] * (tokens // LENGTH), 0)
    first_low = norm(0, stream)
    loads[0].wait()
    for part in range(3):
        span = pl.ds(part * width, width)
        result = times_t(first_low, joint_ref[span, :])
        if part != 1:
            row = 3 if part == 0 else 4
            result = result + bias_ref[row : row + 1, :]
        joint_out[:, span] = result.astype(jnp.bfloat16)
    first, seen = pair_masks(tokens)
    zero = jnp.zeros((), jnp.bfloat16)
    for pair in range(HEADS // 2):
        queries = joint_out[:, pl.ds(pair * 128, 128)]
        key_heads = joint_out[:, pl.ds(width + pair * 128, 128)]
        values = joint_out[:, pl.ds(2 * width + pair * 128, 128)]
        parts = []
        for mine in (first, ~first):
            probs = head_probs(jnp.where(mine, queries, zero), key_heads, seen)
            parts.append(plain(probs.astype(jnp.bfloat16), values))
        context_ref[:, pl.ds(pair * 128, 128)] = jnp.where(first, *parts).astype(jnp.bfloat16)
    loads[1].wait()
    stream = stream + times_t(context_ref[...], output_ref[...]) + bias_ref[5:6, :]
    second_low = norm(1, stream)
    stream = stream + bias_ref[6:7, :]
    loads[2].wait()
    loads[3].wait()
    for part in range(expand_ref.shape[0] // width):
        span = pl.ds(part * width, width)
        upward = times_t(second_low, expand_ref[span, :]) + bias_ref[7 + part : 8 + part, :]
        upward_ref[:, span] = upward
        stream = stream + plain(gelu_tanh(upward).astype(jnp.bfloat16), reduce_ref[span, :])
    low_ref[...] = norm(2, stream)


def layer_forward(embedded, positions, norm_gains, bias_rows, weights):
    tokens, width = embedded.shape
    vmem, any_space = pl.BlockSpec(memory_space=pltpu.VMEM), pl.BlockSpec(memory_space=pl.ANY)
    shape = jax.ShapeDtypeStruct
    hidden = weights[2].shape[0]
    return pl.pallas_call(
        forward_kernel,
        out_shape=(
            shape((tokens, width), jnp.bfloat16),
            shape((3, tokens, width), jnp.float32),
            shape((3, tokens, 128), jnp.float32),
            shape((tokens, 3 * width), jnp.bfloat16),
            shape((tokens, width), jnp.bfloat16),
            shape((tokens, hidden), jnp.float32),
        ),
        in_specs=[vmem] * 4 + [any_space] * 4,
        out_specs=[vmem] * 6,
        scratch_shapes=[pltpu.VMEM(w.shape, w.dtype) for w in weights]
        + [pltpu.SemaphoreType.DMA((4,))],
        compiler_params=pltpu.CompilerParams(vmem_limit_bytes=63 * MIB),
        name="layer_forward",
    )(embedded, positions, norm_gains, bias_rows, *weights)


def gelu_slope(values):
    inner = math.sqrt(2.0 / math.pi)
    squared = values * values
    bent = jnp.tanh(inner * (values + 0.044715 * squared * values))
    return 0.5 * values * (1.0 + bent), 0.5 * (1.0 + bent) + 0.5 * values * (
        1.0 - bent * bent
    ) * (inner * (1.0 + 3 * 0.044715 * squared))


def backward_flow(ins, outs, scratch):
    (final_ref, gain_ref, bias_ref, normed_ref, inverse_ref, joint_in, context_ref, upward_ref) = ins
    (stream_ref, small_ref, front_ref, expand_out, reduce_out) = outs
    (joint_ref, output_ref, expand_ref, reduce_ref, waits) = scratch
    hold = reduce_ref
    tokens, width = final_ref.shape
    _, ups, height, _ = front_ref.shape
    groups = 2 * ups

    def put(ref, start, grad):
        for group in range(groups):
            low = max(group * height, start)
            high = min((group + 1) * height, start + grad.shape[0])
            if low < high:
                ref[group % 2, group // 2, pl.ds(low - group * height, high - low), :] = grad[
                    low - start : high - start
                ]

    def gain(number):
        return gain_ref[number : number + 1, :]

    def normed_low(number):
        return (normed_ref[number] * gain(number) + bias_ref[number : number + 1, :]).astype(
            jnp.bfloat16
        )

    def back(number, upstream):
        inner, gain_row, shift_row = norm_backward(
            upstream, normed_ref[number], inverse_ref[number][:, :1], gain(number)
        )
        small_ref[number : number + 1, :] = gain_row
        small_ref[3 + number : 4 + number, :] = shift_row
        return inner

    small_ref[...] = jnp.zeros_like(small_ref)
    back_f = back(2, final_ref[...])
    down = back_f.astype(jnp.bfloat16)
    small_ref[9:10, :] = column_sum(down)
    second_low = normed_low(1)
    second_grad = jnp.zeros((tokens, width), jnp.float32)
    waits[2].wait()
    waits[3].wait()
    for part in range(expand_ref.shape[0] // width):
        span = pl.ds(part * width, width)
        active, slope = gelu_slope(upward_ref[:, span])
        upward_grad = (times_t(down, reduce_ref[span, :]) * slope).astype(jnp.bfloat16)
        small_ref[10 + part : 11 + part, :] = column_sum(upward_grad)
        second_grad = second_grad + plain(upward_grad, expand_ref[span, :])
        put(expand_out, part * width, outer_sum(upward_grad, second_low).astype(jnp.bfloat16))
        put(reduce_out, part * width, outer_sum(active.astype(jnp.bfloat16), down).astype(jnp.bfloat16))
    yield 0.0
    mid_grad = back_f + back(1, second_grad)
    stream_ref[...] = mid_grad
    attn_grad = mid_grad.astype(jnp.bfloat16)
    small_ref[8:9, :] = column_sum(attn_grad)
    waits[1].wait()
    last = pl.ds(3 * tokens, tokens)
    hold[last, :] = plain(attn_grad, output_ref[...]).astype(jnp.bfloat16)
    output_grad = outer_sum(attn_grad, context_ref[...]).astype(jnp.bfloat16)
    rows = width // groups
    joint_rows = height - rows
    for group in range(groups):
        front_ref[group % 2, group // 2, pl.ds(joint_rows, rows), :] = output_grad[
            group * rows : (group + 1) * rows
        ]
    yield 2.0
    first, seen = pair_masks(tokens)
    zero = jnp.zeros((), jnp.bfloat16)
    for pair in range(HEADS // 2):
        spans = [pl.ds(part * width + pair * 128, 128) for part in range(3)]
        queries, key_heads, values = (joint_in[:, span] for span in spans)
        upstream = hold[last, spans[0]]
        parts = []
        for mine in (first, ~first):
            probs = head_probs(jnp.where(mine, queries, zero), key_heads, seen)
            probs_grad = times_t(jnp.where(mine, upstream, zero), values)
            score_grad = (
                probs * (probs_grad - jnp.sum(probs * probs_grad, -1, keepdims=True))
            ).astype(jnp.bfloat16)
            parts.append(
                (
                    plain(score_grad, key_heads) * HEAD ** (-0.5),
                    outer_sum(score_grad, queries) * HEAD ** (-0.5),
                    outer_sum(probs.astype(jnp.bfloat16), upstream),
                )
            )
        for part, (one, two) in enumerate(zip(*parts)):
            hold[pl.ds(part * tokens, tokens), spans[0]] = jnp.where(first, one, two).astype(
                jnp.bfloat16
            )
        yield 1.5
    first_low = normed_low(0)
    waits[0].wait()
    first_grad = jnp.zeros((tokens, width), jnp.float32)
    for part in range(3):
        span = pl.ds(part * width, width)
        piece = hold[pl.ds(part * tokens, tokens), :]
        if part != 1:
            row = 6 if part == 0 else 7
            small_ref[row : row + 1, :] = column_sum(piece)
        first_grad = first_grad + plain(piece, joint_ref[span, :])
        grad = outer_sum(piece, first_low).astype(jnp.bfloat16)
        for group in range(groups):
            start = max(group * joint_rows, part * width)
            end = min((group + 1) * joint_rows, (part + 1) * width)
            if start < end:
                front_ref[
                    group % 2, group // 2, pl.ds(start - group * joint_rows, end - start), :
                ] = grad[start - part * width : end - part * width]
        yield 1.5
    stream = stream_ref[...] + back(0, first_grad)
    stream_ref[...] = stream
    placed = stream[:LENGTH]
    for sequence in range(1, tokens // LENGTH):
        placed = placed + stream[sequence * LENGTH : (sequence + 1) * LENGTH]
    small_ref[14 : 14 + LENGTH, :] = placed


def adam_step(weight, moment, square, gradient, rate, decay):
    moment = BETA_ONE * moment + (1 - BETA_ONE) * gradient
    square = BETA_TWO * square + (1 - BETA_TWO) * gradient * gradient
    unbiased = moment / (1 - BETA_ONE**STEP)
    spread = square / (1 - BETA_TWO**STEP)
    return (
        weight - rate * (unbiased / (jnp.sqrt(spread) + 1e-08) + decay * weight),
        moment,
        square,
    )


def log_two(size):
    return size.bit_length() - 1


def lanes():
    wide, narrow = lax.axis_size("wide"), lax.axis_size("narrow")
    across = wide // 4
    x_bits = [("wide", 1 << i) for i in range(log_two(across))]
    z_bits = [("wide", across << i) for i in range(log_two(wide // across))]
    y_bits = [("narrow", 2 << i) for i in range(log_two(narrow // 2))]
    return ("narrow", 1), x_bits, y_bits, z_bits


def swap(array, bit):
    axis, mask = bit
    return lax.ppermute(array, axis, [(i, i ^ mask) for i in range(lax.axis_size(axis))])


def side(bit):
    axis, mask = bit
    return (lax.axis_index(axis) // mask) % 2


def join(mine, other, bit, dim=0):
    own = side(bit)
    return jnp.where(
        own == 0, jnp.concatenate([mine, other], dim), jnp.concatenate([other, mine], dim)
    )


def halves(array, bit):
    own = side(bit)
    half = array.shape[0] // 2
    keep = lax.dynamic_slice_in_dim(array, own * half, half)
    send = lax.dynamic_slice_in_dim(array, (1 - own) * half, half)
    return keep, send


def group_bits():
    _, _, y_bits, z_bits = lanes()
    return z_bits + y_bits


SPREAD_ORDERS = ("nyf", "fny", "nfy", "fyn")
COLLECT_ORDERS = ("yfn", "ynf", "nyf", "fyn")


def routes(rows, orders):
    _, _, y_bits, z_bits = lanes()
    kinds = {"y": y_bits, "n": z_bits[:1], "f": z_bits[1:]}
    size = rows // len(orders)
    return [
        (number * size, size, [bit for kind in order for bit in kinds[kind]])
        for number, order in enumerate(orders)
    ]


def flat_mask(bit):
    axis, mask = bit
    return mask * lax.axis_size("narrow") if axis == "wide" else mask


def group_masks():
    masks = [0]
    for bit in group_bits():
        masks = masks + [other ^ flat_mask(bit) for other in masks]
    return masks


def neighbour(bit):
    axis, mask = bit
    wide, narrow = lax.axis_index("wide"), lax.axis_index("narrow")
    if axis == "wide":
        return wide + mask * (1 - 2 * ((wide // mask) % 2)), narrow
    return wide, narrow + mask * (1 - 2 * ((narrow // mask) % 2))


def greet(devices):
    barrier = pltpu.get_barrier_semaphore()
    for device in devices:
        pl.semaphore_signal(barrier, inc=1, device_id=device, device_id_type=MESH)
    pl.semaphore_wait(barrier, len(devices))


class Mail:
    def __init__(self, send_sem, recv_sem, lane_bits):
        core, x_bits, y_bits, z_bits = lane_bits
        self.send_sem, self.recv_sem = send_sem, recv_sem
        self.used, self.sent, self.open = 0, [], []
        self.links = {core: (("core", 1 / 600e3),)}
        self.links.update({bit: (("x", 2 / 91e3),) for bit in x_bits})
        self.links.update({bit: (("y", 2 / 91e3),) for bit in y_bits})
        self.links.update({bit: (("z", 2 / 91e3),) for bit in z_bits[:1]})
        self.links.update({bit: (("z", 2 / 91e3), ("far", 4 / 91e3)) for bit in z_bits[1:]})
        self.free, self.now, self.ready = {}, 0.0, []

    def expect(self, source, bit):
        size = math.prod(source.shape) * source.dtype.itemsize
        due = self.now
        for link, rate in self.links[bit]:
            self.free[link] = max(self.free.get(link, 0.0), self.now) + size * rate
            due = max(due, self.free[link])
        return due + 3.5

    def post(self, source, target, bit):
        copy = pltpu.make_async_remote_copy(
            src_ref=source,
            dst_ref=target,
            send_sem=self.send_sem.at[self.used],
            recv_sem=self.recv_sem.at[self.used],
            device_id=neighbour(bit),
            device_id_type=MESH,
        )
        copy.start()
        self.due = self.expect(source, bit)
        self.used += 1
        self.sent.append(copy)
        self.open.append(copy)
        return copy

    def keep(self, source, target):
        copy = pltpu.make_async_copy(source, target, self.recv_sem.at[self.used])
        copy.start()
        self.used += 1
        self.open.append(copy)
        return copy

    def take(self, copy):
        if any(other is copy for other in self.open):
            self.open = [other for other in self.open if other is not copy]
            if any(other is copy for other in self.sent):
                copy.wait_recv()
            else:
                copy.wait()

    def spend(self, time):
        self.now += time
        return self.now

    def run(self, flows):
        waiting = [(next(flow, None), flow) for flow in flows]
        while True:
            waiting += [(next(flow, None), flow) for flow in self.ready]
            self.ready = []
            waiting = [entry for entry in waiting if entry[0] is not None]
            if not waiting:
                return
            place = min(range(len(waiting)), key=lambda i: waiting[i][0])
            due, flow = waiting.pop(place)
            self.now = max(self.now, due) + 0.4
            waiting.append((next(flow, None), flow))

    def close(self):
        for copy in list(self.open):
            self.take(copy)
        for copy in self.sent:
            copy.wait_send()


def mail_sems(count):
    return [pltpu.SemaphoreType.DMA((count,)), pltpu.SemaphoreType.DMA((count,))]


def spread_flow(mail, bits, part, x_ref, out_ref):
    first, rows, order = part
    span = pl.ds(first, rows)
    held = {0: None}
    for bit in order:
        step = 1 << bits.index(bit)
        for block in list(held):
            if block:
                mail.take(held[block])
            source = out_ref.at[block, span] if block else x_ref.at[span]
            held[block ^ step] = mail.post(source, out_ref.at[block ^ step, span], bit)
        yield mail.due


def spread_kernel(lane_bits, plan, x_ref, out_ref, send_sem, recv_sem):
    bits = lane_bits[3] + lane_bits[2]
    greet([neighbour(bit) for bit in bits])
    mail = Mail(send_sem, recv_sem, lane_bits)
    mail.run([spread_flow(mail, bits, part, x_ref, out_ref) for part in plan])
    mail.keep(x_ref, out_ref.at[0])
    mail.close()


def spread(array):
    bits, plan = group_bits(), routes(array.shape[0], SPREAD_ORDERS)
    count = 1 << len(bits)
    return pl.pallas_call(
        functools.partial(spread_kernel, lanes(), plan),
        out_shape=jax.ShapeDtypeStruct((count,) + array.shape, array.dtype),
        in_specs=[pl.BlockSpec(memory_space=pltpu.VMEM)],
        out_specs=pl.BlockSpec(memory_space=pl.ANY),
        scratch_shapes=mail_sems(len(plan) * count),
        compiler_params=pltpu.CompilerParams(
            collective_id=4, has_side_effects=True, vmem_limit_bytes=62 * MIB
        ),
        name="rows_spread",
    )(array)


def collect_flow(mail, bits, part, refs):
    first, rows, order = part
    x_ref, out_ref, sum_ref, got_ref = refs
    span = pl.ds(first, rows)
    held = list(range(1 << len(bits)))
    for stage, bit in enumerate(order):
        step = 1 << bits.index(bit)
        source = sum_ref if stage else x_ref
        held = [block for block in held if not block & step]
        base = (1 << len(bits)) - 2 * len(held)
        copies = [
            mail.post(source.at[block ^ step, span], got_ref.at[base + place, span], bit)
            for place, block in enumerate(held)
        ]
        yield mail.due
        for place, (block, copy) in enumerate(zip(held, copies)):
            mail.take(copy)
            total = source[block, span, :].astype(jnp.float32) + got_ref[
                base + place, span, :
            ].astype(jnp.float32)
            if stage == len(bits) - 1:
                out_ref[span, :] = total
            else:
                sum_ref[block, span, :] = total.astype(jnp.bfloat16)


def head_back_kernel(lane_bits, plan, tile, x_ref, *refs):
    core, _, y_bits, z_bits = lane_bits
    bits = z_bits + y_bits
    if tile:
        slope_ref, rows_ref, out_ref, keep_ref, pass_ref = refs[:5]
        sum_ref, got_ref, send_sem, recv_sem = refs[5:9]
        loads, sent_ref, other_ref, load_sem = refs[9:]
        half = sent_ref.shape[0]
        count = half // tile
        order = [count + i for i in range(count)] + [count - 1 - i for i in range(count)]

        def load(number):
            return pltpu.make_async_copy(
                slope_ref.at[:, pl.ds(order[number] * tile, tile)],
                loads.at[number % 2],
                load_sem.at[number % 2],
            )

        load(0).start()
        greet([neighbour(bit) for bit in bits + [core]])
    else:
        out_ref, sum_ref, got_ref, send_sem, recv_sem = refs
        greet([neighbour(bit) for bit in bits])
    mail = Mail(send_sem, recv_sem, lane_bits)
    flows = [
        collect_flow(mail, bits, part, (x_ref, out_ref, sum_ref, got_ref)) for part in plan
    ]
    if tile:

        def table_flow():
            arrivals = {}
            border = keep_ref.shape[0]
            for number, block in enumerate(order):
                if number + 1 < len(order):
                    load(number + 1).start()
                load(number).wait()
                grad = lax.dot_general(
                    loads[number % 2],
                    rows_ref[...],
                    (((0,), (0,)), ((), ())),
                    preferred_element_type=jnp.float32,
                )
                start = block * tile % half
                span = pl.ds(start, tile)
                if block >= count:
                    sent_ref[span, :] = grad.astype(jnp.bfloat16)
                    arrivals[start] = mail.post(sent_ref.at[span], other_ref.at[span], core)
                else:
                    mail.take(arrivals[start])
                    grad = grad + other_ref[span, :].astype(jnp.float32)
                    lower = min(max(border - start, 0), tile)
                    if lower:
                        keep_ref[pl.ds(start, lower), :] = grad[:lower]
                    if lower < tile:
                        pass_ref[pl.ds(start + lower - border, tile - lower), :] = grad[
                            lower:
                        ].astype(jnp.bfloat16)
                yield mail.spend(2.7)

        flows.append(table_flow())
    mail.run(flows)
    mail.close()


def head_back(array, slopes, group_rows):
    lane_bits = lanes()
    bits, plan = group_bits(), routes(array.shape[1], COLLECT_ORDERS)
    count, rows, width = array.shape
    vocab = slopes.shape[1]
    half = vocab // 2
    tile = 640 if half % 640 == 0 else 0
    vmem = pl.BlockSpec(memory_space=pltpu.VMEM)
    shapes = [jax.ShapeDtypeStruct((rows, width), jnp.float32)]
    scratch = [
        pltpu.VMEM((count, rows, width), jnp.bfloat16),
        pltpu.VMEM((count - 1, rows, width), jnp.bfloat16),
    ] + mail_sems(len(plan) * count + (half // tile if tile else 0))
    operands, specs = [array], [vmem]
    if tile:
        shapes += [
            jax.ShapeDtypeStruct((half // 2, width), jnp.float32),
            jax.ShapeDtypeStruct((half // 2, width), jnp.bfloat16),
        ]
        scratch += [
            pltpu.VMEM((2, slopes.shape[0], tile), jnp.bfloat16),
            pltpu.VMEM((half, width), jnp.bfloat16),
            pltpu.VMEM((half, width), jnp.bfloat16),
            pltpu.SemaphoreType.DMA((2,)),
        ]
        operands += [slopes, group_rows]
        specs += [pl.BlockSpec(memory_space=pl.ANY), vmem]
    outs = pl.pallas_call(
        functools.partial(head_back_kernel, lane_bits, plan, tile),
        out_shape=shapes,
        in_specs=specs,
        out_specs=[vmem] * len(shapes),
        scratch_shapes=scratch,
        compiler_params=pltpu.CompilerParams(
            collective_id=5, has_side_effects=True, vmem_limit_bytes=56 * MIB
        ),
        name="head_back",
    )(*operands)
    if tile:
        return outs
    core = lane_bits[0]
    other = swap(outer_sum(slopes[:, half:], group_rows).astype(jnp.bfloat16), core)
    table_sum = outer_sum(slopes[:, :half], group_rows) + other.astype(jnp.float32)
    return outs[0], table_sum[: half // 2], table_sum[half // 2 :].astype(jnp.bfloat16)


def chip_sizes():
    wides, groups = lax.axis_size("wide"), lax.axis_size("narrow")
    return wides, groups // 2


class Rows:
    def __init__(self, sizes, x_ref, out_ref, send_sem, recv_sem):
        self.sizes, self.x_ref, self.out_ref = sizes, x_ref, out_ref
        self.send_sem, self.recv_sem = send_sem, recv_sem
        self.count = sizes[0] * sizes[1]
        self.place = Place(sizes[0], 2 * sizes[1])

    def peer(self, k):
        ups = self.sizes[1]
        return self.place.peer(k // ups, 2 * (k % ups))

    def each(self, step):
        for k in range(1, self.count):
            step(k)

    def copy(self, k):
        return pltpu.make_async_remote_copy(
            src_ref=self.x_ref.at[k],
            dst_ref=self.out_ref.at[k],
            send_sem=self.send_sem.at[k],
            recv_sem=self.recv_sem.at[k],
            device_id=self.peer(k),
            device_id_type=MESH,
        )

    def greet(self, others):
        self.call(others)
        self.meet(others)

    def call(self, others):
        barrier = pltpu.get_barrier_semaphore()
        self.each(
            lambda k: pl.semaphore_signal(
                barrier, inc=1, device_id=self.peer(k), device_id_type=MESH
            )
        )
        for device in others:
            pl.semaphore_signal(barrier, inc=1, device_id=device, device_id_type=MESH)

    def meet(self, others):
        pl.semaphore_wait(pltpu.get_barrier_semaphore(), self.count - 1 + len(others))

    def start(self):
        self.each(lambda k: self.copy(k).start())

    def own(self):
        return pltpu.make_async_copy(self.x_ref.at[0], self.out_ref.at[0], self.recv_sem.at[0])


def swap_rows_kernel(sizes, x_ref, out_ref, send_sem, recv_sem):
    rows = Rows(sizes, x_ref, out_ref, send_sem, recv_sem)
    rows.greet([])
    rows.start()
    own = rows.own()
    own.start()
    own.wait()
    rows.each(lambda k: rows.copy(k).wait())


def swap_rows(rows):
    sizes = chip_sizes()
    count = sizes[0] * sizes[1]
    return pl.pallas_call(
        functools.partial(swap_rows_kernel, sizes),
        out_shape=jax.ShapeDtypeStruct(rows.shape, rows.dtype),
        in_specs=[pl.BlockSpec(memory_space=pltpu.VMEM)],
        out_specs=pl.BlockSpec(memory_space=pl.ANY),
        scratch_shapes=mail_sems(count),
        compiler_params=pltpu.CompilerParams(collective_id=2, has_side_effects=True),
        name="token_rows",
    )(rows)


def load_kernel(sizes, lane_bits, *refs):
    core, x_bits, y_bits, z_bits = lane_bits
    near = z_bits[0]
    table_ref, weight_refs, rows_ref = refs[0], refs[1:5], refs[5]
    table_out, weight_outs, rows_out = refs[6], refs[7:11], refs[11]
    send_sem, recv_sem, rows_send, rows_recv, pass_send, pass_recv = refs[12:]
    wide, narrow = lax.axis_index("wide"), lax.axis_index("narrow")
    rows = Rows(sizes, rows_ref, rows_out.at[0], rows_send, rows_recv)
    rows.greet([neighbour(core)])
    mail = Mail(send_sem, recv_sem, lane_bits)
    side_near = (wide // near[1]) % 2

    def part(ref, number, half):
        count = ref.shape[1] // 2
        return ref.at[number, pl.ds(pl.multiple_of(half * count, 16), count)]

    def own_part(ref, half):
        count = ref.shape[0] // 2
        return ref.at[pl.ds(pl.multiple_of(half * count, 16), count)]

    tables = {0: mail.keep(table_ref, table_out.at[0, 0])}
    if x_bits:
        tables[1] = mail.post(table_ref, table_out.at[0, 1], x_bits[0])
    held = [0]
    first = []
    for ref, out in zip(weight_refs, weight_outs):
        if y_bits:
            first.append(
                mail.post(own_part(ref, side_near), part(out, narrow, side_near), y_bits[0])
            )
    rows.start()
    own_rows = rows.own()
    own_rows.start()
    mail.post(table_ref, table_out.at[1, 0], core)
    for ref, out in zip(weight_refs, weight_outs):
        mail.keep(ref, out.at[narrow])
        mail.post(ref, out.at[narrow], core)
    own_rows.wait()
    place = narrow
    blocks = [narrow]
    for level, bit in enumerate(y_bits):
        fresh = []
        arrivals = []
        for number, (ref, out) in enumerate(zip(weight_refs, weight_outs)):
            for spot, block in enumerate(blocks):
                other = block + bit[1] * (1 - 2 * ((block // bit[1]) % 2))
                if level == 0:
                    copy = first[number]
                else:
                    copy = mail.post(
                        part(out, block, side_near), part(out, block, side_near), bit
                    )
                arrivals.append((out, other, copy))
                if number == 0:
                    fresh.append(other)
        seconds = []
        for out, other, copy in arrivals:
            mail.take(copy)
            seconds.append(
                mail.post(part(out, other, side_near), part(out, other, side_near), near)
            )
            mail.post(part(out, other, side_near), part(out, other, side_near), core)
        for (out, other, _), copy in zip(arrivals, seconds):
            mail.take(copy)
            mail.post(part(out, other, 1 - side_near), part(out, other, 1 - side_near), core)
        blocks = blocks + fresh

    def hand(k):
        return pltpu.make_async_remote_copy(
            src_ref=rows_out.at[0, k],
            dst_ref=rows_out.at[1, k],
            send_sem=pass_send.at[k],
            recv_sem=pass_recv.at[k],
            device_id=neighbour(core),
            device_id_type=MESH,
        )

    hand(0).start()

    def forward(k):
        rows.copy(k).wait()
        hand(k).start()

    rows.each(forward)
    for level, bit in enumerate(x_bits):
        for block in range(1 << level):
            spot = block + (1 << level)
            if spot not in tables:
                tables[spot] = mail.post(table_out.at[0, block], table_out.at[0, spot], bit)
        for block in range(1 << level):
            spot = block + (1 << level)
            mail.take(tables[spot])
            mail.post(table_out.at[0, spot], table_out.at[1, spot], core)
    hand(0).wait()
    rows.each(lambda k: hand(k).wait())
    mail.close()


def load_all(table, weights, rows):
    lane_bits = lanes()
    sizes = chip_sizes()
    count = sizes[0] * sizes[1]
    groups = lax.axis_size("narrow")
    across = 1 << len(lane_bits[1])
    any_space = pl.BlockSpec(memory_space=pl.ANY)
    shapes = (
        [jax.ShapeDtypeStruct((2, across) + table.shape, table.dtype)]
        + [jax.ShapeDtypeStruct((groups,) + w.shape, w.dtype) for w in weights]
        + [jax.ShapeDtypeStruct((2,) + rows.shape, rows.dtype)]
    )
    table_all, *weights_all, rows_all = pl.pallas_call(
        functools.partial(load_kernel, sizes, lane_bits),
        out_shape=shapes,
        in_specs=[pl.BlockSpec(memory_space=pltpu.VMEM)] * 6,
        out_specs=[any_space] * 6,
        scratch_shapes=mail_sems(8 * 2 * groups + 2 * across + 4)
        + mail_sems(count)
        + mail_sems(count),
        compiler_params=pltpu.CompilerParams(
            collective_id=6, has_side_effects=True, vmem_limit_bytes=62 * MIB
        ),
        name="load_rows",
    )(table, *weights, rows)
    model = table.shape[1]
    return (
        table_all.reshape(-1, model),
        tuple(w.reshape(-1, model) for w in weights_all),
        rows_all,
    )


def tile_of(rows):
    return next(size for size in (128, 96, 64, 48, 32, 16) if rows % size == 0)


def back_reduce_kernel(sizes, lane_bits, kinds, *refs):
    core, x_bits, y_bits, z_bits = lane_bits
    ins, wanted_ref, hbm = refs[:8], refs[8], refs[9:13]
    out_refs, small_out, rows_out, square_out, low_out = refs[13:16], *refs[16:20]
    scratch = refs[20:]
    weights, load_sem, stream_ref, small_ref = scratch[:4], scratch[4], scratch[5], small_out
    grad_refs = scratch[6:9]
    both_ref, core_got = scratch[9:11]
    small_sum, small_got, send_sem, recv_sem, rows_send, rows_recv = scratch[11:17]
    rest = scratch[17:]
    got_refs = []
    for _, _, _, path in kinds:
        got_refs.append(rest[: len(path) + 1])
        rest = rest[len(path) + 1 :]
    waits = [
        pltpu.make_async_copy(source, target, load_sem.at[number])
        for number, (source, target) in enumerate(zip(hbm, weights))
    ]
    for load in waits:
        load.start()
    place = {"wide": lax.axis_index("wide"), "narrow": lax.axis_index("narrow")}
    rows = Rows(sizes, both_ref.at[0], rows_out, rows_send, rows_recv)
    rows.call([neighbour(core)])
    mail = Mail(send_sem, recv_sem, lane_bits)
    ups = grad_refs[0].shape[1]
    own = place["narrow"] % 2
    square_out[...] = jnp.zeros_like(square_out)

    def side_of(bit):
        return (place[bit[0]] // bit[1]) % 2

    def add(total_ref, got_ref, box):
        up, ups_here, first, height = box
        tile = tile_of(height)

        def step(i, carry):
            at = i // (height // tile)
            down = (i % (height // tile)) * tile
            span = pl.ds(pl.multiple_of(first + down, 16), tile)
            got = got_ref[at, pl.ds(pl.multiple_of(down, 16), tile), :]
            total = total_ref[own, up + at, span, :].astype(jnp.float32) + got.astype(jnp.float32)
            total_ref[own, up + at, span, :] = total.astype(jnp.bfloat16)
            return carry

        lax.fori_loop(0, ups_here * (height // tile), step, 0)

    def view(ref, box):
        up, ups_here, first, height = box
        return ref.at[own, pl.ds(up, ups_here), pl.ds(pl.multiple_of(first, 16), height)]

    def flow(number):
        which, offset, height, path = kinds[number]
        total_ref, got, out_ref = grad_refs[which], got_refs[number], out_refs[which]
        span = pl.ds(offset, height)
        copy = mail.post(total_ref.at[1 - own, :, span], got[0], core)
        yield mail.due
        mail.take(copy)
        box = (0, ups, offset, height)
        add(total_ref, got[0], box)
        for stage, (bit, halve) in enumerate(path):
            up, ups_here, first, height = box
            side = side_of(bit)
            if bit[0] == "narrow":
                half = ups_here // 2
                mine = (up + side * half, half, first, height)
                theirs = (up + (1 - side) * half, half, first, height)
            elif halve:
                half = height // 2
                mine = (up, ups_here, first + side * half, half)
                theirs = (up, ups_here, first + (1 - side) * half, half)
            else:
                mine = theirs = box
            copy = mail.post(view(total_ref, theirs), got[stage + 1], bit)
            yield mail.due
            mail.take(copy)
            if not halve:
                copy.wait_send()
                mail.sent = [other for other in mail.sent if other is not copy]
            box = mine
            add(total_ref, got[stage + 1], box)
        up, _, first, height = box
        piece = total_ref[own, up, pl.ds(pl.multiple_of(first, 16), height), :]
        out_ref[pl.ds(pl.multiple_of(first, 16), height), :] = piece
        full = piece.astype(jnp.float32)
        square_out[...] += jnp.sum((full * full).reshape(height // 8, 8, -1), 0)
        for bit, halve in reversed(path):
            if bit[0] == "wide" and halve:
                span = pl.ds(pl.multiple_of(first, 16), height)
                copy = mail.post(out_ref.at[span], out_ref.at[span], bit)
                yield mail.due
                mail.take(copy)
                first = first - side_of(bit) * height
                height = 2 * height

    def small_flow():
        bits = [core] + x_bits + y_bits + z_bits
        small_sum[0] = small_ref[...].astype(jnp.bfloat16)
        for stage, bit in enumerate(bits):
            copy = mail.post(small_sum.at[stage], small_got.at[stage], bit)
            yield mail.due
            mail.take(copy)
            total = small_sum[stage].astype(jnp.float32) + small_got[stage].astype(jnp.float32)
            if stage == len(bits) - 1:
                small_out[...] = total
            else:
                small_sum[stage + 1] = total.astype(jnp.bfloat16)

    def rows_flow():
        low = stream_ref[...].astype(jnp.bfloat16)
        low_out[...] = low
        both = outer_sum(wanted_ref[...], low).astype(jnp.bfloat16)
        both_ref[...] = both.reshape(both_ref.shape)
        copy = mail.post(both_ref.at[1], core_got, core)
        yield mail.due
        mail.take(copy)
        summed = both_ref[0].astype(jnp.float32) + core_got[...].astype(jnp.float32)
        both_ref[0] = summed.astype(jnp.bfloat16)
        rows.start()
        own_rows = rows.own()
        own_rows.start()
        yield mail.due
        own_rows.wait()

    back = backward_flow(
        ins,
        (stream_ref, small_ref) + tuple(grad_refs),
        (*weights, waits),
    )
    next(back)
    rows.meet([neighbour(core)])

    def back_flow():
        for cost in back:
            yield mail.spend(cost)
        mail.ready += [flow(number) for number in range(4, len(kinds))]
        mail.ready += [rows_flow(), small_flow()]

    mail.run([flow(number) for number in range(4)] + [back_flow()])
    rows.each(lambda k: rows.copy(k).wait())
    mail.close()


def back_reduce(final_grad, norm_gains, bias_rows, saved, weights, wanted):
    lane_bits = lanes()
    core, x_bits, y_bits, z_bits = lane_bits
    sizes = chip_sizes()
    tokens, width = final_grad.shape
    ups = sizes[1]
    height = 4 * width // (2 * ups)
    half = height // 2
    bits = {"x": x_bits, "y": y_bits[::-1], "z": z_bits[:1], "f": z_bits[1:]}
    kinds, got_shapes = [], []
    for which, offset, order in (
        (1, 0, "yzfx"),
        (2, 0, "yxzf"),
        (1, half, "yzxf"),
        (2, half, "zyxf"),
        (0, 0, "yxfz"),
        (0, half, "yxzf"),
    ):
        path, ups_here, height_here = [], ups, half
        shapes = [(ups_here, height_here, width)]
        for bit in [bit for kind in order for bit in bits[kind]]:
            halve = True
            if bit[0] == "narrow":
                ups_here //= 2
            else:
                halve = (height_here // 2) % 16 == 0
                height_here = height_here // 2 if halve else height_here
            path.append((bit, halve))
            shapes.append((ups_here, height_here, width))
        kinds.append((which, offset, half, path))
        got_shapes += shapes
    count = sizes[0] * sizes[1]
    steps = 1 + len(kinds[0][3])
    small_rows = 14 + LENGTH
    small = (small_rows + -small_rows % 16, width)
    row_shape = (count, slots(), width)
    vmem, any_space = pl.BlockSpec(memory_space=pltpu.VMEM), pl.BlockSpec(memory_space=pl.ANY)
    shape, low = jax.ShapeDtypeStruct, jnp.bfloat16
    outs = pl.pallas_call(
        functools.partial(back_reduce_kernel, sizes, lane_bits, kinds),
        out_shape=[shape((height, width), low)] * 3
        + [
            shape(small, jnp.float32),
            shape(row_shape, low),
            shape((8, width), jnp.float32),
            shape((tokens, width), low),
        ],
        in_specs=[vmem] * 9 + [any_space] * 4,
        out_specs=[vmem] * 4 + [any_space, vmem, vmem],
        scratch_shapes=[pltpu.VMEM(w.shape, w.dtype) for w in weights]
        + [
            pltpu.SemaphoreType.DMA((4,)),
            pltpu.VMEM((tokens, width), jnp.float32),
        ]
        + [pltpu.VMEM((2, ups, height, width), low) for _ in range(3)]
        + [pltpu.VMEM((2,) + row_shape, low), pltpu.VMEM(row_shape, low)]
        + [pltpu.VMEM((steps,) + small, low), pltpu.VMEM((steps,) + small, low)]
        + mail_sems(len(kinds) * 2 * steps + steps + 1)
        + mail_sems(count)
        + [pltpu.VMEM(one, low) for one in got_shapes],
        compiler_params=pltpu.CompilerParams(
            collective_id=7, has_side_effects=True, vmem_limit_bytes=63 * MIB
        ),
        name="back_reduce",
    )(final_grad, norm_gains, bias_rows, *saved, wanted, *weights)
    repeats = 1
    for bit, halve in kinds[0][3]:
        repeats *= 1 if halve else 2
    return outs[:3], outs[3], outs[4], outs[5] / repeats, outs[6]


class Place:
    def __init__(self, wides, groups):
        self.wide, self.narrow = lax.axis_index("wide"), lax.axis_index("narrow")
        self.wide_steps = self.steps(self.wide, wides)
        self.narrow_steps = self.steps(self.narrow, groups)

    def steps(self, place, size):
        masks = [1 << bit for bit in range(log_two(size))]
        return {mask: mask * (1 - 2 * ((place // mask) % 2)) for mask in masks}

    def peer(self, wide_mask, narrow_mask):
        wide, narrow = self.wide, self.narrow
        for mask, step in self.wide_steps.items():
            wide = wide + step if mask & wide_mask else wide
        for mask, step in self.narrow_steps.items():
            narrow = narrow + step if mask & narrow_mask else narrow
        return wide, narrow


def exchange_kernel(masks, sizes, whole, x_ref, out_ref, send_sem, recv_sem, own_sem):
    wides, groups = sizes
    place = Place(wides, groups)
    masks = list(range(wides * groups)) if masks is None else masks
    count = len(masks)

    def peer(mask):
        return place.peer(mask // groups, mask % groups)

    def each(step):
        for k in range(1, count):
            step(k, masks[k])

    def copy(k, mask):
        return pltpu.make_async_remote_copy(
            src_ref=x_ref if whole else x_ref.at[k],
            dst_ref=out_ref.at[k],
            send_sem=send_sem.at[k],
            recv_sem=recv_sem.at[k],
            device_id=peer(mask),
            device_id_type=MESH,
        )

    barrier = pltpu.get_barrier_semaphore()
    each(
        lambda k, mask: pl.semaphore_signal(
            barrier, inc=1, device_id=peer(mask), device_id_type=MESH
        )
    )
    pl.semaphore_wait(barrier, count - 1)
    each(lambda k, mask: copy(k, mask).start())
    own = pltpu.make_async_copy(x_ref if whole else x_ref.at[0], out_ref.at[0], own_sem)
    own.start()
    own.wait()
    each(lambda k, mask: copy(k, mask).wait())


def exchange(array, number, name, masks=None, whole=True):
    sizes = (lax.axis_size("wide"), lax.axis_size("narrow"))
    count = sizes[0] * sizes[1] if masks is None else len(masks)
    shape = (count,) + array.shape if whole else array.shape
    return pl.pallas_call(
        functools.partial(exchange_kernel, masks, sizes, whole),
        out_shape=jax.ShapeDtypeStruct(shape, array.dtype),
        in_specs=[pl.BlockSpec(memory_space=pltpu.VMEM)],
        out_specs=pl.BlockSpec(memory_space=pltpu.VMEM),
        scratch_shapes=[
            pltpu.SemaphoreType.DMA((count,)),
            pltpu.SemaphoreType.DMA((count,)),
            pltpu.SemaphoreType.DMA,
        ],
        compiler_params=pltpu.CompilerParams(
            collective_id=number, has_side_effects=True, vmem_limit_bytes=32 * MIB
        ),
        name=name,
    )(array)


def merge_stats(stats):
    masks = group_masks()
    rows = stats.shape[1] // 4
    parts = exchange(stats, 1, "stats_swap", masks, False)
    top, total, picked = (parts[:, i * rows : (i + 1) * rows] for i in range(3))
    highest = jnp.max(top, 0)
    own = highest + jnp.log(jnp.sum(total * jnp.exp(top - highest), 0))
    share = exchange(jnp.pad(own, ((0, -rows % 8), (0, 0))), 8, "stats_share", masks)
    return share[:, :rows], own, jnp.sum(picked, 0)


def put_columns(rows_ref, column_ref):
    turned = rows_ref[...].T
    for place in range(rows_ref.shape[0]):
        column_ref[pl.ds(place * 128, 128), :] = turned[:, place : place + 1]


def as_rows(column):
    count = column.shape[0] // 128
    return jnp.concatenate(
        [column[place * 128 : (place + 1) * 128] for place in range(count)], 1
    ).T


def score_kernel(
    rows_ref, table_ref, target_ref, exps_ref, max_ref, stat_ref, sum_ref, pick_ref, column_ref
):
    tile = pl.program_id(0)
    width = table_ref.shape[0]

    @pl.when(tile == 0)
    def _():
        max_ref[...] = jnp.full_like(max_ref, -jnp.inf)
        sum_ref[...] = jnp.zeros_like(sum_ref)
        pick_ref[...] = jnp.zeros_like(pick_ref)
        put_columns(target_ref, column_ref)

    def step(block, carry):
        rows = pl.ds(pl.multiple_of(block * TOKEN_TILE, TOKEN_TILE), TOKEN_TILE)
        scores = lax.dot_general(
            rows_ref[rows, :],
            table_ref[...],
            (((1,), (1,)), ((), ())),
            preferred_element_type=jnp.float32,
        )
        top = jnp.max(scores, -1, keepdims=True)
        powers = jnp.exp(scores - top)
        exps_ref[rows, :] = powers.astype(jnp.bfloat16)
        total = jnp.sum(powers, -1, keepdims=True)
        columns = lax.broadcasted_iota(jnp.int32, (TOKEN_TILE, width), 1)
        wanted = column_ref[rows, :] - tile * width
        hit = jnp.sum(jnp.where(columns == wanted, scores, 0.0), -1, keepdims=True)
        here = lax.broadcasted_iota(jnp.int32, (TOKEN_TILE, 128), 1) == tile
        max_ref[rows, :] = jnp.where(here, top, max_ref[rows, :])
        sum_ref[rows, :] = jnp.where(here, total, sum_ref[rows, :])
        pick_ref[rows, :] = jnp.where(here, hit, pick_ref[rows, :])
        return carry

    lax.fori_loop(0, rows_ref.shape[0] // TOKEN_TILE, step, 0, unroll=8)

    @pl.when(tile == pl.num_programs(0) - 1)
    def _():
        maxima = max_ref[...]
        top = jnp.max(maxima, -1, keepdims=True)
        total = jnp.sum(sum_ref[...] * jnp.exp(maxima - top), -1, keepdims=True)
        picked = jnp.sum(pick_ref[...], -1, keepdims=True)
        blocks, height, _ = stat_ref.shape
        rows = height // 4
        stat_ref[...] = jnp.zeros_like(stat_ref)
        for number, column in enumerate((top, total, picked)):
            lines = as_rows(column)
            for block in range(blocks):
                stat_ref[block, pl.ds(number * rows, rows), :] = lines[
                    block * rows : (block + 1) * rows
                ]


def vocab_tile(vocab):
    return 1280 if vocab % 1280 == 0 else 640


def head_scores(rows, table, targets, blocks):
    tokens, model = rows.shape
    vocab = table.shape[0]
    width = vocab_tile(vocab)
    stat = pltpu.VMEM((tokens, 128), jnp.float32)
    whole = pl.BlockSpec((tokens, 128), lambda j: (0, 0))
    height = 4 * (tokens // blocks // 128)
    return pl.pallas_call(
        score_kernel,
        grid=(vocab // width,),
        out_shape=(
            jax.ShapeDtypeStruct((tokens, vocab), jnp.bfloat16),
            jax.ShapeDtypeStruct((tokens, 128), jnp.float32),
            jax.ShapeDtypeStruct((blocks, height, 128), jnp.float32),
        ),
        in_specs=[
            pl.BlockSpec((tokens, model), lambda j: (0, 0)),
            pl.BlockSpec((width, model), lambda j: (j, 0)),
            pl.BlockSpec(targets.shape, lambda j: (0, 0)),
        ],
        out_specs=(
            pl.BlockSpec((tokens, width), lambda j: (0, j)),
            whole,
            pl.BlockSpec((blocks, height, 128), lambda j: (0, 0, 0)),
        ),
        scratch_shapes=[stat, stat, pltpu.VMEM((tokens, 1), jnp.int32)],
        compiler_params=pltpu.CompilerParams(vmem_limit_bytes=60 * MIB),
        cost_estimate=pl.CostEstimate(
            flops=3 * tokens * vocab * model,
            bytes_accessed=2 * tokens * vocab,
            transcendentals=tokens * vocab,
        ),
        name="head_scores",
    )(rows, table, targets)


def slope_kernel(
    exps_ref,
    max_ref,
    log_ref,
    target_ref,
    table_ref,
    slope_ref,
    grad_ref,
    total_ref,
    column_ref,
    log_column_ref,
):
    tile = pl.program_id(0)
    width = table_ref.shape[0]

    @pl.when(tile == 0)
    def _():
        total_ref[...] = jnp.zeros_like(total_ref)
        put_columns(target_ref, column_ref)
        put_columns(log_ref, log_column_ref)

    def step(block, carry):
        rows = pl.ds(pl.multiple_of(block * TOKEN_TILE, TOKEN_TILE), TOKEN_TILE)
        here = lax.broadcasted_iota(jnp.int32, (TOKEN_TILE, 128), 1) == tile
        top = jnp.sum(jnp.where(here, max_ref[rows, :], 0.0), -1, keepdims=True)
        scale = jnp.exp(top - log_column_ref[rows, :])
        columns = lax.broadcasted_iota(jnp.int32, (TOKEN_TILE, width), 1)
        wanted = column_ref[rows, :] - tile * width
        probs = exps_ref[rows, :].astype(jnp.float32) * scale
        slope = jnp.where(columns == wanted, probs - 1.0, probs).astype(jnp.bfloat16)
        slope_ref[rows, :] = slope
        total_ref[rows, :] += jnp.dot(slope, table_ref[...], preferred_element_type=jnp.float32)
        return carry

    lax.fori_loop(0, exps_ref.shape[0] // TOKEN_TILE, step, 0, unroll=8)

    @pl.when(tile == pl.num_programs(0) - 1)
    def _():
        grad_ref[...] = total_ref[...].astype(jnp.bfloat16)


def head_slopes(exps, maxima, logs, targets, table):
    tokens, vocab = exps.shape
    model = table.shape[1]
    width = vocab_tile(vocab)
    return pl.pallas_call(
        slope_kernel,
        grid=(vocab // width,),
        out_shape=(
            jax.ShapeDtypeStruct((tokens, vocab), jnp.bfloat16),
            jax.ShapeDtypeStruct((tokens, model), jnp.bfloat16),
        ),
        in_specs=[
            pl.BlockSpec((tokens, width), lambda j: (0, j)),
            pl.BlockSpec((tokens, 128), lambda j: (0, 0)),
            pl.BlockSpec(logs.shape, lambda j: (0, 0)),
            pl.BlockSpec(targets.shape, lambda j: (0, 0)),
            pl.BlockSpec((width, model), lambda j: (j, 0)),
        ],
        out_specs=(
            pl.BlockSpec((tokens, width), lambda j: (0, j)),
            pl.BlockSpec((tokens, model), lambda j: (0, 0)),
        ),
        scratch_shapes=[
            pltpu.VMEM((tokens, model), jnp.float32),
            pltpu.VMEM((tokens, 1), jnp.int32),
            pltpu.VMEM((tokens, 1), jnp.float32),
        ],
        compiler_params=pltpu.CompilerParams(vmem_limit_bytes=60 * MIB),
        cost_estimate=pl.CostEstimate(
            flops=3 * tokens * vocab * model,
            bytes_accessed=4 * tokens * vocab,
            transcendentals=0,
        ),
        input_output_aliases={0: 0},
        name="head_slopes",
    )(exps, maxima, logs, targets, table)


def slots():
    wides, ups = chip_sizes()
    return 32 if wides * ups <= 16 else 16


def one_hot(places, size):
    return (places.reshape(-1, 1) == jnp.arange(size)[None]).astype(jnp.bfloat16)


def token_plan(ids_all, shard_rows):
    chips, tokens = ids_all.shape
    wides, ups = chip_sizes()
    wide, narrow = lax.axis_index("wide"), lax.axis_index("narrow")
    own_core = narrow % 2
    own_chip = wide * ups + narrow // 2
    owner = ids_all // shard_rows
    owner_core = jnp.bitwise_xor(owner % 2, own_core)
    owner_chip = jnp.bitwise_xor(owner // 2, own_chip)
    local = ids_all % shard_rows
    row = lax.broadcasted_iota(jnp.int32, (tokens, tokens), 0)
    column = lax.broadcasted_iota(jnp.int32, (tokens, tokens), 1)
    before = column < row
    alike = ids_all[:, :, None] == ids_all[:, None, :]
    first = ~jnp.any(alike & before[None], 2)
    served = first & (owner_chip == 0) & (owner_core == 0)
    served_rank = times_t(served.astype(jnp.bfloat16), before.astype(jnp.bfloat16)).astype(
        jnp.int32
    )
    half = tokens // 2
    mine = lambda array: lax.dynamic_slice_in_dim(array, own_core * half, half)
    own_first = mine(jnp.min(jnp.where(alike[0], column, tokens), 1))
    same_owner = mine(owner[0])[:, None] == owner[0][None]
    own_rank = jnp.sum(
        (same_owner & first[0][None] & (column[:half] < own_first[:, None])).astype(jnp.int32), 1
    )
    own_block = mine(owner_core[0]) * chips + mine(owner_chip[0])
    most = jnp.max(
        jnp.sum(
            (
                first[:, None, :]
                & (owner[:, None, :] == jnp.arange(2 * chips)[None, :, None])
            ).astype(jnp.int32),
            2,
        )
    )
    rounds = (most + slots() - 1) // slots()

    def plan(turn):
        slot = jnp.arange(slots())[None, :, None] + turn * slots()
        chosen = served[:, None, :] & (served_rank[:, None, :] == slot)
        slot_rows = jnp.sum(jnp.where(chosen, local[:, None, :] + 1, 0), 2) - 1
        inside = own_rank - turn * slots()
        valid = (inside >= 0) & (inside < slots())
        own_slots = jnp.where(valid, own_block * slots() + inside, -1)
        return slot_rows, one_hot(own_slots, 2 * chips * slots())

    return plan, rounds


def later_rounds(rounds, turn, total):
    return lax.while_loop(
        lambda state: state[0] < rounds,
        lambda state: (state[0] + 1, state[1] + turn(state[0])),
        (jnp.ones((), jnp.int32), total),
    )[1]


def norm_kernel(sizes, tile, table_ref, passed_ref, slot_ref, rows_ref, small_ref, matrix_ref, scalar_ref, *refs):
    total_ref, sum_ref, sent_ref, got_ref, send_sem, recv_sem = refs
    wides, groups = sizes
    place = Place(wides, groups)
    count = wides * groups
    barrier = pltpu.get_barrier_semaphore()
    for k in range(1, count):
        pl.semaphore_signal(
            barrier, inc=1, device_id=place.peer(k // groups, k % groups), device_id_type=MESH
        )
    width = table_ref.shape[1]

    def step(i, squares):
        span = pl.ds(pl.multiple_of(i * tile, 8), tile)
        row = lax.broadcasted_iota(jnp.int32, (tile, slot_ref.shape[1]), 0) + i * tile
        hot = (row == slot_ref[...]).astype(jnp.float32).astype(jnp.bfloat16)
        total = table_ref[span, :] + passed_ref[span, :].astype(jnp.float32)
        total = total + plain(hot, rows_ref[...])
        total_ref[span, :] = total
        return squares + jnp.sum((total * total).reshape(tile // 8, 8, width), 0)

    squares = lax.fori_loop(
        0, table_ref.shape[0] // tile, step, jnp.zeros((8, width), jnp.float32)
    )
    own = jnp.sum(squares + matrix_ref[...], keepdims=True)
    lane = lax.broadcasted_iota(jnp.int32, (8, 128), 1)
    sent_ref[...] = scalar_ref[...] + jnp.where(lane == 2, own, 0.0)
    pl.semaphore_wait(barrier, count - 1)

    def copy(k):
        return pltpu.make_async_remote_copy(
            src_ref=sent_ref,
            dst_ref=got_ref.at[k],
            send_sem=send_sem.at[k],
            recv_sem=recv_sem.at[k],
            device_id=place.peer(k // groups, k % groups),
            device_id_type=MESH,
        )

    for k in range(1, count):
        copy(k).start()
    got_ref[0] = sent_ref[...]
    small = small_ref[...]
    copied = jnp.sum(small * small, keepdims=True)
    for k in range(1, count):
        copy(k).wait()
    both = got_ref[...]
    total = jnp.zeros((8, 128), jnp.float32)
    order = device_order(place, wides, groups, both)
    for one in order:
        total = total + one
    sum_ref[...] = total + jnp.where(lane == 2, copied, 0.0)


def device_order(place, wides, groups, blocks):
    flat = [blocks[k] for k in range(wides * groups)]
    sides = [(groups << bit, place.wide // (1 << bit) % 2) for bit in range(log_two(wides))]
    sides += [(1 << bit, place.narrow // (1 << bit) % 2) for bit in range(log_two(groups))]
    for step, side in sides:
        one = side == 1
        flat = [jnp.where(one, flat[k ^ step], flat[k]) for k in range(len(flat))]
    return flat


def table_norm(table_sum, passed, slot_rows, rows, small, matrix_squares, scalars):
    sizes = (lax.axis_size("wide"), lax.axis_size("narrow"))
    count = sizes[0] * sizes[1]
    height, width = table_sum.shape
    tile = next(size for size in (400, 80, 16) if height % size == 0)
    vmem = pl.BlockSpec(memory_space=pltpu.VMEM)
    return pl.pallas_call(
        functools.partial(norm_kernel, sizes, tile),
        out_shape=(
            jax.ShapeDtypeStruct((height, width), jnp.float32),
            jax.ShapeDtypeStruct((8, 128), jnp.float32),
        ),
        in_specs=[vmem] * 7,
        out_specs=(vmem, vmem),
        scratch_shapes=[
            pltpu.VMEM((8, 128), jnp.float32),
            pltpu.VMEM((count, 8, 128), jnp.float32),
        ]
        + mail_sems(count),
        compiler_params=pltpu.CompilerParams(
            collective_id=3, has_side_effects=True, vmem_limit_bytes=62 * MIB
        ),
        name="table_norm",
    )(table_sum, passed, slot_rows.reshape(1, -1), rows, small, matrix_squares, scalars)


def upper_blocks(count):
    return [(i, j) for i in range(count) for j in range(i, count)]


def muon_kernel(lane_bits, *refs):
    core, _, y_bits, _ = lane_bits
    low_refs, factor_ref, table_refs = refs[:4], refs[4], refs[5:9]
    rest_out, size_out, table_outs = *refs[9:11], refs[11:14]
    gram, sent, got, back, full, total, half, low_a, low_b, low_c, send_sem, recv_sem = refs[14:26]
    in_tiles, out_tiles, in_sem, out_sem = refs[26:]
    width = full.shape[0]
    block = gram.shape[-1]
    places = upper_blocks(width // block)
    greet([neighbour(bit) for bit in [core] + y_bits])
    mail = Mail(send_sem, recv_sem, lane_bits)

    def adam_flow():
        tile = in_tiles.shape[2]
        count = table_refs[0].shape[0] // tile

        def loads(number):
            span = pl.ds(number * tile, tile)
            return [
                pltpu.make_async_copy(
                    ref.at[span], in_tiles.at[number % 2, kind], in_sem.at[number % 2, kind]
                )
                for kind, ref in enumerate(table_refs)
            ]

        def stores(number):
            span = pl.ds(number * tile, tile)
            return [
                pltpu.make_async_copy(
                    out_tiles.at[number % 2, kind], ref.at[span], out_sem.at[number % 2, kind]
                )
                for kind, ref in enumerate(table_outs)
            ]

        for copy in loads(0):
            copy.start()
        yield mail.now
        for number in range(count):
            if number + 1 < count:
                for copy in loads(number + 1):
                    copy.start()
            for copy in loads(number):
                copy.wait()
            if number >= 2:
                for copy in stores(number - 2):
                    copy.wait()
            weight, moment, square, grad = (in_tiles[number % 2, kind] for kind in range(4))
            results = adam_step(
                weight, moment, square, grad * factor_ref[0:1, 0:1], EMBED_RATE, DECAY
            )
            for kind, result in enumerate(results):
                out_tiles[number % 2, kind] = result
            for copy in stores(number):
                copy.start()
            yield mail.spend(1.2)
        for number in range(max(count - 2, 0), count):
            for copy in stores(number):
                copy.wait()

    mail.run([muon_flow(mail, lane_bits, refs, places), adam_flow()])
    mail.close()
    for number in range(4):

        def put_out(i, j, piece, number=number):
            rest_out[number, pl.ds(i * block, block), pl.ds(j * block, block)] = piece.astype(
                jnp.bfloat16
            )

        unpack(places, lambda place: back[number, place].astype(jnp.float32), put_out)


def unpack(places, source, target):
    for place, (i, j) in enumerate(places):
        piece = source(place)
        target(i, j, piece)
        if i != j:
            target(j, i, piece.T)


def muon_flow(mail, lane_bits, refs, places):
    core, _, y_bits, _ = lane_bits
    low_refs, size_out = refs[:4], refs[10]
    gram, sent, got, back, full, total, half, low_a, low_b, low_c = refs[14:24]
    width = full.shape[0]
    block = gram.shape[-1]
    narrow = lax.axis_index("narrow")
    own_core, own_up = narrow % 2, (narrow // 2) % 2
    own = 2 * own_core + own_up
    for number, low_ref in enumerate(low_refs):
        for place, (i, j) in enumerate(places):
            product = lax.dot_general(
                low_ref[:, i * block : (i + 1) * block],
                low_ref[:, j * block : (j + 1) * block],
                (((0,), (0,)), ((), ())),
                preferred_element_type=jnp.float32,
            )
            gram[number, place] = product
    for slot in range(2):
        sent[slot] = gram[2 * (1 - own_core) + slot].astype(jnp.bfloat16)
    copy = mail.post(sent.at[pl.ds(0, 2)], got.at[pl.ds(0, 2)], core)
    yield mail.due
    mail.take(copy)

    def add(number, slot):
        for place in range(len(places)):
            gram[number, place] += got[slot, place].astype(jnp.float32)

    def pass_on(number, slot, bit):
        sent[slot] = gram[number].astype(jnp.bfloat16)
        return mail.post(sent.at[slot], got.at[slot], bit)

    other_up = 2 * own_core + 1 - own_up
    if y_bits:
        add(other_up, 1 - own_up)
        over_y = pass_on(other_up, 2, y_bits[0])
        add(own, own_up)
        yield mail.due
        mail.take(over_y)
        add(own, 2)
    for level, bit in enumerate(y_bits[1:]):
        copy = pass_on(own, 3 + level, bit)
        yield mail.due
        mail.take(copy)
        add(own, 3 + level)

    def spans(i, j):
        return pl.ds(i * block, block), pl.ds(j * block, block)

    def put_full(i, j, piece):
        full[spans(i, j)] = piece

    unpack(places, lambda place: gram[own, place], put_full)
    diagonal = lax.broadcasted_iota(jnp.int32, (block, block), 0) == lax.broadcasted_iota(
        jnp.int32, (block, block), 1
    )
    trace = jnp.zeros((1, 1), jnp.float32)
    for i in range(width // block):
        trace = trace + jnp.sum(jnp.where(diagonal, full[spans(i, i)], 0.0), keepdims=True)
    magnitude = jnp.sqrt(trace) + 1e-07
    inverse = 1.0 / magnitude

    def rows(step):
        def body(i, carry):
            step(pl.ds(pl.multiple_of(i * block, block), block))
            return carry

        lax.fori_loop(0, width // block, body, 0)

    def times(left, right, span):
        return jnp.dot(left[span, :], right[...], preferred_element_type=jnp.float32)

    def start(span):
        scaled = full[span, :] * (inverse * inverse)
        full[span, :] = scaled
        low_a[span, :] = scaled.astype(jnp.bfloat16)

    rows(start)
    scale = NS_A
    for cycle_no in range(NS_STEPS):

        def rest_step(span):
            rest = NS_B * full[span, :] + NS_C * times(low_a, low_a, span)
            low_b[span, :] = rest.astype(jnp.bfloat16)
            if cycle_no == 0:
                total[span, :] = rest
            else:
                total[span, :] = NS_A * total[span, :] + scale * rest

        rows(rest_step)
        if cycle_no:

            def total_step(span):
                total[span, :] += times(low_c, low_b, span)

            rows(total_step)
            scale = scale * NS_A
        if cycle_no < NS_STEPS - 1:

            def keep_total(span):
                low_c[span, :] = total[span, :].astype(jnp.bfloat16)

            def half_step(span):
                half[span, :] = NS_A * full[span, :] + times(low_a, low_b, span)

            def full_step(span):
                value = half[span, :]
                low_a[span, :] = value.astype(jnp.bfloat16)
                full[span, :] = NS_A * value + times(low_a, low_b, span)

            def low_step(span):
                low_a[span, :] = full[span, :].astype(jnp.bfloat16)

            rows(keep_total)
            rows(half_step)
            rows(full_step)
            rows(low_step)

    for place, (i, j) in enumerate(places):
        back[own, place] = (total[spans(i, j)] * inverse).astype(jnp.bfloat16)
    lane = lax.broadcasted_iota(jnp.int32, (8, 128), 1)
    size_out[own] = jnp.where(lane >= 0, inverse, 0.0)
    mail.post(back.at[own], back.at[own], core)
    mail.post(size_out.at[own], size_out.at[own], core)
    if y_bits:
        over_size = mail.post(size_out.at[own], size_out.at[own], y_bits[0])
        over_y = mail.post(back.at[own], back.at[own], y_bits[0])
        yield mail.due
        mail.take(over_y)
        mail.take(over_size)
        mail.post(back.at[other_up], back.at[other_up], core)
        mail.post(size_out.at[other_up], size_out.at[other_up], core)


def muon_factors(lows, factor, table):
    width = lows[0].shape[1]
    block = 256
    count = len(upper_blocks(width // block))
    lane_bits = lanes()
    extra = max(len(lane_bits[2]) - 1, 0)
    vmem = pl.BlockSpec(memory_space=pltpu.VMEM)
    square = (width, width)
    height = table[0].shape[0]
    tile = next(size for size in (160, 80, 40, 16, 8) if height % size == 0)
    any_space = pl.BlockSpec(memory_space=pl.ANY)
    whole = jax.ShapeDtypeStruct(table[0].shape, jnp.float32)
    rests, sizes, *table_next = pl.pallas_call(
        functools.partial(muon_kernel, lane_bits),
        out_shape=(
            jax.ShapeDtypeStruct((4,) + square, jnp.bfloat16),
            jax.ShapeDtypeStruct((4, 8, 128), jnp.float32),
            whole,
            whole,
            whole,
        ),
        in_specs=[vmem] * 5 + [any_space] * 4,
        out_specs=(vmem, vmem, any_space, any_space, any_space),
        scratch_shapes=[
            pltpu.VMEM((4, count, block, block), jnp.float32),
            pltpu.VMEM((3 + extra, count, block, block), jnp.bfloat16),
            pltpu.VMEM((3 + extra, count, block, block), jnp.bfloat16),
            pltpu.VMEM((4, count, block, block), jnp.bfloat16),
        ]
        + [pltpu.VMEM(square, jnp.float32) for _ in range(3)]
        + [pltpu.VMEM(square, jnp.bfloat16) for _ in range(3)]
        + mail_sems(32)
        + [
            pltpu.VMEM((2, 4, tile, width), jnp.float32),
            pltpu.VMEM((2, 3, tile, width), jnp.float32),
            pltpu.SemaphoreType.DMA((2, 4)),
            pltpu.SemaphoreType.DMA((2, 3)),
        ],
        compiler_params=pltpu.CompilerParams(
            collective_id=9, has_side_effects=True, vmem_limit_bytes=56 * MIB
        ),
        name="muon_factors",
    )(*lows, jnp.full((8, 128), factor), *table)
    return rests, sizes[:, 0, 0], table_next


def on_device(
    token_ids,
    targets,
    joint_weight,
    output_weight,
    expand_weight,
    reduce_weight,
    joint_velocity,
    output_velocity,
    expand_velocity,
    reduce_velocity,
    embedding,
    embed_moment,
    embed_square,
    positions,
    position_moment,
    position_square,
    norm_gains,
    gain_moment,
    gain_square,
    biases,
    bias_moment,
    bias_square,
):
    core, x_bits, y_bits, z_bits = lanes()
    groups = lax.axis_size("narrow")
    wides = lax.axis_size("wide")
    across = 1 << len(x_bits)
    model_width = embedding.shape[1]
    shard_rows = embedding.shape[0]
    tokens = token_ids.shape[0] * LENGTH
    bias_rows = biases.reshape(-1, model_width)

    own_rows = embedding.astype(jnp.bfloat16)
    labels = jnp.concatenate([token_ids.reshape(-1, 128), targets.reshape(-1, 128)])
    spare = -labels.shape[0] % 8
    labels = exchange(jnp.pad(labels, ((0, spare), (0, 0))), 0, "label_share")
    ids_all = labels[:, : tokens // 128].reshape(-1, tokens)
    lines = tokens // 128
    own_block = lax.axis_index("wide") * groups + lax.axis_index("narrow")
    wides, ups = chip_sizes()
    pairs = ids_all.reshape(wides, ups, 2, tokens)
    other_first = lax.axis_index("narrow") % 2 == 1
    ids_chips = jnp.where(other_first, lax.rev(pairs, (2,)), pairs).reshape(wides * ups, -1)
    plan, rounds = token_plan(ids_chips, shard_rows)

    def serve(slot_rows):
        served = one_hot(slot_rows, shard_rows)
        return plain(served, own_rows).astype(jnp.bfloat16).reshape(-1, slots(), model_width)

    masters = (joint_weight, output_weight, expand_weight, reduce_weight)
    served, wanted = plan(0)
    table, weights, token_rows = load_all(
        own_rows, [master.astype(jnp.bfloat16) for master in masters], serve(served)
    )
    vocab_here = table.shape[0]

    def fetch(turn):
        more, places = plan(turn)
        got = swap_rows(serve(more))
        return plain(places, jnp.stack([got, swap(got, core)]).reshape(-1, model_width))

    embedded = later_rounds(rounds, fetch, plain(wanted, token_rows.reshape(-1, model_width)))

    block_masks = jnp.array(group_masks())
    targets_group = labels[block_masks, lines : 2 * lines].reshape(-1, 128)
    table_mask = groups * (across - 1) + 1
    differ = jnp.bitwise_xor(targets_group // shard_rows, own_block)
    is_owned = (targets_group >= 0) & (jnp.bitwise_and(differ, ~table_mask) == 0)
    place = (differ % 2) * across + (differ // groups) % across
    rows_targets = jnp.where(is_owned, place * shard_rows + targets_group % shard_rows, -1)
    final_low, *saved = layer_forward(embedded, positions, norm_gains, bias_rows, weights)
    group_rows = spread(final_low).reshape(-1, model_width)
    blocks = len(group_masks())
    exps, maxima, stats = head_scores(group_rows, table, rows_targets, blocks)
    logs, own_logs, own_picked = merge_stats(stats)
    loss_part = jnp.sum(
        jnp.where(targets.reshape(-1, 128) >= 0, own_logs - own_picked, 0.0)
    )
    logs = jnp.where(targets_group >= 0, logs.reshape(-1, 128), jnp.inf)
    slopes, final_part = head_slopes(exps, maxima, logs, rows_targets, table)
    final_grad, table_sum, passed = head_back(
        final_part.reshape(-1, tokens, model_width), slopes, group_rows
    )
    for bit in reversed(x_bits):
        passed = swap(passed, bit)
        if bit != x_bits[0]:
            table_sum = table_sum + passed.astype(jnp.float32)
            half = table_sum.shape[0] // 2
            table_sum, passed = table_sum[:half], table_sum[half:].astype(jnp.bfloat16)
    (front, expand_sum, reduce_sum), small, row_sums, squares, low_grad = back_reduce(
        final_grad, norm_gains, bias_rows, saved, weights, wanted
    )
    count_part = jnp.sum((targets >= 0).astype(jnp.float32))

    def bundle(places):
        both = outer_sum(places, low_grad).astype(jnp.bfloat16)
        both = both.reshape(2, -1, slots(), model_width)
        other = swap(both[1], core)
        return (both[0].astype(jnp.float32) + other.astype(jnp.float32)).astype(jnp.bfloat16)

    joint_rows = joint_weight.shape[0]
    def give(turn):
        more, places = plan(turn)
        got = swap_rows(bundle(places)).reshape(-1, model_width)
        return outer_sum(one_hot(more, shard_rows), got)

    table_sum = later_rounds(rounds, give, table_sum)
    places = jnp.stack([loss_part, count_part]).reshape(1, 2)
    table_sum, scalars = table_norm(
        table_sum,
        passed,
        served,
        row_sums.reshape(-1, model_width),
        small,
        squares,
        jnp.pad(places, ((0, 7), (0, 126))),
    )
    matrix_total = [
        part.astype(jnp.float32)
        for part in (front[:joint_rows], front[joint_rows:], expand_sum, reduce_sum)
    ]
    small = small[: 14 + LENGTH]
    loss_sum, loss_count, squares = scalars[0, 0], scalars[0, 1], scalars[0, 2]
    gain_grad, position_grad = small[:3], small[14:]
    bias_grad = small[3:14].reshape(-1)
    grad_norm = jnp.sqrt(squares) / loss_count
    factor = jnp.minimum(1.0, CLIP / (grad_norm + 1e-06)) / loss_count
    previous = (joint_velocity, output_velocity, expand_velocity, reduce_velocity)
    carried = tuple(
        (MOMENTUM * before + gradient * factor for before, gradient in zip(previous, matrix_total))
    )
    lows = [moment.astype(jnp.bfloat16) for moment in carried]
    rests, inverses, table_out = muon_factors(
        lows, factor, (embedding, embed_moment, embed_square, table_sum)
    )
    updated = []
    for number, (master, moment) in enumerate(zip(masters, carried)):
        orth = moment * (NS_A**NS_STEPS * inverses[number]) + plain(
            lows[number], rests[number]
        )
        shape_factor = math.sqrt(max(1.0, master.shape[0] * groups / master.shape[1]))
        updated.append(master * (1 - MUON_RATE * DECAY) - MUON_RATE * shape_factor * orth)
    place_out = adam_step(
        positions, position_moment, position_square, position_grad * factor, PLACE_RATE, DECAY
    )
    gain_out = adam_step(norm_gains, gain_moment, gain_square, gain_grad * factor, SMALL_RATE, 0.0)
    bias_out = adam_step(biases, bias_moment, bias_square, bias_grad * factor, SMALL_RATE, 0.0)
    return (
        loss_sum,
        loss_count,
        grad_norm,
        updated[0],
        updated[1],
        updated[2],
        updated[3],
        carried[0],
        carried[1],
        carried[2],
        carried[3],
        table_out[0],
        table_out[1],
        table_out[2],
        place_out[0],
        place_out[1],
        place_out[2],
        gain_out[0],
        gain_out[1],
        gain_out[2],
        bias_out[0],
        bias_out[1],
        bias_out[2],
    )


def solution(mesh):
    in_specs = (
        P(("wide", "narrow"), None),
        P(("wide", "narrow"), None),
        P("narrow", None),
        P("narrow", None),
        P("narrow", None),
        P("narrow", None),
        P("narrow", None),
        P("narrow", None),
        P("narrow", None),
        P("narrow", None),
        P(("wide", "narrow"), None),
        P(("wide", "narrow"), None),
        P(("wide", "narrow"), None),
        P(),
        P(),
        P(),
        P(),
        P(),
        P(),
        P(),
        P(),
        P(),
    )
    out_specs = (
        P(),
        P(),
        P(),
        P("narrow", None),
        P("narrow", None),
        P("narrow", None),
        P("narrow", None),
        P("narrow", None),
        P("narrow", None),
        P("narrow", None),
        P("narrow", None),
        P(("wide", "narrow"), None),
        P(("wide", "narrow"), None),
        P(("wide", "narrow"), None),
        P(),
        P(),
        P(),
        P(),
        P(),
        P(),
        P(),
        P(),
        P(),
    )
    return jax.shard_map(
        on_device, mesh=mesh, in_specs=in_specs, out_specs=out_specs, check_vma=False
    )
```

```python
import functools
import math

import jax
import jax.numpy as jnp
from jax import lax
from jax.experimental import pallas as pl
from jax.experimental.pallas import tpu as pltpu
from jax.sharding import PartitionSpec as P

HEADS = 12
HEAD = 64
LENGTH = 64
NS_STEPS = 3
STEP = 10


HIGH = lax.Precision.HIGHEST
EPS = 1e-05
CLIP = 0.05
MOMENTUM = 0.95
MUON_RATE = 0.5
DECAY = 0.1
BETA_ONE = 0.9
BETA_TWO = 0.999
EMBED_RATE = 0.02
PLACE_RATE = 0.1
SMALL_RATE = 0.2
NS_A = 3.4445
NS_B = -4.775
NS_C = 2.0315
MESH = pl.DeviceIdType.MESH
MIB = 1 << 20
TOKEN_TILE = 256


def times_t(left, right):
    return lax.dot_general(
        left, right, (((1,), (1,)), ((), ())), preferred_element_type=jnp.float32
    )


def outer_sum(left, right):
    return lax.dot_general(
        left, right, (((0,), (0,)), ((), ())), preferred_element_type=jnp.float32
    )


def plain(left, right):
    return jnp.dot(left, right, preferred_element_type=jnp.float32)


def norm_forward(stream, gain, shift):
    centred = stream - jnp.mean(stream, -1, keepdims=True)
    inverse = lax.rsqrt(jnp.mean(centred * centred, -1, keepdims=True) + EPS)
    normed = centred * inverse
    return (normed * gain + shift, normed, inverse)


def norm_backward(upstream, normed, inverse, gain):
    scaled = upstream * gain
    inner = inverse * (
        scaled
        - jnp.mean(scaled, -1, keepdims=True)
        - normed * jnp.mean(scaled * normed, -1, keepdims=True)
    )
    return (
        inner,
        jnp.sum(upstream * normed, 0, keepdims=True),
        jnp.sum(upstream, 0, keepdims=True),
    )


def gelu_tanh(values):
    return jax.nn.gelu(values, approximate=True)


def column_sum(values):
    return jnp.sum(values.astype(jnp.float32), 0, keepdims=True)


def pair_masks(tokens):
    first = lax.broadcasted_iota(jnp.int32, (tokens, 2 * HEAD), 1) < HEAD
    row = lax.broadcasted_iota(jnp.int32, (tokens, tokens), 0)
    column = lax.broadcasted_iota(jnp.int32, (tokens, tokens), 1)
    return first, (row // LENGTH == column // LENGTH) & (column <= row)


def head_probs(queries, key_heads, seen):
    scores = times_t(queries, key_heads) * HEAD ** (-0.5)
    scores = jnp.where(seen, scores, -1000000000.0)
    powers = jnp.exp(scores - jnp.max(scores, -1, keepdims=True))
    return powers * (1.0 / jnp.sum(powers, -1, keepdims=True))


def forward_kernel(
    x_ref,
    place_ref,
    gain_ref,
    bias_ref,
    joint_hbm,
    output_hbm,
    expand_hbm,
    reduce_hbm,
    low_ref,
    normed_ref,
    inverse_ref,
    joint_out,
    context_ref,
    upward_ref,
    joint_ref,
    output_ref,
    expand_ref,
    reduce_ref,
    load_sem,
):
    pairs = ((joint_hbm, joint_ref), (output_hbm, output_ref), (expand_hbm, expand_ref), (reduce_hbm, reduce_ref))
    loads = [
        pltpu.make_async_copy(source, target, load_sem.at[number])
        for number, (source, target) in enumerate(pairs)
    ]
    for load in loads:
        load.start()
    tokens, width = x_ref.shape

    def norm(number, stream):
        result, normed, inverse = norm_forward(
            stream, gain_ref[number : number + 1, :], bias_ref[number : number + 1, :]
        )
        normed_ref[number] = normed
        inverse_ref[number] = jnp.broadcast_to(inverse, (tokens, 128))
        return result.astype(jnp.bfloat16)

    stream = x_ref[...] + jnp.concatenate([place_ref[...]] * (tokens // LENGTH), 0)
    first_low = norm(0, stream)
    loads[0].wait()
    for part in range(3):
        span = pl.ds(part * width, width)
        result = times_t(first_low, joint_ref[span, :])
        if part != 1:
            row = 3 if part == 0 else 4
            result = result + bias_ref[row : row + 1, :]
        joint_out[:, span] = result.astype(jnp.bfloat16)
    first, seen = pair_masks(tokens)
    zero = jnp.zeros((), jnp.bfloat16)
    for pair in range(HEADS // 2):
        queries = joint_out[:, pl.ds(pair * 128, 128)]
        key_heads = joint_out[:, pl.ds(width + pair * 128, 128)]
        values = joint_out[:, pl.ds(2 * width + pair * 128, 128)]
        parts = []
        for mine in (first, ~first):
            probs = head_probs(jnp.where(mine, queries, zero), key_heads, seen)
            parts.append(plain(probs.astype(jnp.bfloat16), values))
        context_ref[:, pl.ds(pair * 128, 128)] = jnp.where(first, *parts).astype(jnp.bfloat16)
    loads[1].wait()
    stream = stream + times_t(context_ref[...], output_ref[...]) + bias_ref[5:6, :]
    second_low = norm(1, stream)
    stream = stream + bias_ref[6:7, :]
    loads[2].wait()
    loads[3].wait()
    for part in range(expand_ref.shape[0] // width):
        span = pl.ds(part * width, width)
        upward = times_t(second_low, expand_ref[span, :]) + bias_ref[7 + part : 8 + part, :]
        upward_ref[:, span] = upward
        stream = stream + plain(gelu_tanh(upward).astype(jnp.bfloat16), reduce_ref[span, :])
    low_ref[...] = norm(2, stream)


def layer_forward(embedded, positions, norm_gains, bias_rows, weights):
    tokens, width = embedded.shape
    vmem, any_space = pl.BlockSpec(memory_space=pltpu.VMEM), pl.BlockSpec(memory_space=pl.ANY)
    shape = jax.ShapeDtypeStruct
    hidden = weights[2].shape[0]
    return pl.pallas_call(
        forward_kernel,
        out_shape=(
            shape((tokens, width), jnp.bfloat16),
            shape((3, tokens, width), jnp.float32),
            shape((3, tokens, 128), jnp.float32),
            shape((tokens, 3 * width), jnp.bfloat16),
            shape((tokens, width), jnp.bfloat16),
            shape((tokens, hidden), jnp.float32),
        ),
        in_specs=[vmem] * 4 + [any_space] * 4,
        out_specs=[vmem] * 6,
        scratch_shapes=[pltpu.VMEM(w.shape, w.dtype) for w in weights]
        + [pltpu.SemaphoreType.DMA((4,))],
        compiler_params=pltpu.CompilerParams(vmem_limit_bytes=63 * MIB),
        name="layer_forward",
    )(embedded, positions, norm_gains, bias_rows, *weights)


def gelu_slope(values):
    inner = math.sqrt(2.0 / math.pi)
    squared = values * values
    bent = jnp.tanh(inner * (values + 0.044715 * squared * values))
    return 0.5 * values * (1.0 + bent), 0.5 * (1.0 + bent) + 0.5 * values * (
        1.0 - bent * bent
    ) * (inner * (1.0 + 3 * 0.044715 * squared))


def backward_flow(ins, outs, scratch):
    (final_ref, gain_ref, bias_ref, normed_ref, inverse_ref, joint_in, context_ref, upward_ref) = ins
    (stream_ref, small_ref, front_ref, expand_out, reduce_out) = outs
    (joint_ref, output_ref, expand_ref, reduce_ref, waits) = scratch
    hold = reduce_ref
    tokens, width = final_ref.shape
    _, ups, height, _ = front_ref.shape
    groups = 2 * ups

    def put(ref, start, grad):
        for group in range(groups):
            low = max(group * height, start)
            high = min((group + 1) * height, start + grad.shape[0])
            if low < high:
                ref[group % 2, group // 2, pl.ds(low - group * height, high - low), :] = grad[
                    low - start : high - start
                ]

    def gain(number):
        return gain_ref[number : number + 1, :]

    def normed_low(number):
        return (normed_ref[number] * gain(number) + bias_ref[number : number + 1, :]).astype(
            jnp.bfloat16
        )

    def back(number, upstream):
        inner, gain_row, shift_row = norm_backward(
            upstream, normed_ref[number], inverse_ref[number][:, :1], gain(number)
        )
        small_ref[number : number + 1, :] = gain_row
        small_ref[3 + number : 4 + number, :] = shift_row
        return inner

    small_ref[...] = jnp.zeros_like(small_ref)
    back_f = back(2, final_ref[...])
    down = back_f.astype(jnp.bfloat16)
    small_ref[9:10, :] = column_sum(down)
    second_low = normed_low(1)
    second_grad = jnp.zeros((tokens, width), jnp.float32)
    waits[2].wait()
    waits[3].wait()
    for part in range(expand_ref.shape[0] // width):
        span = pl.ds(part * width, width)
        active, slope = gelu_slope(upward_ref[:, span])
        upward_grad = (times_t(down, reduce_ref[span, :]) * slope).astype(jnp.bfloat16)
        small_ref[10 + part : 11 + part, :] = column_sum(upward_grad)
        second_grad = second_grad + plain(upward_grad, expand_ref[span, :])
        put(expand_out, part * width, outer_sum(upward_grad, second_low).astype(jnp.bfloat16))
        put(reduce_out, part * width, outer_sum(active.astype(jnp.bfloat16), down).astype(jnp.bfloat16))
    yield 0.0
    mid_grad = back_f + back(1, second_grad)
    stream_ref[...] = mid_grad
    attn_grad = mid_grad.astype(jnp.bfloat16)
    small_ref[8:9, :] = column_sum(attn_grad)
    waits[1].wait()
    last = pl.ds(3 * tokens, tokens)
    hold[last, :] = plain(attn_grad, output_ref[...]).astype(jnp.bfloat16)
    output_grad = outer_sum(attn_grad, context_ref[...]).astype(jnp.bfloat16)
    rows = width // groups
    joint_rows = height - rows
    for group in range(groups):
        front_ref[group % 2, group // 2, pl.ds(joint_rows, rows), :] = output_grad[
            group * rows : (group + 1) * rows
        ]
    yield 2.0
    first, seen = pair_masks(tokens)
    zero = jnp.zeros((), jnp.bfloat16)
    for pair in range(HEADS // 2):
        spans = [pl.ds(part * width + pair * 128, 128) for part in range(3)]
        queries, key_heads, values = (joint_in[:, span] for span in spans)
        upstream = hold[last, spans[0]]
        parts = []
        for mine in (first, ~first):
            probs = head_probs(jnp.where(mine, queries, zero), key_heads, seen)
            probs_grad = times_t(jnp.where(mine, upstream, zero), values)
            score_grad = (
                probs * (probs_grad - jnp.sum(probs * probs_grad, -1, keepdims=True))
            ).astype(jnp.bfloat16)
            parts.append(
                (
                    plain(score_grad, key_heads) * HEAD ** (-0.5),
                    outer_sum(score_grad, queries) * HEAD ** (-0.5),
                    outer_sum(probs.astype(jnp.bfloat16), upstream),
                )
            )
        for part, (one, two) in enumerate(zip(*parts)):
            hold[pl.ds(part * tokens, tokens), spans[0]] = jnp.where(first, one, two).astype(
                jnp.bfloat16
            )
        yield 1.5
    first_low = normed_low(0)
    waits[0].wait()
    first_grad = jnp.zeros((tokens, width), jnp.float32)
    for part in range(3):
        span = pl.ds(part * width, width)
        piece = hold[pl.ds(part * tokens, tokens), :]
        if part != 1:
            row = 6 if part == 0 else 7
            small_ref[row : row + 1, :] = column_sum(piece)
        first_grad = first_grad + plain(piece, joint_ref[span, :])
        grad = outer_sum(piece, first_low).astype(jnp.bfloat16)
        for group in range(groups):
            start = max(group * joint_rows, part * width)
            end = min((group + 1) * joint_rows, (part + 1) * width)
            if start < end:
                front_ref[
                    group % 2, group // 2, pl.ds(start - group * joint_rows, end - start), :
                ] = grad[start - part * width : end - part * width]
        yield 1.5
    stream = stream_ref[...] + back(0, first_grad)
    stream_ref[...] = stream
    placed = stream[:LENGTH]
    for sequence in range(1, tokens // LENGTH):
        placed = placed + stream[sequence * LENGTH : (sequence + 1) * LENGTH]
    small_ref[14 : 14 + LENGTH, :] = placed


def adam_step(weight, moment, square, gradient, rate, decay):
    moment = BETA_ONE * moment + (1 - BETA_ONE) * gradient
    square = BETA_TWO * square + (1 - BETA_TWO) * gradient * gradient
    unbiased = moment / (1 - BETA_ONE**STEP)
    spread = square / (1 - BETA_TWO**STEP)
    return (
        weight - rate * (unbiased / (jnp.sqrt(spread) + 1e-08) + decay * weight),
        moment,
        square,
    )


def log_two(size):
    return size.bit_length() - 1


def lanes():
    wide, narrow = lax.axis_size("wide"), lax.axis_size("narrow")
    across = wide // 4
    x_bits = [("wide", 1 << i) for i in range(log_two(across))]
    z_bits = [("wide", across << i) for i in range(log_two(wide // across))]
    y_bits = [("narrow", 2 << i) for i in range(log_two(narrow // 2))]
    return ("narrow", 1), x_bits, y_bits, z_bits


def swap(array, bit):
    axis, mask = bit
    return lax.ppermute(array, axis, [(i, i ^ mask) for i in range(lax.axis_size(axis))])


def side(bit):
    axis, mask = bit
    return (lax.axis_index(axis) // mask) % 2


def join(mine, other, bit, dim=0):
    own = side(bit)
    return jnp.where(
        own == 0, jnp.concatenate([mine, other], dim), jnp.concatenate([other, mine], dim)
    )


def halves(array, bit):
    own = side(bit)
    half = array.shape[0] // 2
    keep = lax.dynamic_slice_in_dim(array, own * half, half)
    send = lax.dynamic_slice_in_dim(array, (1 - own) * half, half)
    return keep, send


def group_bits():
    _, _, y_bits, z_bits = lanes()
    return z_bits + y_bits


SPREAD_ORDERS = ("nyf", "fny", "nfy", "fyn")
COLLECT_ORDERS = ("yfn", "ynf", "nyf", "fyn")


def routes(rows, orders):
    _, _, y_bits, z_bits = lanes()
    kinds = {"y": y_bits, "n": z_bits[:1], "f": z_bits[1:]}
    size = rows // len(orders)
    return [
        (number * size, size, [bit for kind in order for bit in kinds[kind]])
        for number, order in enumerate(orders)
    ]


def flat_mask(bit):
    axis, mask = bit
    return mask * lax.axis_size("narrow") if axis == "wide" else mask


def group_masks():
    masks = [0]
    for bit in group_bits():
        masks = masks + [other ^ flat_mask(bit) for other in masks]
    return masks


def neighbour(bit):
    axis, mask = bit
    wide, narrow = lax.axis_index("wide"), lax.axis_index("narrow")
    if axis == "wide":
        return wide + mask * (1 - 2 * ((wide // mask) % 2)), narrow
    return wide, narrow + mask * (1 - 2 * ((narrow // mask) % 2))


def greet(devices):
    barrier = pltpu.get_barrier_semaphore()
    for device in devices:
        pl.semaphore_signal(barrier, inc=1, device_id=device, device_id_type=MESH)
    pl.semaphore_wait(barrier, len(devices))


class Mail:
    def __init__(self, send_sem, recv_sem, lane_bits):
        core, x_bits, y_bits, z_bits = lane_bits
        self.send_sem, self.recv_sem = send_sem, recv_sem
        self.used, self.sent, self.open = 0, [], []
        self.links = {core: (("core", 1 / 600e3),)}
        self.links.update({bit: (("x", 2 / 91e3),) for bit in x_bits})
        self.links.update({bit: (("y", 2 / 91e3),) for bit in y_bits})
        self.links.update({bit: (("z", 2 / 91e3),) for bit in z_bits[:1]})
        self.links.update({bit: (("z", 2 / 91e3), ("far", 4 / 91e3)) for bit in z_bits[1:]})
        self.free, self.now, self.ready = {}, 0.0, []

    def expect(self, source, bit):
        size = math.prod(source.shape) * source.dtype.itemsize
        due = self.now
        for link, rate in self.links[bit]:
            self.free[link] = max(self.free.get(link, 0.0), self.now) + size * rate
            due = max(due, self.free[link])
        return due + 3.5

    def post(self, source, target, bit):
        copy = pltpu.make_async_remote_copy(
            src_ref=source,
            dst_ref=target,
            send_sem=self.send_sem.at[self.used],
            recv_sem=self.recv_sem.at[self.used],
            device_id=neighbour(bit),
            device_id_type=MESH,
        )
        copy.start()
        self.due = self.expect(source, bit)
        self.used += 1
        self.sent.append(copy)
        self.open.append(copy)
        return copy

    def keep(self, source, target):
        copy = pltpu.make_async_copy(source, target, self.recv_sem.at[self.used])
        copy.start()
        self.used += 1
        self.open.append(copy)
        return copy

    def take(self, copy):
        if any(other is copy for other in self.open):
            self.open = [other for other in self.open if other is not copy]
            if any(other is copy for other in self.sent):
                copy.wait_recv()
            else:
                copy.wait()

    def spend(self, time):
        self.now += time
        return self.now

    def run(self, flows):
        waiting = [(next(flow, None), flow) for flow in flows]
        while True:
            waiting += [(next(flow, None), flow) for flow in self.ready]
            self.ready = []
            waiting = [entry for entry in waiting if entry[0] is not None]
            if not waiting:
                return
            place = min(range(len(waiting)), key=lambda i: waiting[i][0])
            due, flow = waiting.pop(place)
            self.now = max(self.now, due) + 0.4
            waiting.append((next(flow, None), flow))

    def close(self):
        for copy in list(self.open):
            self.take(copy)
        for copy in self.sent:
            copy.wait_send()


def mail_sems(count):
    return [pltpu.SemaphoreType.DMA((count,)), pltpu.SemaphoreType.DMA((count,))]


def spread_flow(mail, bits, part, x_ref, out_ref):
    first, rows, order = part
    span = pl.ds(first, rows)
    held = {0: None}
    for bit in order:
        step = 1 << bits.index(bit)
        for block in list(held):
            if block:
                mail.take(held[block])
            source = out_ref.at[block, span] if block else x_ref.at[span]
            held[block ^ step] = mail.post(source, out_ref.at[block ^ step, span], bit)
        yield mail.due


def spread_kernel(lane_bits, plan, x_ref, *refs):
    core, x_bits, y_bits, z_bits = lane_bits
    count = 1 << len(x_bits)
    table_refs, out_ref, table_out, send_sem, recv_sem = refs[:count], *refs[count:]
    bits = z_bits + y_bits
    greet([neighbour(bit) for bit in bits + [core]])
    mail = Mail(send_sem, recv_sem, lane_bits)

    def table_flow():
        yield 1.0
        for place, ref in enumerate(table_refs):
            mail.post(ref, table_out.at[1, place], core)
            mail.keep(ref, table_out.at[0, place])

    mail.run([spread_flow(mail, bits, part, x_ref, out_ref) for part in plan] + [table_flow()])
    mail.keep(x_ref, out_ref.at[0])
    mail.close()


def spread(array, tables):
    bits, plan = group_bits(), routes(array.shape[0], SPREAD_ORDERS)
    count = 1 << len(bits)
    vmem, any_space = pl.BlockSpec(memory_space=pltpu.VMEM), pl.BlockSpec(memory_space=pl.ANY)
    blocks, table = pl.pallas_call(
        functools.partial(spread_kernel, lanes(), plan),
        out_shape=(
            jax.ShapeDtypeStruct((count,) + array.shape, array.dtype),
            jax.ShapeDtypeStruct((2, len(tables)) + tables[0].shape, array.dtype),
        ),
        in_specs=[vmem] * (1 + len(tables)),
        out_specs=(any_space, any_space),
        scratch_shapes=mail_sems(len(plan) * count + 2 * len(tables)),
        compiler_params=pltpu.CompilerParams(
            collective_id=4, has_side_effects=True, vmem_limit_bytes=62 * MIB
        ),
        name="rows_spread",
    )(array, *tables)
    width = array.shape[1]
    return blocks.reshape(-1, width), table.reshape(-1, width)


def collect_flow(mail, bits, part, refs):
    first, rows, order = part
    x_ref, out_ref, sum_ref, got_ref = refs
    span = pl.ds(first, rows)
    held = list(range(1 << len(bits)))
    for stage, bit in enumerate(order):
        step = 1 << bits.index(bit)
        source = sum_ref if stage else x_ref
        held = [block for block in held if not block & step]
        base = (1 << len(bits)) - 2 * len(held)
        copies = [
            mail.post(source.at[block ^ step, span], got_ref.at[base + place, span], bit)
            for place, block in enumerate(held)
        ]
        yield mail.due
        for place, (block, copy) in enumerate(zip(held, copies)):
            mail.take(copy)
            total = source[block, span, :].astype(jnp.float32) + got_ref[
                base + place, span, :
            ].astype(jnp.float32)
            if stage == len(bits) - 1:
                out_ref[span, :] = total
            else:
                sum_ref[block, span, :] = total.astype(jnp.bfloat16)


def head_back_kernel(lane_bits, plan, tile, x_ref, *refs):
    core, _, y_bits, z_bits = lane_bits
    bits = z_bits + y_bits
    if tile:
        slope_ref, rows_ref, out_ref, keep_ref, pass_ref = refs[:5]
        sum_ref, got_ref, send_sem, recv_sem = refs[5:9]
        loads, sent_ref, other_ref, load_sem = refs[9:]
        half = sent_ref.shape[0]
        count = half // tile
        order = [count + i for i in range(count)] + [count - 1 - i for i in range(count)]

        def load(number):
            return pltpu.make_async_copy(
                slope_ref.at[:, pl.ds(order[number] * tile, tile)],
                loads.at[number % 2],
                load_sem.at[number % 2],
            )

        load(0).start()
        greet([neighbour(bit) for bit in bits + [core]])
    else:
        out_ref, sum_ref, got_ref, send_sem, recv_sem = refs
        greet([neighbour(bit) for bit in bits])
    mail = Mail(send_sem, recv_sem, lane_bits)
    flows = [
        collect_flow(mail, bits, part, (x_ref, out_ref, sum_ref, got_ref)) for part in plan
    ]
    if tile:

        def table_flow():
            arrivals = {}
            border = keep_ref.shape[0]
            for number, block in enumerate(order):
                if number + 1 < len(order):
                    load(number + 1).start()
                load(number).wait()
                grad = lax.dot_general(
                    loads[number % 2],
                    rows_ref[...],
                    (((0,), (0,)), ((), ())),
                    preferred_element_type=jnp.float32,
                )
                start = block * tile % half
                span = pl.ds(start, tile)
                if block >= count:
                    sent_ref[span, :] = grad.astype(jnp.bfloat16)
                    arrivals[start] = mail.post(sent_ref.at[span], other_ref.at[span], core)
                else:
                    mail.take(arrivals[start])
                    grad = grad + other_ref[span, :].astype(jnp.float32)
                    lower = min(max(border - start, 0), tile)
                    if lower:
                        keep_ref[pl.ds(start, lower), :] = grad[:lower]
                    if lower < tile:
                        pass_ref[pl.ds(start + lower - border, tile - lower), :] = grad[
                            lower:
                        ].astype(jnp.bfloat16)
                yield mail.spend(2.7)

        flows.append(table_flow())
    mail.run(flows)
    mail.close()


def head_back(array, slopes, group_rows):
    lane_bits = lanes()
    bits, plan = group_bits(), routes(array.shape[1], COLLECT_ORDERS)
    count, rows, width = array.shape
    vocab = slopes.shape[1]
    half = vocab // 2
    tile = 640 if half % 640 == 0 else 0
    vmem = pl.BlockSpec(memory_space=pltpu.VMEM)
    shapes = [jax.ShapeDtypeStruct((rows, width), jnp.float32)]
    scratch = [
        pltpu.VMEM((count, rows, width), jnp.bfloat16),
        pltpu.VMEM((count - 1, rows, width), jnp.bfloat16),
    ] + mail_sems(len(plan) * count + (half // tile if tile else 0))
    operands, specs = [array], [vmem]
    if tile:
        shapes += [
            jax.ShapeDtypeStruct((half // 2, width), jnp.float32),
            jax.ShapeDtypeStruct((half // 2, width), jnp.bfloat16),
        ]
        scratch += [
            pltpu.VMEM((2, slopes.shape[0], tile), jnp.bfloat16),
            pltpu.VMEM((half, width), jnp.bfloat16),
            pltpu.VMEM((half, width), jnp.bfloat16),
            pltpu.SemaphoreType.DMA((2,)),
        ]
        operands += [slopes, group_rows]
        specs += [pl.BlockSpec(memory_space=pl.ANY), vmem]
    outs = pl.pallas_call(
        functools.partial(head_back_kernel, lane_bits, plan, tile),
        out_shape=shapes,
        in_specs=specs,
        out_specs=[vmem] * len(shapes),
        scratch_shapes=scratch,
        compiler_params=pltpu.CompilerParams(
            collective_id=5, has_side_effects=True, vmem_limit_bytes=56 * MIB
        ),
        name="head_back",
    )(*operands)
    if tile:
        return outs
    core = lane_bits[0]
    other = swap(outer_sum(slopes[:, half:], group_rows).astype(jnp.bfloat16), core)
    table_sum = outer_sum(slopes[:, :half], group_rows) + other.astype(jnp.float32)
    return outs[0], table_sum[: half // 2], table_sum[half // 2 :].astype(jnp.bfloat16)


def chip_sizes():
    wides, groups = lax.axis_size("wide"), lax.axis_size("narrow")
    return wides, groups // 2


class Rows:
    def __init__(self, sizes, x_ref, out_ref, send_sem, recv_sem):
        self.sizes, self.x_ref, self.out_ref = sizes, x_ref, out_ref
        self.send_sem, self.recv_sem = send_sem, recv_sem
        self.count = sizes[0] * sizes[1]
        self.place = Place(sizes[0], 2 * sizes[1])

    def peer(self, k):
        ups = self.sizes[1]
        return self.place.peer(k // ups, 2 * (k % ups))

    def each(self, step):
        for k in range(1, self.count):
            step(k)

    def copy(self, k):
        return pltpu.make_async_remote_copy(
            src_ref=self.x_ref.at[k],
            dst_ref=self.out_ref.at[k],
            send_sem=self.send_sem.at[k],
            recv_sem=self.recv_sem.at[k],
            device_id=self.peer(k),
            device_id_type=MESH,
        )

    def greet(self, others):
        self.call(others)
        self.meet(others)

    def call(self, others):
        barrier = pltpu.get_barrier_semaphore()
        self.each(
            lambda k: pl.semaphore_signal(
                barrier, inc=1, device_id=self.peer(k), device_id_type=MESH
            )
        )
        for device in others:
            pl.semaphore_signal(barrier, inc=1, device_id=device, device_id_type=MESH)

    def meet(self, others):
        pl.semaphore_wait(pltpu.get_barrier_semaphore(), self.count - 1 + len(others))

    def start(self):
        self.each(lambda k: self.copy(k).start())

    def own(self):
        return pltpu.make_async_copy(self.x_ref.at[0], self.out_ref.at[0], self.recv_sem.at[0])


def swap_rows_kernel(sizes, x_ref, out_ref, send_sem, recv_sem):
    rows = Rows(sizes, x_ref, out_ref, send_sem, recv_sem)
    rows.greet([])
    rows.start()
    own = rows.own()
    own.start()
    own.wait()
    rows.each(lambda k: rows.copy(k).wait())


def swap_rows(rows):
    sizes = chip_sizes()
    count = sizes[0] * sizes[1]
    return pl.pallas_call(
        functools.partial(swap_rows_kernel, sizes),
        out_shape=jax.ShapeDtypeStruct(rows.shape, rows.dtype),
        in_specs=[pl.BlockSpec(memory_space=pltpu.VMEM)],
        out_specs=pl.BlockSpec(memory_space=pl.ANY),
        scratch_shapes=mail_sems(count),
        compiler_params=pltpu.CompilerParams(collective_id=2, has_side_effects=True),
        name="token_rows",
    )(rows)


def load_kernel(sizes, lane_bits, *refs):
    core, x_bits, y_bits, z_bits = lane_bits
    near = z_bits[0]
    weight_refs, rows_ref = refs[:4], refs[4]
    weight_outs, rows_out = refs[5:9], refs[9]
    send_sem, recv_sem, rows_send, rows_recv, pass_send, pass_recv = refs[10:]
    wide, narrow = lax.axis_index("wide"), lax.axis_index("narrow")
    rows = Rows(sizes, rows_ref, rows_out.at[0], rows_send, rows_recv)
    rows.greet([neighbour(core)])
    mail = Mail(send_sem, recv_sem, lane_bits)
    side_near = (wide // near[1]) % 2

    def across(block, bit):
        return block + bit[1] * (1 - 2 * ((block // bit[1]) % 2))

    def pieces(height):
        half = height // 2
        count = 2 if height == weight_refs[3].shape[0] and half % 32 == 0 else 1
        return [(place * (half // count), half // count) for place in range(count)]

    def part(ref, number, side, piece):
        start = side * (ref.shape[1] // 2) + piece[0]
        return ref.at[number, pl.ds(pl.multiple_of(start, 16), piece[1])]

    def own_part(ref, side, piece):
        start = side * (ref.shape[0] // 2) + piece[0]
        return ref.at[pl.ds(pl.multiple_of(start, 16), piece[1])]

    first = [
        mail.post(own_part(ref, side_near, piece), part(out, narrow, side_near, piece), y_bits[0])
        for ref, out in zip(weight_refs, weight_outs)
        for piece in pieces(ref.shape[0])
    ]
    rows.start()
    own_rows = rows.own()
    own_rows.start()
    keeps = []
    for ref, out in zip(weight_refs, weight_outs):
        keeps.append(mail.keep(ref, out.at[narrow]))
        mail.post(ref, out.at[narrow], core)
    own_rows.wait()
    blocks = [narrow]
    for level, bit in enumerate(y_bits):
        if level:
            for copy in keeps:
                mail.take(copy)
        arrivals, number = [], 0
        for ref, out in zip(weight_refs, weight_outs):
            for piece in pieces(ref.shape[0]):
                for block in blocks:
                    if level:
                        source = part(out, block, side_near, piece)
                        copy = mail.post(source, source, bit)
                    else:
                        copy = first[number]
                        number += 1
                    arrivals.append((out, across(block, bit), piece, copy))
        seconds = []
        for out, other, piece, copy in arrivals:
            mail.take(copy)
            source = part(out, other, side_near, piece)
            seconds.append(mail.post(source, source, near))
            mail.post(source, source, core)
        for (out, other, piece, _), copy in zip(arrivals, seconds):
            mail.take(copy)
            source = part(out, other, 1 - side_near, piece)
            mail.post(source, source, core)
        blocks = blocks + [across(block, bit) for block in blocks]

    def hand(k):
        return pltpu.make_async_remote_copy(
            src_ref=rows_out.at[0, k],
            dst_ref=rows_out.at[1, k],
            send_sem=pass_send.at[k],
            recv_sem=pass_recv.at[k],
            device_id=neighbour(core),
            device_id_type=MESH,
        )

    hand(0).start()

    def forward(k):
        rows.copy(k).wait()
        hand(k).start()

    rows.each(forward)
    hand(0).wait()
    rows.each(lambda k: hand(k).wait())
    mail.close()


def load_all(weights, rows):
    lane_bits = lanes()
    sizes = chip_sizes()
    count = sizes[0] * sizes[1]
    groups = lax.axis_size("narrow")
    any_space = pl.BlockSpec(memory_space=pl.ANY)
    shapes = [jax.ShapeDtypeStruct((groups,) + w.shape, w.dtype) for w in weights]
    shapes.append(jax.ShapeDtypeStruct((2,) + rows.shape, rows.dtype))
    *weights_all, rows_all = pl.pallas_call(
        functools.partial(load_kernel, sizes, lane_bits),
        out_shape=shapes,
        in_specs=[pl.BlockSpec(memory_space=pltpu.VMEM)] * 5,
        out_specs=[any_space] * 5,
        scratch_shapes=mail_sems(8 * 4 * groups) + mail_sems(count) + mail_sems(count),
        compiler_params=pltpu.CompilerParams(
            collective_id=6, has_side_effects=True, vmem_limit_bytes=62 * MIB
        ),
        name="load_rows",
    )(*weights, rows)
    return tuple(w.reshape(-1, w.shape[-1]) for w in weights_all), rows_all


def tile_of(rows):
    return next(size for size in (128, 96, 64, 48, 32, 16) if rows % size == 0)


def back_reduce_kernel(sizes, lane_bits, kinds, *refs):
    core, x_bits, y_bits, z_bits = lane_bits
    ins, wanted_ref, hbm = refs[:8], refs[8], refs[9:13]
    out_refs, small_out, rows_out, square_out, low_out = refs[13:16], *refs[16:20]
    scratch = refs[20:]
    weights, load_sem, stream_ref, small_ref = scratch[:4], scratch[4], scratch[5], small_out
    grad_refs = scratch[6:9]
    both_ref, core_got = scratch[9:11]
    small_sum, small_got, send_sem, recv_sem, rows_send, rows_recv = scratch[11:17]
    rest = scratch[17:]
    got_refs = []
    for _, _, _, path in kinds:
        got_refs.append(rest[: len(path) + 1])
        rest = rest[len(path) + 1 :]
    waits = [
        pltpu.make_async_copy(source, target, load_sem.at[number])
        for number, (source, target) in enumerate(zip(hbm, weights))
    ]
    for load in waits:
        load.start()
    place = {"wide": lax.axis_index("wide"), "narrow": lax.axis_index("narrow")}
    rows = Rows(sizes, both_ref.at[0], rows_out, rows_send, rows_recv)
    rows.call([neighbour(core)])
    mail = Mail(send_sem, recv_sem, lane_bits)
    ups = grad_refs[0].shape[1]
    own = place["narrow"] % 2
    square_out[...] = jnp.zeros_like(square_out)

    def side_of(bit):
        return (place[bit[0]] // bit[1]) % 2

    def add(total_ref, got_ref, box):
        up, ups_here, first, height = box
        tile = tile_of(height)

        def step(i, carry):
            at = i // (height // tile)
            down = (i % (height // tile)) * tile
            span = pl.ds(pl.multiple_of(first + down, 16), tile)
            got = got_ref[at, pl.ds(pl.multiple_of(down, 16), tile), :]
            total = total_ref[own, up + at, span, :].astype(jnp.float32) + got.astype(jnp.float32)
            total_ref[own, up + at, span, :] = total.astype(jnp.bfloat16)
            return carry

        lax.fori_loop(0, ups_here * (height // tile), step, 0)

    def view(ref, box):
        up, ups_here, first, height = box
        return ref.at[own, pl.ds(up, ups_here), pl.ds(pl.multiple_of(first, 16), height)]

    def flow(number):
        which, offset, height, path = kinds[number]
        total_ref, got, out_ref = grad_refs[which], got_refs[number], out_refs[which]
        span = pl.ds(offset, height)
        copy = mail.post(total_ref.at[1 - own, :, span], got[0], core)
        yield mail.due
        mail.take(copy)
        box = (0, ups, offset, height)
        add(total_ref, got[0], box)
        for stage, (bit, halve) in enumerate(path):
            up, ups_here, first, height = box
            side = side_of(bit)
            if bit[0] == "narrow":
                half = ups_here // 2
                mine = (up + side * half, half, first, height)
                theirs = (up + (1 - side) * half, half, first, height)
            elif halve:
                half = height // 2
                mine = (up, ups_here, first + side * half, half)
                theirs = (up, ups_here, first + (1 - side) * half, half)
            else:
                mine = theirs = box
            copy = mail.post(view(total_ref, theirs), got[stage + 1], bit)
            yield mail.due
            mail.take(copy)
            if not halve:
                copy.wait_send()
                mail.sent = [other for other in mail.sent if other is not copy]
            box = mine
            add(total_ref, got[stage + 1], box)
        up, _, first, height = box
        piece = total_ref[own, up, pl.ds(pl.multiple_of(first, 16), height), :]
        out_ref[pl.ds(pl.multiple_of(first, 16), height), :] = piece
        full = piece.astype(jnp.float32)
        square_out[...] += jnp.sum((full * full).reshape(height // 8, 8, -1), 0)
        for bit, halve in reversed(path):
            if bit[0] == "wide" and halve:
                span = pl.ds(pl.multiple_of(first, 16), height)
                copy = mail.post(out_ref.at[span], out_ref.at[span], bit)
                yield mail.due
                mail.take(copy)
                first = first - side_of(bit) * height
                height = 2 * height

    def small_flow():
        bits = [core] + x_bits + y_bits + z_bits
        small_sum[0] = small_ref[...].astype(jnp.bfloat16)
        for stage, bit in enumerate(bits):
            copy = mail.post(small_sum.at[stage], small_got.at[stage], bit)
            yield mail.due
            mail.take(copy)
            total = small_sum[stage].astype(jnp.float32) + small_got[stage].astype(jnp.float32)
            if stage == len(bits) - 1:
                small_out[...] = total
            else:
                small_sum[stage + 1] = total.astype(jnp.bfloat16)

    def rows_flow():
        low = stream_ref[...].astype(jnp.bfloat16)
        low_out[...] = low
        both = outer_sum(wanted_ref[...], low).astype(jnp.bfloat16)
        both_ref[...] = both.reshape(both_ref.shape)
        copy = mail.post(both_ref.at[1], core_got, core)
        yield mail.due
        mail.take(copy)
        summed = both_ref[0].astype(jnp.float32) + core_got[...].astype(jnp.float32)
        both_ref[0] = summed.astype(jnp.bfloat16)
        rows.start()
        own_rows = rows.own()
        own_rows.start()
        yield mail.due
        own_rows.wait()

    back = backward_flow(
        ins,
        (stream_ref, small_ref) + tuple(grad_refs),
        (*weights, waits),
    )
    next(back)
    rows.meet([neighbour(core)])

    def back_flow():
        for cost in back:
            yield mail.spend(cost)
        mail.ready += [flow(number) for number in range(4, len(kinds))]
        mail.ready += [rows_flow(), small_flow()]

    mail.run([flow(number) for number in range(4)] + [back_flow()])
    rows.each(lambda k: rows.copy(k).wait())
    mail.close()


def back_reduce(final_grad, norm_gains, bias_rows, saved, weights, wanted):
    lane_bits = lanes()
    core, x_bits, y_bits, z_bits = lane_bits
    sizes = chip_sizes()
    tokens, width = final_grad.shape
    ups = sizes[1]
    height = 4 * width // (2 * ups)
    half = height // 2
    bits = {"x": x_bits, "y": y_bits[::-1], "z": z_bits[:1], "f": z_bits[1:]}
    kinds, got_shapes = [], []
    for which, offset, order in (
        (1, 0, "yzfx"),
        (2, 0, "yxzf"),
        (1, half, "yzxf"),
        (2, half, "zyxf"),
        (0, 0, "yxfz"),
        (0, half, "yxzf"),
    ):
        path, ups_here, height_here = [], ups, half
        shapes = [(ups_here, height_here, width)]
        for bit in [bit for kind in order for bit in bits[kind]]:
            halve = True
            if bit[0] == "narrow":
                ups_here //= 2
            else:
                halve = (height_here // 2) % 16 == 0
                height_here = height_here // 2 if halve else height_here
            path.append((bit, halve))
            shapes.append((ups_here, height_here, width))
        kinds.append((which, offset, half, path))
        got_shapes += shapes
    count = sizes[0] * sizes[1]
    steps = 1 + len(kinds[0][3])
    small_rows = 14 + LENGTH
    small = (small_rows + -small_rows % 16, width)
    row_shape = (count, slots(), width)
    vmem, any_space = pl.BlockSpec(memory_space=pltpu.VMEM), pl.BlockSpec(memory_space=pl.ANY)
    shape, low = jax.ShapeDtypeStruct, jnp.bfloat16
    outs = pl.pallas_call(
        functools.partial(back_reduce_kernel, sizes, lane_bits, kinds),
        out_shape=[shape((height, width), low)] * 3
        + [
            shape(small, jnp.float32),
            shape(row_shape, low),
            shape((8, width), jnp.float32),
            shape((tokens, width), low),
        ],
        in_specs=[vmem] * 9 + [any_space] * 4,
        out_specs=[vmem] * 4 + [any_space, vmem, vmem],
        scratch_shapes=[pltpu.VMEM(w.shape, w.dtype) for w in weights]
        + [
            pltpu.SemaphoreType.DMA((4,)),
            pltpu.VMEM((tokens, width), jnp.float32),
        ]
        + [pltpu.VMEM((2, ups, height, width), low) for _ in range(3)]
        + [pltpu.VMEM((2,) + row_shape, low), pltpu.VMEM(row_shape, low)]
        + [pltpu.VMEM((steps,) + small, low), pltpu.VMEM((steps,) + small, low)]
        + mail_sems(len(kinds) * 2 * steps + steps + 1)
        + mail_sems(count)
        + [pltpu.VMEM(one, low) for one in got_shapes],
        compiler_params=pltpu.CompilerParams(
            collective_id=7, has_side_effects=True, vmem_limit_bytes=63 * MIB
        ),
        name="back_reduce",
    )(final_grad, norm_gains, bias_rows, *saved, wanted, *weights)
    repeats = 1
    for bit, halve in kinds[0][3]:
        repeats *= 1 if halve else 2
    return outs[:3], outs[3], outs[4], outs[5] / repeats, outs[6]


class Place:
    def __init__(self, wides, groups):
        self.wide, self.narrow = lax.axis_index("wide"), lax.axis_index("narrow")
        self.wide_steps = self.steps(self.wide, wides)
        self.narrow_steps = self.steps(self.narrow, groups)

    def steps(self, place, size):
        masks = [1 << bit for bit in range(log_two(size))]
        return {mask: mask * (1 - 2 * ((place // mask) % 2)) for mask in masks}

    def peer(self, wide_mask, narrow_mask):
        wide, narrow = self.wide, self.narrow
        for mask, step in self.wide_steps.items():
            wide = wide + step if mask & wide_mask else wide
        for mask, step in self.narrow_steps.items():
            narrow = narrow + step if mask & narrow_mask else narrow
        return wide, narrow


def exchange_kernel(masks, sizes, whole, x_ref, out_ref, send_sem, recv_sem, own_sem):
    wides, groups = sizes
    place = Place(wides, groups)
    masks = list(range(wides * groups)) if masks is None else masks
    count = len(masks)

    def peer(mask):
        return place.peer(mask // groups, mask % groups)

    def each(step):
        for k in range(1, count):
            step(k, masks[k])

    def copy(k, mask):
        return pltpu.make_async_remote_copy(
            src_ref=x_ref if whole else x_ref.at[k],
            dst_ref=out_ref.at[k],
            send_sem=send_sem.at[k],
            recv_sem=recv_sem.at[k],
            device_id=peer(mask),
            device_id_type=MESH,
        )

    barrier = pltpu.get_barrier_semaphore()
    each(
        lambda k, mask: pl.semaphore_signal(
            barrier, inc=1, device_id=peer(mask), device_id_type=MESH
        )
    )
    pl.semaphore_wait(barrier, count - 1)
    each(lambda k, mask: copy(k, mask).start())
    own = pltpu.make_async_copy(x_ref if whole else x_ref.at[0], out_ref.at[0], own_sem)
    own.start()
    own.wait()
    each(lambda k, mask: copy(k, mask).wait())


def exchange(array, number, name, masks=None, whole=True):
    sizes = (lax.axis_size("wide"), lax.axis_size("narrow"))
    count = sizes[0] * sizes[1] if masks is None else len(masks)
    shape = (count,) + array.shape if whole else array.shape
    return pl.pallas_call(
        functools.partial(exchange_kernel, masks, sizes, whole),
        out_shape=jax.ShapeDtypeStruct(shape, array.dtype),
        in_specs=[pl.BlockSpec(memory_space=pltpu.VMEM)],
        out_specs=pl.BlockSpec(memory_space=pltpu.VMEM),
        scratch_shapes=[
            pltpu.SemaphoreType.DMA((count,)),
            pltpu.SemaphoreType.DMA((count,)),
            pltpu.SemaphoreType.DMA,
        ],
        compiler_params=pltpu.CompilerParams(
            collective_id=number, has_side_effects=True, vmem_limit_bytes=32 * MIB
        ),
        name=name,
    )(array)


def stats_kernel(masks, sizes, x_ref, target_ref, log_ref, loss_ref, got_ref, send_sem, recv_sem):
    wides, groups = sizes
    place = Place(wides, groups)
    peers = [place.peer(mask // groups, mask % groups) for mask in masks]
    greet(peers[1:])

    def copy(k):
        return pltpu.make_async_remote_copy(
            src_ref=x_ref,
            dst_ref=got_ref.at[k],
            send_sem=send_sem.at[k],
            recv_sem=recv_sem.at[k],
            device_id=peers[k],
            device_id_type=MESH,
        )

    blocks, height, _ = x_ref.shape
    rows = height // 4
    for k in range(1, blocks):
        copy(k).start()
    got_ref[0] = x_ref[...]
    for k in range(1, blocks):
        copy(k).wait()
    for block in range(blocks):
        parts = [got_ref[k, block ^ k] for k in range(blocks)]
        top = functools.reduce(jnp.maximum, [part[:rows] for part in parts])
        total = sum(part[rows : 2 * rows] * jnp.exp(part[:rows] - top) for part in parts)
        logs = top + jnp.log(total)
        span = pl.ds(block * rows, rows)
        counted = target_ref[span, :] >= 0
        log_ref[span, :] = jnp.where(counted, logs, jnp.inf)
        if block == 0:
            picked = sum(part[2 * rows : 3 * rows] for part in parts)
            loss_ref[...] = jnp.where(counted, logs - picked, 0.0)


def merge_stats(stats, targets):
    sizes = (lax.axis_size("wide"), lax.axis_size("narrow"))
    blocks, height, lanes_here = stats.shape
    rows = height // 4
    vmem = pl.BlockSpec(memory_space=pltpu.VMEM)
    return pl.pallas_call(
        functools.partial(stats_kernel, group_masks(), sizes),
        out_shape=(
            jax.ShapeDtypeStruct((blocks * rows, lanes_here), jnp.float32),
            jax.ShapeDtypeStruct((rows, lanes_here), jnp.float32),
        ),
        in_specs=[vmem, vmem],
        out_specs=(vmem, vmem),
        scratch_shapes=[pltpu.VMEM((blocks,) + stats.shape, jnp.float32)] + mail_sems(blocks),
        compiler_params=pltpu.CompilerParams(
            collective_id=1, has_side_effects=True, vmem_limit_bytes=32 * MIB
        ),
        name="stats_share",
    )(stats, targets)


def put_columns(rows_ref, column_ref):
    turned = rows_ref[...].T
    for place in range(rows_ref.shape[0]):
        column_ref[pl.ds(place * 128, 128), :] = turned[:, place : place + 1]


def as_rows(column):
    count = column.shape[0] // 128
    return jnp.concatenate(
        [column[place * 128 : (place + 1) * 128] for place in range(count)], 1
    ).T


def score_kernel(
    rows_ref, table_ref, target_ref, exps_ref, max_ref, stat_ref, sum_ref, pick_ref, column_ref
):
    tile = pl.program_id(0)
    width = table_ref.shape[0]

    @pl.when(tile == 0)
    def _():
        max_ref[...] = jnp.full_like(max_ref, -jnp.inf)
        sum_ref[...] = jnp.zeros_like(sum_ref)
        pick_ref[...] = jnp.zeros_like(pick_ref)
        put_columns(target_ref, column_ref)

    def step(block, carry):
        rows = pl.ds(pl.multiple_of(block * TOKEN_TILE, TOKEN_TILE), TOKEN_TILE)
        scores = lax.dot_general(
            rows_ref[rows, :],
            table_ref[...],
            (((1,), (1,)), ((), ())),
            preferred_element_type=jnp.float32,
        )
        top = jnp.max(scores, -1, keepdims=True)
        powers = jnp.exp(scores - top)
        exps_ref[rows, :] = powers.astype(jnp.bfloat16)
        total = jnp.sum(powers, -1, keepdims=True)
        columns = lax.broadcasted_iota(jnp.int32, (TOKEN_TILE, width), 1)
        wanted = column_ref[rows, :] - tile * width
        hit = jnp.sum(jnp.where(columns == wanted, scores, 0.0), -1, keepdims=True)
        here = lax.broadcasted_iota(jnp.int32, (TOKEN_TILE, 128), 1) == tile
        max_ref[rows, :] = jnp.where(here, top, max_ref[rows, :])
        sum_ref[rows, :] = jnp.where(here, total, sum_ref[rows, :])
        pick_ref[rows, :] = jnp.where(here, hit, pick_ref[rows, :])
        return carry

    lax.fori_loop(0, rows_ref.shape[0] // TOKEN_TILE, step, 0, unroll=8)

    @pl.when(tile == pl.num_programs(0) - 1)
    def _():
        maxima = max_ref[...]
        top = jnp.max(maxima, -1, keepdims=True)
        total = jnp.sum(sum_ref[...] * jnp.exp(maxima - top), -1, keepdims=True)
        picked = jnp.sum(pick_ref[...], -1, keepdims=True)
        blocks, height, _ = stat_ref.shape
        rows = height // 4
        stat_ref[...] = jnp.zeros_like(stat_ref)
        for number, column in enumerate((top, total, picked)):
            lines = as_rows(column)
            for block in range(blocks):
                stat_ref[block, pl.ds(number * rows, rows), :] = lines[
                    block * rows : (block + 1) * rows
                ]


def vocab_tile(vocab):
    return 1280 if vocab % 1280 == 0 else 640


def head_scores(rows, table, targets, blocks):
    tokens, model = rows.shape
    vocab = table.shape[0]
    width = vocab_tile(vocab)
    stat = pltpu.VMEM((tokens, 128), jnp.float32)
    whole = pl.BlockSpec((tokens, 128), lambda j: (0, 0))
    height = 4 * (tokens // blocks // 128)
    return pl.pallas_call(
        score_kernel,
        grid=(vocab // width,),
        out_shape=(
            jax.ShapeDtypeStruct((tokens, vocab), jnp.bfloat16),
            jax.ShapeDtypeStruct((tokens, 128), jnp.float32),
            jax.ShapeDtypeStruct((blocks, height, 128), jnp.float32),
        ),
        in_specs=[
            pl.BlockSpec((tokens, model), lambda j: (0, 0)),
            pl.BlockSpec((width, model), lambda j: (j, 0)),
            pl.BlockSpec(targets.shape, lambda j: (0, 0)),
        ],
        out_specs=(
            pl.BlockSpec((tokens, width), lambda j: (0, j)),
            whole,
            pl.BlockSpec((blocks, height, 128), lambda j: (0, 0, 0)),
        ),
        scratch_shapes=[stat, stat, pltpu.VMEM((tokens, 1), jnp.int32)],
        compiler_params=pltpu.CompilerParams(vmem_limit_bytes=60 * MIB),
        cost_estimate=pl.CostEstimate(
            flops=3 * tokens * vocab * model,
            bytes_accessed=2 * tokens * vocab,
            transcendentals=tokens * vocab,
        ),
        name="head_scores",
    )(rows, table, targets)


def slope_kernel(
    exps_ref,
    max_ref,
    log_ref,
    target_ref,
    table_ref,
    slope_ref,
    grad_ref,
    total_ref,
    column_ref,
    log_column_ref,
):
    tile = pl.program_id(0)
    width = table_ref.shape[0]

    @pl.when(tile == 0)
    def _():
        total_ref[...] = jnp.zeros_like(total_ref)
        put_columns(target_ref, column_ref)
        put_columns(log_ref, log_column_ref)

    def step(block, carry):
        rows = pl.ds(pl.multiple_of(block * TOKEN_TILE, TOKEN_TILE), TOKEN_TILE)
        here = lax.broadcasted_iota(jnp.int32, (TOKEN_TILE, 128), 1) == tile
        top = jnp.sum(jnp.where(here, max_ref[rows, :], 0.0), -1, keepdims=True)
        scale = jnp.exp(top - log_column_ref[rows, :])
        columns = lax.broadcasted_iota(jnp.int32, (TOKEN_TILE, width), 1)
        wanted = column_ref[rows, :] - tile * width
        probs = exps_ref[rows, :].astype(jnp.float32) * scale
        slope = jnp.where(columns == wanted, probs - 1.0, probs).astype(jnp.bfloat16)
        slope_ref[rows, :] = slope
        total_ref[rows, :] += jnp.dot(slope, table_ref[...], preferred_element_type=jnp.float32)
        return carry

    lax.fori_loop(0, exps_ref.shape[0] // TOKEN_TILE, step, 0, unroll=8)

    @pl.when(tile == pl.num_programs(0) - 1)
    def _():
        grad_ref[...] = total_ref[...].astype(jnp.bfloat16)


def head_slopes(exps, maxima, logs, targets, table):
    tokens, vocab = exps.shape
    model = table.shape[1]
    width = vocab_tile(vocab)
    return pl.pallas_call(
        slope_kernel,
        grid=(vocab // width,),
        out_shape=(
            jax.ShapeDtypeStruct((tokens, vocab), jnp.bfloat16),
            jax.ShapeDtypeStruct((tokens, model), jnp.bfloat16),
        ),
        in_specs=[
            pl.BlockSpec((tokens, width), lambda j: (0, j)),
            pl.BlockSpec((tokens, 128), lambda j: (0, 0)),
            pl.BlockSpec(logs.shape, lambda j: (0, 0)),
            pl.BlockSpec(targets.shape, lambda j: (0, 0)),
            pl.BlockSpec((width, model), lambda j: (j, 0)),
        ],
        out_specs=(
            pl.BlockSpec((tokens, width), lambda j: (0, j)),
            pl.BlockSpec((tokens, model), lambda j: (0, 0)),
        ),
        scratch_shapes=[
            pltpu.VMEM((tokens, model), jnp.float32),
            pltpu.VMEM((tokens, 1), jnp.int32),
            pltpu.VMEM((tokens, 1), jnp.float32),
        ],
        compiler_params=pltpu.CompilerParams(vmem_limit_bytes=60 * MIB),
        cost_estimate=pl.CostEstimate(
            flops=3 * tokens * vocab * model,
            bytes_accessed=4 * tokens * vocab,
            transcendentals=0,
        ),
        input_output_aliases={0: 0},
        name="head_slopes",
    )(exps, maxima, logs, targets, table)


def slots():
    wides, ups = chip_sizes()
    return 32 if wides * ups <= 16 else 16


def one_hot(places, size):
    return (places.reshape(-1, 1) == jnp.arange(size)[None]).astype(jnp.bfloat16)


def token_plan(ids_all, shard_rows):
    chips, tokens = ids_all.shape
    wides, ups = chip_sizes()
    wide, narrow = lax.axis_index("wide"), lax.axis_index("narrow")
    own_core = narrow % 2
    own_chip = wide * ups + narrow // 2
    owner = ids_all // shard_rows
    owner_core = jnp.bitwise_xor(owner % 2, own_core)
    owner_chip = jnp.bitwise_xor(owner // 2, own_chip)
    local = ids_all % shard_rows
    row = lax.broadcasted_iota(jnp.int32, (tokens, tokens), 0)
    column = lax.broadcasted_iota(jnp.int32, (tokens, tokens), 1)
    before = column < row
    alike = ids_all[:, :, None] == ids_all[:, None, :]
    first = ~jnp.any(alike & before[None], 2)
    served = first & (owner_chip == 0) & (owner_core == 0)
    served_rank = times_t(served.astype(jnp.bfloat16), before.astype(jnp.bfloat16)).astype(
        jnp.int32
    )
    half = tokens // 2
    mine = lambda array: lax.dynamic_slice_in_dim(array, own_core * half, half)
    own_first = mine(jnp.min(jnp.where(alike[0], column, tokens), 1))
    same_owner = mine(owner[0])[:, None] == owner[0][None]
    own_rank = jnp.sum(
        (same_owner & first[0][None] & (column[:half] < own_first[:, None])).astype(jnp.int32), 1
    )
    own_block = mine(owner_core[0]) * chips + mine(owner_chip[0])
    most = jnp.max(
        jnp.sum(
            (
                first[:, None, :]
                & (owner[:, None, :] == jnp.arange(2 * chips)[None, :, None])
            ).astype(jnp.int32),
            2,
        )
    )
    rounds = (most + slots() - 1) // slots()

    def plan(turn):
        slot = jnp.arange(slots())[None, :, None] + turn * slots()
        chosen = served[:, None, :] & (served_rank[:, None, :] == slot)
        slot_rows = jnp.sum(jnp.where(chosen, local[:, None, :] + 1, 0), 2) - 1
        inside = own_rank - turn * slots()
        valid = (inside >= 0) & (inside < slots())
        own_slots = jnp.where(valid, own_block * slots() + inside, -1)
        return slot_rows, one_hot(own_slots, 2 * chips * slots())

    return plan, rounds


def later_rounds(rounds, turn, total):
    return lax.while_loop(
        lambda state: state[0] < rounds,
        lambda state: (state[0] + 1, state[1] + turn(state[0])),
        (jnp.ones((), jnp.int32), total),
    )[1]


def norm_kernel(sizes, tile, table_ref, passed_ref, slot_ref, rows_ref, small_ref, matrix_ref, scalar_ref, *refs):
    total_ref, sum_ref, sent_ref, got_ref, send_sem, recv_sem = refs
    wides, groups = sizes
    place = Place(wides, groups)
    count = wides * groups
    barrier = pltpu.get_barrier_semaphore()
    for k in range(1, count):
        pl.semaphore_signal(
            barrier, inc=1, device_id=place.peer(k // groups, k % groups), device_id_type=MESH
        )
    width = table_ref.shape[1]

    def step(i, squares):
        span = pl.ds(pl.multiple_of(i * tile, 8), tile)
        row = lax.broadcasted_iota(jnp.int32, (tile, slot_ref.shape[1]), 0) + i * tile
        hot = (row == slot_ref[...]).astype(jnp.float32).astype(jnp.bfloat16)
        total = table_ref[span, :] + passed_ref[span, :].astype(jnp.float32)
        total = total + plain(hot, rows_ref[...])
        total_ref[span, :] = total
        return squares + jnp.sum((total * total).reshape(tile // 8, 8, width), 0)

    squares = lax.fori_loop(
        0, table_ref.shape[0] // tile, step, jnp.zeros((8, width), jnp.float32)
    )
    own = jnp.sum(squares + matrix_ref[...], keepdims=True)
    lane = lax.broadcasted_iota(jnp.int32, (8, 128), 1)
    sent_ref[...] = scalar_ref[...] + jnp.where(lane == 2, own, 0.0)
    pl.semaphore_wait(barrier, count - 1)

    def copy(k):
        return pltpu.make_async_remote_copy(
            src_ref=sent_ref,
            dst_ref=got_ref.at[k],
            send_sem=send_sem.at[k],
            recv_sem=recv_sem.at[k],
            device_id=place.peer(k // groups, k % groups),
            device_id_type=MESH,
        )

    for k in range(1, count):
        copy(k).start()
    got_ref[0] = sent_ref[...]
    small = small_ref[...]
    copied = jnp.sum(small * small, keepdims=True)
    for k in range(1, count):
        copy(k).wait()
    both = got_ref[...]
    total = jnp.zeros((8, 128), jnp.float32)
    order = device_order(place, wides, groups, both)
    for one in order:
        total = total + one
    sum_ref[...] = total + jnp.where(lane == 2, copied, 0.0)


def device_order(place, wides, groups, blocks):
    flat = [blocks[k] for k in range(wides * groups)]
    sides = [(groups << bit, place.wide // (1 << bit) % 2) for bit in range(log_two(wides))]
    sides += [(1 << bit, place.narrow // (1 << bit) % 2) for bit in range(log_two(groups))]
    for step, side in sides:
        one = side == 1
        flat = [jnp.where(one, flat[k ^ step], flat[k]) for k in range(len(flat))]
    return flat


def table_norm(table_sum, passed, slot_rows, rows, small, matrix_squares, scalars):
    sizes = (lax.axis_size("wide"), lax.axis_size("narrow"))
    count = sizes[0] * sizes[1]
    height, width = table_sum.shape
    tile = next(size for size in (400, 80, 16) if height % size == 0)
    vmem = pl.BlockSpec(memory_space=pltpu.VMEM)
    return pl.pallas_call(
        functools.partial(norm_kernel, sizes, tile),
        out_shape=(
            jax.ShapeDtypeStruct((height, width), jnp.float32),
            jax.ShapeDtypeStruct((8, 128), jnp.float32),
        ),
        in_specs=[vmem] * 7,
        out_specs=(vmem, vmem),
        scratch_shapes=[
            pltpu.VMEM((8, 128), jnp.float32),
            pltpu.VMEM((count, 8, 128), jnp.float32),
        ]
        + mail_sems(count),
        compiler_params=pltpu.CompilerParams(
            collective_id=3, has_side_effects=True, vmem_limit_bytes=62 * MIB
        ),
        name="table_norm",
    )(table_sum, passed, slot_rows.reshape(1, -1), rows, small, matrix_squares, scalars)


def upper_blocks(count):
    return [(i, j) for i in range(count) for j in range(i, count)]


def muon_kernel(lane_bits, *refs):
    core, _, y_bits, _ = lane_bits
    low_refs, factor_ref, table_refs = refs[:4], refs[4], refs[5:9]
    rest_out, size_out, table_outs = *refs[9:11], refs[11:14]
    gram, sent, got, back, full, total, half, low_a, low_b, low_c, send_sem, recv_sem = refs[14:26]
    in_tiles, out_tiles, in_sem, out_sem = refs[26:]
    width = full.shape[0]
    block = gram.shape[-1]
    places = upper_blocks(width // block)
    greet([neighbour(bit) for bit in [core] + y_bits])
    mail = Mail(send_sem, recv_sem, lane_bits)

    def adam_flow():
        tile = in_tiles.shape[2]
        count = table_refs[0].shape[0] // tile

        def loads(number):
            span = pl.ds(number * tile, tile)
            return [
                pltpu.make_async_copy(
                    ref.at[span], in_tiles.at[number % 2, kind], in_sem.at[number % 2, kind]
                )
                for kind, ref in enumerate(table_refs)
            ]

        def stores(number):
            span = pl.ds(number * tile, tile)
            return [
                pltpu.make_async_copy(
                    out_tiles.at[number % 2, kind], ref.at[span], out_sem.at[number % 2, kind]
                )
                for kind, ref in enumerate(table_outs)
            ]

        for copy in loads(0):
            copy.start()
        yield mail.now
        for number in range(count):
            if number + 1 < count:
                for copy in loads(number + 1):
                    copy.start()
            for copy in loads(number):
                copy.wait()
            if number >= 2:
                for copy in stores(number - 2):
                    copy.wait()
            weight, moment, square, grad = (in_tiles[number % 2, kind] for kind in range(4))
            results = adam_step(
                weight, moment, square, grad * factor_ref[0:1, 0:1], EMBED_RATE, DECAY
            )
            for kind, result in enumerate(results):
                out_tiles[number % 2, kind] = result
            for copy in stores(number):
                copy.start()
            yield mail.spend(1.2)
        for number in range(max(count - 2, 0), count):
            for copy in stores(number):
                copy.wait()

    mail.run([muon_flow(mail, lane_bits, refs, places), adam_flow()])
    mail.close()
    for number in range(4):

        def put_out(i, j, piece, number=number):
            rest_out[number, pl.ds(i * block, block), pl.ds(j * block, block)] = piece.astype(
                jnp.bfloat16
            )

        unpack(places, lambda place: back[number, place].astype(jnp.float32), put_out)


def unpack(places, source, target):
    for place, (i, j) in enumerate(places):
        piece = source(place)
        target(i, j, piece)
        if i != j:
            target(j, i, piece.T)


def muon_flow(mail, lane_bits, refs, places):
    core, _, y_bits, _ = lane_bits
    low_refs, size_out = refs[:4], refs[10]
    gram, sent, got, back, full, total, half, low_a, low_b, low_c = refs[14:24]
    width = full.shape[0]
    block = gram.shape[-1]
    narrow = lax.axis_index("narrow")
    own_core, own_up = narrow % 2, (narrow // 2) % 2
    own = 2 * own_core + own_up
    for number, low_ref in enumerate(low_refs):
        for place, (i, j) in enumerate(places):
            product = lax.dot_general(
                low_ref[:, i * block : (i + 1) * block],
                low_ref[:, j * block : (j + 1) * block],
                (((0,), (0,)), ((), ())),
                preferred_element_type=jnp.float32,
            )
            gram[number, place] = product
    for slot in range(2):
        sent[slot] = gram[2 * (1 - own_core) + slot].astype(jnp.bfloat16)
    copy = mail.post(sent.at[pl.ds(0, 2)], got.at[pl.ds(0, 2)], core)
    yield mail.due
    mail.take(copy)

    def add(number, slot):
        for place in range(len(places)):
            gram[number, place] += got[slot, place].astype(jnp.float32)

    def pass_on(number, slot, bit):
        sent[slot] = gram[number].astype(jnp.bfloat16)
        return mail.post(sent.at[slot], got.at[slot], bit)

    other_up = 2 * own_core + 1 - own_up
    if y_bits:
        add(other_up, 1 - own_up)
        over_y = pass_on(other_up, 2, y_bits[0])
        add(own, own_up)
        yield mail.due
        mail.take(over_y)
        add(own, 2)
    for level, bit in enumerate(y_bits[1:]):
        copy = pass_on(own, 3 + level, bit)
        yield mail.due
        mail.take(copy)
        add(own, 3 + level)

    def spans(i, j):
        return pl.ds(i * block, block), pl.ds(j * block, block)

    def put_full(i, j, piece):
        full[spans(i, j)] = piece

    unpack(places, lambda place: gram[own, place], put_full)
    diagonal = lax.broadcasted_iota(jnp.int32, (block, block), 0) == lax.broadcasted_iota(
        jnp.int32, (block, block), 1
    )
    trace = jnp.zeros((1, 1), jnp.float32)
    for i in range(width // block):
        trace = trace + jnp.sum(jnp.where(diagonal, full[spans(i, i)], 0.0), keepdims=True)
    magnitude = jnp.sqrt(trace) + 1e-07
    inverse = 1.0 / magnitude

    def rows(step):
        def body(i, carry):
            step(pl.ds(pl.multiple_of(i * block, block), block))
            return carry

        lax.fori_loop(0, width // block, body, 0)

    def times(left, right, span):
        return jnp.dot(left[span, :], right[...], preferred_element_type=jnp.float32)

    def start(span):
        scaled = full[span, :] * (inverse * inverse)
        full[span, :] = scaled
        low_a[span, :] = scaled.astype(jnp.bfloat16)

    rows(start)
    scale = NS_A
    for cycle_no in range(NS_STEPS):

        def rest_step(span):
            rest = NS_B * full[span, :] + NS_C * times(low_a, low_a, span)
            low_b[span, :] = rest.astype(jnp.bfloat16)
            if cycle_no == 0:
                total[span, :] = rest
            else:
                total[span, :] = NS_A * total[span, :] + scale * rest

        rows(rest_step)
        if cycle_no:

            def total_step(span):
                total[span, :] += times(low_c, low_b, span)

            rows(total_step)
            scale = scale * NS_A
        if cycle_no < NS_STEPS - 1:

            def keep_total(span):
                low_c[span, :] = total[span, :].astype(jnp.bfloat16)

            def half_step(span):
                half[span, :] = NS_A * full[span, :] + times(low_a, low_b, span)

            def full_step(span):
                value = half[span, :]
                low_a[span, :] = value.astype(jnp.bfloat16)
                full[span, :] = NS_A * value + times(low_a, low_b, span)

            def low_step(span):
                low_a[span, :] = full[span, :].astype(jnp.bfloat16)

            rows(keep_total)
            rows(half_step)
            rows(full_step)
            rows(low_step)

    for place, (i, j) in enumerate(places):
        back[own, place] = (total[spans(i, j)] * inverse).astype(jnp.bfloat16)
    lane = lax.broadcasted_iota(jnp.int32, (8, 128), 1)
    size_out[own] = jnp.where(lane >= 0, inverse, 0.0)
    mail.post(back.at[own], back.at[own], core)
    mail.post(size_out.at[own], size_out.at[own], core)
    if y_bits:
        over_size = mail.post(size_out.at[own], size_out.at[own], y_bits[0])
        over_y = mail.post(back.at[own], back.at[own], y_bits[0])
        yield mail.due
        mail.take(over_y)
        mail.take(over_size)
        mail.post(back.at[other_up], back.at[other_up], core)
        mail.post(size_out.at[other_up], size_out.at[other_up], core)


def muon_factors(lows, factor, table):
    width = lows[0].shape[1]
    block = 256
    count = len(upper_blocks(width // block))
    lane_bits = lanes()
    extra = max(len(lane_bits[2]) - 1, 0)
    vmem = pl.BlockSpec(memory_space=pltpu.VMEM)
    square = (width, width)
    height = table[0].shape[0]
    tile = next(size for size in (160, 80, 40, 16, 8) if height % size == 0)
    any_space = pl.BlockSpec(memory_space=pl.ANY)
    whole = jax.ShapeDtypeStruct(table[0].shape, jnp.float32)
    rests, sizes, *table_next = pl.pallas_call(
        functools.partial(muon_kernel, lane_bits),
        out_shape=(
            jax.ShapeDtypeStruct((4,) + square, jnp.bfloat16),
            jax.ShapeDtypeStruct((4, 8, 128), jnp.float32),
            whole,
            whole,
            whole,
        ),
        in_specs=[vmem] * 5 + [any_space] * 4,
        out_specs=(vmem, vmem, any_space, any_space, any_space),
        scratch_shapes=[
            pltpu.VMEM((4, count, block, block), jnp.float32),
            pltpu.VMEM((3 + extra, count, block, block), jnp.bfloat16),
            pltpu.VMEM((3 + extra, count, block, block), jnp.bfloat16),
            pltpu.VMEM((4, count, block, block), jnp.bfloat16),
        ]
        + [pltpu.VMEM(square, jnp.float32) for _ in range(3)]
        + [pltpu.VMEM(square, jnp.bfloat16) for _ in range(3)]
        + mail_sems(32)
        + [
            pltpu.VMEM((2, 4, tile, width), jnp.float32),
            pltpu.VMEM((2, 3, tile, width), jnp.float32),
            pltpu.SemaphoreType.DMA((2, 4)),
            pltpu.SemaphoreType.DMA((2, 3)),
        ],
        compiler_params=pltpu.CompilerParams(
            collective_id=9, has_side_effects=True, vmem_limit_bytes=56 * MIB
        ),
        name="muon_factors",
    )(*lows, jnp.full((8, 128), factor), *table)
    return rests, sizes[:, 0, 0], table_next


def on_device(
    token_ids,
    targets,
    joint_weight,
    output_weight,
    expand_weight,
    reduce_weight,
    joint_velocity,
    output_velocity,
    expand_velocity,
    reduce_velocity,
    embedding,
    embed_moment,
    embed_square,
    positions,
    position_moment,
    position_square,
    norm_gains,
    gain_moment,
    gain_square,
    biases,
    bias_moment,
    bias_square,
):
    core, x_bits, y_bits, z_bits = lanes()
    groups = lax.axis_size("narrow")
    wides = lax.axis_size("wide")
    across = 1 << len(x_bits)
    model_width = embedding.shape[1]
    shard_rows = embedding.shape[0]
    tokens = token_ids.shape[0] * LENGTH
    bias_rows = biases.reshape(-1, model_width)

    own_rows = embedding.astype(jnp.bfloat16)
    labels = jnp.concatenate([token_ids.reshape(-1, 128), targets.reshape(-1, 128)])
    spare = -labels.shape[0] % 8
    labels = exchange(jnp.pad(labels, ((0, spare), (0, 0))), 0, "label_share")
    ids_all = labels[:, : tokens // 128].reshape(-1, tokens)
    lines = tokens // 128
    own_block = lax.axis_index("wide") * groups + lax.axis_index("narrow")
    wides, ups = chip_sizes()
    pairs = ids_all.reshape(wides, ups, 2, tokens)
    other_first = lax.axis_index("narrow") % 2 == 1
    ids_chips = jnp.where(other_first, lax.rev(pairs, (2,)), pairs).reshape(wides * ups, -1)
    plan, rounds = token_plan(ids_chips, shard_rows)

    def serve(slot_rows):
        served = one_hot(slot_rows, shard_rows)
        return plain(served, own_rows).astype(jnp.bfloat16).reshape(-1, slots(), model_width)

    masters = (joint_weight, output_weight, expand_weight, reduce_weight)
    served, wanted = plan(0)
    token_rows = serve(served)
    sent_rows, token_rows = lax.optimization_barrier((own_rows, token_rows))
    tables = [sent_rows]
    for bit in x_bits:
        tables = tables + [swap(part, bit) for part in tables]
    weights, token_rows = load_all([master.astype(jnp.bfloat16) for master in masters], token_rows)

    def fetch(turn):
        more, places = plan(turn)
        got = swap_rows(serve(more))
        return plain(places, jnp.stack([got, swap(got, core)]).reshape(-1, model_width))

    embedded = later_rounds(rounds, fetch, plain(wanted, token_rows.reshape(-1, model_width)))

    block_masks = jnp.array(group_masks())
    targets_group = labels[block_masks, lines : 2 * lines].reshape(-1, 128)
    table_mask = groups * (across - 1) + 1
    differ = jnp.bitwise_xor(targets_group // shard_rows, own_block)
    is_owned = (targets_group >= 0) & (jnp.bitwise_and(differ, ~table_mask) == 0)
    place = (differ % 2) * across + (differ // groups) % across
    rows_targets = jnp.where(is_owned, place * shard_rows + targets_group % shard_rows, -1)
    final_low, *saved = layer_forward(embedded, positions, norm_gains, bias_rows, weights)
    group_rows, table = spread(final_low, tables)
    blocks = len(group_masks())
    exps, maxima, stats = head_scores(group_rows, table, rows_targets, blocks)
    logs, losses = merge_stats(stats, targets_group)
    loss_part = jnp.sum(losses)
    slopes, final_part = head_slopes(exps, maxima, logs, rows_targets, table)
    final_grad, table_sum, passed = head_back(
        final_part.reshape(-1, tokens, model_width), slopes, group_rows
    )
    for bit in reversed(x_bits):
        passed = swap(passed, bit)
        if bit != x_bits[0]:
            table_sum = table_sum + passed.astype(jnp.float32)
            half = table_sum.shape[0] // 2
            table_sum, passed = table_sum[:half], table_sum[half:].astype(jnp.bfloat16)
    (front, expand_sum, reduce_sum), small, row_sums, squares, low_grad = back_reduce(
        final_grad, norm_gains, bias_rows, saved, weights, wanted
    )
    count_part = jnp.sum((targets >= 0).astype(jnp.float32))

    def bundle(places):
        both = outer_sum(places, low_grad).astype(jnp.bfloat16)
        both = both.reshape(2, -1, slots(), model_width)
        other = swap(both[1], core)
        return (both[0].astype(jnp.float32) + other.astype(jnp.float32)).astype(jnp.bfloat16)

    joint_rows = joint_weight.shape[0]
    def give(turn):
        more, places = plan(turn)
        got = swap_rows(bundle(places)).reshape(-1, model_width)
        return outer_sum(one_hot(more, shard_rows), got)

    table_sum = later_rounds(rounds, give, table_sum)
    places = jnp.stack([loss_part, count_part]).reshape(1, 2)
    table_sum, scalars = table_norm(
        table_sum,
        passed,
        served,
        row_sums.reshape(-1, model_width),
        small,
        squares,
        jnp.pad(places, ((0, 7), (0, 126))),
    )
    matrix_total = [
        part.astype(jnp.float32)
        for part in (front[:joint_rows], front[joint_rows:], expand_sum, reduce_sum)
    ]
    small = small[: 14 + LENGTH]
    loss_sum, loss_count, squares = scalars[0, 0], scalars[0, 1], scalars[0, 2]
    gain_grad, position_grad = small[:3], small[14:]
    bias_grad = small[3:14].reshape(-1)
    grad_norm = jnp.sqrt(squares) / loss_count
    factor = jnp.minimum(1.0, CLIP / (grad_norm + 1e-06)) / loss_count
    previous = (joint_velocity, output_velocity, expand_velocity, reduce_velocity)
    carried = tuple(
        (MOMENTUM * before + gradient * factor for before, gradient in zip(previous, matrix_total))
    )
    lows = [moment.astype(jnp.bfloat16) for moment in carried]
    rests, inverses, table_out = muon_factors(
        lows, factor, (embedding, embed_moment, embed_square, table_sum)
    )
    updated = []
    for number, (master, moment) in enumerate(zip(masters, carried)):
        orth = moment * (NS_A**NS_STEPS * inverses[number]) + plain(
            lows[number], rests[number]
        )
        shape_factor = math.sqrt(max(1.0, master.shape[0] * groups / master.shape[1]))
        updated.append(master * (1 - MUON_RATE * DECAY) - MUON_RATE * shape_factor * orth)
    place_out = adam_step(
        positions, position_moment, position_square, position_grad * factor, PLACE_RATE, DECAY
    )
    gain_out = adam_step(norm_gains, gain_moment, gain_square, gain_grad * factor, SMALL_RATE, 0.0)
    bias_out = adam_step(biases, bias_moment, bias_square, bias_grad * factor, SMALL_RATE, 0.0)
    return (
        loss_sum,
        loss_count,
        grad_norm,
        updated[0],
        updated[1],
        updated[2],
        updated[3],
        carried[0],
        carried[1],
        carried[2],
        carried[3],
        table_out[0],
        table_out[1],
        table_out[2],
        place_out[0],
        place_out[1],
        place_out[2],
        gain_out[0],
        gain_out[1],
        gain_out[2],
        bias_out[0],
        bias_out[1],
        bias_out[2],
    )


def solution(mesh):
    in_specs = (
        P(("wide", "narrow"), None),
        P(("wide", "narrow"), None),
        P("narrow", None),
        P("narrow", None),
        P("narrow", None),
        P("narrow", None),
        P("narrow", None),
        P("narrow", None),
        P("narrow", None),
        P("narrow", None),
        P(("wide", "narrow"), None),
        P(("wide", "narrow"), None),
        P(("wide", "narrow"), None),
        P(),
        P(),
        P(),
        P(),
        P(),
        P(),
        P(),
        P(),
        P(),
    )
    out_specs = (
        P(),
        P(),
        P(),
        P("narrow", None),
        P("narrow", None),
        P("narrow", None),
        P("narrow", None),
        P("narrow", None),
        P("narrow", None),
        P("narrow", None),
        P("narrow", None),
        P(("wide", "narrow"), None),
        P(("wide", "narrow"), None),
        P(("wide", "narrow"), None),
        P(),
        P(),
        P(),
        P(),
        P(),
        P(),
        P(),
        P(),
        P(),
    )
    return jax.shard_map(
        on_device, mesh=mesh, in_specs=in_specs, out_specs=out_specs, check_vma=False
    )
```

```python
import functools
import math

import jax
import jax.numpy as jnp
from jax import lax
from jax.experimental import pallas as pl
from jax.experimental.pallas import tpu as pltpu
from jax.sharding import PartitionSpec as P

HEADS = 12
HEAD = 64
LENGTH = 64
NS_STEPS = 3
STEP = 10


HIGH = lax.Precision.HIGHEST
EPS = 1e-05
CLIP = 0.05
MOMENTUM = 0.95
MUON_RATE = 0.5
DECAY = 0.1
BETA_ONE = 0.9
BETA_TWO = 0.999
EMBED_RATE = 0.02
PLACE_RATE = 0.1
SMALL_RATE = 0.2
NS_A = 3.4445
NS_B = -4.775
NS_C = 2.0315
MESH = pl.DeviceIdType.MESH
MIB = 1 << 20
TOKEN_TILE = 256


def times_t(left, right):
    return lax.dot_general(
        left, right, (((1,), (1,)), ((), ())), preferred_element_type=jnp.float32
    )


def outer_sum(left, right):
    return lax.dot_general(
        left, right, (((0,), (0,)), ((), ())), preferred_element_type=jnp.float32
    )


def plain(left, right):
    return jnp.dot(left, right, preferred_element_type=jnp.float32)


def norm_forward(stream, gain, shift):
    centred = stream - jnp.mean(stream, -1, keepdims=True)
    inverse = lax.rsqrt(jnp.mean(centred * centred, -1, keepdims=True) + EPS)
    normed = centred * inverse
    return (normed * gain + shift, normed, inverse)


def norm_backward(upstream, normed, inverse, gain):
    scaled = upstream * gain
    inner = inverse * (
        scaled
        - jnp.mean(scaled, -1, keepdims=True)
        - normed * jnp.mean(scaled * normed, -1, keepdims=True)
    )
    return (
        inner,
        jnp.sum(upstream * normed, 0, keepdims=True),
        jnp.sum(upstream, 0, keepdims=True),
    )


def gelu_tanh(values):
    return jax.nn.gelu(values, approximate=True)


def column_sum(values):
    return jnp.sum(values.astype(jnp.float32), 0, keepdims=True)


def pair_masks(tokens):
    first = lax.broadcasted_iota(jnp.int32, (tokens, 2 * HEAD), 1) < HEAD
    row = lax.broadcasted_iota(jnp.int32, (tokens, tokens), 0)
    column = lax.broadcasted_iota(jnp.int32, (tokens, tokens), 1)
    return first, (row // LENGTH == column // LENGTH) & (column <= row)


def head_probs(queries, key_heads, seen):
    scores = times_t(queries, key_heads) * HEAD ** (-0.5)
    scores = jnp.where(seen, scores, -1000000000.0)
    powers = jnp.exp(scores - jnp.max(scores, -1, keepdims=True))
    return powers * (1.0 / jnp.sum(powers, -1, keepdims=True))


def forward_kernel(
    x_ref,
    place_ref,
    gain_ref,
    bias_ref,
    joint_hbm,
    output_hbm,
    expand_hbm,
    reduce_hbm,
    low_ref,
    normed_ref,
    inverse_ref,
    joint_out,
    context_ref,
    upward_ref,
    joint_ref,
    output_ref,
    expand_ref,
    reduce_ref,
    load_sem,
):
    pairs = ((joint_hbm, joint_ref), (output_hbm, output_ref), (expand_hbm, expand_ref), (reduce_hbm, reduce_ref))
    loads = [
        pltpu.make_async_copy(source, target, load_sem.at[number])
        for number, (source, target) in enumerate(pairs)
    ]
    for load in loads:
        load.start()
    tokens, width = x_ref.shape

    def norm(number, stream):
        result, normed, inverse = norm_forward(
            stream, gain_ref[number : number + 1, :], bias_ref[number : number + 1, :]
        )
        normed_ref[number] = normed
        inverse_ref[number] = jnp.broadcast_to(inverse, (tokens, 128))
        return result.astype(jnp.bfloat16)

    stream = x_ref[...] + jnp.concatenate([place_ref[...]] * (tokens // LENGTH), 0)
    first_low = norm(0, stream)
    loads[0].wait()
    for part in range(3):
        span = pl.ds(part * width, width)
        result = times_t(first_low, joint_ref[span, :])
        if part != 1:
            row = 3 if part == 0 else 4
            result = result + bias_ref[row : row + 1, :]
        joint_out[:, span] = result.astype(jnp.bfloat16)
    first, seen = pair_masks(tokens)
    zero = jnp.zeros((), jnp.bfloat16)
    for pair in range(HEADS // 2):
        queries = joint_out[:, pl.ds(pair * 128, 128)]
        key_heads = joint_out[:, pl.ds(width + pair * 128, 128)]
        values = joint_out[:, pl.ds(2 * width + pair * 128, 128)]
        parts = []
        for mine in (first, ~first):
            probs = head_probs(jnp.where(mine, queries, zero), key_heads, seen)
            parts.append(plain(probs.astype(jnp.bfloat16), values))
        context_ref[:, pl.ds(pair * 128, 128)] = jnp.where(first, *parts).astype(jnp.bfloat16)
    loads[1].wait()
    stream = stream + times_t(context_ref[...], output_ref[...]) + bias_ref[5:6, :]
    second_low = norm(1, stream)
    stream = stream + bias_ref[6:7, :]
    loads[2].wait()
    loads[3].wait()
    for part in range(expand_ref.shape[0] // width):
        span = pl.ds(part * width, width)
        upward = times_t(second_low, expand_ref[span, :]) + bias_ref[7 + part : 8 + part, :]
        upward_ref[:, span] = upward
        stream = stream + plain(gelu_tanh(upward).astype(jnp.bfloat16), reduce_ref[span, :])
    low_ref[...] = norm(2, stream)


def layer_forward(embedded, positions, norm_gains, bias_rows, weights):
    tokens, width = embedded.shape
    vmem, any_space = pl.BlockSpec(memory_space=pltpu.VMEM), pl.BlockSpec(memory_space=pl.ANY)
    shape = jax.ShapeDtypeStruct
    hidden = weights[2].shape[0]
    return pl.pallas_call(
        forward_kernel,
        out_shape=(
            shape((tokens, width), jnp.bfloat16),
            shape((3, tokens, width), jnp.float32),
            shape((3, tokens, 128), jnp.float32),
            shape((tokens, 3 * width), jnp.bfloat16),
            shape((tokens, width), jnp.bfloat16),
            shape((tokens, hidden), jnp.float32),
        ),
        in_specs=[vmem] * 4 + [any_space] * 4,
        out_specs=[vmem] * 6,
        scratch_shapes=[pltpu.VMEM(w.shape, w.dtype) for w in weights]
        + [pltpu.SemaphoreType.DMA((4,))],
        compiler_params=pltpu.CompilerParams(vmem_limit_bytes=63 * MIB),
        name="layer_forward",
    )(embedded, positions, norm_gains, bias_rows, *weights)


def gelu_slope(values):
    inner = math.sqrt(2.0 / math.pi)
    squared = values * values
    bent = jnp.tanh(inner * (values + 0.044715 * squared * values))
    return 0.5 * values * (1.0 + bent), 0.5 * (1.0 + bent) + 0.5 * values * (
        1.0 - bent * bent
    ) * (inner * (1.0 + 3 * 0.044715 * squared))


def backward_flow(ins, outs, scratch):
    (final_ref, gain_ref, bias_ref, normed_ref, inverse_ref, joint_in, context_ref, upward_ref) = ins
    (stream_ref, small_ref, front_ref, expand_out, reduce_out) = outs
    (joint_ref, output_ref, expand_ref, reduce_ref, waits) = scratch
    hold = reduce_ref
    tokens, width = final_ref.shape
    _, ups, height, _ = front_ref.shape
    groups = 2 * ups

    def put(ref, start, grad):
        for group in range(groups):
            low = max(group * height, start)
            high = min((group + 1) * height, start + grad.shape[0])
            if low < high:
                ref[group % 2, group // 2, pl.ds(low - group * height, high - low), :] = grad[
                    low - start : high - start
                ]

    def gain(number):
        return gain_ref[number : number + 1, :]

    def normed_low(number):
        return (normed_ref[number] * gain(number) + bias_ref[number : number + 1, :]).astype(
            jnp.bfloat16
        )

    def back(number, upstream):
        inner, gain_row, shift_row = norm_backward(
            upstream, normed_ref[number], inverse_ref[number][:, :1], gain(number)
        )
        small_ref[number : number + 1, :] = gain_row
        small_ref[3 + number : 4 + number, :] = shift_row
        return inner

    small_ref[...] = jnp.zeros_like(small_ref)
    back_f = back(2, final_ref[...])
    down = back_f.astype(jnp.bfloat16)
    small_ref[9:10, :] = column_sum(down)
    parts = expand_ref.shape[0] // width
    for part in range(parts):
        active, _ = gelu_slope(upward_ref[:, pl.ds(part * width, width)])
        put(reduce_out, part * width, outer_sum(active.astype(jnp.bfloat16), down).astype(jnp.bfloat16))
    yield 0.0
    second_low = normed_low(1)
    second_grad = jnp.zeros((tokens, width), jnp.float32)
    waits[2].wait()
    waits[3].wait()
    for part in range(parts):
        span = pl.ds(part * width, width)
        _, slope = gelu_slope(upward_ref[:, span])
        upward_grad = (times_t(down, reduce_ref[span, :]) * slope).astype(jnp.bfloat16)
        small_ref[10 + part : 11 + part, :] = column_sum(upward_grad)
        second_grad = second_grad + plain(upward_grad, expand_ref[span, :])
        put(expand_out, part * width, outer_sum(upward_grad, second_low).astype(jnp.bfloat16))
        yield 2.3
    mid_grad = back_f + back(1, second_grad)
    stream_ref[...] = mid_grad
    attn_grad = mid_grad.astype(jnp.bfloat16)
    small_ref[8:9, :] = column_sum(attn_grad)
    waits[1].wait()
    last = pl.ds(3 * tokens, tokens)
    hold[last, :] = plain(attn_grad, output_ref[...]).astype(jnp.bfloat16)
    output_grad = outer_sum(attn_grad, context_ref[...]).astype(jnp.bfloat16)
    rows = width // groups
    joint_rows = height - rows
    for group in range(groups):
        front_ref[group % 2, group // 2, pl.ds(joint_rows, rows), :] = output_grad[
            group * rows : (group + 1) * rows
        ]
    yield 2.0
    first, seen = pair_masks(tokens)
    zero = jnp.zeros((), jnp.bfloat16)
    for pair in range(HEADS // 2):
        spans = [pl.ds(part * width + pair * 128, 128) for part in range(3)]
        queries, key_heads, values = (joint_in[:, span] for span in spans)
        upstream = hold[last, spans[0]]
        parts = []
        for mine in (first, ~first):
            probs = head_probs(jnp.where(mine, queries, zero), key_heads, seen)
            probs_grad = times_t(jnp.where(mine, upstream, zero), values)
            score_grad = (
                probs * (probs_grad - jnp.sum(probs * probs_grad, -1, keepdims=True))
            ).astype(jnp.bfloat16)
            parts.append(
                (
                    plain(score_grad, key_heads) * HEAD ** (-0.5),
                    outer_sum(score_grad, queries) * HEAD ** (-0.5),
                    outer_sum(probs.astype(jnp.bfloat16), upstream),
                )
            )
        for part, (one, two) in enumerate(zip(*parts)):
            hold[pl.ds(part * tokens, tokens), spans[0]] = jnp.where(first, one, two).astype(
                jnp.bfloat16
            )
        yield 1.5
    first_low = normed_low(0)
    waits[0].wait()
    first_grad = jnp.zeros((tokens, width), jnp.float32)
    for part in range(3):
        span = pl.ds(part * width, width)
        piece = hold[pl.ds(part * tokens, tokens), :]
        if part != 1:
            row = 6 if part == 0 else 7
            small_ref[row : row + 1, :] = column_sum(piece)
        first_grad = first_grad + plain(piece, joint_ref[span, :])
        grad = outer_sum(piece, first_low).astype(jnp.bfloat16)
        for group in range(groups):
            start = max(group * joint_rows, part * width)
            end = min((group + 1) * joint_rows, (part + 1) * width)
            if start < end:
                front_ref[
                    group % 2, group // 2, pl.ds(start - group * joint_rows, end - start), :
                ] = grad[start - part * width : end - part * width]
        yield 1.5
    stream = stream_ref[...] + back(0, first_grad)
    stream_ref[...] = stream
    placed = stream[:LENGTH]
    for sequence in range(1, tokens // LENGTH):
        placed = placed + stream[sequence * LENGTH : (sequence + 1) * LENGTH]
    small_ref[14 : 14 + LENGTH, :] = placed


def adam_step(weight, moment, square, gradient, rate, decay):
    moment = BETA_ONE * moment + (1 - BETA_ONE) * gradient
    square = BETA_TWO * square + (1 - BETA_TWO) * gradient * gradient
    unbiased = moment / (1 - BETA_ONE**STEP)
    spread = square / (1 - BETA_TWO**STEP)
    return (
        weight - rate * (unbiased / (jnp.sqrt(spread) + 1e-08) + decay * weight),
        moment,
        square,
    )


def log_two(size):
    return size.bit_length() - 1


def lanes():
    wide, narrow = lax.axis_size("wide"), lax.axis_size("narrow")
    across = wide // 4
    x_bits = [("wide", 1 << i) for i in range(log_two(across))]
    z_bits = [("wide", across << i) for i in range(log_two(wide // across))]
    y_bits = [("narrow", 2 << i) for i in range(log_two(narrow // 2))]
    return ("narrow", 1), x_bits, y_bits, z_bits


def swap(array, bit):
    axis, mask = bit
    return lax.ppermute(array, axis, [(i, i ^ mask) for i in range(lax.axis_size(axis))])


def side(bit):
    axis, mask = bit
    return (lax.axis_index(axis) // mask) % 2


def join(mine, other, bit, dim=0):
    own = side(bit)
    return jnp.where(
        own == 0, jnp.concatenate([mine, other], dim), jnp.concatenate([other, mine], dim)
    )


def halves(array, bit):
    own = side(bit)
    half = array.shape[0] // 2
    keep = lax.dynamic_slice_in_dim(array, own * half, half)
    send = lax.dynamic_slice_in_dim(array, (1 - own) * half, half)
    return keep, send


def group_bits():
    _, _, y_bits, z_bits = lanes()
    return z_bits + y_bits


SPREAD_ORDERS = ("nyf", "fny", "nfy", "fyn")
COLLECT_ORDERS = ("yfn", "ynf", "nyf", "fyn")


def routes(rows, orders):
    _, _, y_bits, z_bits = lanes()
    kinds = {"y": y_bits, "n": z_bits[:1], "f": z_bits[1:]}
    size = rows // len(orders)
    return [
        (number * size, size, [bit for kind in order for bit in kinds[kind]])
        for number, order in enumerate(orders)
    ]


def flat_mask(bit):
    axis, mask = bit
    return mask * lax.axis_size("narrow") if axis == "wide" else mask


def group_masks():
    masks = [0]
    for bit in group_bits():
        masks = masks + [other ^ flat_mask(bit) for other in masks]
    return masks


def neighbour(bit):
    axis, mask = bit
    wide, narrow = lax.axis_index("wide"), lax.axis_index("narrow")
    if axis == "wide":
        return wide + mask * (1 - 2 * ((wide // mask) % 2)), narrow
    return wide, narrow + mask * (1 - 2 * ((narrow // mask) % 2))


def greet(devices):
    barrier = pltpu.get_barrier_semaphore()
    for device in devices:
        pl.semaphore_signal(barrier, inc=1, device_id=device, device_id_type=MESH)
    pl.semaphore_wait(barrier, len(devices))


class Mail:
    def __init__(self, send_sem, recv_sem, lane_bits):
        core, x_bits, y_bits, z_bits = lane_bits
        self.send_sem, self.recv_sem = send_sem, recv_sem
        self.used, self.sent, self.open = 0, [], []
        self.links = {core: (("core", 1 / 600e3),)}
        self.links.update({bit: (("x", 2 / 91e3),) for bit in x_bits})
        self.links.update({bit: (("y", 2 / 91e3),) for bit in y_bits})
        self.links.update({bit: (("z", 2 / 91e3),) for bit in z_bits[:1]})
        self.links.update({bit: (("z", 2 / 91e3), ("far", 4 / 91e3)) for bit in z_bits[1:]})
        self.free, self.now, self.ready = {}, 0.0, []

    def expect(self, source, bit):
        size = math.prod(source.shape) * source.dtype.itemsize
        due = self.now
        for link, rate in self.links[bit]:
            self.free[link] = max(self.free.get(link, 0.0), self.now) + size * rate
            due = max(due, self.free[link])
        return due + 3.5

    def post(self, source, target, bit):
        copy = pltpu.make_async_remote_copy(
            src_ref=source,
            dst_ref=target,
            send_sem=self.send_sem.at[self.used],
            recv_sem=self.recv_sem.at[self.used],
            device_id=neighbour(bit),
            device_id_type=MESH,
        )
        copy.start()
        self.due = self.expect(source, bit)
        self.used += 1
        self.sent.append(copy)
        self.open.append(copy)
        return copy

    def keep(self, source, target):
        copy = pltpu.make_async_copy(source, target, self.recv_sem.at[self.used])
        copy.start()
        self.used += 1
        self.open.append(copy)
        return copy

    def take(self, copy):
        if any(other is copy for other in self.open):
            self.open = [other for other in self.open if other is not copy]
            if any(other is copy for other in self.sent):
                copy.wait_recv()
            else:
                copy.wait()

    def spend(self, time):
        self.now += time
        return self.now

    def run(self, flows):
        waiting = [(next(flow, None), flow) for flow in flows]
        while True:
            waiting += [(next(flow, None), flow) for flow in self.ready]
            self.ready = []
            waiting = [entry for entry in waiting if entry[0] is not None]
            if not waiting:
                return
            place = min(range(len(waiting)), key=lambda i: waiting[i][0])
            due, flow = waiting.pop(place)
            self.now = max(self.now, due) + 0.4
            waiting.append((next(flow, None), flow))

    def close(self):
        for copy in list(self.open):
            self.take(copy)
        for copy in self.sent:
            copy.wait_send()


def mail_sems(count):
    return [pltpu.SemaphoreType.DMA((count,)), pltpu.SemaphoreType.DMA((count,))]


def spread_flow(mail, bits, part, x_ref, out_ref):
    first, rows, order = part
    span = pl.ds(first, rows)
    held = {0: None}
    for bit in order:
        step = 1 << bits.index(bit)
        for block in list(held):
            if block:
                mail.take(held[block])
            source = out_ref.at[block, span] if block else x_ref.at[span]
            held[block ^ step] = mail.post(source, out_ref.at[block ^ step, span], bit)
        yield mail.due


def spread_kernel(lane_bits, plan, x_ref, *refs):
    core, x_bits, y_bits, z_bits = lane_bits
    count = 1 << len(x_bits)
    table_refs, out_ref, table_out, send_sem, recv_sem = refs[:count], *refs[count:]
    bits = z_bits + y_bits
    greet([neighbour(bit) for bit in bits + [core]])
    mail = Mail(send_sem, recv_sem, lane_bits)

    def table_flow():
        yield 1.0
        for place, ref in enumerate(table_refs):
            mail.post(ref, table_out.at[1, place], core)
            mail.keep(ref, table_out.at[0, place])

    mail.run([spread_flow(mail, bits, part, x_ref, out_ref) for part in plan] + [table_flow()])
    mail.keep(x_ref, out_ref.at[0])
    mail.close()


def spread(array, tables):
    bits, plan = group_bits(), routes(array.shape[0], SPREAD_ORDERS)
    count = 1 << len(bits)
    vmem, any_space = pl.BlockSpec(memory_space=pltpu.VMEM), pl.BlockSpec(memory_space=pl.ANY)
    blocks, table = pl.pallas_call(
        functools.partial(spread_kernel, lanes(), plan),
        out_shape=(
            jax.ShapeDtypeStruct((count,) + array.shape, array.dtype),
            jax.ShapeDtypeStruct((2, len(tables)) + tables[0].shape, array.dtype),
        ),
        in_specs=[vmem] * (1 + len(tables)),
        out_specs=(any_space, any_space),
        scratch_shapes=mail_sems(len(plan) * count + 2 * len(tables)),
        compiler_params=pltpu.CompilerParams(
            collective_id=4, has_side_effects=True, vmem_limit_bytes=62 * MIB
        ),
        name="rows_spread",
    )(array, *tables)
    width = array.shape[1]
    return blocks.reshape(-1, width), table.reshape(-1, width)


def collect_flow(mail, bits, part, refs):
    first, rows, order = part
    x_ref, out_ref, sum_ref, got_ref = refs
    span = pl.ds(first, rows)
    held = list(range(1 << len(bits)))
    for stage, bit in enumerate(order):
        step = 1 << bits.index(bit)
        source = sum_ref if stage else x_ref
        held = [block for block in held if not block & step]
        base = (1 << len(bits)) - 2 * len(held)
        copies = [
            mail.post(source.at[block ^ step, span], got_ref.at[base + place, span], bit)
            for place, block in enumerate(held)
        ]
        yield mail.due
        for place, (block, copy) in enumerate(zip(held, copies)):
            mail.take(copy)
            total = source[block, span, :].astype(jnp.float32) + got_ref[
                base + place, span, :
            ].astype(jnp.float32)
            if stage == len(bits) - 1:
                out_ref[span, :] = total
            else:
                sum_ref[block, span, :] = total.astype(jnp.bfloat16)


def head_back_kernel(lane_bits, plan, tile, x_ref, *refs):
    core, _, y_bits, z_bits = lane_bits
    bits = z_bits + y_bits
    if tile:
        slope_ref, rows_ref, out_ref, keep_ref, pass_ref = refs[:5]
        sum_ref, got_ref, send_sem, recv_sem = refs[5:9]
        loads, sent_ref, other_ref, load_sem = refs[9:]
        half = sent_ref.shape[0]
        count = half // tile
        order = [count + i for i in range(count)] + [count - 1 - i for i in range(count)]

        def load(number):
            return pltpu.make_async_copy(
                slope_ref.at[:, pl.ds(order[number] * tile, tile)],
                loads.at[number % 2],
                load_sem.at[number % 2],
            )

        load(0).start()
        greet([neighbour(bit) for bit in bits + [core]])
    else:
        out_ref, sum_ref, got_ref, send_sem, recv_sem = refs
        greet([neighbour(bit) for bit in bits])
    mail = Mail(send_sem, recv_sem, lane_bits)
    flows = [
        collect_flow(mail, bits, part, (x_ref, out_ref, sum_ref, got_ref)) for part in plan
    ]
    if tile:

        def table_flow():
            arrivals = {}
            border = keep_ref.shape[0]
            for number, block in enumerate(order):
                if number + 1 < len(order):
                    load(number + 1).start()
                load(number).wait()
                grad = lax.dot_general(
                    loads[number % 2],
                    rows_ref[...],
                    (((0,), (0,)), ((), ())),
                    preferred_element_type=jnp.float32,
                )
                start = block * tile % half
                span = pl.ds(start, tile)
                if block >= count:
                    sent_ref[span, :] = grad.astype(jnp.bfloat16)
                    arrivals[start] = mail.post(sent_ref.at[span], other_ref.at[span], core)
                else:
                    mail.take(arrivals[start])
                    grad = grad + other_ref[span, :].astype(jnp.float32)
                    lower = min(max(border - start, 0), tile)
                    if lower:
                        keep_ref[pl.ds(start, lower), :] = grad[:lower]
                    if lower < tile:
                        pass_ref[pl.ds(start + lower - border, tile - lower), :] = grad[
                            lower:
                        ].astype(jnp.bfloat16)
                yield mail.spend(2.7)

        flows.append(table_flow())
    mail.run(flows)
    mail.close()


def head_back(array, slopes, group_rows):
    lane_bits = lanes()
    bits, plan = group_bits(), routes(array.shape[1], COLLECT_ORDERS)
    count, rows, width = array.shape
    vocab = slopes.shape[1]
    half = vocab // 2
    tile = 640 if half % 640 == 0 else 0
    vmem = pl.BlockSpec(memory_space=pltpu.VMEM)
    shapes = [jax.ShapeDtypeStruct((rows, width), jnp.float32)]
    scratch = [
        pltpu.VMEM((count, rows, width), jnp.bfloat16),
        pltpu.VMEM((count - 1, rows, width), jnp.bfloat16),
    ] + mail_sems(len(plan) * count + (half // tile if tile else 0))
    operands, specs = [array], [vmem]
    if tile:
        shapes += [
            jax.ShapeDtypeStruct((half // 2, width), jnp.float32),
            jax.ShapeDtypeStruct((half // 2, width), jnp.bfloat16),
        ]
        scratch += [
            pltpu.VMEM((2, slopes.shape[0], tile), jnp.bfloat16),
            pltpu.VMEM((half, width), jnp.bfloat16),
            pltpu.VMEM((half, width), jnp.bfloat16),
            pltpu.SemaphoreType.DMA((2,)),
        ]
        operands += [slopes, group_rows]
        specs += [pl.BlockSpec(memory_space=pl.ANY), vmem]
    outs = pl.pallas_call(
        functools.partial(head_back_kernel, lane_bits, plan, tile),
        out_shape=shapes,
        in_specs=specs,
        out_specs=[vmem] * len(shapes),
        scratch_shapes=scratch,
        compiler_params=pltpu.CompilerParams(
            collective_id=5, has_side_effects=True, vmem_limit_bytes=56 * MIB
        ),
        name="head_back",
    )(*operands)
    if tile:
        return outs
    core = lane_bits[0]
    other = swap(outer_sum(slopes[:, half:], group_rows).astype(jnp.bfloat16), core)
    table_sum = outer_sum(slopes[:, :half], group_rows) + other.astype(jnp.float32)
    return outs[0], table_sum[: half // 2], table_sum[half // 2 :].astype(jnp.bfloat16)


def chip_sizes():
    wides, groups = lax.axis_size("wide"), lax.axis_size("narrow")
    return wides, groups // 2


class Rows:
    def __init__(self, sizes, x_ref, out_ref, send_sem, recv_sem):
        self.sizes, self.x_ref, self.out_ref = sizes, x_ref, out_ref
        self.send_sem, self.recv_sem = send_sem, recv_sem
        self.count = sizes[0] * sizes[1]
        self.place = Place(sizes[0], 2 * sizes[1])

    def peer(self, k):
        ups = self.sizes[1]
        return self.place.peer(k // ups, 2 * (k % ups))

    def each(self, step):
        for k in range(1, self.count):
            step(k)

    def copy(self, k):
        return pltpu.make_async_remote_copy(
            src_ref=self.x_ref.at[k],
            dst_ref=self.out_ref.at[k],
            send_sem=self.send_sem.at[k],
            recv_sem=self.recv_sem.at[k],
            device_id=self.peer(k),
            device_id_type=MESH,
        )

    def greet(self, others):
        self.call(others)
        self.meet(others)

    def call(self, others):
        barrier = pltpu.get_barrier_semaphore()
        self.each(
            lambda k: pl.semaphore_signal(
                barrier, inc=1, device_id=self.peer(k), device_id_type=MESH
            )
        )
        for device in others:
            pl.semaphore_signal(barrier, inc=1, device_id=device, device_id_type=MESH)

    def meet(self, others):
        pl.semaphore_wait(pltpu.get_barrier_semaphore(), self.count - 1 + len(others))

    def start(self):
        self.each(lambda k: self.copy(k).start())

    def own(self):
        return pltpu.make_async_copy(self.x_ref.at[0], self.out_ref.at[0], self.recv_sem.at[0])


def swap_rows_kernel(sizes, x_ref, out_ref, send_sem, recv_sem):
    rows = Rows(sizes, x_ref, out_ref, send_sem, recv_sem)
    rows.greet([])
    rows.start()
    own = rows.own()
    own.start()
    own.wait()
    rows.each(lambda k: rows.copy(k).wait())


def swap_rows(rows):
    sizes = chip_sizes()
    count = sizes[0] * sizes[1]
    return pl.pallas_call(
        functools.partial(swap_rows_kernel, sizes),
        out_shape=jax.ShapeDtypeStruct(rows.shape, rows.dtype),
        in_specs=[pl.BlockSpec(memory_space=pltpu.VMEM)],
        out_specs=pl.BlockSpec(memory_space=pl.ANY),
        scratch_shapes=mail_sems(count),
        compiler_params=pltpu.CompilerParams(collective_id=2, has_side_effects=True),
        name="token_rows",
    )(rows)


def load_kernel(sizes, lane_bits, *refs):
    core, x_bits, y_bits, z_bits = lane_bits
    near = z_bits[0]
    weight_refs, rows_ref = refs[:4], refs[4]
    weight_outs, rows_out = refs[5:9], refs[9]
    send_sem, recv_sem, rows_send, rows_recv, pass_send, pass_recv = refs[10:]
    wide, narrow = lax.axis_index("wide"), lax.axis_index("narrow")
    rows = Rows(sizes, rows_ref, rows_out.at[0], rows_send, rows_recv)
    rows.greet([neighbour(core)])
    mail = Mail(send_sem, recv_sem, lane_bits)
    side_near = (wide // near[1]) % 2

    def across(block, bit):
        return block + bit[1] * (1 - 2 * ((block // bit[1]) % 2))

    def pieces(height):
        half = height // 2
        count = 2 if height == weight_refs[3].shape[0] and half % 32 == 0 else 1
        return [(place * (half // count), half // count) for place in range(count)]

    def part(ref, number, side, piece):
        start = side * (ref.shape[1] // 2) + piece[0]
        return ref.at[number, pl.ds(pl.multiple_of(start, 16), piece[1])]

    def own_part(ref, side, piece):
        start = side * (ref.shape[0] // 2) + piece[0]
        return ref.at[pl.ds(pl.multiple_of(start, 16), piece[1])]

    first = [
        mail.post(own_part(ref, side_near, piece), part(out, narrow, side_near, piece), y_bits[0])
        for ref, out in zip(weight_refs, weight_outs)
        for piece in pieces(ref.shape[0])
    ]
    rows.start()
    own_rows = rows.own()
    own_rows.start()
    keeps = []
    for ref, out in zip(weight_refs, weight_outs):
        keeps.append(mail.keep(ref, out.at[narrow]))
        mail.post(ref, out.at[narrow], core)
    own_rows.wait()
    blocks = [narrow]
    for level, bit in enumerate(y_bits):
        if level:
            for copy in keeps:
                mail.take(copy)
        arrivals, number = [], 0
        for ref, out in zip(weight_refs, weight_outs):
            for piece in pieces(ref.shape[0]):
                for block in blocks:
                    if level:
                        source = part(out, block, side_near, piece)
                        copy = mail.post(source, source, bit)
                    else:
                        copy = first[number]
                        number += 1
                    arrivals.append((out, across(block, bit), piece, copy))
        seconds = []
        for out, other, piece, copy in arrivals:
            mail.take(copy)
            source = part(out, other, side_near, piece)
            seconds.append(mail.post(source, source, near))
            mail.post(source, source, core)
        for (out, other, piece, _), copy in zip(arrivals, seconds):
            mail.take(copy)
            source = part(out, other, 1 - side_near, piece)
            mail.post(source, source, core)
        blocks = blocks + [across(block, bit) for block in blocks]

    def hand(k):
        return pltpu.make_async_remote_copy(
            src_ref=rows_out.at[0, k],
            dst_ref=rows_out.at[1, k],
            send_sem=pass_send.at[k],
            recv_sem=pass_recv.at[k],
            device_id=neighbour(core),
            device_id_type=MESH,
        )

    hand(0).start()

    def forward(k):
        rows.copy(k).wait()
        hand(k).start()

    rows.each(forward)
    hand(0).wait()
    rows.each(lambda k: hand(k).wait())
    mail.close()


def load_all(weights, rows):
    lane_bits = lanes()
    sizes = chip_sizes()
    count = sizes[0] * sizes[1]
    groups = lax.axis_size("narrow")
    any_space = pl.BlockSpec(memory_space=pl.ANY)
    shapes = [jax.ShapeDtypeStruct((groups,) + w.shape, w.dtype) for w in weights]
    shapes.append(jax.ShapeDtypeStruct((2,) + rows.shape, rows.dtype))
    *weights_all, rows_all = pl.pallas_call(
        functools.partial(load_kernel, sizes, lane_bits),
        out_shape=shapes,
        in_specs=[pl.BlockSpec(memory_space=pltpu.VMEM)] * 5,
        out_specs=[any_space] * 5,
        scratch_shapes=mail_sems(8 * 4 * groups) + mail_sems(count) + mail_sems(count),
        compiler_params=pltpu.CompilerParams(
            collective_id=6, has_side_effects=True, vmem_limit_bytes=62 * MIB
        ),
        name="load_rows",
    )(*weights, rows)
    return tuple(w.reshape(-1, w.shape[-1]) for w in weights_all), rows_all


def tile_of(rows):
    return next(size for size in (128, 96, 64, 48, 32, 16) if rows % size == 0)


def back_reduce_kernel(sizes, lane_bits, kinds, *refs):
    core, x_bits, y_bits, z_bits = lane_bits
    ins, wanted_ref, hbm = refs[:8], refs[8], refs[9:13]
    out_refs, small_out, rows_out, square_out, low_out = refs[13:16], *refs[16:20]
    scratch = refs[20:]
    weights, load_sem, stream_ref, small_ref = scratch[:4], scratch[4], scratch[5], small_out
    grad_refs = scratch[6:9]
    both_ref, core_got = scratch[9:11]
    small_sum, small_got, send_sem, recv_sem, rows_send, rows_recv = scratch[11:17]
    rest = scratch[17:]
    got_refs = []
    for _, _, _, path in kinds:
        got_refs.append(rest[: len(path) + 1])
        rest = rest[len(path) + 1 :]
    waits = [
        pltpu.make_async_copy(source, target, load_sem.at[number])
        for number, (source, target) in enumerate(zip(hbm, weights))
    ]
    for load in waits:
        load.start()
    place = {"wide": lax.axis_index("wide"), "narrow": lax.axis_index("narrow")}
    rows = Rows(sizes, both_ref.at[0], rows_out, rows_send, rows_recv)
    rows.call([neighbour(core)])
    mail = Mail(send_sem, recv_sem, lane_bits)
    ups = grad_refs[0].shape[1]
    own = place["narrow"] % 2
    square_out[...] = jnp.zeros_like(square_out)

    def side_of(bit):
        return (place[bit[0]] // bit[1]) % 2

    def add(total_ref, got_ref, box):
        up, ups_here, first, height = box
        tile = tile_of(height)

        def step(i, carry):
            at = i // (height // tile)
            down = (i % (height // tile)) * tile
            span = pl.ds(pl.multiple_of(first + down, 16), tile)
            got = got_ref[at, pl.ds(pl.multiple_of(down, 16), tile), :]
            total = total_ref[own, up + at, span, :].astype(jnp.float32) + got.astype(jnp.float32)
            total_ref[own, up + at, span, :] = total.astype(jnp.bfloat16)
            return carry

        lax.fori_loop(0, ups_here * (height // tile), step, 0)

    def view(ref, box):
        up, ups_here, first, height = box
        return ref.at[own, pl.ds(up, ups_here), pl.ds(pl.multiple_of(first, 16), height)]

    def flow(number):
        which, offset, height, path = kinds[number]
        total_ref, got, out_ref = grad_refs[which], got_refs[number], out_refs[which]
        span = pl.ds(offset, height)
        copy = mail.post(total_ref.at[1 - own, :, span], got[0], core)
        yield mail.due
        mail.take(copy)
        box = (0, ups, offset, height)
        add(total_ref, got[0], box)
        for stage, (bit, halve) in enumerate(path):
            up, ups_here, first, height = box
            side = side_of(bit)
            if bit[0] == "narrow":
                half = ups_here // 2
                mine = (up + side * half, half, first, height)
                theirs = (up + (1 - side) * half, half, first, height)
            elif halve:
                half = height // 2
                mine = (up, ups_here, first + side * half, half)
                theirs = (up, ups_here, first + (1 - side) * half, half)
            else:
                mine = theirs = box
            copy = mail.post(view(total_ref, theirs), got[stage + 1], bit)
            yield mail.due
            mail.take(copy)
            if not halve:
                copy.wait_send()
                mail.sent = [other for other in mail.sent if other is not copy]
            box = mine
            add(total_ref, got[stage + 1], box)
        up, _, first, height = box
        piece = total_ref[own, up, pl.ds(pl.multiple_of(first, 16), height), :]
        out_ref[pl.ds(pl.multiple_of(first, 16), height), :] = piece
        full = piece.astype(jnp.float32)
        square_out[...] += jnp.sum((full * full).reshape(height // 8, 8, -1), 0)
        for bit, halve in reversed(path):
            if bit[0] == "wide" and halve:
                span = pl.ds(pl.multiple_of(first, 16), height)
                copy = mail.post(out_ref.at[span], out_ref.at[span], bit)
                yield mail.due
                mail.take(copy)
                first = first - side_of(bit) * height
                height = 2 * height

    def small_flow():
        bits = [core] + x_bits + y_bits + z_bits
        small_sum[0] = small_ref[...].astype(jnp.bfloat16)
        for stage, bit in enumerate(bits):
            copy = mail.post(small_sum.at[stage], small_got.at[stage], bit)
            yield mail.due
            mail.take(copy)
            total = small_sum[stage].astype(jnp.float32) + small_got[stage].astype(jnp.float32)
            if stage == len(bits) - 1:
                small_out[...] = total
            else:
                small_sum[stage + 1] = total.astype(jnp.bfloat16)

    def rows_flow():
        low = stream_ref[...].astype(jnp.bfloat16)
        low_out[...] = low
        both = outer_sum(wanted_ref[...], low).astype(jnp.bfloat16)
        both_ref[...] = both.reshape(both_ref.shape)
        copy = mail.post(both_ref.at[1], core_got, core)
        yield mail.due
        mail.take(copy)
        summed = both_ref[0].astype(jnp.float32) + core_got[...].astype(jnp.float32)
        both_ref[0] = summed.astype(jnp.bfloat16)
        rows.start()
        own_rows = rows.own()
        own_rows.start()
        yield mail.due
        own_rows.wait()

    back = backward_flow(
        ins,
        (stream_ref, small_ref) + tuple(grad_refs),
        (*weights, waits),
    )
    final_width = ins[0].shape[1]
    next(back)
    rows.meet([neighbour(core)])

    def back_flow():
        for turn, cost in enumerate(back):
            due = mail.spend(cost)
            if turn == weights[2].shape[0] // final_width - 1:
                mail.ready += [flow(number) for number, kind in enumerate(kinds) if kind[0] == 1]
            yield due
        mail.ready += [flow(number) for number, kind in enumerate(kinds) if kind[0] == 0]
        mail.ready += [rows_flow(), small_flow()]

    first = [flow(number) for number, kind in enumerate(kinds) if kind[0] == 2]
    mail.run(first + [back_flow()])
    rows.each(lambda k: rows.copy(k).wait())
    mail.close()


def back_reduce(final_grad, norm_gains, bias_rows, saved, weights, wanted):
    lane_bits = lanes()
    core, x_bits, y_bits, z_bits = lane_bits
    sizes = chip_sizes()
    tokens, width = final_grad.shape
    ups = sizes[1]
    height = 4 * width // (2 * ups)
    half = height // 2
    bits = {"x": x_bits, "y": y_bits[::-1], "z": z_bits[:1], "f": z_bits[1:]}
    kinds, got_shapes = [], []
    for which, offset, order in (
        (1, 0, "yzfx"),
        (2, 0, "yxzf"),
        (1, half, "yzxf"),
        (2, half, "zyxf"),
        (0, 0, "yxfz"),
        (0, half, "yxzf"),
    ):
        path, ups_here, height_here = [], ups, half
        shapes = [(ups_here, height_here, width)]
        for bit in [bit for kind in order for bit in bits[kind]]:
            halve = True
            if bit[0] == "narrow":
                ups_here //= 2
            else:
                halve = (height_here // 2) % 16 == 0
                height_here = height_here // 2 if halve else height_here
            path.append((bit, halve))
            shapes.append((ups_here, height_here, width))
        kinds.append((which, offset, half, path))
        got_shapes += shapes
    count = sizes[0] * sizes[1]
    steps = 1 + len(kinds[0][3])
    small_rows = 14 + LENGTH
    small = (small_rows + -small_rows % 16, width)
    row_shape = (count, slots(), width)
    vmem, any_space = pl.BlockSpec(memory_space=pltpu.VMEM), pl.BlockSpec(memory_space=pl.ANY)
    shape, low = jax.ShapeDtypeStruct, jnp.bfloat16
    outs = pl.pallas_call(
        functools.partial(back_reduce_kernel, sizes, lane_bits, kinds),
        out_shape=[shape((height, width), low)] * 3
        + [
            shape(small, jnp.float32),
            shape(row_shape, low),
            shape((8, width), jnp.float32),
            shape((tokens, width), low),
        ],
        in_specs=[vmem] * 9 + [any_space] * 4,
        out_specs=[vmem] * 4 + [any_space, vmem, vmem],
        scratch_shapes=[pltpu.VMEM(w.shape, w.dtype) for w in weights]
        + [
            pltpu.SemaphoreType.DMA((4,)),
            pltpu.VMEM((tokens, width), jnp.float32),
        ]
        + [pltpu.VMEM((2, ups, height, width), low) for _ in range(3)]
        + [pltpu.VMEM((2,) + row_shape, low), pltpu.VMEM(row_shape, low)]
        + [pltpu.VMEM((steps,) + small, low), pltpu.VMEM((steps,) + small, low)]
        + mail_sems(len(kinds) * 2 * steps + steps + 1)
        + mail_sems(count)
        + [pltpu.VMEM(one, low) for one in got_shapes],
        compiler_params=pltpu.CompilerParams(
            collective_id=7, has_side_effects=True, vmem_limit_bytes=63 * MIB
        ),
        name="back_reduce",
    )(final_grad, norm_gains, bias_rows, *saved, wanted, *weights)
    repeats = 1
    for bit, halve in kinds[0][3]:
        repeats *= 1 if halve else 2
    return outs[:3], outs[3], outs[4], outs[5] / repeats, outs[6]


class Place:
    def __init__(self, wides, groups):
        self.wide, self.narrow = lax.axis_index("wide"), lax.axis_index("narrow")
        self.wide_steps = self.steps(self.wide, wides)
        self.narrow_steps = self.steps(self.narrow, groups)

    def steps(self, place, size):
        masks = [1 << bit for bit in range(log_two(size))]
        return {mask: mask * (1 - 2 * ((place // mask) % 2)) for mask in masks}

    def peer(self, wide_mask, narrow_mask):
        wide, narrow = self.wide, self.narrow
        for mask, step in self.wide_steps.items():
            wide = wide + step if mask & wide_mask else wide
        for mask, step in self.narrow_steps.items():
            narrow = narrow + step if mask & narrow_mask else narrow
        return wide, narrow


def exchange_kernel(masks, sizes, whole, x_ref, out_ref, send_sem, recv_sem, own_sem):
    wides, groups = sizes
    place = Place(wides, groups)
    masks = list(range(wides * groups)) if masks is None else masks
    count = len(masks)

    def peer(mask):
        return place.peer(mask // groups, mask % groups)

    def each(step):
        for k in range(1, count):
            step(k, masks[k])

    def copy(k, mask):
        return pltpu.make_async_remote_copy(
            src_ref=x_ref if whole else x_ref.at[k],
            dst_ref=out_ref.at[k],
            send_sem=send_sem.at[k],
            recv_sem=recv_sem.at[k],
            device_id=peer(mask),
            device_id_type=MESH,
        )

    barrier = pltpu.get_barrier_semaphore()
    each(
        lambda k, mask: pl.semaphore_signal(
            barrier, inc=1, device_id=peer(mask), device_id_type=MESH
        )
    )
    pl.semaphore_wait(barrier, count - 1)
    each(lambda k, mask: copy(k, mask).start())
    own = pltpu.make_async_copy(x_ref if whole else x_ref.at[0], out_ref.at[0], own_sem)
    own.start()
    own.wait()
    each(lambda k, mask: copy(k, mask).wait())


def exchange(array, number, name, masks=None, whole=True):
    sizes = (lax.axis_size("wide"), lax.axis_size("narrow"))
    count = sizes[0] * sizes[1] if masks is None else len(masks)
    shape = (count,) + array.shape if whole else array.shape
    return pl.pallas_call(
        functools.partial(exchange_kernel, masks, sizes, whole),
        out_shape=jax.ShapeDtypeStruct(shape, array.dtype),
        in_specs=[pl.BlockSpec(memory_space=pltpu.VMEM)],
        out_specs=pl.BlockSpec(memory_space=pltpu.VMEM),
        scratch_shapes=[
            pltpu.SemaphoreType.DMA((count,)),
            pltpu.SemaphoreType.DMA((count,)),
            pltpu.SemaphoreType.DMA,
        ],
        compiler_params=pltpu.CompilerParams(
            collective_id=number, has_side_effects=True, vmem_limit_bytes=32 * MIB
        ),
        name=name,
    )(array)


def stats_kernel(masks, sizes, x_ref, target_ref, log_ref, loss_ref, got_ref, send_sem, recv_sem):
    wides, groups = sizes
    place = Place(wides, groups)
    peers = [place.peer(mask // groups, mask % groups) for mask in masks]
    greet(peers[1:])

    def copy(k):
        return pltpu.make_async_remote_copy(
            src_ref=x_ref,
            dst_ref=got_ref.at[k],
            send_sem=send_sem.at[k],
            recv_sem=recv_sem.at[k],
            device_id=peers[k],
            device_id_type=MESH,
        )

    blocks, height, _ = x_ref.shape
    rows = height // 4
    for k in range(1, blocks):
        copy(k).start()
    got_ref[0] = x_ref[...]
    for k in range(1, blocks):
        copy(k).wait()
    for block in range(blocks):
        parts = [got_ref[k, block ^ k] for k in range(blocks)]
        top = functools.reduce(jnp.maximum, [part[:rows] for part in parts])
        total = sum(part[rows : 2 * rows] * jnp.exp(part[:rows] - top) for part in parts)
        logs = top + jnp.log(total)
        span = pl.ds(block * rows, rows)
        counted = target_ref[span, :] >= 0
        log_ref[span, :] = jnp.where(counted, logs, jnp.inf)
        if block == 0:
            picked = sum(part[2 * rows : 3 * rows] for part in parts)
            loss_ref[...] = jnp.where(counted, logs - picked, 0.0)


def merge_stats(stats, targets):
    sizes = (lax.axis_size("wide"), lax.axis_size("narrow"))
    blocks, height, lanes_here = stats.shape
    rows = height // 4
    vmem = pl.BlockSpec(memory_space=pltpu.VMEM)
    return pl.pallas_call(
        functools.partial(stats_kernel, group_masks(), sizes),
        out_shape=(
            jax.ShapeDtypeStruct((blocks * rows, lanes_here), jnp.float32),
            jax.ShapeDtypeStruct((rows, lanes_here), jnp.float32),
        ),
        in_specs=[vmem, vmem],
        out_specs=(vmem, vmem),
        scratch_shapes=[pltpu.VMEM((blocks,) + stats.shape, jnp.float32)] + mail_sems(blocks),
        compiler_params=pltpu.CompilerParams(
            collective_id=1, has_side_effects=True, vmem_limit_bytes=32 * MIB
        ),
        name="stats_share",
    )(stats, targets)


def put_columns(rows_ref, column_ref):
    turned = rows_ref[...].T
    for place in range(rows_ref.shape[0]):
        column_ref[pl.ds(place * 128, 128), :] = turned[:, place : place + 1]


def as_rows(column):
    count = column.shape[0] // 128
    return jnp.concatenate(
        [column[place * 128 : (place + 1) * 128] for place in range(count)], 1
    ).T


def score_kernel(
    rows_ref, table_ref, target_ref, exps_ref, max_ref, stat_ref, sum_ref, pick_ref, column_ref
):
    tile = pl.program_id(0)
    width = table_ref.shape[0]

    @pl.when(tile == 0)
    def _():
        max_ref[...] = jnp.full_like(max_ref, -jnp.inf)
        sum_ref[...] = jnp.zeros_like(sum_ref)
        pick_ref[...] = jnp.zeros_like(pick_ref)
        put_columns(target_ref, column_ref)

    def step(block, carry):
        rows = pl.ds(pl.multiple_of(block * TOKEN_TILE, TOKEN_TILE), TOKEN_TILE)
        scores = lax.dot_general(
            rows_ref[rows, :],
            table_ref[...],
            (((1,), (1,)), ((), ())),
            preferred_element_type=jnp.float32,
        )
        top = jnp.max(scores, -1, keepdims=True)
        powers = jnp.exp(scores - top)
        exps_ref[rows, :] = powers.astype(jnp.bfloat16)
        total = jnp.sum(powers, -1, keepdims=True)
        columns = lax.broadcasted_iota(jnp.int32, (TOKEN_TILE, width), 1)
        wanted = column_ref[rows, :] - tile * width
        hit = jnp.sum(jnp.where(columns == wanted, scores, 0.0), -1, keepdims=True)
        here = lax.broadcasted_iota(jnp.int32, (TOKEN_TILE, 128), 1) == tile
        max_ref[rows, :] = jnp.where(here, top, max_ref[rows, :])
        sum_ref[rows, :] = jnp.where(here, total, sum_ref[rows, :])
        pick_ref[rows, :] = jnp.where(here, hit, pick_ref[rows, :])
        return carry

    lax.fori_loop(0, rows_ref.shape[0] // TOKEN_TILE, step, 0, unroll=8)

    @pl.when(tile == pl.num_programs(0) - 1)
    def _():
        maxima = max_ref[...]
        top = jnp.max(maxima, -1, keepdims=True)
        total = jnp.sum(sum_ref[...] * jnp.exp(maxima - top), -1, keepdims=True)
        picked = jnp.sum(pick_ref[...], -1, keepdims=True)
        blocks, height, _ = stat_ref.shape
        rows = height // 4
        stat_ref[...] = jnp.zeros_like(stat_ref)
        for number, column in enumerate((top, total, picked)):
            lines = as_rows(column)
            for block in range(blocks):
                stat_ref[block, pl.ds(number * rows, rows), :] = lines[
                    block * rows : (block + 1) * rows
                ]


def vocab_tile(vocab):
    return 1280 if vocab % 1280 == 0 else 640


def head_scores(rows, table, targets, blocks):
    tokens, model = rows.shape
    vocab = table.shape[0]
    width = vocab_tile(vocab)
    stat = pltpu.VMEM((tokens, 128), jnp.float32)
    whole = pl.BlockSpec((tokens, 128), lambda j: (0, 0))
    height = 4 * (tokens // blocks // 128)
    return pl.pallas_call(
        score_kernel,
        grid=(vocab // width,),
        out_shape=(
            jax.ShapeDtypeStruct((tokens, vocab), jnp.bfloat16),
            jax.ShapeDtypeStruct((tokens, 128), jnp.float32),
            jax.ShapeDtypeStruct((blocks, height, 128), jnp.float32),
        ),
        in_specs=[
            pl.BlockSpec((tokens, model), lambda j: (0, 0)),
            pl.BlockSpec((width, model), lambda j: (j, 0)),
            pl.BlockSpec(targets.shape, lambda j: (0, 0)),
        ],
        out_specs=(
            pl.BlockSpec((tokens, width), lambda j: (0, j)),
            whole,
            pl.BlockSpec((blocks, height, 128), lambda j: (0, 0, 0)),
        ),
        scratch_shapes=[stat, stat, pltpu.VMEM((tokens, 1), jnp.int32)],
        compiler_params=pltpu.CompilerParams(vmem_limit_bytes=60 * MIB),
        cost_estimate=pl.CostEstimate(
            flops=3 * tokens * vocab * model,
            bytes_accessed=2 * tokens * vocab,
            transcendentals=tokens * vocab,
        ),
        name="head_scores",
    )(rows, table, targets)


def slope_kernel(
    exps_ref,
    max_ref,
    log_ref,
    target_ref,
    table_ref,
    slope_ref,
    grad_ref,
    total_ref,
    column_ref,
    log_column_ref,
):
    tile = pl.program_id(0)
    width = table_ref.shape[0]

    @pl.when(tile == 0)
    def _():
        total_ref[...] = jnp.zeros_like(total_ref)
        put_columns(target_ref, column_ref)
        put_columns(log_ref, log_column_ref)

    def step(block, carry):
        rows = pl.ds(pl.multiple_of(block * TOKEN_TILE, TOKEN_TILE), TOKEN_TILE)
        here = lax.broadcasted_iota(jnp.int32, (TOKEN_TILE, 128), 1) == tile
        top = jnp.sum(jnp.where(here, max_ref[rows, :], 0.0), -1, keepdims=True)
        scale = jnp.exp(top - log_column_ref[rows, :])
        columns = lax.broadcasted_iota(jnp.int32, (TOKEN_TILE, width), 1)
        wanted = column_ref[rows, :] - tile * width
        probs = exps_ref[rows, :].astype(jnp.float32) * scale
        slope = jnp.where(columns == wanted, probs - 1.0, probs).astype(jnp.bfloat16)
        slope_ref[rows, :] = slope
        total_ref[rows, :] += jnp.dot(slope, table_ref[...], preferred_element_type=jnp.float32)
        return carry

    lax.fori_loop(0, exps_ref.shape[0] // TOKEN_TILE, step, 0, unroll=8)

    @pl.when(tile == pl.num_programs(0) - 1)
    def _():
        grad_ref[...] = total_ref[...].astype(jnp.bfloat16)


def head_slopes(exps, maxima, logs, targets, table):
    tokens, vocab = exps.shape
    model = table.shape[1]
    width = vocab_tile(vocab)
    return pl.pallas_call(
        slope_kernel,
        grid=(vocab // width,),
        out_shape=(
            jax.ShapeDtypeStruct((tokens, vocab), jnp.bfloat16),
            jax.ShapeDtypeStruct((tokens, model), jnp.bfloat16),
        ),
        in_specs=[
            pl.BlockSpec((tokens, width), lambda j: (0, j)),
            pl.BlockSpec((tokens, 128), lambda j: (0, 0)),
            pl.BlockSpec(logs.shape, lambda j: (0, 0)),
            pl.BlockSpec(targets.shape, lambda j: (0, 0)),
            pl.BlockSpec((width, model), lambda j: (j, 0)),
        ],
        out_specs=(
            pl.BlockSpec((tokens, width), lambda j: (0, j)),
            pl.BlockSpec((tokens, model), lambda j: (0, 0)),
        ),
        scratch_shapes=[
            pltpu.VMEM((tokens, model), jnp.float32),
            pltpu.VMEM((tokens, 1), jnp.int32),
            pltpu.VMEM((tokens, 1), jnp.float32),
        ],
        compiler_params=pltpu.CompilerParams(vmem_limit_bytes=60 * MIB),
        cost_estimate=pl.CostEstimate(
            flops=3 * tokens * vocab * model,
            bytes_accessed=4 * tokens * vocab,
            transcendentals=0,
        ),
        input_output_aliases={0: 0},
        name="head_slopes",
    )(exps, maxima, logs, targets, table)


def slots():
    wides, ups = chip_sizes()
    return 32 if wides * ups <= 16 else 16


def one_hot(places, size):
    return (places.reshape(-1, 1) == jnp.arange(size)[None]).astype(jnp.bfloat16)


def token_plan(ids_all, shard_rows):
    chips, tokens = ids_all.shape
    wides, ups = chip_sizes()
    wide, narrow = lax.axis_index("wide"), lax.axis_index("narrow")
    own_core = narrow % 2
    own_chip = wide * ups + narrow // 2
    owner = ids_all // shard_rows
    owner_core = jnp.bitwise_xor(owner % 2, own_core)
    owner_chip = jnp.bitwise_xor(owner // 2, own_chip)
    local = ids_all % shard_rows
    row = lax.broadcasted_iota(jnp.int32, (tokens, tokens), 0)
    column = lax.broadcasted_iota(jnp.int32, (tokens, tokens), 1)
    before = column < row
    alike = ids_all[:, :, None] == ids_all[:, None, :]
    first = ~jnp.any(alike & before[None], 2)
    served = first & (owner_chip == 0) & (owner_core == 0)
    served_rank = times_t(served.astype(jnp.bfloat16), before.astype(jnp.bfloat16)).astype(
        jnp.int32
    )
    half = tokens // 2
    mine = lambda array: lax.dynamic_slice_in_dim(array, own_core * half, half)
    own_first = mine(jnp.min(jnp.where(alike[0], column, tokens), 1))
    same_owner = mine(owner[0])[:, None] == owner[0][None]
    own_rank = jnp.sum(
        (same_owner & first[0][None] & (column[:half] < own_first[:, None])).astype(jnp.int32), 1
    )
    own_block = mine(owner_core[0]) * chips + mine(owner_chip[0])
    most = jnp.max(
        jnp.sum(
            (
                first[:, None, :]
                & (owner[:, None, :] == jnp.arange(2 * chips)[None, :, None])
            ).astype(jnp.int32),
            2,
        )
    )
    rounds = (most + slots() - 1) // slots()

    def plan(turn):
        slot = jnp.arange(slots())[None, :, None] + turn * slots()
        chosen = served[:, None, :] & (served_rank[:, None, :] == slot)
        slot_rows = jnp.sum(jnp.where(chosen, local[:, None, :] + 1, 0), 2) - 1
        inside = own_rank - turn * slots()
        valid = (inside >= 0) & (inside < slots())
        own_slots = jnp.where(valid, own_block * slots() + inside, -1)
        return slot_rows, one_hot(own_slots, 2 * chips * slots())

    return plan, rounds


def later_rounds(rounds, turn, total):
    return lax.while_loop(
        lambda state: state[0] < rounds,
        lambda state: (state[0] + 1, state[1] + turn(state[0])),
        (jnp.ones((), jnp.int32), total),
    )[1]


def norm_kernel(sizes, tile, table_ref, passed_ref, slot_ref, rows_ref, small_ref, matrix_ref, scalar_ref, *refs):
    total_ref, sum_ref, sent_ref, got_ref, send_sem, recv_sem = refs
    wides, groups = sizes
    place = Place(wides, groups)
    count = wides * groups
    barrier = pltpu.get_barrier_semaphore()
    for k in range(1, count):
        pl.semaphore_signal(
            barrier, inc=1, device_id=place.peer(k // groups, k % groups), device_id_type=MESH
        )
    width = table_ref.shape[1]

    def step(i, squares):
        span = pl.ds(pl.multiple_of(i * tile, 8), tile)
        row = lax.broadcasted_iota(jnp.int32, (tile, slot_ref.shape[1]), 0) + i * tile
        hot = (row == slot_ref[...]).astype(jnp.float32).astype(jnp.bfloat16)
        total = table_ref[span, :] + passed_ref[span, :].astype(jnp.float32)
        total = total + plain(hot, rows_ref[...])
        total_ref[span, :] = total
        return squares + jnp.sum((total * total).reshape(tile // 8, 8, width), 0)

    squares = lax.fori_loop(
        0, table_ref.shape[0] // tile, step, jnp.zeros((8, width), jnp.float32)
    )
    own = jnp.sum(squares + matrix_ref[...], keepdims=True)
    lane = lax.broadcasted_iota(jnp.int32, (8, 128), 1)
    sent_ref[...] = scalar_ref[...] + jnp.where(lane == 2, own, 0.0)
    pl.semaphore_wait(barrier, count - 1)

    def copy(k):
        return pltpu.make_async_remote_copy(
            src_ref=sent_ref,
            dst_ref=got_ref.at[k],
            send_sem=send_sem.at[k],
            recv_sem=recv_sem.at[k],
            device_id=place.peer(k // groups, k % groups),
            device_id_type=MESH,
        )

    for k in range(1, count):
        copy(k).start()
    got_ref[0] = sent_ref[...]
    small = small_ref[...]
    copied = jnp.sum(small * small, keepdims=True)
    for k in range(1, count):
        copy(k).wait()
    both = got_ref[...]
    total = jnp.zeros((8, 128), jnp.float32)
    order = device_order(place, wides, groups, both)
    for one in order:
        total = total + one
    sum_ref[...] = total + jnp.where(lane == 2, copied, 0.0)


def device_order(place, wides, groups, blocks):
    flat = [blocks[k] for k in range(wides * groups)]
    sides = [(groups << bit, place.wide // (1 << bit) % 2) for bit in range(log_two(wides))]
    sides += [(1 << bit, place.narrow // (1 << bit) % 2) for bit in range(log_two(groups))]
    for step, side in sides:
        one = side == 1
        flat = [jnp.where(one, flat[k ^ step], flat[k]) for k in range(len(flat))]
    return flat


def table_norm(table_sum, passed, slot_rows, rows, small, matrix_squares, scalars):
    sizes = (lax.axis_size("wide"), lax.axis_size("narrow"))
    count = sizes[0] * sizes[1]
    height, width = table_sum.shape
    tile = next(size for size in (400, 80, 16) if height % size == 0)
    vmem = pl.BlockSpec(memory_space=pltpu.VMEM)
    return pl.pallas_call(
        functools.partial(norm_kernel, sizes, tile),
        out_shape=(
            jax.ShapeDtypeStruct((height, width), jnp.float32),
            jax.ShapeDtypeStruct((8, 128), jnp.float32),
        ),
        in_specs=[vmem] * 7,
        out_specs=(vmem, vmem),
        scratch_shapes=[
            pltpu.VMEM((8, 128), jnp.float32),
            pltpu.VMEM((count, 8, 128), jnp.float32),
        ]
        + mail_sems(count),
        compiler_params=pltpu.CompilerParams(
            collective_id=3, has_side_effects=True, vmem_limit_bytes=62 * MIB
        ),
        name="table_norm",
    )(table_sum, passed, slot_rows.reshape(1, -1), rows, small, matrix_squares, scalars)


def upper_blocks(count):
    return [(i, j) for i in range(count) for j in range(i, count)]


def muon_kernel(lane_bits, *refs):
    core, _, y_bits, _ = lane_bits
    low_refs, factor_ref, table_refs = refs[:4], refs[4], refs[5:9]
    rest_out, size_out, table_outs = *refs[9:11], refs[11:14]
    gram, sent, got, back, full, total, half, low_a, low_b, low_c, send_sem, recv_sem = refs[14:26]
    in_tiles, out_tiles, in_sem, out_sem = refs[26:]
    width = full.shape[0]
    block = gram.shape[-1]
    places = upper_blocks(width // block)
    greet([neighbour(bit) for bit in [core] + y_bits])
    mail = Mail(send_sem, recv_sem, lane_bits)

    def adam_flow():
        tile = in_tiles.shape[2]
        count = table_refs[0].shape[0] // tile

        def loads(number):
            span = pl.ds(number * tile, tile)
            return [
                pltpu.make_async_copy(
                    ref.at[span], in_tiles.at[number % 2, kind], in_sem.at[number % 2, kind]
                )
                for kind, ref in enumerate(table_refs)
            ]

        def stores(number):
            span = pl.ds(number * tile, tile)
            return [
                pltpu.make_async_copy(
                    out_tiles.at[number % 2, kind], ref.at[span], out_sem.at[number % 2, kind]
                )
                for kind, ref in enumerate(table_outs)
            ]

        for copy in loads(0):
            copy.start()
        yield mail.now
        for number in range(count):
            if number + 1 < count:
                for copy in loads(number + 1):
                    copy.start()
            for copy in loads(number):
                copy.wait()
            if number >= 2:
                for copy in stores(number - 2):
                    copy.wait()
            weight, moment, square, grad = (in_tiles[number % 2, kind] for kind in range(4))
            results = adam_step(
                weight, moment, square, grad * factor_ref[0:1, 0:1], EMBED_RATE, DECAY
            )
            for kind, result in enumerate(results):
                out_tiles[number % 2, kind] = result
            for copy in stores(number):
                copy.start()
            yield mail.spend(1.2)
        for number in range(max(count - 2, 0), count):
            for copy in stores(number):
                copy.wait()

    mail.run([muon_flow(mail, lane_bits, refs, places), adam_flow()])
    mail.close()
    for number in range(4):

        def put_out(i, j, piece, number=number):
            rest_out[number, pl.ds(i * block, block), pl.ds(j * block, block)] = piece.astype(
                jnp.bfloat16
            )

        unpack(places, lambda place: back[number, place].astype(jnp.float32), put_out)


def unpack(places, source, target):
    for place, (i, j) in enumerate(places):
        piece = source(place)
        target(i, j, piece)
        if i != j:
            target(j, i, piece.T)


def muon_flow(mail, lane_bits, refs, places):
    core, _, y_bits, _ = lane_bits
    low_refs, size_out = refs[:4], refs[10]
    gram, sent, got, back, full, total, half, low_a, low_b, low_c = refs[14:24]
    width = full.shape[0]
    block = gram.shape[-1]
    narrow = lax.axis_index("narrow")
    own_core, own_up = narrow % 2, (narrow // 2) % 2
    own = 2 * own_core + own_up
    for number, low_ref in enumerate(low_refs):
        for place, (i, j) in enumerate(places):
            product = lax.dot_general(
                low_ref[:, i * block : (i + 1) * block],
                low_ref[:, j * block : (j + 1) * block],
                (((0,), (0,)), ((), ())),
                preferred_element_type=jnp.float32,
            )
            gram[number, place] = product
    for slot in range(2):
        sent[slot] = gram[2 * (1 - own_core) + slot].astype(jnp.bfloat16)
    copy = mail.post(sent.at[pl.ds(0, 2)], got.at[pl.ds(0, 2)], core)
    yield mail.due
    mail.take(copy)

    def add(number, slot):
        for place in range(len(places)):
            gram[number, place] += got[slot, place].astype(jnp.float32)

    def pass_on(number, slot, bit):
        sent[slot] = gram[number].astype(jnp.bfloat16)
        return mail.post(sent.at[slot], got.at[slot], bit)

    other_up = 2 * own_core + 1 - own_up
    if y_bits:
        add(other_up, 1 - own_up)
        over_y = pass_on(other_up, 2, y_bits[0])
        add(own, own_up)
        yield mail.due
        mail.take(over_y)
        add(own, 2)
    for level, bit in enumerate(y_bits[1:]):
        copy = pass_on(own, 3 + level, bit)
        yield mail.due
        mail.take(copy)
        add(own, 3 + level)

    def spans(i, j):
        return pl.ds(i * block, block), pl.ds(j * block, block)

    def put_full(i, j, piece):
        full[spans(i, j)] = piece

    unpack(places, lambda place: gram[own, place], put_full)
    diagonal = lax.broadcasted_iota(jnp.int32, (block, block), 0) == lax.broadcasted_iota(
        jnp.int32, (block, block), 1
    )
    trace = jnp.zeros((1, 1), jnp.float32)
    for i in range(width // block):
        trace = trace + jnp.sum(jnp.where(diagonal, full[spans(i, i)], 0.0), keepdims=True)
    magnitude = jnp.sqrt(trace) + 1e-07
    inverse = 1.0 / magnitude

    def rows(step):
        def body(i, carry):
            step(pl.ds(pl.multiple_of(i * block, block), block))
            return carry

        lax.fori_loop(0, width // block, body, 0)

    def times(left, right, span):
        return jnp.dot(left[span, :], right[...], preferred_element_type=jnp.float32)

    def start(span):
        scaled = full[span, :] * (inverse * inverse)
        full[span, :] = scaled
        low_a[span, :] = scaled.astype(jnp.bfloat16)

    rows(start)
    scale = NS_A
    for cycle_no in range(NS_STEPS):

        def rest_step(span):
            rest = NS_B * full[span, :] + NS_C * times(low_a, low_a, span)
            low_b[span, :] = rest.astype(jnp.bfloat16)
            if cycle_no == 0:
                total[span, :] = rest
            else:
                total[span, :] = NS_A * total[span, :] + scale * rest

        rows(rest_step)
        if cycle_no:

            def total_step(span):
                total[span, :] += times(low_c, low_b, span)

            rows(total_step)
            scale = scale * NS_A
        if cycle_no < NS_STEPS - 1:

            def keep_total(span):
                low_c[span, :] = total[span, :].astype(jnp.bfloat16)

            def half_step(span):
                half[span, :] = NS_A * full[span, :] + times(low_a, low_b, span)

            def full_step(span):
                value = half[span, :]
                low_a[span, :] = value.astype(jnp.bfloat16)
                full[span, :] = NS_A * value + times(low_a, low_b, span)

            def low_step(span):
                low_a[span, :] = full[span, :].astype(jnp.bfloat16)

            rows(keep_total)
            rows(half_step)
            rows(full_step)
            rows(low_step)

    for place, (i, j) in enumerate(places):
        back[own, place] = (total[spans(i, j)] * inverse).astype(jnp.bfloat16)
    lane = lax.broadcasted_iota(jnp.int32, (8, 128), 1)
    size_out[own] = jnp.where(lane >= 0, inverse, 0.0)
    mail.post(back.at[own], back.at[own], core)
    mail.post(size_out.at[own], size_out.at[own], core)
    if y_bits:
        over_size = mail.post(size_out.at[own], size_out.at[own], y_bits[0])
        over_y = mail.post(back.at[own], back.at[own], y_bits[0])
        yield mail.due
        mail.take(over_y)
        mail.take(over_size)
        mail.post(back.at[other_up], back.at[other_up], core)
        mail.post(size_out.at[other_up], size_out.at[other_up], core)


def muon_factors(lows, factor, table):
    width = lows[0].shape[1]
    block = 256
    count = len(upper_blocks(width // block))
    lane_bits = lanes()
    extra = max(len(lane_bits[2]) - 1, 0)
    vmem = pl.BlockSpec(memory_space=pltpu.VMEM)
    square = (width, width)
    height = table[0].shape[0]
    tile = next(size for size in (160, 80, 40, 16, 8) if height % size == 0)
    any_space = pl.BlockSpec(memory_space=pl.ANY)
    whole = jax.ShapeDtypeStruct(table[0].shape, jnp.float32)
    rests, sizes, *table_next = pl.pallas_call(
        functools.partial(muon_kernel, lane_bits),
        out_shape=(
            jax.ShapeDtypeStruct((4,) + square, jnp.bfloat16),
            jax.ShapeDtypeStruct((4, 8, 128), jnp.float32),
            whole,
            whole,
            whole,
        ),
        in_specs=[vmem] * 5 + [any_space] * 4,
        out_specs=(vmem, vmem, any_space, any_space, any_space),
        scratch_shapes=[
            pltpu.VMEM((4, count, block, block), jnp.float32),
            pltpu.VMEM((3 + extra, count, block, block), jnp.bfloat16),
            pltpu.VMEM((3 + extra, count, block, block), jnp.bfloat16),
            pltpu.VMEM((4, count, block, block), jnp.bfloat16),
        ]
        + [pltpu.VMEM(square, jnp.float32) for _ in range(3)]
        + [pltpu.VMEM(square, jnp.bfloat16) for _ in range(3)]
        + mail_sems(32)
        + [
            pltpu.VMEM((2, 4, tile, width), jnp.float32),
            pltpu.VMEM((2, 3, tile, width), jnp.float32),
            pltpu.SemaphoreType.DMA((2, 4)),
            pltpu.SemaphoreType.DMA((2, 3)),
        ],
        compiler_params=pltpu.CompilerParams(
            collective_id=9, has_side_effects=True, vmem_limit_bytes=56 * MIB
        ),
        name="muon_factors",
    )(*lows, jnp.full((8, 128), factor), *table)
    return rests, sizes[:, 0, 0], table_next


def on_device(
    token_ids,
    targets,
    joint_weight,
    output_weight,
    expand_weight,
    reduce_weight,
    joint_velocity,
    output_velocity,
    expand_velocity,
    reduce_velocity,
    embedding,
    embed_moment,
    embed_square,
    positions,
    position_moment,
    position_square,
    norm_gains,
    gain_moment,
    gain_square,
    biases,
    bias_moment,
    bias_square,
):
    core, x_bits, y_bits, z_bits = lanes()
    groups = lax.axis_size("narrow")
    wides = lax.axis_size("wide")
    across = 1 << len(x_bits)
    model_width = embedding.shape[1]
    shard_rows = embedding.shape[0]
    tokens = token_ids.shape[0] * LENGTH
    bias_rows = biases.reshape(-1, model_width)

    own_rows = embedding.astype(jnp.bfloat16)
    labels = jnp.concatenate([token_ids.reshape(-1, 128), targets.reshape(-1, 128)])
    spare = -labels.shape[0] % 8
    labels = exchange(jnp.pad(labels, ((0, spare), (0, 0))), 0, "label_share")
    ids_all = labels[:, : tokens // 128].reshape(-1, tokens)
    lines = tokens // 128
    own_block = lax.axis_index("wide") * groups + lax.axis_index("narrow")
    wides, ups = chip_sizes()
    pairs = ids_all.reshape(wides, ups, 2, tokens)
    other_first = lax.axis_index("narrow") % 2 == 1
    ids_chips = jnp.where(other_first, lax.rev(pairs, (2,)), pairs).reshape(wides * ups, -1)
    plan, rounds = token_plan(ids_chips, shard_rows)

    def serve(slot_rows):
        served = one_hot(slot_rows, shard_rows)
        return plain(served, own_rows).astype(jnp.bfloat16).reshape(-1, slots(), model_width)

    masters = (joint_weight, output_weight, expand_weight, reduce_weight)
    served, wanted = plan(0)
    token_rows = serve(served)
    sent_rows, token_rows = lax.optimization_barrier((own_rows, token_rows))
    tables = [sent_rows]
    for bit in x_bits:
        tables = tables + [swap(part, bit) for part in tables]
    weights, token_rows = load_all([master.astype(jnp.bfloat16) for master in masters], token_rows)

    def fetch(turn):
        more, places = plan(turn)
        got = swap_rows(serve(more))
        return plain(places, jnp.stack([got, swap(got, core)]).reshape(-1, model_width))

    embedded = later_rounds(rounds, fetch, plain(wanted, token_rows.reshape(-1, model_width)))

    block_masks = jnp.array(group_masks())
    targets_group = labels[block_masks, lines : 2 * lines].reshape(-1, 128)
    table_mask = groups * (across - 1) + 1
    differ = jnp.bitwise_xor(targets_group // shard_rows, own_block)
    is_owned = (targets_group >= 0) & (jnp.bitwise_and(differ, ~table_mask) == 0)
    place = (differ % 2) * across + (differ // groups) % across
    rows_targets = jnp.where(is_owned, place * shard_rows + targets_group % shard_rows, -1)
    final_low, *saved = layer_forward(embedded, positions, norm_gains, bias_rows, weights)
    group_rows, table = spread(final_low, tables)
    blocks = len(group_masks())
    exps, maxima, stats = head_scores(group_rows, table, rows_targets, blocks)
    logs, losses = merge_stats(stats, targets_group)
    loss_part = jnp.sum(losses)
    slopes, final_part = head_slopes(exps, maxima, logs, rows_targets, table)
    final_grad, table_sum, passed = head_back(
        final_part.reshape(-1, tokens, model_width), slopes, group_rows
    )
    for bit in reversed(x_bits):
        passed = swap(passed, bit)
        if bit != x_bits[0]:
            table_sum = table_sum + passed.astype(jnp.float32)
            half = table_sum.shape[0] // 2
            table_sum, passed = table_sum[:half], table_sum[half:].astype(jnp.bfloat16)
    (front, expand_sum, reduce_sum), small, row_sums, squares, low_grad = back_reduce(
        final_grad, norm_gains, bias_rows, saved, weights, wanted
    )
    count_part = jnp.sum((targets >= 0).astype(jnp.float32))

    def bundle(places):
        both = outer_sum(places, low_grad).astype(jnp.bfloat16)
        both = both.reshape(2, -1, slots(), model_width)
        other = swap(both[1], core)
        return (both[0].astype(jnp.float32) + other.astype(jnp.float32)).astype(jnp.bfloat16)

    joint_rows = joint_weight.shape[0]
    def give(turn):
        more, places = plan(turn)
        got = swap_rows(bundle(places)).reshape(-1, model_width)
        return outer_sum(one_hot(more, shard_rows), got)

    table_sum = later_rounds(rounds, give, table_sum)
    places = jnp.stack([loss_part, count_part]).reshape(1, 2)
    table_sum, scalars = table_norm(
        table_sum,
        passed,
        served,
        row_sums.reshape(-1, model_width),
        small,
        squares,
        jnp.pad(places, ((0, 7), (0, 126))),
    )
    matrix_total = [
        part.astype(jnp.float32)
        for part in (front[:joint_rows], front[joint_rows:], expand_sum, reduce_sum)
    ]
    small = small[: 14 + LENGTH]
    loss_sum, loss_count, squares = scalars[0, 0], scalars[0, 1], scalars[0, 2]
    gain_grad, position_grad = small[:3], small[14:]
    bias_grad = small[3:14].reshape(-1)
    grad_norm = jnp.sqrt(squares) / loss_count
    factor = jnp.minimum(1.0, CLIP / (grad_norm + 1e-06)) / loss_count
    previous = (joint_velocity, output_velocity, expand_velocity, reduce_velocity)
    carried = tuple(
        (MOMENTUM * before + gradient * factor for before, gradient in zip(previous, matrix_total))
    )
    lows = [moment.astype(jnp.bfloat16) for moment in carried]
    rests, inverses, table_out = muon_factors(
        lows, factor, (embedding, embed_moment, embed_square, table_sum)
    )
    updated = []
    for number, (master, moment) in enumerate(zip(masters, carried)):
        orth = moment * (NS_A**NS_STEPS * inverses[number]) + plain(
            lows[number], rests[number]
        )
        shape_factor = math.sqrt(max(1.0, master.shape[0] * groups / master.shape[1]))
        updated.append(master * (1 - MUON_RATE * DECAY) - MUON_RATE * shape_factor * orth)
    place_out = adam_step(
        positions, position_moment, position_square, position_grad * factor, PLACE_RATE, DECAY
    )
    gain_out = adam_step(norm_gains, gain_moment, gain_square, gain_grad * factor, SMALL_RATE, 0.0)
    bias_out = adam_step(biases, bias_moment, bias_square, bias_grad * factor, SMALL_RATE, 0.0)
    return (
        loss_sum,
        loss_count,
        grad_norm,
        updated[0],
        updated[1],
        updated[2],
        updated[3],
        carried[0],
        carried[1],
        carried[2],
        carried[3],
        table_out[0],
        table_out[1],
        table_out[2],
        place_out[0],
        place_out[1],
        place_out[2],
        gain_out[0],
        gain_out[1],
        gain_out[2],
        bias_out[0],
        bias_out[1],
        bias_out[2],
    )


def solution(mesh):
    in_specs = (
        P(("wide", "narrow"), None),
        P(("wide", "narrow"), None),
        P("narrow", None),
        P("narrow", None),
        P("narrow", None),
        P("narrow", None),
        P("narrow", None),
        P("narrow", None),
        P("narrow", None),
        P("narrow", None),
        P(("wide", "narrow"), None),
        P(("wide", "narrow"), None),
        P(("wide", "narrow"), None),
        P(),
        P(),
        P(),
        P(),
        P(),
        P(),
        P(),
        P(),
        P(),
    )
    out_specs = (
        P(),
        P(),
        P(),
        P("narrow", None),
        P("narrow", None),
        P("narrow", None),
        P("narrow", None),
        P("narrow", None),
        P("narrow", None),
        P("narrow", None),
        P("narrow", None),
        P(("wide", "narrow"), None),
        P(("wide", "narrow"), None),
        P(("wide", "narrow"), None),
        P(),
        P(),
        P(),
        P(),
        P(),
        P(),
        P(),
        P(),
        P(),
    )
    return jax.shard_map(
        on_device, mesh=mesh, in_specs=in_specs, out_specs=out_specs, check_vma=False
    )
```
